32 devices in a mesh: lat: 8 (over z, y), lvl: 4 (over x, core).
Axes of the slice: x: 2, y: 2, z: 4, core: 2. Of those that a mesh axis runs over, the one named last changes fastest.
Arguments:
- fields: bfloat16 [80, 2, 256, 192], P('lvl', None, 'lat'), may hold values from -6 to 6
- targets: bfloat16 [80, 2, 256, 192], P('lvl', None, 'lat'), may hold values from -6 to 6
- ocean_depth: int32 [256, 192], P('lat', 'lvl'), may hold values from 0 to 19, as said below
- thickness_class: int32 [19], replicated, may hold values from 1 to 8
- params: float32 [2306304], P(('lat', 'lvl'))
- moment1: float32 [2306304], P(('lat', 'lvl'))
- moment2: float32 [2306304], P(('lat', 'lvl')), as said below
Outputs:
- loss_sum: float32 [], replicated
- loss_count: float32 [], replicated
- grad_norm: float32 [], replicated
- new_params: float32 [2306304], P(('lat', 'lvl'))
- new_moment1: float32 [2306304], P(('lat', 'lvl'))
- new_moment2: float32 [2306304], P(('lat', 'lvl'))
The draws below stay inside these ranges and needn't reach their ends.
Inputs may be any that keep to these rules, and one draw needn't show every extreme that they name: `ocean_depth`: land cells are 0; every draw has a land cell and a cell with all 19 levels. `moment2`: all entries positive.
All inputs are finite; a program needn't handle non-finite values.
Results may differ from the reference program's by a relative error of at most 0.0045.
Values may be sent and summed in bfloat16 or wider, within the bound.
No kernel may reach another device: no remote copies, remote signals or barrier semaphores. Data moves between devices by JAX's collectives and lax.ppermute only.
A program may use at most 192 MiB of HBM per device.

```python
import math
import jax
import jax.numpy as jnp
from jax import lax

CIN = 80
WIDTH = 200
EXPAND = 800
WIDTH2 = 400
EXPAND2 = 1600
KSIZE = 7
LEVELS = 19
BATCH = 2
STEP = 10
H = 256
W = 192
NPARAM = 2306280
PTOTAL = 2306304


def draw_ocean_depth(key, part):
    key = jax.random.fold_in(key, 11)
    first, second = jax.random.split(key)
    rows = jnp.arange(H, dtype=jnp.int32)[:, None]
    cols = jnp.arange(W, dtype=jnp.int32)[None, :]
    limit = 15 + 45 * rows // H + 30 * cols // W
    rolls = jax.random.randint(first, (H, W), 0, 100)
    levels = jax.random.randint(second, (H, W), 1, LEVELS + 1)
    depth = jnp.where(rolls < limit, levels, 0)
    return depth.at[0, 0].set(0).at[H - 1, W - 1].set(LEVELS).astype(jnp.int32)


def block_table(chans, hidden):
    return [(chans * KSIZE * KSIZE, 0.0, 1.0 / KSIZE), (chans, 1.0, 0.1), (chans, 0.0, 0.3), (hidden * chans, 0.0, chans ** (-0.5)), (hidden, 0.0, 0.3), (chans * hidden, 0.0, hidden ** (-0.5)), (chans, 0.0, 0.3)]


def draw_params(key, part):
    key = jax.random.fold_in(key, 12)
    noise = jax.random.normal(key, (PTOTAL,), jnp.float32)
    index = jnp.arange(PTOTAL, dtype=jnp.int32)
    segments = [(WIDTH * CIN, 0.0, CIN ** (-0.5))] + block_table(WIDTH, EXPAND) + [(WIDTH2 * 4 * WIDTH, 0.0, (4 * WIDTH) ** (-0.5)), (WIDTH2, 0.0, 0.3)] + block_table(WIDTH2, EXPAND2) + [(4 * WIDTH * WIDTH2, 0.0, WIDTH2 ** (-0.5)), (WIDTH, 0.0, 0.3), (CIN * WIDTH, 0.0, WIDTH ** (-0.5)), (CIN, 0.0, 0.3)]
    base = jnp.zeros((PTOTAL,), jnp.float32)
    spread = jnp.zeros((PTOTAL,), jnp.float32)
    start = 0
    for amount, centre, scale in segments:
        inside = (index >= start) & (index < start + amount)
        base = jnp.where(inside, centre, base)
        spread = jnp.where(inside, scale, spread)
        start += amount
    return base + spread * noise


def draw_moment1(key, part):
    key = jax.random.fold_in(key, 13)
    return 0.0011 / NPARAM ** 0.5 * jax.random.normal(key, (PTOTAL,), jnp.float32)


def draw_moment2(key, part):
    key = jax.random.fold_in(key, 14)
    lowest = jnp.log(1e-07 / NPARAM)
    expo = jax.random.uniform(key, (PTOTAL,), jnp.float32, lowest, lowest + jnp.log(4.0))
    return jnp.exp(expo)


def plant(values, key, smallest, high):
    shape = values.shape
    index_at = [jax.random.randint(jax.random.fold_in(key, axis), (), 0, shape[axis]) for axis in range(len(shape))]
    values = values.at[tuple(index_at)].set(smallest)
    longest = shape.index(max(shape))
    index_at[longest] = (index_at[longest] + 1) % shape[longest]
    return values.at[tuple(index_at)].set(high)


def steps_of(own_key, dims, shards, smallest, largest):
    def one(dim, shards_of):
        steps = jax.random.uniform(jax.random.fold_in(jax.random.fold_in(own_key, 6), dim), (shards_of,), jnp.float32, smallest / len(shards), largest / len(shards))
        return jnp.repeat(jnp.exp(steps), dims[dim] // shards_of).reshape((-1,) + (1,) * (len(dims) - dim - 1))

    factor_of = one(*shards[0])
    for cut in shards[1:]:
        factor_of = factor_of * one(*cut)
    return factor_of


def gaussian(own_key, extent, deviation, reach, cuts=(), kind=jnp.bfloat16):
    values = jax.random.normal(own_key, extent, jnp.float32) * deviation
    if len(cuts) > 0:
        values = steps_of(own_key, extent, cuts, -0.22, 0.18) * values
    return jnp.clip(values, min=-reach, max=reach).astype(kind)


def setup_inputs(seed: int = 0) -> dict:
    splits = jax.random.split(jax.random.key(seed), 8)
    return {
        "fields": gaussian(splits[0], (CIN, BATCH, H, W), 1.0, 6.0, ((0, 4), (2, 8))),
        "targets": gaussian(splits[1], (CIN, BATCH, H, W), 1.0, 6.0, ((0, 4), (2, 8))),
        "ocean_depth": draw_ocean_depth(jax.random.fold_in(splits[7], 71), 0),
        "thickness_class": plant(jax.random.randint(splits[3], (LEVELS,), 1, 9), jax.random.fold_in(splits[3], 1), 1, 8).astype(jnp.int32),
        "params": draw_params(jax.random.fold_in(splits[7], 71), 0),
        "moment1": draw_moment1(jax.random.fold_in(splits[7], 71), 0),
        "moment2": draw_moment2(jax.random.fold_in(splits[7], 71), 0),
    }


CLIP = 0.01
LRATE = 0.05
BETA_ONE = 0.9
BETA_TWO = 0.999
ADAM_EPS = 1e-08
DECAY = 0.1
HEAT_WEIGHT = 40.0
NORM_EPS = 1e-05

@jax.custom_vjp
def low(v):
    return lax.optimization_barrier(v.astype(jnp.bfloat16)).astype(jnp.float32)

@jax.custom_vjp
def low_back(v):
    return v

def low_keep(v):
    return (low(v), None)

def low_pass(ocean_kept, grad):
    return (grad,)

def back_keep(v):
    return (v, None)

def back_low(ocean_kept, grad):
    return (low(grad),)
low.defvjp(low_keep, low_pass)
low_back.defvjp(back_keep, back_low)

def block_shapes(chans, hidden):
    return [(chans, KSIZE * KSIZE), (chans,), (chans,), (hidden, chans), (hidden,), (chans, hidden), (chans,)]

def pieces_of(flat):
    shapes = [(WIDTH, CIN)] + block_shapes(WIDTH, EXPAND) + [(WIDTH2, 4 * WIDTH), (WIDTH2,)] + block_shapes(WIDTH2, EXPAND2) + [(4 * WIDTH, WIDTH2), (WIDTH,), (CIN, WIDTH), (CIN,)]
    result = []
    start = 0
    for shape in shapes:
        amount = math.prod(shape)
        result.append(flat[start:start + amount].reshape(shape))
        start += amount
    return result

def channel_tables(depth, thick):
    channel = jnp.arange(CIN, dtype=jnp.int32)
    level = jnp.where(channel < 4 * LEVELS, channel // 4, 0)
    onehot = (level[:, None] == jnp.arange(LEVELS, dtype=jnp.int32)[None, :]).astype(jnp.float32)
    thickf = thick.astype(jnp.float32)
    chosen = ((channel % 4 == 0) & (channel < 4 * LEVELS)).astype(jnp.float32)
    heat_take = chosen * lax.optimization_barrier(jnp.sum(onehot * thickf[None, :], axis=1)) / jnp.sum(thickf)
    ocean = (level[:, None, None] < depth[None]).astype(jnp.float32)[:, None]
    surface_field = (depth > 0).astype(jnp.float32)[None]
    coarse = lax.optimization_barrier(jnp.max(depth.reshape(depth.shape[0] // 2, 2, depth.shape[1] // 2, 2), axis=(1, 3)))
    surface_two = (coarse > 0).astype(jnp.float32)[None]
    return (heat_take, ocean, surface_field, surface_two)

def depthwise(border_padded, kernel, rows, cols):
    total = jnp.zeros((border_padded.shape[0], border_padded.shape[1], rows, cols), jnp.float32)
    for p in range(KSIZE):
        for q in range(KSIZE):
            total = total + kernel[:, p * KSIZE + q][:, None, None, None] * border_padded[:, :, p:p + rows, q:q + cols]
    return total

def to_patches(grid):
    chans, batch, rows, cols = grid.shape
    split = grid.reshape(chans, batch, rows // 2, 2, cols // 2, 2)
    return split.transpose(0, 3, 5, 1, 2, 4).reshape(chans * 4, -1)

def from_patches(rows_of, batch, rows, cols):
    chans = rows_of.shape[0] // 4
    split = rows_of.reshape(chans, 2, 2, batch, rows, cols)
    return split.transpose(0, 3, 4, 1, 5, 2).reshape(chans, batch, rows * 2, cols * 2)

def mat_product(left, right):
    return jnp.dot(left, right, precision=lax.Precision.HIGHEST, preferred_element_type=jnp.float32)

def block(hin, weights, surface_field, ocean_cell_total):
    kernel, norm_gain, shift, up, up_bias, down, down_bias = weights
    chans, batch, rows, cols = hin.shape
    border_padded = jnp.pad(hin, ((0, 0), (0, 0), (3, 3), (3, 3)))
    depthwise_conv_output = low_back(depthwise(border_padded, kernel, rows, cols))
    ocean_mean = lax.optimization_barrier(jnp.sum(depthwise_conv_output * surface_field, axis=(1, 2, 3))) / ocean_cell_total
    var = lax.optimization_barrier(jnp.sum(depthwise_conv_output * depthwise_conv_output * surface_field, axis=(1, 2, 3))) / ocean_cell_total - ocean_mean * ocean_mean
    inverse_deviation = lax.rsqrt(var + NORM_EPS)
    normalized_output = (depthwise_conv_output - ocean_mean[:, None, None, None]) * (inverse_deviation * norm_gain)[:, None, None, None] + shift[:, None, None, None]
    normalized_output = low(normalized_output).reshape(chans, -1)
    act = low_back(mat_product(up, normalized_output) + up_bias[:, None])
    gelu_gated = low(jax.nn.gelu(act))
    branch = low_back(mat_product(down, gelu_gated) + down_bias[:, None])
    return low(hin + branch.reshape(hin.shape))

def forward(flat, fields, targets, tables, count, ocean_cell_total, cells_two):
    heat_take, ocean, surface_field, surface_two = tables
    parts = pieces_of(low(flat))
    stem, downs, downs_bias, ups, ups_bias, head, head_bias = (parts[0], parts[8], parts[9], parts[17], parts[18], parts[19], parts[20])
    shape = fields.shape
    batch, rows, cols = (shape[1], shape[2], shape[3])
    hzero = low_back(low(mat_product(stem, fields.reshape(CIN, -1)))).reshape(WIDTH, batch, rows, cols)
    hone = block(hzero, parts[1:8], surface_field, ocean_cell_total)
    coarse = low_back(low(mat_product(downs, to_patches(hone)) + downs_bias[:, None]))
    coarse = coarse.reshape(WIDTH2, batch, rows // 2, cols // 2)
    htwo = block(coarse, parts[10:17], surface_two, cells_two)
    upped = mat_product(ups, htwo.reshape(WIDTH2, -1)) + jnp.repeat(ups_bias, 4)[:, None]
    upped = low_back(from_patches(upped, batch, rows // 2, cols // 2))
    skip = low(hone + upped).reshape(WIDTH, -1)
    out = low_back(mat_product(head, skip) + head_bias[:, None]).reshape(shape)
    err = out - targets
    heat = lax.optimization_barrier(jnp.sum(heat_take[:, None, None, None] * ocean * err, axis=0))
    loss_total = jnp.sum(ocean * err * err) + HEAT_WEIGHT * jnp.sum(surface_field * heat * heat)
    return (loss_total / count, loss_total)

def reference(fields, targets, ocean_depth, thickness_class, params, moment1, moment2):
    tables = channel_tables(ocean_depth, thickness_class)
    count = BATCH * jnp.sum(tables[1])
    ocean_cell_total = BATCH * jnp.sum(tables[2])
    cells_two = BATCH * jnp.sum(tables[3])
    fieldf = fields.astype(jnp.float32)
    targetf = targets.astype(jnp.float32)
    value, pull, loss_total = jax.vjp(lambda flat: forward(flat, fieldf, targetf, tables, count, ocean_cell_total, cells_two), params, has_aux=True)
    grad = pull(jnp.ones((), jnp.float32))[0]
    norm = jnp.sqrt(jnp.sum(grad * grad))
    clipped = grad * jnp.minimum(1.0, CLIP / norm)
    first = BETA_ONE * moment1 + (1.0 - BETA_ONE) * clipped
    second = BETA_TWO * moment2 + (1.0 - BETA_TWO) * clipped * clipped
    ratio = first / (1.0 - BETA_ONE ** STEP) / (jnp.sqrt(second / (1.0 - BETA_TWO ** STEP)) + ADAM_EPS)
    updated = params - LRATE * (ratio + DECAY * params)
    return (loss_total, count, norm, updated, first, second)
```

```python
import math

import jax
import jax.numpy as jnp
from jax import lax
from jax.sharding import PartitionSpec as P

CIN = 80
WIDTH = 200
EXPAND = 800
WIDTH2 = 400
EXPAND2 = 1600
KSIZE = 7
LEVELS = 19
STEP = 10


CLIP = 0.01
LRATE = 0.05
BETA_ONE = 0.9
BETA_TWO = 0.999
ADAM_EPS = 1e-08
DECAY = 0.1
HEAT_WEIGHT = 40.0
NORM_EPS = 1e-05

AXES = ("lat", "lvl")


def bit_list():
    bits = []
    for axis in AXES:
        count = lax.axis_size(axis)
        step = count // 2
        while step >= 1:
            bits.append((axis, count, step))
            step //= 2
    return bits


def exchange(values, axis, count, step):
    return lax.ppermute(values, axis, [(i, i ^ step) for i in range(count)])


def gather_blocks(block):
    blocks = block[None]
    for axis, count, step in bit_list():
        other = exchange(blocks, axis, count, step)
        high = (lax.axis_index(axis) // step) % 2 == 1
        blocks = jnp.stack(
            [jnp.where(high, other, blocks), jnp.where(high, blocks, other)], axis=1
        ).reshape((-1,) + block.shape)
    return blocks


def scatter_blocks(blocks):
    for turn, (axis, count, step) in enumerate(reversed(bit_list())):
        pairs = blocks.reshape((blocks.shape[0] // 2, 2) + blocks.shape[1:])
        high = (lax.axis_index(axis) // step) % 2 == 1
        keep = jnp.where(high, pairs[:, 1], pairs[:, 0])
        send = jnp.where(high, pairs[:, 0], pairs[:, 1])
        if turn > 0:
            send = send.astype(jnp.bfloat16)
        blocks = keep + exchange(send, axis, count, step).astype(jnp.float32)
    return blocks[0]


def total_of(*values):
    flat = jnp.concatenate([v.reshape(-1).astype(jnp.float32) for v in values])
    amount = flat.shape[0]
    rows = -(-amount // 1024) * 8
    tile = jnp.pad(flat, (0, rows * 128 - amount)).reshape(1, rows, 128)
    count = lax.axis_size(AXES)
    got = lax.all_to_all(jnp.broadcast_to(tile, (count, rows, 128)), AXES, 0, 0, tiled=True)
    summed = jnp.sum(got, axis=0).reshape(-1)
    result = []
    start = 0
    for v in values:
        result.append(summed[start : start + v.size].reshape(v.shape))
        start += v.size
    return result


def padded(cells, sides, width):
    for axis, dim in sides:
        count = lax.axis_size(axis)
        ends = count - 1
        head = lax.slice_in_dim(cells, 0, width, axis=dim)
        tail = lax.slice_in_dim(cells, cells.shape[dim] - width, cells.shape[dim], axis=dim)
        cells = jnp.concatenate(
            [
                lax.ppermute(tail, axis, [(i, (i + 1) % count) for i in range(ends)]),
                cells,
                lax.ppermute(head, axis, [((i + 1) % count, i) for i in range(ends)]),
            ],
            axis=dim,
        )
    return cells


def block_shapes(chans, hidden):
    return [
        (chans, KSIZE * KSIZE),
        (chans,),
        (chans,),
        (hidden, chans),
        (hidden,),
        (chans, hidden),
        (chans,),
    ]


def pieces_of(flat):
    shapes = (
        [(WIDTH, CIN)]
        + block_shapes(WIDTH, EXPAND)
        + [(WIDTH2, 4 * WIDTH), (WIDTH2,)]
        + block_shapes(WIDTH2, EXPAND2)
        + [(4 * WIDTH, WIDTH2), (WIDTH,), (CIN, WIDTH), (CIN,)]
    )
    result = []
    start = 0
    for shape in shapes:
        amount = math.prod(shape)
        result.append(flat[start : start + amount].reshape(shape))
        start += amount
    return result


def channel_tables(depth, thick):
    channel = jnp.arange(CIN, dtype=jnp.int32)
    level = jnp.where(channel < 4 * LEVELS, channel // 4, 0)
    onehot = (level[:, None] == jnp.arange(LEVELS, dtype=jnp.int32)[None, :]).astype(jnp.float32)
    thickf = thick.astype(jnp.float32)
    chosen = ((channel % 4 == 0) & (channel < 4 * LEVELS)).astype(jnp.float32)
    heat_take = chosen * jnp.sum(onehot * thickf[None, :], axis=1) / jnp.sum(thickf)
    ocean = (level[:, None, None] < depth[None]).astype(jnp.float32)[:, None]
    surface_field = (depth > 0).astype(jnp.float32)[None]
    coarse = jnp.max(depth.reshape(depth.shape[0] // 2, 2, depth.shape[1] // 2, 2), axis=(1, 3))
    surface_two = (coarse > 0).astype(jnp.float32)[None]
    return (heat_take, ocean, surface_field, surface_two)


def depthwise(border_padded, kernel, rows, cols):
    total = jnp.zeros((border_padded.shape[0], border_padded.shape[1], rows, cols), jnp.float32)
    for p in range(KSIZE):
        for q in range(KSIZE):
            total = (
                total
                + kernel[:, p * KSIZE + q][:, None, None, None]
                * border_padded[:, :, p : p + rows, q : q + cols]
            )
    return total


def to_patches(grid):
    chans, batch, rows, cols = grid.shape
    split = grid.reshape(chans, batch, rows // 2, 2, cols // 2, 2)
    return split.transpose(0, 3, 5, 1, 2, 4).reshape(chans * 4, -1)


def from_patches(rows_of, batch, rows, cols):
    chans = rows_of.shape[0] // 4
    split = rows_of.reshape(chans, 2, 2, batch, rows, cols)
    return split.transpose(0, 3, 4, 1, 5, 2).reshape(chans, batch, rows * 2, cols * 2)


def mult(left, right):
    return jnp.dot(left, right, preferred_element_type=jnp.float32)


def contract_cells(left, right):
    return lax.dot_general(
        left, right, (((1,), (1,)), ((), ())), preferred_element_type=jnp.float32
    )


def contract_rows(left, right):
    return lax.dot_general(
        left, right, (((0,), (0,)), ((), ())), preferred_element_type=jnp.float32
    )


def block_forward(border_padded, centre, weights, surface_field, extra):
    kernel, norm_gain, shift, up, up_bias, down, down_bias = weights
    chans, batch, rows, cols = centre.shape
    depthwise_conv_output = depthwise(border_padded, kernel.astype(jnp.float32), rows, cols)
    sums, squares, ocean_cell_total, extra_total = total_of(
            jnp.sum(depthwise_conv_output * surface_field, axis=(1, 2, 3)),
            jnp.sum(depthwise_conv_output * depthwise_conv_output * surface_field, axis=(1, 2, 3)),
            batch * jnp.sum(surface_field),
            extra,
    )
    ocean_mean = sums / ocean_cell_total
    inverse_deviation = lax.rsqrt(squares / ocean_cell_total - ocean_mean * ocean_mean + NORM_EPS)
    mean_removed = depthwise_conv_output - ocean_mean[:, None, None, None]
    standardized_input = mean_removed * inverse_deviation[:, None, None, None]
    normalized_output = (
        standardized_input * norm_gain.astype(jnp.float32)[:, None, None, None]
        + shift.astype(jnp.float32)[:, None, None, None]
    )
    normalized_output = normalized_output.astype(jnp.bfloat16).reshape(chans, -1)
    act = mult(up, normalized_output) + up_bias.astype(jnp.float32)[:, None]
    gelu_out, gelu_backward_pull = jax.vjp(jax.nn.gelu, act)
    gelu_gated = gelu_out.astype(jnp.bfloat16)
    branch = mult(down, gelu_gated) + down_bias.astype(jnp.float32)[:, None]
    hout = (centre.astype(jnp.float32) + branch.reshape(centre.shape)).astype(jnp.bfloat16)
    ocean_kept = (
        border_padded,
        depthwise_conv_output,
        mean_removed,
        standardized_input,
        ocean_mean,
        inverse_deviation,
        ocean_cell_total,
        normalized_output,
        gelu_gated,
        gelu_backward_pull,
    )
    return (hout, extra_total, ocean_kept)


def block_backward(grad_hout, ocean_kept, weights, surface_field):
    kernel, norm_gain, shift, up, up_bias, down, down_bias = weights
    (
        border_padded,
        depthwise_conv_output,
        mean_removed,
        standardized_input,
        ocean_mean,
        inverse_deviation,
        ocean_cell_total,
        normalized_output,
        gelu_gated,
        gelu_backward_pull,
    ) = ocean_kept
    chans, batch, rows, cols = depthwise_conv_output.shape
    kernelf = kernel.astype(jnp.float32)
    grad_branch = grad_hout.astype(jnp.bfloat16).reshape(chans, -1)
    g_down = contract_cells(grad_branch, gelu_gated)
    g_down_bias = jnp.sum(grad_branch.astype(jnp.float32), axis=1)
    grad_gated = contract_rows(down, grad_branch)
    grad_act = gelu_backward_pull(grad_gated)[0].astype(jnp.bfloat16)
    g_up = contract_cells(grad_act, normalized_output)
    g_up_bias = jnp.sum(grad_act.astype(jnp.float32), axis=1)
    norm_input_gradient = contract_rows(up, grad_act).reshape(depthwise_conv_output.shape)
    gain_gradient = jnp.sum(norm_input_gradient * standardized_input, axis=(1, 2, 3))
    g_shift = jnp.sum(norm_input_gradient, axis=(1, 2, 3))
    standardized_gradient = norm_input_gradient * norm_gain.astype(jnp.float32)[:, None, None, None]
    total_a, total_b = total_of(
            jnp.sum(standardized_gradient, axis=(1, 2, 3)),
            jnp.sum(standardized_gradient * mean_removed, axis=(1, 2, 3)),
    )
    grad_var = -0.5 * inverse_deviation * inverse_deviation * inverse_deviation * total_b
    grad_first = (-inverse_deviation * total_a - 2.0 * ocean_mean * grad_var) / ocean_cell_total
    grad_second = grad_var / ocean_cell_total
    conv_gradient = standardized_gradient * inverse_deviation[
        :, None, None, None
    ] + surface_field * (
        grad_first[:, None, None, None]
        + 2.0 * (mean_removed + ocean_mean[:, None, None, None]) * grad_second[:, None, None, None]
    )
    conv_gradient = conv_gradient.astype(jnp.bfloat16)
    grad_convf = conv_gradient.astype(jnp.float32)
    kernel_terms = []
    for p in range(KSIZE):
        for q in range(KSIZE):
            kernel_terms.append(
                jnp.sum(
                    border_padded[:, :, p : p + rows, q : q + cols] * grad_convf, axis=(1, 2, 3)
                )
            )
    g_kernel = jnp.stack(kernel_terms, axis=1)
    grad_pad = padded(conv_gradient, (("lat", 2), ("lvl", 3)), 3).astype(jnp.float32)
    flipped = jnp.flip(kernelf.reshape(chans, KSIZE, KSIZE), axis=(1, 2)).reshape(
        chans, KSIZE * KSIZE
    )
    grad_in = grad_hout + depthwise(grad_pad, flipped, rows, cols)
    return (grad_in, [g_kernel, gain_gradient, g_shift, g_up, g_up_bias, g_down, g_down_bias])


def body(fields, targets, ocean_depth, thickness_class, params, moment1, moment2):
    shard_len = params.shape[0]
    room = -(-shard_len // 2048) * 2048
    block = jnp.pad(params.astype(jnp.bfloat16), (0, room - shard_len)).reshape(-1, 128)
    flat_low = gather_blocks(block).reshape(-1, room)[:, :shard_len].reshape(-1)
    parts = pieces_of(flat_low)
    stem, downs, downs_bias, ups, ups_bias, head, head_bias = (
        parts[0],
        parts[8],
        parts[9],
        parts[17],
        parts[18],
        parts[19],
        parts[20],
    )
    fine_weights = parts[1:8]
    coarse_weights = parts[10:17]
    inputs, goal = (
        lax.all_to_all(fields, "lvl", split_axis=3, concat_axis=0, tiled=True),
        lax.all_to_all(targets, "lvl", split_axis=3, concat_axis=0, tiled=True),
    )
    batch, rows, cols = (inputs.shape[1], inputs.shape[2], inputs.shape[3])
    heat_take, ocean, surface_field, surface_two = channel_tables(ocean_depth, thickness_class)
    flat_in = inputs.reshape(CIN, -1)
    hzero = mult(stem, flat_in).astype(jnp.bfloat16).reshape(WIDTH, batch, rows, cols)
    border_padded = padded(hzero, (("lat", 2), ("lvl", 3)), 3).astype(jnp.float32)
    hone, count, kept_fine = block_forward(
        border_padded, hzero, fine_weights, surface_field, batch * jnp.sum(ocean)
    )
    patches = to_patches(hone)
    coarse = (mult(downs, patches) + downs_bias.astype(jnp.float32)[:, None]).astype(jnp.bfloat16)
    coarse = coarse.reshape(WIDTH2, batch, rows // 2, cols // 2)
    coarse_pad = padded(coarse, (("lat", 2), ("lvl", 3)), 3).astype(jnp.float32)
    htwo, unused, kept_coarse = block_forward(
        coarse_pad, coarse, coarse_weights, surface_two, jnp.zeros((), jnp.float32)
    )
    htwo_flat = htwo.reshape(WIDTH2, -1)
    upped = mult(ups, htwo_flat) + jnp.repeat(ups_bias.astype(jnp.float32), 4)[:, None]
    upped = from_patches(upped, batch, rows // 2, cols // 2)
    skip = (hone.astype(jnp.float32) + upped).astype(jnp.bfloat16).reshape(WIDTH, -1)
    out = (mult(head, skip) + head_bias.astype(jnp.float32)[:, None]).reshape(
        CIN, batch, rows, cols
    )
    err = out - goal.astype(jnp.float32)
    heat = jnp.sum(heat_take[:, None, None, None] * ocean * err, axis=0)
    loss_part = jnp.sum(ocean * err * err) + HEAT_WEIGHT * jnp.sum(surface_field * heat * heat)
    grad_out = (
        2.0
        / count
        * ocean
        * (err + HEAT_WEIGHT * heat_take[:, None, None, None] * (surface_field * heat)[None])
    )
    grad_out = grad_out.astype(jnp.bfloat16).reshape(CIN, -1)
    g_head = contract_cells(grad_out, skip)
    g_head_bias = jnp.sum(grad_out.astype(jnp.float32), axis=1)
    grad_skip = contract_rows(head, grad_out).reshape(WIDTH, batch, rows, cols)
    grad_up_rows = to_patches(grad_skip.astype(jnp.bfloat16))
    g_ups = contract_cells(grad_up_rows, htwo_flat)
    g_ups_bias = jnp.sum(
        jnp.sum(grad_up_rows.astype(jnp.float32), axis=1).reshape(WIDTH, 4), axis=1
    )
    grad_two = contract_rows(ups, grad_up_rows).reshape(htwo.shape)
    grad_coarse, g_coarse = block_backward(grad_two, kept_coarse, coarse_weights, surface_two)
    grad_coarse = grad_coarse.astype(jnp.bfloat16).reshape(WIDTH2, -1)
    g_downs = contract_cells(grad_coarse, patches)
    g_downs_bias = jnp.sum(grad_coarse.astype(jnp.float32), axis=1)
    grad_hone = grad_skip + from_patches(
        contract_rows(downs, grad_coarse), batch, rows // 2, cols // 2
    )
    grad_zero, g_fine = block_backward(grad_hone, kept_fine, fine_weights, surface_field)
    grad_zero = grad_zero.astype(jnp.bfloat16).reshape(WIDTH, -1)
    g_stem = contract_cells(grad_zero, flat_in)
    pieces = (
        [g_stem]
        + g_fine
        + [g_downs, g_downs_bias]
        + g_coarse
        + [g_ups, g_ups_bias, g_head, g_head_bias]
    )
    joined = jnp.concatenate([piece.reshape(-1) for piece in pieces])
    joined = jnp.pad(joined, (0, shard_len * lax.axis_size(AXES) - joined.shape[0]))
    joined = jnp.pad(joined.reshape(-1, shard_len), ((0, 0), (0, room - shard_len)))
    mine = scatter_blocks(joined.reshape(-1, room // 128, 128)).reshape(-1)[:shard_len]
    loss_total, square_sum = total_of(loss_part, jnp.sum(mine * mine))
    norm = jnp.sqrt(square_sum)
    clipped = mine * jnp.minimum(1.0, CLIP / norm)
    first = BETA_ONE * moment1 + (1.0 - BETA_ONE) * clipped
    second = BETA_TWO * moment2 + (1.0 - BETA_TWO) * clipped * clipped
    ratio = first / (1.0 - BETA_ONE**STEP) / (jnp.sqrt(second / (1.0 - BETA_TWO**STEP)) + ADAM_EPS)
    updated = params - LRATE * (ratio + DECAY * params)
    return (loss_total, count, norm, updated, first, second)


def solution(mesh):
    in_specs = (
        P("lvl", None, "lat", None),
        P("lvl", None, "lat", None),
        P("lat", "lvl"),
        P(),
        P(("lat", "lvl")),
        P(("lat", "lvl")),
        P(("lat", "lvl")),
    )
    out_specs = (P(), P(), P(), P(("lat", "lvl")), P(("lat", "lvl")), P(("lat", "lvl")))
    return jax.shard_map(body, mesh=mesh, in_specs=in_specs, out_specs=out_specs, check_vma=False)
```

```python
import math

import jax
import jax.numpy as jnp
from jax import lax
from jax.experimental import pallas as pl
from jax.experimental.pallas import tpu as pltpu
from jax.sharding import PartitionSpec as P

CIN = 80
WIDTH = 200
EXPAND = 800
WIDTH2 = 400
EXPAND2 = 1600
KSIZE = 7
TAPS = KSIZE * KSIZE
LEVELS = 19
STEP = 10

CLIP = 0.01
LRATE = 0.05
BETA_ONE = 0.9
BETA_TWO = 0.999
ADAM_EPS = 1e-08
DECAY = 0.1
HEAT_WEIGHT = 40.0
NORM_EPS = 1e-05

AXES = ("lat", "lvl")

CI = 128
C1 = 256
H1 = 896
C2 = 512
H2 = 1664
BLOCKS = 8
LANES = 128
REACH = KSIZE // 2
GROUPS = 17

f32 = jnp.float32
bf16 = jnp.bfloat16
VMEM_LIMIT = 60 * 1024 * 1024


def bit_list():
    bits = []
    for axis in AXES:
        count = lax.axis_size(axis)
        step = count // 2
        while step >= 1:
            bits.append((axis, count, step))
            step //= 2
    return bits


def exchange(values, axis, count, step):
    return lax.ppermute(values, axis, [(i, i ^ step) for i in range(count)])


def gather_blocks(block):
    blocks = block[None]
    for axis, count, step in bit_list():
        blocks = jnp.concatenate([blocks, exchange(blocks, axis, count, step)], axis=0)
    return blocks


def scatter_blocks(keep, send):
    for turn, (axis, count, step) in enumerate(reversed(bit_list())):
        if turn > 0:
            half = keep.shape[0] // 2
            keep, send = keep[:half], keep[half:].astype(bf16)
        keep = keep + exchange(send, axis, count, step).astype(f32)
    return keep[0]


def spread(tile):
    count = lax.axis_size(AXES)
    copies = jnp.broadcast_to(tile[None], (count,) + tile.shape)
    return lax.all_to_all(copies, AXES, 0, 0, tiled=True)


def neighbours(axis):
    ends = lax.axis_size(axis) - 1
    return [(i, i + 1) for i in range(ends)], [(i + 1, i) for i in range(ends)]


def with_halo(cells):
    rows, cols, blocks, chans = cells.shape
    bands = blocks // 2
    onward, back = neighbours("lvl")
    left = lax.ppermute(cells[:, cols - REACH :], "lvl", onward)
    right = lax.ppermute(cells[:, :REACH], "lvl", back)
    cells = jnp.concatenate([left, cells, right], axis=1)
    cells = cells.reshape(rows, cols + 2 * REACH, 2, bands, chans)
    onward, back = neighbours("lat")
    above = lax.ppermute(cells[rows - REACH :, :, :, bands - 1], "lat", onward)
    below = lax.ppermute(cells[:REACH, :, :, 0], "lat", back)
    top = jnp.concatenate([above[:, :, :, None], cells[rows - REACH :, :, :, : bands - 1]], axis=3)
    bottom = jnp.concatenate([cells[:REACH, :, :, 1:], below[:, :, :, None]], axis=3)
    return jnp.concatenate([top, cells, bottom], axis=0).reshape(
        rows + 2 * REACH, cols + 2 * REACH, blocks, chans
    )


def to_cells(grid):
    chans, batch, rows, cols = grid.shape
    bands = BLOCKS // batch
    split = grid.reshape(chans, batch, bands, rows // bands, cols)
    return split.transpose(3, 4, 1, 2, 0).reshape(rows // bands, cols, BLOCKS, chans)


def depth_cells(depth, batch):
    rows, cols = depth.shape
    bands = BLOCKS // batch
    split = depth.reshape(bands, rows // bands, cols).transpose(1, 2, 0)
    return jnp.concatenate([split] * batch, axis=2)


def block_shapes(chans, hidden):
    return [
        (chans, TAPS),
        (chans,),
        (chans,),
        (hidden, chans),
        (hidden,),
        (chans, hidden),
        (chans,),
    ]


def shapes_of():
    return (
        [(WIDTH, CIN)]
        + block_shapes(WIDTH, EXPAND)
        + [(WIDTH2, 4 * WIDTH), (WIDTH2,)]
        + block_shapes(WIDTH2, EXPAND2)
        + [(4 * WIDTH, WIDTH2), (WIDTH,), (CIN, WIDTH), (CIN,)]
    )


def fill(values, *shape):
    return jnp.pad(values, [(0, n - m) for n, m in zip(shape, values.shape)])


def nt(left, right):
    return lax.dot_general(left, right, (((1,), (1,)), ((), ())), preferred_element_type=f32)


def nn(left, right):
    return lax.dot_general(left, right, (((1,), (0,)), ((), ())), preferred_element_type=f32)


def tn(left, right):
    return lax.dot_general(left, right, (((0,), (0,)), ((), ())), preferred_element_type=f32)


def rows8(start, amount):
    return pl.ds(pl.multiple_of(start * 8, 8), amount * 8)


def convolve(source, taps, rows, cols, emit, carry, flip=False):
    width = cols + 2 * REACH
    strips = cols // 8

    def strip(turn, carry):
        row = turn // strips
        col = (turn % strips) * 8
        total = jnp.zeros((8, 8, LANES), f32)
        for p in range(KSIZE):
            seen = source[rows8((row + p) * width + col, 8 + 2 * REACH), :]
            seen = seen.reshape(8 + 2 * REACH, 8, LANES)
            for q in range(KSIZE):
                tap = p * KSIZE + q
                total = total + seen[q : q + 8] * taps[TAPS - 1 - tap if flip else tap][None]
        return emit(rows8(row * cols + col, 8), total, carry)

    return lax.fori_loop(0, rows * strips, strip, carry)


def row_sum(values):
    return jnp.sum(values, axis=0, keepdims=True)


def norm_rows(got):
    total = jnp.sum(got[...], axis=0)
    cells = total[2:3]
    mean = total[0:1] / cells
    inverse = lax.rsqrt(total[1:2] / cells - mean * mean + NORM_EPS)
    return mean, inverse, cells, total[3:4]


def gelu_pair(act):
    square = act * act
    flat = 0.7978845608028654
    cube = 0.044715
    bent = jnp.tanh(act * (flat + (flat * cube) * square))
    half = 0.5 + 0.5 * bent
    slope = half + 0.5 * act * (1.0 - bent * bent) * (flat + (3.0 * flat * cube) * square)
    return act * half, slope


def quarter(values, rows, cols, p, q):
    chans = values.shape[-1]
    split = values.reshape(rows // 2, 2, cols // 2, 2, 8, chans)
    return split[:, p, :, q].reshape(rows * cols * 2, chans)


def from_quarters(parts, rows, cols):
    chans = parts[0].shape[-1]
    cells = [part.reshape(rows // 2, cols // 2, 8, chans) for part in parts]
    lines = [jnp.stack(cells[2 * p : 2 * p + 2], axis=2) for p in range(2)]
    return jnp.stack(lines, axis=1).reshape(rows * cols * 8, chans)


def call(kernel, outs, grid=(), ins=None, out_specs=None, scratch=(), flops=0, name=None):
    params = dict(out_shape=[jax.ShapeDtypeStruct(s, t) for s, t in outs])
    if ins:
        params.update(in_specs=ins)
    if grid:
        params.update(grid=grid, out_specs=out_specs)
    return pl.pallas_call(
        kernel,
        scratch_shapes=list(scratch),
        compiler_params=pltpu.CompilerParams(vmem_limit_bytes=VMEM_LIMIT),
        cost_estimate=pl.CostEstimate(flops=flops, bytes_accessed=1000000, transcendentals=0),
        name=name,
        **params,
    )


def whole(*shape):
    return pl.BlockSpec(shape, lambda i: (0,) * len(shape))


def band(rows, cols):
    return pl.BlockSpec((rows, cols), lambda i: (i, 0))


def lane_tile(rows):
    return pl.BlockSpec((rows, LANES), lambda i: (0, i))


TAP_TILE = pl.BlockSpec((TAPS, 8, LANES), lambda i: (0, 0, i))


def conv_sums(source, taps, depth, counts, out, stats, rows, cols, masked=None):
    def emit(place, total, carry):
        flat = total.reshape(64, LANES)
        out[place, :] = flat
        kept = jnp.where(depth[place, :] > 0.0, flat, 0.0)
        if masked is not None:
            masked[place, :] = kept.astype(bf16)
        kept_cells = kept.reshape(8, 8, LANES)
        return (carry[0] + jnp.sum(kept_cells, axis=0), carry[1] + jnp.sum(kept_cells * total, axis=0))

    zero = jnp.zeros((8, LANES), f32)
    first, second = convolve(source, taps, rows, cols, emit, (zero, zero))
    stats[...] = counts[...]
    stats[0:1, :] = row_sum(first)
    stats[1:2, :] = row_sum(second)


def stem_kernel(rows, cols, fields, stem, taps, depth, counts, hzero, out, stats, source):
    width = cols + 2 * REACH

    def line(row, carry):
        place = rows8(row * width, width)
        source[place, :] = nt(fields[place, :], stem[...]).astype(bf16).astype(f32)
        return carry

    lax.fori_loop(0, rows + 2 * REACH, line, 0)
    for row in range(rows):
        hzero[rows8(row * cols, cols), :] = source[
            rows8((row + REACH) * width + REACH, cols), :
        ].astype(bf16)
    conv_sums(source, taps, depth, counts, out, stats, rows, cols)


def coarse_conv_kernel(rows, cols, border, taps, depth, counts, out, masked, stats, source):
    source[...] = border[...].astype(f32)
    conv_sums(source, taps, depth, counts, out, stats, rows, cols, masked)


def fine_kernel(cols, got, conv, hzero, vecs, up, up_bias, down, perm, downs, down_rows, hone, gated, slope, patches, coarse, held):
    mean, inverse, _, _ = norm_rows(got)
    scale = inverse * vecs[0:1]
    for part in range(2):
        place = pl.ds(part * cols * 8, cols * 8)
        normal = ((conv[place, :] - mean) * scale + vecs[1:2]).astype(bf16)
        act = nt(normal, up[...]) + up_bias[...]
        value, bend = gelu_pair(act)
        value = value.astype(bf16)
        gated[place, :] = value
        slope[place, :] = bend.astype(bf16)
        branch = nt(value, down[...]) + vecs[2:3]
        full = (hzero[place, :].astype(f32) + branch).astype(bf16)
        hone[place, :] = full
        held[place, :] = full.astype(f32)
    cells = held[...]
    mixed = jnp.zeros((cols * 4, H1), f32)
    for p in range(2):
        for q in range(2):
            mixed = mixed + nn(quarter(cells, 2, cols, p, q).astype(bf16), perm[p * 2 + q])
    mixed = mixed.astype(bf16)
    patches[...] = mixed
    coarse[...] = (nt(mixed, downs[...]) + down_rows[0:1]).astype(bf16)


def middle_kernel(
    cols, got, conv, cells, vecs, up, up_bias, down, ups, fine_rows, head, last_rows, tables, hone, targets, depth,
    skip_out, top_out, dy_out, ds_out, du_out, dtop_out, dv_out, gated_out, da_out, normal_out, dn_out, dx_out,
    sums, hidden_sums,
):
    mean, inverse, _, ocean_count = norm_rows(got)
    scale = inverse * vecs[0:1]
    centred = conv[...] - mean
    normal = (centred * scale + vecs[1:2]).astype(bf16)
    normal_out[...] = normal
    value, bend = gelu_pair(nt(normal, up[...]) + up_bias[...])
    value = value.astype(bf16)
    gated_out[...] = value
    top = (cells[...].astype(f32) + nt(value, down[...]) + vecs[2:3]).astype(bf16)
    top_out[...] = top
    raised = from_quarters([nt(top, ups[k]) + fine_rows[0:1] for k in range(4)], 2, cols)
    skip = (hone[...].astype(f32) + raised).astype(bf16)
    skip_out[...] = skip
    err = nt(skip, head[...]) + last_rows[0:1] - targets[...].astype(f32)
    deep = depth[...]
    ocean = tables[0:1] < deep
    heat_take = tables[1:2]
    err = jnp.where(ocean, err, 0.0)
    heat = jnp.sum(heat_take * err, axis=1, keepdims=True)
    heat = jnp.where(deep > 0.0, heat, 0.0)
    loss = row_sum(err * err) + (HEAT_WEIGHT / LANES) * row_sum(heat * heat)
    dy = jnp.where(ocean, err + HEAT_WEIGHT * heat_take * heat, 0.0) * (2.0 / ocean_count[:, :LANES])
    dy = dy.astype(bf16)
    dy_out[...] = dy
    ds = nn(dy, head[...])
    ds_out[...] = ds
    dtop = jnp.zeros(top.shape, f32)
    du_sum = jnp.zeros((1, C1), f32)
    for k in range(4):
        du = quarter(ds, 2, cols, k // 2, k % 2).astype(bf16)
        du_out[k] = du
        du_sum = du_sum + row_sum(du.astype(f32))
        dtop = dtop + nn(du, ups[k])
    dtop_out[...] = dtop
    dv = dtop.astype(bf16)
    dv_out[...] = dv
    da = (nn(dv, down[...]) * bend).astype(bf16)
    da_out[...] = da
    dn = nn(da, up[...])
    dn_out[...] = dn
    dx_out[...] = (dn * vecs[0:1]).astype(bf16)

    @pl.when(pl.program_id(0) == 0)
    def _():
        sums[...] = jnp.zeros(sums.shape, f32)
        hidden_sums[...] = jnp.zeros(hidden_sums.shape, f32)

    sums[0:1, :] += row_sum(dn)
    sums[1:2, :] += row_sum(dn * centred)
    sums[2:3, :] += row_sum(dv.astype(f32))
    sums[3:4, :C1] += du_sum
    sums[4:5, :CI] += row_sum(dy.astype(f32))
    sums[5:6, :LANES] += loss
    hidden_sums[0:1, :] += row_sum(da.astype(f32))


def coarse_weights_kernel(da, normal, dv, gated, du, top, dy, skip, up_out, down_out, ups_out, head_out):
    up_out[...] = tn(da[...], normal[...])
    down_out[...] = tn(dv[...], gated[...])
    for k in range(4):
        ups_out[k] = tn(du[k], top[...])
    head_out[...] = tn(dy[...], skip[...])


def backward_rows(got, back, gain):
    mean, inverse, cells, _ = norm_rows(got)
    total = jnp.sum(back[...], axis=0)
    total_a = gain * total[0:1]
    total_b = gain * total[1:2]
    dvar = -0.5 * inverse * inverse * inverse * total_b
    first = (-inverse * total_a - 2.0 * mean * dvar) / cells
    second = 2.0 * dvar / cells
    return inverse, first, second


def coarse_conv_back_kernel(
    rows, cols, got, back, vecs, border, dx, masked, mask, taps, dtop, dcells, taps_out, source, slope
):
    inverse, first, second = backward_rows(got, back, vecs[0:1])
    source[...] = border[...].astype(f32)
    slope[...] = (
        (
            dx[...].astype(f32) * inverse
            + jnp.where(mask[...] > 0.0, first, 0.0)
            + masked[...].astype(f32) * second
        )
        .astype(bf16)
        .astype(f32)
    )

    def emit(place, total, carry):
        dcells[place, :] = (dtop[place, :] + total.reshape(64, LANES)).astype(bf16)
        return carry

    convolve(slope, taps, rows, cols, emit, 0, flip=True)
    taps_out[...] = jnp.zeros(taps_out.shape, f32)
    width = cols + 2 * REACH
    for p in range(KSIZE):

        def line(turn, sums):
            row = turn // (cols // 8)
            col = (turn % (cols // 8)) * 8
            seen = source[rows8((row + p) * width + col, 8 + 2 * REACH), :]
            seen = seen.reshape(8 + 2 * REACH, 8, LANES)
            here = slope[rows8((row + REACH) * width + REACH + col, 8), :].reshape(8, 8, LANES)
            return tuple(sums[q] + jnp.sum(seen[q : q + 8] * here, axis=0) for q in range(KSIZE))

        zero = jnp.zeros((8, LANES), f32)
        sums = lax.fori_loop(0, rows * (cols // 8), line, (zero,) * KSIZE)
        for q in range(KSIZE):
            taps_out[p * KSIZE + q : p * KSIZE + q + 1, :] = row_sum(sums[q])


def fine_back_kernel(
    cols, got, dcells, downs, ds, vecs, conv, slope, up, down, dv_out, da_out, dn_out, normal_out, sums, hidden_sums, coarse_sums
):
    mean, inverse, _, _ = norm_rows(got)
    dlow = dcells[...]
    dh = ds[...] + from_quarters([nn(dlow, downs[k]) for k in range(4)], 2, cols)
    dv = dh.astype(bf16)
    dv_out[...] = dv

    @pl.when(pl.program_id(0) == 0)
    def _():
        sums[...] = jnp.zeros(sums.shape, f32)
        hidden_sums[...] = jnp.zeros(hidden_sums.shape, f32)
        coarse_sums[...] = jnp.zeros(coarse_sums.shape, f32)

    coarse_sums[0:1, :] += row_sum(dlow.astype(f32))
    sums[2:3, :] += row_sum(dv.astype(f32))
    for part in range(2):
        place = pl.ds(part * cols * 8, cols * 8)
        centred = conv[place, :] - mean
        normal_out[place, :] = (centred * (inverse * vecs[0:1]) + vecs[1:2]).astype(bf16)
        da = (nn(dv_out[place, :], down[...]) * slope[place, :].astype(f32)).astype(bf16)
        da_out[place, :] = da
        hidden_sums[0:1, :] += row_sum(da.astype(f32))
        dn = nn(da, up[...])
        dn_out[place, :] = dn
        sums[0:1, :] += row_sum(dn)
        sums[1:2, :] += row_sum(dn * centred)


def fine_weights_kernel(da, normal, dv, gated, dcells, patches, up_out, down_out, downs_out):
    up_out[...] = tn(da[...], normal[...])
    down_out[...] = tn(dv[...], gated[...])
    downs_out[...] = tn(dcells[...], patches[...])


def stem_back_kernel(
    rows, cols, got, back, vecs, dn, conv, depth, dv, first_cells, second_cells, third_cells, near, stem, pick,
    stem_out, taps_out, turned, acc, tap_acc, stem3,
):
    inverse, first, second = backward_rows(got, back, vecs[0:1])
    scale = inverse * vecs[0:1]
    amount = cols * 8

    def turn(row, carry):
        place = pl.ds(pl.multiple_of(row * amount, amount), amount)
        ocean = depth[place, :] > 0.0
        ocean = jnp.concatenate([ocean, ocean], axis=1)
        slope = dn[place, :] * scale + jnp.where(ocean, first + conv[place, :] * second, 0.0)
        turned[:, place] = slope.T.astype(bf16)
        return carry

    lax.fori_loop(0, rows, turn, 0)
    acc[...] = tn(dv[...], second_cells[pl.ds(REACH * amount, rows * amount), :])
    lane = lax.broadcasted_iota(jnp.int32, acc.shape, 1)
    acc[...] = jnp.where(lane < CIN, acc[...], 0.0)
    tap_acc[...] = jnp.zeros(tap_acc.shape, f32)
    wide = jnp.concatenate([stem[...].astype(f32), jnp.zeros((C1, C1 - CI), f32)], axis=1)
    stem3[...] = wide + pltpu.roll(wide, CIN, 1) + pltpu.roll(wide, 2 * CIN, 1)

    def group(index, cells, row):
        place = pl.ds(pl.multiple_of(row * amount, amount), rows * amount)
        part = nn(turned[...], cells[place, :])
        acc[...] += part * nt(near[...], pick[index])
        tap_acc[...] += nn((part * stem3[...]).astype(bf16), pick[index])

    def pair(p, carry):
        group(p, first_cells, p)
        group(p + KSIZE, second_cells, p)
        return carry

    lax.fori_loop(0, KSIZE, pair, 0)

    def triple(k, carry):
        group(k + 2 * KSIZE, third_cells, 3 * k)
        return carry

    lax.fori_loop(0, 3, triple, 0)
    full = acc[...]
    stem_out[...] = (
        full[:, :LANES]
        + pltpu.roll(full, C1 - CIN, 1)[:, :LANES]
        + pltpu.roll(full, C1 - 2 * CIN, 1)[:, :LANES]
    )
    taps_out[...] = tap_acc[...]


def period(length):
    return LANES // math.gcd(length, LANES)


def offsets():
    starts = []
    start = 0
    for shape in shapes_of():
        starts.append(start)
        start += math.prod(shape)
    return starts


def shard_places(devices, shard_len):
    firsts = [e * shard_len // 2048 * 16 for e in range(devices)]
    needed = [(e * shard_len % 2048 + shard_len + 2047) // 2048 * 16 for e in range(devices)]
    return firsts, max(needed)


def lane_ids(rows):
    return lax.broadcasted_iota(jnp.int32, (rows, LANES), 1)


def turn_lanes(values, amount):
    amount = amount % LANES
    return values if amount == 0 else pltpu.roll(values, amount, 1)


def read_rows(lines, base, rows, length, put):
    cycle = period(length)
    count = rows // cycle
    step = cycle * length // LANES
    lane = lane_ids(count)
    tiles = -(-length // LANES)
    for s in range(cycle):
        start = base + s * length
        line, phase = start // LANES, start % LANES
        held = [
            lines[pl.ds(line + k, count, stride=step), :] for k in range(-(-(phase + length) // LANES))
        ]
        for m in range(tiles):
            value = held[m]
            if phase and m + 1 < len(held):
                value = jnp.where(lane >= phase, value, held[m + 1])
            value = turn_lanes(value, -phase)
            if length - m * LANES < LANES:
                value = jnp.where(lane < length - m * LANES, value, 0.0)
            put(s, cycle, count, m, value)


def read_vector(lines, base, length, put):
    line, phase = base // LANES, base % LANES
    lane = lane_ids(1)
    for m in range(-(-length // LANES)):
        value = lines[line + m : line + m + 1, :]
        if phase and phase + length > (m + 1) * LANES:
            value = jnp.where(lane >= phase, value, lines[line + m + 1 : line + m + 2, :])
        value = turn_lanes(value, -phase)
        if length - m * LANES < LANES:
            value = jnp.where(lane < length - m * LANES, value, 0.0)
        put(m, value)


def write_rows(lines, base, rows, length, get):
    cycle = period(length)
    count = rows // cycle
    step = cycle * length // LANES
    line, phase = base // LANES, base % LANES
    for k in range(step):
        shared = k == 0 and phase > 0
        amount = count + 1 if shared else count
        lane = lane_ids(amount)
        total = None
        at = 0
        while at < LANES:
            place = k * LANES - phase + at
            row, col = place // length, place % length
            run = min(length - col, LANES - at)
            tile = col // LANES
            value = get(row, cycle, amount, tile)
            if col % LANES + run > LANES:
                value = jnp.where(lane >= col % LANES, value, get(row, cycle, amount, tile + 1))
            value = turn_lanes(value, at - col)
            total = value if total is None else jnp.where(lane >= at, value, total)
            at += run
        put_lines(lines, line + k, amount, step, total, shared)


def put_lines(lines, line, amount, step, values, shared):
    if not shared:
        lines[pl.ds(line, amount, stride=step), :] = values
        return
    before = lines[line : line + 1, :]
    lines[pl.ds(line, amount, stride=step), :] = values
    lines[line : line + 1, :] = lines[line : line + 1, :] + before


def write_vector(lines, base, length, get):
    line, phase = base // LANES, base % LANES
    lane = lane_ids(1)
    tiles = -(-length // LANES)
    zero = jnp.zeros((1, LANES), f32)
    for k in range(-(-(phase + length) // LANES)):
        value = get(k) if k < tiles else zero
        if phase:
            earlier = get(k - 1) if k > 0 else zero
            value = turn_lanes(jnp.where(lane >= LANES - phase, earlier, value), phase)
        if k == 0 and phase:
            value = value + lines[line : line + 1, :]
        lines[line + k : line + k + 1, :] = value


def write_short(lines, base, rows, length, get):
    line, phase = base // LANES, base % LANES
    lane = lane_ids(1)
    for k in range(-(-(phase + rows * length) // LANES)):
        low = k * LANES - phase
        total = jnp.zeros((1, LANES), f32)
        for row in range(max(low // length, 0), min(-(-(low + LANES) // length), rows)):
            at = row * length - low
            value = turn_lanes(get(row), at)
            if at < 0:
                value = jnp.where(lane < at + length, value, 0.0)
            elif at + length > LANES:
                value = jnp.where(lane >= at, value, 0.0)
            total = total + value
        if k == 0 and phase:
            total = total + lines[line : line + 1, :]
        lines[line + k : line + k + 1, :] = total


def read_short(lines, base, rows, length, put):
    lane = lane_ids(1)

    def one(row, carry):
        start = base + row * length
        line, phase = start // LANES, start % LANES
        value = jnp.where(lane >= phase, lines[pl.ds(line, 1), :], lines[pl.ds(line + 1, 1), :])
        value = pltpu.roll(value, LANES - phase, 1)
        put(row, jnp.where(lane < length, value, 0.0))
        return carry

    lax.fori_loop(0, rows, one, 0, unroll=8)


STEM, TAPS1, GAIN1, SHIFT1, UP1, UPB1, DOWN1, DOWNB1, DOWNS, DOWNSB = range(10)
TAPS2, GAIN2, SHIFT2, UP2, UPB2, DOWN2, DOWNB2, UPS, UPSB, HEAD, HEADB = range(10, 21)


def collect(devices, shard_len, me, blocks, lines, low, high):
    firsts, tall = shard_places(devices, shard_len)
    started = False
    for e in range(devices):
        end = firsts[e + 1] + 16 if e + 1 < devices else firsts[e] + tall
        if end <= low or firsts[e] >= high:
            continue
        seat = seat_of(me, e, devices)
        first = firsts[e] - low
        skip = max(0, -first)
        take = min(tall, high - firsts[e])
        if started:
            lines[pl.ds(first, 16), :] += blocks[seat, :16, :].astype(f32)
            skip = 16
        started = True
        if take > skip:
            lines[pl.ds(first + skip, take - skip), :] = blocks[seat, skip:take, :].astype(f32)


def seat_of(me, other, devices):
    away = me ^ other
    seat = 0
    bits = devices.bit_length() - 1
    for b in range(bits):
        seat = seat + ((away >> b) & 1) * (1 << (bits - 1 - b))
    return seat


def matrix_out(held, tall, out, tiles, rows):
    for m in range(tiles):
        if tall > rows:
            held[m * tall + rows : (m + 1) * tall, :] = jnp.zeros((tall - rows, LANES), f32)
        out[:, m * LANES : (m + 1) * LANES] = held[m * tall : (m + 1) * tall, :].astype(bf16)


def read_matrix(lines, shift, piece, held, out):
    rows, length = shapes_of()[piece]
    tall = out.shape[0]

    def put(first, stride, count, tile, value):
        held[pl.ds(tile * tall + first, count, stride=stride), :] = value

    read_rows(lines, offsets()[piece] - shift, rows, length, put)
    matrix_out(held, tall, out, -(-length // LANES), rows)


def read_row(lines, shift, piece, out, row):
    def put(tile, value):
        out[row : row + 1, tile * LANES : (tile + 1) * LANES] = value

    read_vector(lines, offsets()[piece] - shift, shapes_of()[piece][0], put)


def read_taps(lines, shift, piece, held, out, tall):
    def put(row, value):
        held[pl.ds(row, 1), :] = value

    rows = shapes_of()[piece][0]
    read_short(lines, offsets()[piece] - shift, rows, TAPS, put)
    held[rows:tall, :] = jnp.zeros((tall - rows, LANES), f32)
    across = held[:tall, :].T
    for t in range(TAPS):
        out[t] = jnp.broadcast_to(across[t : t + 1, :], (8, tall))


def first_end():
    return -(-offsets()[TAPS2] // 2048) * 16


def rest_start():
    return offsets()[TAPS2] // 2048 * 16


def rest_end():
    return -(-(offsets()[HEADB] + CIN) // 2048) * 16


def first_params_kernel(devices, shard_len, me, blocks, perm, stem, taps1, near1, vecs1, up1, bias1, down1, downs, downs_four, down_rows, lines, held):
    collect(devices, shard_len, me[0], blocks, lines, 0, first_end())
    vecs1[...] = jnp.zeros(vecs1.shape, f32)
    down_rows[...] = jnp.zeros(down_rows.shape, f32)
    bias1[...] = jnp.zeros(bias1.shape, f32)
    read_taps(lines, 0, TAPS1, held, taps1, C1)
    near1[...] = held[:C1, :].astype(bf16)
    read_matrix(lines, 0, STEM, held, stem)
    read_row(lines, 0, GAIN1, vecs1, 0)
    read_row(lines, 0, SHIFT1, vecs1, 1)
    read_row(lines, 0, DOWNB1, vecs1, 2)
    read_row(lines, 0, UPB1, bias1, 0)
    read_row(lines, 0, DOWNSB, down_rows, 0)
    read_matrix(lines, 0, UP1, held, up1)
    read_matrix(lines, 0, DOWN1, held, down1)
    read_matrix(lines, 0, DOWNS, held, downs)
    for k in range(4):
        downs_four[k] = nt(downs[...], perm[k]).astype(bf16)


def rest_params_kernel(devices, shard_len, me, blocks, taps2, vecs2, up2, bias2, down2, ups_four, vecs1, head, last, lines, held):
    shift = rest_start() * LANES
    collect(devices, shard_len, me[0], blocks, lines, rest_start(), rest_end())
    for out in (vecs1, vecs2, bias2, last):
        out[...] = jnp.zeros(out.shape, f32)
    read_taps(lines, shift, TAPS2, held, taps2, C2)
    read_row(lines, shift, GAIN2, vecs2, 0)
    read_row(lines, shift, SHIFT2, vecs2, 1)
    read_row(lines, shift, DOWNB2, vecs2, 2)
    read_row(lines, shift, UPB2, bias2, 0)
    read_row(lines, shift, UPSB, vecs1, 0)
    read_row(lines, shift, HEADB, last, 0)
    read_matrix(lines, shift, UP2, held, up2)
    read_matrix(lines, shift, DOWN2, held, down2)
    read_matrix(lines, shift, HEAD, held, head)
    tiles = C2 // LANES

    def put(first, stride, count, tile, value):
        k = first % 4
        held[pl.ds((k * tiles + tile) * C1 + first // 4, count, stride=stride // 4), :] = value

    rows, length = shapes_of()[UPS]
    read_rows(lines, offsets()[UPS] - shift, rows, length, put)
    for k in range(4):
        for m in range(tiles):
            at = (k * tiles + m) * C1
            held[at + WIDTH : at + C1, :] = jnp.zeros((C1 - WIDTH, LANES), f32)
            ups_four[k, :, m * LANES : (m + 1) * LANES] = held[at : at + C1, :].astype(bf16)


FRONT = 16


def hold_matrix(held, values, row_tiles, rows):
    tall = rows + 2 * FRONT
    zero = jnp.zeros((FRONT, LANES), f32)
    for m in range(row_tiles):
        at = m * tall
        held[at : at + FRONT, :] = zero
        held[at + FRONT : at + FRONT + rows, :] = values(m)
        held[at + FRONT + rows : at + tall, :] = zero


def write_matrix(lines, shift, piece, held, source):
    rows, length = shapes_of()[piece]
    tall = rows + 2 * FRONT
    hold_matrix(held, lambda m: source[:rows, m * LANES : (m + 1) * LANES], -(-length // LANES), rows)

    def get(first, stride, count, tile):
        return held[pl.ds(tile * tall + FRONT + first, count, stride=stride), :]

    write_rows(lines, offsets()[piece] - shift, rows, length, get)


def write_row(lines, shift, piece, get):
    write_vector(lines, offsets()[piece] - shift, shapes_of()[piece][0], get)


def row_of(source, row):
    return lambda m: source[row : row + 1, m * LANES : (m + 1) * LANES]


def norm_row(got, sums):
    def get(m):
        place = slice(m * LANES, (m + 1) * LANES)
        total = jnp.sum(got[:, :, place], axis=0)
        mean = total[0:1] / total[2:3]
        inverse = lax.rsqrt(total[1:2] / total[2:3] - mean * mean + NORM_EPS)
        return sums[1:2, place] * inverse

    return get


def flatten_kernel(
    devices, shard_len, me, got1, got2, g_stem, g_taps1, sums1, hidden1, g_up1, g_down1, g_downs, sums_low, g_taps2,
    sums2, hidden2, g_up2, g_down2, g_ups, g_head, keep, send, lines, held,
):
    def matrix(piece, source):
        write_matrix(lines, 0, piece, held, source)

    def row(piece, get):
        write_row(lines, 0, piece, get)

    matrix(STEM, g_stem)
    write_short(lines, offsets()[TAPS1], WIDTH, TAPS, lambda r: g_taps1[r : r + 1, :])
    row(GAIN1, norm_row(got1, sums1))
    row(SHIFT1, row_of(sums1, 0))
    matrix(UP1, g_up1)
    row(UPB1, row_of(hidden1, 0))
    matrix(DOWN1, g_down1)
    row(DOWNB1, row_of(sums1, 2))
    matrix(DOWNS, g_downs)
    row(DOWNSB, row_of(sums_low, 0))
    across = jnp.concatenate([g_taps2[...], jnp.zeros((LANES - g_taps2.shape[0], C2), f32)], axis=0).T
    held[:C2, :] = across
    write_short(lines, offsets()[TAPS2], WIDTH2, TAPS, lambda r: held[r : r + 1, :])
    row(GAIN2, norm_row(got2, sums2))
    row(SHIFT2, row_of(sums2, 0))
    matrix(UP2, g_up2)
    row(UPB2, row_of(hidden2, 0))
    matrix(DOWN2, g_down2)
    row(DOWNB2, row_of(sums2, 2))
    rows, length = shapes_of()[UPS]
    tiles = C2 // LANES
    tall = WIDTH + 2 * FRONT
    for k in range(4):
        for m in range(tiles):
            at = (k * tiles + m) * tall
            held[at : at + FRONT, :] = jnp.zeros((FRONT, LANES), f32)
            held[at + FRONT : at + FRONT + WIDTH, :] = g_ups[k, :WIDTH, m * LANES : (m + 1) * LANES]
            held[at + FRONT + WIDTH : at + tall, :] = jnp.zeros((FRONT, LANES), f32)

    def get(first, stride, count, tile):
        place = ((first % 4) * tiles + tile) * tall + FRONT + first // 4
        return held[pl.ds(place, count, stride=stride // 4), :]

    write_rows(lines, offsets()[UPS], rows, length, get)
    row(UPSB, row_of(sums2, 3))
    matrix(HEAD, g_head)
    row(HEADB, row_of(sums2, 4))
    end = offsets()[HEADB] + CIN
    last = -(-end // LANES)
    lines[last:, :] = jnp.zeros((lines.shape[0] - last, LANES), f32)

    firsts, tall = shard_places(devices, shard_len)
    half = devices // 2
    for e in range(devices):
        seat = seat_of(me[0], e, devices)

        @pl.when(seat < half)
        def _():
            keep[seat] = lines[firsts[e] : firsts[e] + tall, :]

        @pl.when(seat >= half)
        def _():
            send[seat - half] = lines[firsts[e] : firsts[e] + tall, :].astype(bf16)


def group_taps():
    table = []
    for first in (0, 3):
        for p in range(KSIZE):
            table.append([p * KSIZE + first + t for t in range(3)])
    for k in range(3):
        table.append([(3 * k + t) * KSIZE + 6 if 3 * k + t < KSIZE else -1 for t in range(3)])
    return table


def body(fields, targets, ocean_depth, thickness_class, params, moment1, moment2):
    shard_len = params.shape[0]
    devices = lax.axis_size(AXES)
    me = lax.axis_index(AXES)
    _, tall = shard_places(devices, shard_len)
    at = (me * (shard_len % 2048)) % 2048
    block = lax.dynamic_update_slice(jnp.zeros((tall * LANES,), bf16), params.astype(bf16), (at,))
    blocks = gather_blocks(block.reshape(tall, LANES))
    me_row = jnp.broadcast_to(me, (1,)).astype(jnp.int32)

    inputs = to_cells(lax.all_to_all(fields, "lvl", split_axis=3, concat_axis=0, tiled=True))
    goal = to_cells(lax.all_to_all(targets, "lvl", split_axis=3, concat_axis=0, tiled=True))
    rows, cols, _, _ = inputs.shape
    batch = fields.shape[1]
    half_rows, half_cols = rows // 2, cols // 2
    cells, low_cells = rows * cols * 8, half_rows * half_cols * 8
    wide = with_halo(inputs)
    wide_rows, wide_cols = rows + 2 * REACH, cols + 2 * REACH
    border_cells = wide_rows * wide_cols * 8
    low_border = (half_rows + 2 * REACH) * (half_cols + 2 * REACH) * 8
    fields_in = fill(wide, wide_rows, wide_cols, 8, CI).reshape(border_cells, CI)
    later = jnp.pad(wide, ((0, 2), (0, 0), (0, 0), (0, 0)))

    def three(parts):
        joined = jnp.concatenate(parts, axis=3)
        return fill(joined, wide_rows, cols, 8, C1).reshape(wide_rows * cols * 8, C1)

    first_cells = three([wide[:, k : k + cols] for k in range(3)])
    second_cells = three([wide[:, k : k + cols] for k in range(3, 6)])
    third_cells = three([later[k : k + wide_rows, 6 : 6 + cols] for k in range(3)])
    goal = fill(goal, rows, cols, 8, CI).reshape(cells, CI)

    deep = depth_cells(ocean_depth, batch)
    depth_rows = jnp.broadcast_to(deep.astype(f32)[..., None], deep.shape + (LANES,)).reshape(cells, LANES)
    low = jnp.max(deep.reshape(half_rows, 2, half_cols, 2, 8), axis=(1, 3))
    low_mask = (low > 0).astype(bf16)[..., None]
    low_wide = with_halo(jnp.broadcast_to(low_mask, low_mask.shape[:3] + (LANES,)))
    low_wide = low_wide.reshape(low_border, LANES)
    low_rows = jnp.broadcast_to(low.astype(f32)[..., None], low.shape + (LANES,)).reshape(low_cells, LANES)
    channel = jnp.arange(CI, dtype=jnp.int32)
    level = jnp.where(channel < 4 * LEVELS, channel // 4, 0)
    level_row = jnp.where(channel < CIN, level, LEVELS + 1).astype(f32)
    thickf = thickness_class.astype(f32)
    onehot = (level[:, None] == jnp.arange(LEVELS, dtype=jnp.int32)[None, :]).astype(f32)
    chosen = ((channel % 4 == 0) & (channel < 4 * LEVELS)).astype(f32)
    heat_take = chosen * jnp.sum(onehot * thickf[None, :], axis=1) / jnp.sum(thickf)
    ocean_cells = jnp.sum((level_row[None, None, :] < ocean_depth.astype(f32)[:, :, None]).astype(f32))
    ocean_cells = batch * ocean_cells
    surface_cells = jnp.sum((deep > 0).astype(f32))
    low_surface = jnp.sum((low > 0).astype(f32))
    index8 = jnp.arange(8)[:, None]
    counts1 = jnp.where(index8 == 2, surface_cells, jnp.where(index8 == 3, ocean_cells, 0.0))
    counts1 = jnp.broadcast_to(counts1, (8, C1))
    counts2 = jnp.where(index8 == 2, low_surface, jnp.where(index8 == 3, ocean_cells, 0.0))
    counts2 = jnp.broadcast_to(counts2, (8, C2))

    tables = jnp.pad(jnp.stack([level_row, heat_take]), ((0, 6), (0, 0)))
    source_lane = jnp.arange(C1, dtype=jnp.int32)[None, :, None]
    target_lane = jnp.arange(H1, dtype=jnp.int32)[None, None, :]
    quarter_at = jnp.arange(4, dtype=jnp.int32)[:, None, None]
    perm = ((source_lane * 4 + quarter_at == target_lane) & (source_lane < WIDTH)).astype(bf16)
    table = group_taps()
    third_at = jnp.arange(C1, dtype=jnp.int32) // CIN
    wanted = jnp.array([line + [-1] for line in table], dtype=jnp.int32)[:, third_at]
    pick = (wanted[:, :, None] == jnp.arange(LANES, dtype=jnp.int32)[None, None, :]).astype(bf16)
    smem = pl.BlockSpec(memory_space=pltpu.SMEM)
    vmem = pl.BlockSpec(memory_space=pltpu.VMEM)
    held_room = pltpu.VMEM((4 * H2, LANES), f32)
    stem_in, taps_in1, near1, vecs1, up_in1, bias_in1, down_in1, downs_in, downs_four, down_rows = call(
        lambda *refs: first_params_kernel(devices, shard_len, *refs),
        [
            ((C1, CI), bf16), ((TAPS, 8, C1), f32), ((C1, LANES), bf16), ((8, C1), f32), ((H1, C1), bf16),
            ((1, H1), f32), ((C1, H1), bf16), ((C2, H1), bf16), ((4, C2, C1), bf16), ((8, C2), f32),
        ],
        ins=[smem, vmem, vmem],
        scratch=[pltpu.VMEM((first_end(), LANES), f32), held_room],
        name="first_params",
    )(me_row, blocks, perm)
    taps_in2, vecs2, up_in2, bias_in2, down_in2, ups_four, fine_rows, head_in, last_rows = call(
        lambda *refs: rest_params_kernel(devices, shard_len, *refs),
        [
            ((TAPS, 8, C2), f32), ((8, C2), f32), ((H2, C2), bf16), ((1, H2), f32), ((C2, H2), bf16),
            ((4, C1, C2), bf16), ((8, C1), f32), ((CI, C1), bf16), ((8, CI), f32),
        ],
        ins=[smem, vmem],
        scratch=[pltpu.VMEM((rest_end() - rest_start(), LANES), f32), held_room],
        name="rest_params",
    )(me_row, blocks)

    hzero, conv1, stats1 = call(
        lambda *refs: stem_kernel(rows, cols, *refs),
        [((cells, C1), bf16), ((cells, C1), f32), ((8, C1), f32)],
        grid=(C1 // LANES,),
        ins=[
            whole(border_cells, CI),
            pl.BlockSpec((LANES, CI), lambda i: (i, 0)),
            TAP_TILE,
            whole(cells, LANES),
            lane_tile(8),
        ],
        out_specs=[lane_tile(cells), lane_tile(cells), lane_tile(8)],
        scratch=[pltpu.VMEM((border_cells, LANES), f32)],
        flops=cells * C1 * TAPS * 100,
        name="stem_conv",
    )(fields_in, stem_in, taps_in1, depth_rows, counts1)
    got1 = spread(stats1)
    chunk, low_chunk = 2 * cols * 8, half_cols * 8
    hone, gated1, slope1, patches, coarse = call(
        lambda *refs: fine_kernel(cols, *refs),
        [
            ((cells, C1), bf16),
            ((cells, H1), bf16),
            ((cells, H1), bf16),
            ((low_cells, H1), bf16),
            ((low_cells, C2), bf16),
        ],
        grid=(half_rows,),
        ins=[
            whole(devices, 8, C1), band(chunk, C1), band(chunk, C1), whole(8, C1), whole(H1, C1), whole(1, H1),
            whole(C1, H1), whole(4, C1, H1), whole(C2, H1), whole(8, C2),
        ],
        out_specs=[
            band(chunk, C1), band(chunk, H1), band(chunk, H1), band(low_chunk, H1), band(low_chunk, C2),
        ],
        scratch=[pltpu.VMEM((chunk, C1), f32)],
        flops=cells * C1 * H1 * 8,
        name="fine_forward",
    )(got1, conv1, hzero, vecs1, up_in1, bias_in1, down_in1, perm, downs_in, down_rows)

    border2 = with_halo(coarse.reshape(half_rows, half_cols, 8, C2)).reshape(low_border, C2)
    conv2, masked2, stats2 = call(
        lambda *refs: coarse_conv_kernel(half_rows, half_cols, *refs),
        [((low_cells, C2), f32), ((low_cells, C2), bf16), ((8, C2), f32)],
        grid=(C2 // LANES,),
        ins=[lane_tile(low_border), TAP_TILE, whole(low_cells, LANES), lane_tile(8)],
        out_specs=[lane_tile(low_cells), lane_tile(low_cells), lane_tile(8)],
        scratch=[pltpu.VMEM((low_border, LANES), f32)],
        flops=low_cells * C2 * TAPS * 100,
        name="coarse_conv",
    )(border2, taps_in2, low_rows, counts2)
    got2 = spread(stats2)
    masked_wide = with_halo(masked2.reshape(half_rows, half_cols, 8, C2)).reshape(low_border, C2)
    (
        skip, top, dy, ds, du, dtop, dv2, gated2, da2, normal2, dn2, dx2, sums2, hidden2,
    ) = call(
        lambda *refs: middle_kernel(cols, *refs),
        [
            ((cells, C1), bf16), ((low_cells, C2), bf16), ((cells, CI), bf16), ((cells, C1), f32),
            ((4, low_cells, C1), bf16), ((low_cells, C2), f32), ((low_cells, C2), bf16), ((low_cells, H2), bf16),
            ((low_cells, H2), bf16), ((low_cells, C2), bf16), ((low_cells, C2), f32), ((low_cells, C2), bf16),
            ((8, C2), f32), ((8, H2), f32),
        ],
        grid=(half_rows,),
        ins=[
            whole(devices, 8, C2), band(low_chunk, C2), band(low_chunk, C2), whole(8, C2), whole(H2, C2), whole(1, H2),
            whole(C2, H2), whole(4, C1, C2), whole(8, C1), whole(CI, C1), whole(8, CI), whole(8, CI), band(chunk, C1),
            band(chunk, CI), band(chunk, LANES),
        ],
        out_specs=[
            band(chunk, C1), band(low_chunk, C2), band(chunk, CI), band(chunk, C1),
            pl.BlockSpec((4, low_chunk, C1), lambda i: (0, i, 0)), band(low_chunk, C2), band(low_chunk, C2),
            band(low_chunk, H2), band(low_chunk, H2), band(low_chunk, C2), band(low_chunk, C2), band(low_chunk, C2),
            whole(8, C2), whole(8, H2),
        ],
        flops=low_cells * C2 * H2 * 16,
        name="middle",
    )(
        got2, conv2, coarse, vecs2, up_in2, bias_in2, down_in2, ups_four, fine_rows, head_in, last_rows, tables, hone, goal,
        depth_rows,
    )
    back2 = spread(sums2)
    dx_wide = with_halo(dx2.reshape(half_rows, half_cols, 8, C2)).reshape(low_border, C2)
    g_up2, g_down2, g_ups, g_head = call(
        coarse_weights_kernel,
        [((H2, C2), f32), ((C2, H2), f32), ((4, C1, C2), f32), ((CI, C1), f32)],
        flops=low_cells * C2 * H2 * 8,
        name="coarse_weights",
    )(da2, normal2, dv2, gated2, du, top, dy, skip)
    dcells, g_taps2 = call(
        lambda *refs: coarse_conv_back_kernel(half_rows, half_cols, *refs),
        [((low_cells, C2), bf16), ((56, C2), f32)],
        grid=(C2 // LANES,),
        ins=[
            pl.BlockSpec((devices, 8, LANES), lambda i: (0, 0, i)),
            pl.BlockSpec((devices, 8, LANES), lambda i: (0, 0, i)),
            lane_tile(8), lane_tile(low_border), lane_tile(low_border), lane_tile(low_border),
            whole(low_border, LANES), TAP_TILE, lane_tile(low_cells),
        ],
        out_specs=[lane_tile(low_cells), lane_tile(56)],
        scratch=[pltpu.VMEM((low_border, LANES), f32), pltpu.VMEM((low_border, LANES), f32)],
        flops=low_cells * C2 * TAPS * 200,
        name="coarse_conv_back",
    )(got2, back2, vecs2, border2, dx_wide, masked_wide, low_wide, taps_in2, dtop)

    dv1, da1, dn1, normal1, sums1, hidden1, sums_low = call(
        lambda *refs: fine_back_kernel(cols, *refs),
        [
            ((cells, C1), bf16), ((cells, H1), bf16), ((cells, C1), f32), ((cells, C1), bf16),
            ((8, C1), f32), ((8, H1), f32), ((8, C2), f32),
        ],
        grid=(half_rows,),
        ins=[
            whole(devices, 8, C1), band(low_chunk, C2), whole(4, C2, C1), band(chunk, C1), whole(8, C1),
            band(chunk, C1), band(chunk, H1), whole(H1, C1), whole(C1, H1),
        ],
        out_specs=[
            band(chunk, C1), band(chunk, H1), band(chunk, C1), band(chunk, C1), whole(8, C1), whole(8, H1), whole(8, C2),
        ],
        flops=cells * C1 * H1 * 8,
        name="fine_backward",
    )(got1, dcells, downs_four, ds, vecs1, conv1, slope1, up_in1, down_in1)
    back1 = spread(sums1)
    g_up1, g_down1, g_downs = call(
        fine_weights_kernel,
        [((H1, C1), f32), ((C1, H1), f32), ((C2, H1), f32)],
        flops=cells * C1 * H1 * 6,
        name="fine_weights",
    )(da1, normal1, dv1, gated1, dcells, patches)
    g_stem, g_taps1 = call(
        lambda *refs: stem_back_kernel(rows, cols, *refs),
        [((C1, LANES), f32), ((C1, LANES), f32)],
        scratch=[pltpu.VMEM((C1, cells), bf16), pltpu.VMEM((C1, C1), f32), pltpu.VMEM((C1, LANES), f32), pltpu.VMEM((C1, C1), f32)],
        flops=cells * C1 * C1 * GROUPS * 2,
        name="stem_back",
    )(
        got1, back1, vecs1, dn1, conv1, depth_rows, dv1, first_cells, second_cells, third_cells, near1, stem_in,
        pick,
    )

    keep, send = call(
        lambda *refs: flatten_kernel(devices, shard_len, *refs),
        [((devices // 2, tall, LANES), f32), ((devices // 2, tall, LANES), bf16)],
        ins=[smem] + [vmem] * 17,
        scratch=[pltpu.VMEM((rest_end() + tall, LANES), f32), held_room],
        name="flatten",
    )(
        me_row, got1, got2, g_stem, g_taps1, sums1, hidden1, g_up1, g_down1, g_downs, sums_low, g_taps2, sums2, hidden2,
        g_up2, g_down2, g_ups, g_head,
    )
    mine = scatter_blocks(keep, send).reshape(-1)
    mine = lax.dynamic_slice_in_dim(mine, at, shard_len)
    loss_part = jnp.sum(sums2[5, :LANES])
    last = jnp.broadcast_to(
        jnp.where(index8 == 0, loss_part, jnp.where(index8 == 1, jnp.sum(mine * mine), 0.0)), (8, LANES)
    )
    last = jnp.sum(spread(last), axis=0)
    loss_total, norm = last[0, 0], jnp.sqrt(last[1, 0])
    count = jnp.sum(got1[:, 3, 0])
    clipped = mine * jnp.minimum(1.0, CLIP / norm)
    first = BETA_ONE * moment1 + (1.0 - BETA_ONE) * clipped
    second = BETA_TWO * moment2 + (1.0 - BETA_TWO) * clipped * clipped
    ratio = first / (1.0 - BETA_ONE**STEP) / (jnp.sqrt(second / (1.0 - BETA_TWO**STEP)) + ADAM_EPS)
    updated = params - LRATE * (ratio + DECAY * params)
    return (loss_total, count, norm, updated, first, second)


def solution(mesh):
    in_specs = (
        P("lvl", None, "lat", None),
        P("lvl", None, "lat", None),
        P("lat", "lvl"),
        P(),
        P(("lat", "lvl")),
        P(("lat", "lvl")),
        P(("lat", "lvl")),
    )
    out_specs = (P(), P(), P(), P(("lat", "lvl")), P(("lat", "lvl")), P(("lat", "lvl")))
    return jax.shard_map(body, mesh=mesh, in_specs=in_specs, out_specs=out_specs, check_vma=False)
```

```python
import math

import jax
import jax.numpy as jnp
from jax import lax
from jax.experimental import pallas as pl
from jax.experimental.pallas import tpu as pltpu
from jax.sharding import PartitionSpec as P

CIN = 80
WIDTH = 200
EXPAND = 800
WIDTH2 = 400
EXPAND2 = 1600
KSIZE = 7
TAPS = KSIZE * KSIZE
LEVELS = 19
STEP = 10

CLIP = 0.01
LRATE = 0.05
BETA_ONE = 0.9
BETA_TWO = 0.999
ADAM_EPS = 1e-08
DECAY = 0.1
HEAT_WEIGHT = 40.0
NORM_EPS = 1e-05

AXES = ("lat", "lvl")

CI = 128
C1 = 256
H1 = 896
C2 = 512
H2 = 1664
BLOCKS = 8
LANES = 128
REACH = KSIZE // 2
GROUPS = 17

f32 = jnp.float32
bf16 = jnp.bfloat16
VMEM_LIMIT = 34 * 1024 * 1024


def plane_bits():
    bits = []
    for axis in AXES:
        count = lax.axis_size(axis)
        step = count // 2
        while step >= 1:
            bits.append((axis, count, step))
            step //= 2
    across = [b for b in bits if b[0] == "lat" and b[2] > 1]
    within = [b for b in bits if b not in across]
    return across, within


def exchange(values, axis, count, step):
    return lax.ppermute(values, axis, [(i, i ^ step) for i in range(count)])


def half_rows_of(tall):
    return -(-tall // 32) * 16


def gather_steps(near, far):
    across, (first, second, *others) = plane_bits()

    def plane_step(bit):
        return lambda blocks: jnp.concatenate([blocks, exchange(blocks, *bit)], axis=0)

    def pick(blocks):
        planes = blocks.shape[0]
        plane = lax.axis_index("lat") // 2
        found = [lax.dynamic_index_in_dim(blocks, seat_of(plane, p, planes), 0, False) for p in range(planes)]
        return [jnp.stack([found[p] for p in group]) for group in (near, far)]

    return [plane_step(bit) for bit in across], pick


def within_steps():
    _, (first, second, *others) = plane_bits()

    def halves(blocks):
        cut = half_rows_of(blocks.shape[1])
        left, right = blocks[:, :cut], blocks[:, cut:]
        left = jnp.stack([left, exchange(left, *first)], axis=0)
        right = jnp.stack([right, exchange(right, *second)], axis=0)
        return left, right

    def join(state):
        left, right = state
        left = jnp.stack([left, exchange(left, *second)], axis=0)
        right = jnp.stack([right, exchange(right, *first)], axis=1)
        both = jnp.concatenate([left, right], axis=3)
        return both.reshape((-1,) + both.shape[3:])

    def rest(both):
        for bit in others:
            both = jnp.concatenate([both, exchange(both, *bit)], axis=0)
        return both

    return [halves, join, rest]


def scatter_steps(keep, send, planes):
    _, (first, second, *others) = plane_bits()
    cut = half_rows_of(keep.shape[1])

    def inner(turn, bit):
        def step(state):
            keep, send = state
            if turn > 0:
                half = keep.shape[0] // 2
                keep, send = keep[:half], keep[half:].astype(bf16)
            keep = keep + exchange(send, *bit).astype(f32)
            return keep, None

        return step

    def outer(state):
        keep, _ = state
        parts = keep.reshape((2, 2, len(planes)) + keep.shape[1:])
        left, right = parts[:, :, :, :cut], parts[:, :, :, cut:]
        left = left[0] + exchange(left[1].astype(bf16), *second).astype(f32)
        right = right[:, 0] + exchange(right[:, 1].astype(bf16), *first).astype(f32)
        return left, right

    def last(state):
        left, right = state
        left = left[0] + exchange(left[1].astype(bf16), *first).astype(f32)
        right = right[0] + exchange(right[1].astype(bf16), *second).astype(f32)
        return jnp.concatenate([left, right], axis=1)

    steps = [inner(turn, bit) for turn, bit in enumerate(reversed(others))]
    return (keep, send), steps + [outer, last, lambda sums: scatter_planes(sums, planes)]


def tie(first, second):
    return lax.optimization_barrier((first, second))


def scatter_planes(sums, planes):
    count = lax.axis_size("lat")
    total = count // 2
    plane = lax.axis_index("lat") // 2
    empty = jnp.zeros(sums.shape[1:], f32)
    rows = jnp.stack([sums[planes.index(p)] if p in planes else empty for p in range(total)])
    mine = lax.dynamic_index_in_dim(rows, plane, 0, False)
    for away in range(1, total):
        pairs = [(i, i ^ (2 * away)) for i in range(count) if (i // 2) ^ away in planes]
        part = lax.dynamic_index_in_dim(rows, plane ^ away, 0, False).astype(bf16)
        mine = mine + lax.ppermute(part, "lat", pairs).astype(f32)
    return mine


def swap(copies):
    return lax.all_to_all(copies, AXES, 0, 0, tiled=True)


def neighbours(axis):
    ends = lax.axis_size(axis) - 1
    return [(i, i + 1) for i in range(ends)], [(i + 1, i) for i in range(ends)]


def columns_out(cells, rows, cols):
    split = cells.reshape(rows, cols, 8, cells.shape[-1])
    onward, back = neighbours("lvl")
    left = lax.ppermute(split[:, cols - REACH :].reshape(-1, cells.shape[-1]), "lvl", onward)
    right = lax.ppermute(split[:, :REACH].reshape(-1, cells.shape[-1]), "lvl", back)
    return left, right


def lines_out(lower, upper):
    onward, back = neighbours("lat")
    return lax.ppermute(lower, "lat", onward), lax.ppermute(upper, "lat", back)


def depth_cells(depth, batch):
    rows, cols = depth.shape
    bands = BLOCKS // batch
    split = depth.reshape(bands, rows // bands, cols).transpose(1, 2, 0)
    return jnp.concatenate([split] * batch, axis=2)


def block_shapes(chans, hidden):
    return [
        (chans, TAPS),
        (chans,),
        (chans,),
        (hidden, chans),
        (hidden,),
        (chans, hidden),
        (chans,),
    ]


def shapes_of():
    return (
        [(WIDTH, CIN)]
        + block_shapes(WIDTH, EXPAND)
        + [(WIDTH2, 4 * WIDTH), (WIDTH2,)]
        + block_shapes(WIDTH2, EXPAND2)
        + [(4 * WIDTH, WIDTH2), (WIDTH,), (CIN, WIDTH), (CIN,)]
    )


def fill(values, *shape):
    return jnp.pad(values, [(0, n - m) for n, m in zip(shape, values.shape)])


def nt(left, right):
    return lax.dot_general(left, right, (((1,), (1,)), ((), ())), preferred_element_type=f32)


def nn(left, right):
    return lax.dot_general(left, right, (((1,), (0,)), ((), ())), preferred_element_type=f32)


def tn(left, right):
    return lax.dot_general(left, right, (((0,), (0,)), ((), ())), preferred_element_type=f32)


def rows8(start, amount):
    return pl.ds(pl.multiple_of(start * 8, 8), amount * 8)


def convolve(source, taps, rows, cols, emit, carry, flip=False):
    width = cols + 2 * REACH
    strips = cols // 8

    def strip(turn, carry):
        row = turn // strips
        col = (turn % strips) * 8
        total = jnp.zeros((8, 8, LANES), f32)
        for p in range(KSIZE):
            seen = source[rows8((row + p) * width + col, 8 + 2 * REACH), :]
            seen = seen.reshape(8 + 2 * REACH, 8, LANES)
            for q in range(KSIZE):
                tap = p * KSIZE + q
                total = total + seen[q : q + 8] * taps[TAPS - 1 - tap if flip else tap][None]
        return emit(rows8(row * cols + col, 8), total, carry)

    return lax.fori_loop(0, rows * strips, strip, carry)


def row_sum(values):
    return jnp.sum(values, axis=0, keepdims=True)


def norm_rows(got):
    total = jnp.sum(got[...], axis=0)
    cells = total[2:3]
    mean = total[0:1] / cells
    inverse = lax.rsqrt(total[1:2] / cells - mean * mean + NORM_EPS)
    return mean, inverse, cells, total[3:4]


def gelu_pair(act):
    square = act * act
    flat = 0.7978845608028654
    cube = 0.044715
    bent = jnp.tanh(act * (flat + (flat * cube) * square))
    half = 0.5 + 0.5 * bent
    slope = half + 0.5 * act * (1.0 - bent * bent) * (flat + (3.0 * flat * cube) * square)
    return act * half, slope


def quarter(values, rows, cols, p, q):
    chans = values.shape[-1]
    split = values.reshape(rows // 2, 2, cols // 2, 2, 8, chans)
    return split[:, p, :, q].reshape(rows * cols * 2, chans)


def from_quarters(parts, rows, cols):
    chans = parts[0].shape[-1]
    cells = [part.reshape(rows // 2, cols // 2, 8, chans) for part in parts]
    lines = [jnp.stack(cells[2 * p : 2 * p + 2], axis=2) for p in range(2)]
    return jnp.stack(lines, axis=1).reshape(rows * cols * 8, chans)


def call(kernel, outs, grid=(), ins=None, out_specs=None, scratch=(), micros=5, name=None):
    params = dict(out_shape=[jax.ShapeDtypeStruct(s, t) for s, t in outs])
    if ins:
        params.update(in_specs=ins)
    if grid:
        params.update(grid=grid, out_specs=out_specs)
    return pl.pallas_call(
        kernel,
        scratch_shapes=list(scratch),
        compiler_params=pltpu.CompilerParams(vmem_limit_bytes=VMEM_LIMIT),
        cost_estimate=pl.CostEstimate(flops=int(micros * 1.1e9), bytes_accessed=100000, transcendentals=0),
        name=name,
        **params,
    )


def whole(*shape):
    return pl.BlockSpec(shape, lambda i: (0,) * len(shape))


def band(rows, cols):
    return pl.BlockSpec((rows, cols), lambda i: (i, 0))


def lane_tile(rows):
    return pl.BlockSpec((rows, LANES), lambda i: (0, i))


def stats_tile(devices):
    return pl.BlockSpec((devices, 8, LANES), lambda i: (0, 0, i))


TAP_TILE = pl.BlockSpec((TAPS, 8, LANES), lambda i: (0, 0, i))


def conv_sums(source, taps, depth, counts, out, stats, rows, cols, masked=None):
    lane = lax.broadcasted_iota(jnp.int32, (64, LANES), 1)
    mark = jnp.where(pl.program_id(0) == WIDTH2 // LANES, WIDTH2 % LANES, -1)

    def emit(place, total, carry):
        flat = total.reshape(64, LANES)
        out[place, :] = flat
        ocean = depth[place, :] > 0.0
        kept = jnp.where(ocean, flat, 0.0)
        if masked is not None:
            masked[place, :] = jnp.where(lane == mark, jnp.where(ocean, 1.0, 0.0), kept).astype(bf16)
        kept_cells = kept.reshape(8, 8, LANES)
        return (carry[0] + jnp.sum(kept_cells, axis=0), carry[1] + jnp.sum(kept_cells * total, axis=0))

    zero = jnp.zeros((8, LANES), f32)
    first, second = convolve(source, taps, rows, cols, emit, (zero, zero))
    index = lax.broadcasted_iota(jnp.int32, (8, LANES), 0)
    tile = jnp.where(index == 0, row_sum(first), jnp.where(index == 1, row_sum(second), counts[...]))
    stats[...] = jnp.broadcast_to(tile[None], stats.shape)


def lay_border(rows, cols, source, held, centre, left, right, above, below):
    width = cols + 2 * REACH
    sides = [part[...].astype(f32) for part in (left, right)]
    for row in range(rows):
        start = (row + REACH) * width
        source[rows8(start + REACH, cols), :] = centre[rows8(row * cols, cols), :].astype(f32)
        for side, place in zip(sides, (0, cols + REACH)):
            source[rows8(start + place, REACH), :] = side[row * REACH * 8 : (row + 1) * REACH * 8]
    for t in range(REACH):
        for start, target, way in ((rows + t, t, 1), (REACH + t, rows + REACH + t, 7)):
            line = source[rows8(start * width, width), :].reshape(width, 8, LANES)
            source[rows8(target * width, width), :] = pltpu.roll(line, way, 1).reshape(width * 8, LANES)
    amount = REACH * width
    for part, base in ((above, 0), (below, (rows + REACH) * width * 8 + BLOCKS // 2 - 1)):
        held[...] = part[...].astype(f32)
        for b in range(2):
            values = held[pl.ds(b, amount, stride=2), :]
            source[pl.ds(base + b * (BLOCKS // 2), amount, stride=8), :] = values


def pack_kernel(parts, cols, reach, values, out, tiles, turned, flat):
    total = values.shape[1]
    width = cols + 2 * reach
    lanes = out.shape[2]
    for k in range(-(-total // LANES)):
        size = min(LANES, total - k * LANES)
        tiles[k, :, :size] = values[:, k * LANES : k * LANES + size].astype(f32)
    turned[...] = jnp.zeros(turned.shape, f32)
    depth = values.shape[0] // lanes
    for row in range(depth):
        for k in range(-(-total // LANES)):
            size = min(LANES, total - k * LANES)
            piece = tiles[k, pl.ds(row, lanes, stride=depth), :].T
            turned[8 + k * LANES : 8 + k * LANES + size, :] = piece[:size]
        for part in range(parts):
            start = 8 + part * cols - reach
            flat[part, row * width : (row + 1) * width, :] = turned[start : start + width, :]
    for part in range(parts):
        out[part] = flat[part].astype(bf16)


def unpack_cells(packed, parts, cells):
    lanes = packed.shape[2]
    chans = lanes // BLOCKS
    amount = packed.shape[1]
    source = lax.broadcasted_iota(jnp.int32, (lanes, LANES), 0)
    target = lax.broadcasted_iota(jnp.int32, (lanes, LANES), 1)
    for s in range(BLOCKS):
        total = jnp.zeros((amount, LANES), f32)
        for part in range(parts):
            pick = ((target - part * chans) * BLOCKS + s == source).astype(bf16)
            total = total + nn(packed[part], pick)
        cells[pl.ds(s, amount, stride=BLOCKS), :] = total


def targets_kernel(parts, packed, out, cells):
    unpack_cells(packed, parts, cells)
    out[...] = cells[...].astype(bf16)


def fields_kernel(parts, rows, cols, packed, cells, lower, upper, held):
    unpack_cells(packed, parts, cells)
    width = cols + 2 * REACH
    room = -(-width // 8) * 8
    held[...] = jnp.zeros(held.shape, f32)
    for out, low, band in ((lower, rows - REACH, BLOCKS // 2 - 1), (upper, 0, 0)):
        for b in range(2):
            for t in range(REACH):
                start = (low + t) * width * 8 + band + b * (BLOCKS // 2)
                at = (b * REACH + t) * room
                held[at : at + width, :] = cells[pl.ds(start, width, stride=8), :]
        out[...] = held[...].astype(bf16)


def shift_kernel(rows, cols, cells, above, below, first, second, third, ends, far, farther):
    width = cols + 2 * REACH
    room = -(-width // 8) * 8
    line = width * 8
    for t in range(REACH):
        for k, row, way in ((t, rows - REACH + t, 1), (REACH + t, t, 7)):
            values = cells[row * line : (row + 1) * line, :].reshape(width, 8, LANES)
            ends[k * line : (k + 1) * line, :] = pltpu.roll(values, way, 1).reshape(line, LANES)
    for part, base, band in ((above, 0, 0), (below, REACH, BLOCKS // 2 - 1)):
        values = part[...].astype(f32)
        for b in range(2):
            for t in range(REACH):
                at = (b * REACH + t) * room
                start = (base + t) * line + band + b * (BLOCKS // 2)
                ends[pl.ds(start, width, stride=8), :] = values[at : at + width]

    def row_values(row):
        if row < REACH:
            return ends, row * line
        if row < REACH + rows:
            return cells, (row - REACH) * line
        return ends, (row - rows) * line

    total = rows + 2 * REACH
    for row in range(total):
        ref, start = row_values(row)
        values = ref[start : start + line, :]
        far[row * line : (row + 1) * line, :] = pltpu.roll(values, CIN, 1)
        farther[row * line : (row + 1) * line, :] = pltpu.roll(values, 2 * CIN - LANES, 1)
    for k in range(2):
        far[(total + k) * line : (total + k + 1) * line, :] = jnp.zeros((line, LANES), f32)
        farther[(total + k) * line : (total + k + 1) * line, :] = jnp.zeros((line, LANES), f32)
    amount = cols * 8
    lane = lax.broadcasted_iota(jnp.int32, (amount, LANES), 1)
    for row in range(total):
        ref, start = row_values(row)
        for out, near, middle, last in (
            (first, 0, row * line + 8, row * line + 16),
            (second, 24, row * line + 32, row * line + 40),
            (third, 48, (row + 1) * line + 48, (row + 2) * line + 48),
        ):
            mid = far[middle : middle + amount, :]
            place = slice(row * amount, (row + 1) * amount)
            out[place, :LANES] = jnp.where(lane < CIN, ref[start + near : start + near + amount, :], mid).astype(bf16)
            out[place, LANES:] = jnp.where(lane < 2 * CIN - LANES, mid, farther[last : last + amount, :]).astype(bf16)


def wide_stem(stem):
    return jnp.concatenate([stem.astype(f32), jnp.zeros((C1, C1 - CI), f32)], axis=1)


def triple_stem(stem):
    wide = wide_stem(stem)
    return wide + pltpu.roll(wide, CIN, 1) + pltpu.roll(wide, 2 * CIN, 1)


def stem_kernel(
    rows, cols, first, second, third, near, stem, pick, depth, counts, hzero, out, stats, weights, stem3, sums
):
    amount = cols * 8
    stem3[...] = triple_stem(stem[...])

    def weight(index, carry):
        both = nt(near[...], pick[index]) * stem3[...]
        weights[pl.ds(pl.multiple_of(index * C1, C1), C1), :] = both.astype(bf16)
        return carry

    lax.fori_loop(0, GROUPS, weight, 0)
    wide = wide_stem(stem[...]).astype(bf16)
    sums[...] = jnp.zeros(sums.shape, f32)

    def line(row, carry):
        def place(shift):
            return pl.ds(pl.multiple_of((row + shift) * amount, amount), amount)

        total = jnp.zeros((amount, C1), f32)
        for p in range(KSIZE):
            total = total + nt(first[place(p), :], weights[p * C1 : (p + 1) * C1, :])
            total = total + nt(second[place(p), :], weights[(KSIZE + p) * C1 : (KSIZE + p + 1) * C1, :])
        for k in range(3):
            at = (2 * KSIZE + k) * C1
            total = total + nt(third[place(3 * k), :], weights[at : at + C1, :])
        out[place(0), :] = total
        hzero[place(0), :] = nt(second[place(REACH), :], wide).astype(bf16)
        ocean = depth[place(0), :] > 0.0
        kept = jnp.where(jnp.concatenate([ocean, ocean], axis=1), total, 0.0)
        sums[0:1, :] += row_sum(kept)
        sums[1:2, :] += row_sum(kept * total)
        return carry

    lax.fori_loop(0, rows, line, 0)
    stats[...] = jnp.broadcast_to((sums[...] + counts[...])[None], stats.shape)


def edge_kernel(rows, cols, count, *refs):
    inputs, (lower, upper, held, edge) = refs[: 3 * count], refs[3 * count :]
    width = cols + 2 * REACH
    lines = edge_lines(cols)
    amount = rows * cols * 8
    side = rows * REACH * 8
    for k in range(count):
        for tile in range(C2 // LANES):
            lanes = slice(tile * LANES, (tile + 1) * LANES)
            for ref, start, size in zip(inputs[3 * k : 3 * k + 3], (0, amount, amount + side), (amount, side, side)):
                held[start : start + size, :] = ref[:, lanes].astype(f32)
            for out, low, band in ((lower, rows - REACH, BLOCKS // 2 - 1), (upper, 0, 0)):
                edge[lines - 16 :, :] = jnp.zeros((16, LANES), f32)
                for t in range(REACH):
                    for b in range(2):
                        s = band + b * (BLOCKS // 2)
                        at = t * width * 2 + b
                        for start, wide, col in ((amount, REACH, 0), (0, cols, REACH), (amount + side, REACH, REACH + cols)):
                            values = held[pl.ds(start + (low + t) * wide * 8 + s, wide, stride=8), :]
                            edge[pl.ds(at + 2 * col, wide, stride=2), :] = values
                out[k * lines : (k + 1) * lines, lanes] = edge[...].astype(bf16)


def edge_lines(cols):
    return -(-REACH * (cols + 2 * REACH) * 2 // 16) * 16


def coarse_conv_kernel(rows, cols, centre, left, right, above, below, taps, depth, counts, out, masked, stats, source, held):
    lay_border(rows, cols, source, held, centre, left, right, above, below)
    conv_sums(source, taps, depth, counts, out, stats, rows, cols, masked)


def fine_kernel(cols, got, conv, hzero, vecs, up, up_bias, down, perm, downs, down_rows, hone, gated, slope, patches, coarse, held):
    mean, inverse, _, _ = norm_rows(got)
    scale = inverse * vecs[0:1]
    for part in range(2):
        place = pl.ds(part * cols * 8, cols * 8)
        normal = ((conv[place, :] - mean) * scale + vecs[1:2]).astype(bf16)
        act = nt(normal, up[...]) + up_bias[...]
        value, bend = gelu_pair(act)
        value = value.astype(bf16)
        gated[place, :] = value
        slope[place, :] = bend.astype(bf16)
        branch = nt(value, down[...]) + vecs[2:3]
        full = (hzero[place, :].astype(f32) + branch).astype(bf16)
        hone[place, :] = full
        held[place, :] = full.astype(f32)
    cells = held[...]
    mixed = jnp.zeros((cols * 4, H1), f32)
    for p in range(2):
        for q in range(2):
            mixed = mixed + nn(quarter(cells, 2, cols, p, q).astype(bf16), perm[p * 2 + q])
    mixed = mixed.astype(bf16)
    patches[...] = mixed
    coarse[...] = (nt(mixed, downs[...]) + down_rows[0:1]).astype(bf16)


def middle_kernel(
    cols, got, conv, cells, vecs, up, up_bias, down, ups, fine_rows, head, last_rows, tables, hone, targets, depth,
    skip_out, top_out, dy_out, ds_out, du_out, dtop_out, dv_out, gated_out, da_out, normal_out, dx_out,
    sums, hidden_sums, copies,
):
    mean, inverse, _, ocean_count = norm_rows(got)
    scale = inverse * vecs[0:1]
    centred = conv[...] - mean
    normal = (centred * scale + vecs[1:2]).astype(bf16)
    normal_out[...] = normal
    value, bend = gelu_pair(nt(normal, up[...]) + up_bias[...])
    value = value.astype(bf16)
    gated_out[...] = value
    top = (cells[...].astype(f32) + nt(value, down[...]) + vecs[2:3]).astype(bf16)
    top_out[...] = top
    raised = from_quarters([nt(top, ups[k]) + fine_rows[0:1] for k in range(4)], 2, cols)
    skip = (hone[...].astype(f32) + raised).astype(bf16)
    skip_out[...] = skip
    err = nt(skip, head[...]) + last_rows[0:1] - targets[...].astype(f32)
    deep = depth[...]
    ocean = tables[0:1] < deep
    heat_take = tables[1:2]
    err = jnp.where(ocean, err, 0.0)
    heat = jnp.sum(heat_take * err, axis=1, keepdims=True)
    heat = jnp.where(deep > 0.0, heat, 0.0)
    loss = row_sum(err * err) + (HEAT_WEIGHT / LANES) * row_sum(heat * heat)
    dy = jnp.where(ocean, err + HEAT_WEIGHT * heat_take * heat, 0.0) * (2.0 / ocean_count[:, :LANES])
    dy = dy.astype(bf16)
    dy_out[...] = dy
    ds = nn(dy, head[...])
    ds_out[...] = ds
    dtop = jnp.zeros(top.shape, f32)
    du_sum = jnp.zeros((1, C1), f32)
    for k in range(4):
        du = quarter(ds, 2, cols, k // 2, k % 2).astype(bf16)
        du_out[k] = du
        du_sum = du_sum + row_sum(du.astype(f32))
        dtop = dtop + nn(du, ups[k])
    dtop_out[...] = dtop
    dv = dtop.astype(bf16)
    dv_out[...] = dv
    da = (nn(dv, down[...]) * bend).astype(bf16)
    da_out[...] = da
    dn = nn(da, up[...])
    dx_out[...] = (dn * vecs[0:1]).astype(bf16)

    @pl.when(pl.program_id(0) == 0)
    def _():
        sums[...] = jnp.zeros(sums.shape, f32)
        hidden_sums[...] = jnp.zeros(hidden_sums.shape, f32)

    sums[0:1, :] += row_sum(dn)
    sums[1:2, :] += row_sum(dn * centred)
    sums[2:3, :] += row_sum(dv.astype(f32))
    sums[3:4, :C1] += du_sum
    sums[4:5, :CI] += row_sum(dy.astype(f32))
    sums[5:6, :LANES] += loss
    hidden_sums[0:1, :] += row_sum(da.astype(f32))

    @pl.when(pl.program_id(0) == pl.num_programs(0) - 1)
    def _():
        copies[...] = jnp.broadcast_to(sums[...][None], copies.shape)


def coarse_weights_kernel(da, normal, dv, gated, du, top, dy, skip, up_out, down_out, ups_out, head_out):
    up_out[...] = tn(da[...], normal[...])
    down_out[...] = tn(dv[...], gated[...])
    for k in range(4):
        ups_out[k] = tn(du[k], top[...])
    head_out[...] = tn(dy[...], skip[...])


def backward_rows(got, back, gain):
    mean, inverse, cells, _ = norm_rows(got)
    total = jnp.sum(back[...], axis=0)
    total_a = gain * total[0:1]
    total_b = gain * total[1:2]
    dvar = -0.5 * inverse * inverse * inverse * total_b
    first = (-inverse * total_a - 2.0 * mean * dvar) / cells
    second = 2.0 * dvar / cells
    return inverse, first, second


def coarse_conv_back_kernel(rows, cols, *refs):
    got, back, vecs = refs[:3]
    border, dx, masked, mask = refs[3:8], refs[8:13], refs[13:18], refs[18:23]
    taps, dtop, dcells, taps_out, source, slope, held, ocean = refs[23:]

    @pl.when(pl.program_id(0) == 0)
    def _():
        lay_border(rows, cols, source, held, *mask)
        at = WIDTH2 % LANES
        ocean[...] = jnp.broadcast_to(source[:, at : at + 1], ocean.shape)

    inverse, first, second = backward_rows(got, back, vecs[0:1])
    lay_border(rows, cols, source, held, *dx)
    slope[...] = source[...] * inverse + ocean[...] * first
    lay_border(rows, cols, source, held, *masked)
    slope[...] = (slope[...] + source[...] * second).astype(bf16).astype(f32)
    lay_border(rows, cols, source, held, *border)

    def emit(place, total, carry):
        dcells[place, :] = (dtop[place, :] + total.reshape(64, LANES)).astype(bf16)
        return carry

    convolve(slope, taps, rows, cols, emit, 0, flip=True)
    taps_out[...] = jnp.zeros(taps_out.shape, f32)
    width = cols + 2 * REACH
    for p in range(KSIZE):

        def line(turn, sums):
            row = turn // (cols // 8)
            col = (turn % (cols // 8)) * 8
            seen = source[rows8((row + p) * width + col, 8 + 2 * REACH), :]
            seen = seen.reshape(8 + 2 * REACH, 8, LANES)
            here = slope[rows8((row + REACH) * width + REACH + col, 8), :].reshape(8, 8, LANES)
            return tuple(sums[q] + jnp.sum(seen[q : q + 8] * here, axis=0) for q in range(KSIZE))

        zero = jnp.zeros((8, LANES), f32)
        sums = lax.fori_loop(0, rows * (cols // 8), line, (zero,) * KSIZE)
        for q in range(KSIZE):
            taps_out[p * KSIZE + q : p * KSIZE + q + 1, :] = row_sum(sums[q])


def fine_back_kernel(
    cols, got, dcells, downs, ds, vecs, conv, slope, up, down, dv_out, da_out, dn_out, normal_out, sums, hidden_sums, coarse_sums, copies
):
    mean, inverse, _, _ = norm_rows(got)
    dlow = dcells[...]
    dh = ds[...] + from_quarters([nn(dlow, downs[k]) for k in range(4)], 2, cols)
    dv = dh.astype(bf16)
    dv_out[...] = dv

    @pl.when(pl.program_id(0) == 0)
    def _():
        sums[...] = jnp.zeros(sums.shape, f32)
        hidden_sums[...] = jnp.zeros(hidden_sums.shape, f32)
        coarse_sums[...] = jnp.zeros(coarse_sums.shape, f32)

    coarse_sums[0:1, :] += row_sum(dlow.astype(f32))
    sums[2:3, :] += row_sum(dv.astype(f32))
    for part in range(2):
        place = pl.ds(part * cols * 8, cols * 8)
        centred = conv[place, :] - mean
        normal_out[place, :] = (centred * (inverse * vecs[0:1]) + vecs[1:2]).astype(bf16)
        da = (nn(dv_out[place, :], down[...]) * slope[place, :].astype(f32)).astype(bf16)
        da_out[place, :] = da
        hidden_sums[0:1, :] += row_sum(da.astype(f32))
        dn = nn(da, up[...])
        dn_out[place, :] = dn
        sums[0:1, :] += row_sum(dn)
        sums[1:2, :] += row_sum(dn * centred)

    @pl.when(pl.program_id(0) == pl.num_programs(0) - 1)
    def _():
        copies[...] = jnp.broadcast_to(sums[...][None], copies.shape)


def fine_weights_kernel(da, normal, dv, gated, dcells, patches, up_out, down_out, downs_out):
    up_out[...] = tn(da[...], normal[...])
    down_out[...] = tn(dv[...], gated[...])
    downs_out[...] = tn(dcells[...], patches[...])


def stem_back_kernel(
    rows, cols, got, back, vecs, dn, conv, depth, dv, first_cells, second_cells, third_cells, near, stem, pick, sums,
    tail, turned, acc, tap_acc, stem3, lines, held,
):
    inverse, first, second = backward_rows(got, back, vecs[0:1])
    scale = inverse * vecs[0:1]
    amount = cols * 8

    def turn(row, carry):
        place = pl.ds(pl.multiple_of(row * amount, amount), amount)
        ocean = depth[place, :] > 0.0
        ocean = jnp.concatenate([ocean, ocean], axis=1)
        slope = dn[place, :] * scale + jnp.where(ocean, first + conv[place, :] * second, 0.0)
        turned[:, place] = slope.T.astype(bf16)
        return carry

    lax.fori_loop(0, rows, turn, 0)
    acc[...] = tn(dv[...], second_cells[pl.ds(REACH * amount, rows * amount), :])
    lane = lax.broadcasted_iota(jnp.int32, acc.shape, 1)
    acc[...] = jnp.where(lane < CIN, acc[...], 0.0)
    tap_acc[...] = jnp.zeros(tap_acc.shape, f32)
    stem3[...] = triple_stem(stem[...])

    def group(index, cells, row):
        place = pl.ds(pl.multiple_of(row * amount, amount), rows * amount)
        part = nn(turned[...], cells[place, :])
        acc[...] += part * nt(near[...], pick[index])
        tap_acc[...] += nn((part * stem3[...]).astype(bf16), pick[index])

    def pair(p, carry):
        group(p, first_cells, p)
        group(p + KSIZE, second_cells, p)
        return carry

    lax.fori_loop(0, KSIZE, pair, 0)

    def triple(k, carry):
        group(k + 2 * KSIZE, third_cells, 3 * k)
        return carry

    lax.fori_loop(0, 3, triple, 0)
    full = acc[...]
    acc[:, :LANES] = (
        full[:, :LANES]
        + pltpu.roll(full, C1 - CIN, 1)[:, :LANES]
        + pltpu.roll(full, C1 - 2 * CIN, 1)[:, :LANES]
    )
    lines[...] = jnp.zeros(lines.shape, f32)
    write_matrix(lines, 0, STEM, held, acc)
    write_short(lines, offsets()[TAPS1], WIDTH, TAPS, lambda r: tap_acc[r : r + 1, :])
    write_row(lines, 0, GAIN1, norm_row(got, sums))
    write_row(lines, 0, SHIFT1, row_of(sums, 0))
    tail[...] = lines[...].reshape(tail.shape)


def period(length):
    return LANES // math.gcd(length, LANES)


def offsets():
    starts = []
    start = 0
    for shape in shapes_of():
        starts.append(start)
        start += math.prod(shape)
    return starts


def shard_places(devices, shard_len):
    firsts = [e * shard_len // 2048 * 16 for e in range(devices)]
    needed = [(e * shard_len % 2048 + shard_len + 2047) // 2048 * 16 for e in range(devices)]
    return firsts, max(needed)


def lane_ids(rows):
    return lax.broadcasted_iota(jnp.int32, (rows, LANES), 1)


def turn_lanes(values, amount):
    amount = amount % LANES
    return values if amount == 0 else pltpu.roll(values, amount, 1)


def read_rows(lines, base, rows, length, put):
    cycle = period(length)
    count = rows // cycle
    step = cycle * length // LANES
    lane = lane_ids(count)
    tiles = -(-length // LANES)
    for s in range(cycle):
        start = base + s * length
        line, phase = start // LANES, start % LANES
        held = [
            lines[pl.ds(line + k, count, stride=step), :] for k in range(-(-(phase + length) // LANES))
        ]
        for m in range(tiles):
            value = held[m]
            if phase and m + 1 < len(held):
                value = jnp.where(lane >= phase, value, held[m + 1])
            value = turn_lanes(value, -phase)
            if length - m * LANES < LANES:
                value = jnp.where(lane < length - m * LANES, value, 0.0)
            put(s, cycle, count, m, value)


def read_vector(lines, base, length, put):
    line, phase = base // LANES, base % LANES
    lane = lane_ids(1)
    for m in range(-(-length // LANES)):
        value = lines[line + m : line + m + 1, :]
        if phase and phase + length > (m + 1) * LANES:
            value = jnp.where(lane >= phase, value, lines[line + m + 1 : line + m + 2, :])
        value = turn_lanes(value, -phase)
        if length - m * LANES < LANES:
            value = jnp.where(lane < length - m * LANES, value, 0.0)
        put(m, value)


def write_rows(lines, base, rows, length, get):
    cycle = period(length)
    count = rows // cycle
    step = cycle * length // LANES
    line, phase = base // LANES, base % LANES
    for k in range(step):
        shared = k == 0 and phase > 0
        amount = count + 1 if shared else count
        lane = lane_ids(amount)
        total = None
        at = 0
        while at < LANES:
            place = k * LANES - phase + at
            row, col = place // length, place % length
            run = min(length - col, LANES - at)
            tile = col // LANES
            value = get(row, cycle, amount, tile)
            if col % LANES + run > LANES:
                value = jnp.where(lane >= col % LANES, value, get(row, cycle, amount, tile + 1))
            value = turn_lanes(value, at - col)
            total = value if total is None else jnp.where(lane >= at, value, total)
            at += run
        put_lines(lines, line + k, amount, step, total, shared)


def put_lines(lines, line, amount, step, values, shared):
    if not shared:
        lines[pl.ds(line, amount, stride=step), :] = values
        return
    before = lines[line : line + 1, :]
    lines[pl.ds(line, amount, stride=step), :] = values
    lines[line : line + 1, :] = lines[line : line + 1, :] + before


def write_vector(lines, base, length, get):
    line, phase = base // LANES, base % LANES
    lane = lane_ids(1)
    tiles = -(-length // LANES)
    zero = jnp.zeros((1, LANES), f32)
    for k in range(-(-(phase + length) // LANES)):
        value = get(k) if k < tiles else zero
        if phase:
            earlier = get(k - 1) if k > 0 else zero
            value = turn_lanes(jnp.where(lane >= LANES - phase, earlier, value), phase)
        if k == 0 and phase:
            value = value + lines[line : line + 1, :]
        lines[line + k : line + k + 1, :] = value


def write_short(lines, base, rows, length, get):
    line, phase = base // LANES, base % LANES
    lane = lane_ids(1)
    for k in range(-(-(phase + rows * length) // LANES)):
        low = k * LANES - phase
        total = jnp.zeros((1, LANES), f32)
        for row in range(max(low // length, 0), min(-(-(low + LANES) // length), rows)):
            at = row * length - low
            value = turn_lanes(get(row), at)
            if at < 0:
                value = jnp.where(lane < at + length, value, 0.0)
            elif at + length > LANES:
                value = jnp.where(lane >= at, value, 0.0)
            total = total + value
        if k == 0 and phase:
            total = total + lines[line : line + 1, :]
        lines[line + k : line + k + 1, :] = total


def read_short(lines, base, rows, length, put):
    lane = lane_ids(1)

    def one(row, carry):
        start = base + row * length
        line, phase = start // LANES, start % LANES
        value = jnp.where(lane >= phase, lines[pl.ds(line, 1), :], lines[pl.ds(line + 1, 1), :])
        value = pltpu.roll(value, LANES - phase, 1)
        put(row, jnp.where(lane < length, value, 0.0))
        return carry

    lax.fori_loop(0, rows, one, 0, unroll=8)


STEM, TAPS1, GAIN1, SHIFT1, UP1, UPB1, DOWN1, DOWNB1, DOWNS, DOWNSB = range(10)
TAPS2, GAIN2, SHIFT2, UP2, UPB2, DOWN2, DOWNB2, UPS, UPSB, HEAD, HEADB = range(10, 21)


def planes_of(devices, shard_len, low, high, plane_size):
    firsts, tall = shard_places(devices, shard_len)
    found = {e // plane_size for e in range(devices) if firsts[e] < high and firsts[e] + tall > low}
    return sorted(found)


def collect(devices, shard_len, plane_size, place, parts, lines, low, high):
    firsts, tall = shard_places(devices, shard_len)
    started = False
    for e in range(devices):
        end = firsts[e + 1] + 16 if e + 1 < devices else firsts[e] + tall
        if end <= low or firsts[e] >= high:
            continue
        plane, blocks = next((p.index(e // plane_size), b) for p, b in parts if e // plane_size in p)
        planes = next(len(p) for p, b in parts if e // plane_size in p)
        seat = seat_of(place, e % plane_size, plane_size) * planes + plane
        first = firsts[e] - low
        skip = max(0, -first)
        take = min(tall, high - firsts[e])
        if started:
            lines[pl.ds(first, 16), :] += blocks[seat, :16, :].astype(f32)
            skip = 16
        started = True
        if take > skip:
            lines[pl.ds(first + skip, take - skip), :] = blocks[seat, skip:take, :].astype(f32)


def seat_of(me, other, devices):
    away = me ^ other
    seat = 0
    bits = devices.bit_length() - 1
    for b in range(bits):
        seat = seat + ((away >> b) & 1) * (1 << (bits - 1 - b))
    return seat


def matrix_out(held, tall, out, tiles, rows):
    for m in range(tiles):
        if tall > rows:
            held[m * tall + rows : (m + 1) * tall, :] = jnp.zeros((tall - rows, LANES), f32)
        out[:, m * LANES : (m + 1) * LANES] = held[m * tall : (m + 1) * tall, :].astype(bf16)


def read_matrix(lines, shift, piece, held, out):
    rows, length = shapes_of()[piece]
    tall = out.shape[0]

    def put(first, stride, count, tile, value):
        held[pl.ds(tile * tall + first, count, stride=stride), :] = value

    read_rows(lines, offsets()[piece] - shift, rows, length, put)
    matrix_out(held, tall, out, -(-length // LANES), rows)


def read_row(lines, shift, piece, out, row):
    def put(tile, value):
        out[row : row + 1, tile * LANES : (tile + 1) * LANES] = value

    read_vector(lines, offsets()[piece] - shift, shapes_of()[piece][0], put)


def read_taps(lines, shift, piece, held, out, tall):
    def put(row, value):
        held[pl.ds(row, 1), :] = value

    rows = shapes_of()[piece][0]
    read_short(lines, offsets()[piece] - shift, rows, TAPS, put)
    held[rows:tall, :] = jnp.zeros((tall - rows, LANES), f32)
    if out is None:
        return
    across = held[:tall, :].T
    for t in range(TAPS):
        out[t] = jnp.broadcast_to(across[t : t + 1, :], (8, tall))


def first_end():
    return -(-offsets()[TAPS2] // 2048) * 16


def rest_start():
    return offsets()[TAPS2] // 2048 * 16


def rest_end():
    return -(-(offsets()[HEADB] + CIN) // 2048) * 16


def first_params_kernel(devices, shard_len, plane_size, planes, place, blocks, perm, stem, near1, vecs1, up1, bias1, down1, downs, downs_four, down_rows, lines, held):
    collect(devices, shard_len, plane_size, place[0], [(planes, blocks)], lines, 0, first_end())
    vecs1[...] = jnp.zeros(vecs1.shape, f32)
    down_rows[...] = jnp.zeros(down_rows.shape, f32)
    bias1[...] = jnp.zeros(bias1.shape, f32)
    read_taps(lines, 0, TAPS1, held, None, C1)
    near1[...] = held[:C1, :].astype(bf16)
    read_matrix(lines, 0, STEM, held, stem)
    read_row(lines, 0, GAIN1, vecs1, 0)
    read_row(lines, 0, SHIFT1, vecs1, 1)
    read_row(lines, 0, DOWNB1, vecs1, 2)
    read_row(lines, 0, UPB1, bias1, 0)
    read_row(lines, 0, DOWNSB, down_rows, 0)
    read_matrix(lines, 0, UP1, held, up1)
    read_matrix(lines, 0, DOWN1, held, down1)
    read_matrix(lines, 0, DOWNS, held, downs)
    for k in range(4):
        downs_four[k] = nt(downs[...], perm[k]).astype(bf16)


def rest_params_kernel(devices, shard_len, plane_size, planes, others, place, blocks, more, taps2, vecs2, up2, bias2, down2, ups_four, vecs1, head, last, lines, held):
    shift = rest_start() * LANES
    parts = [(planes, blocks), (others, more)]
    collect(devices, shard_len, plane_size, place[0], parts, lines, rest_start(), rest_end())
    for out in (vecs1, vecs2, bias2, last):
        out[...] = jnp.zeros(out.shape, f32)
    read_taps(lines, shift, TAPS2, held, taps2, C2)
    read_row(lines, shift, GAIN2, vecs2, 0)
    read_row(lines, shift, SHIFT2, vecs2, 1)
    read_row(lines, shift, DOWNB2, vecs2, 2)
    read_row(lines, shift, UPB2, bias2, 0)
    read_row(lines, shift, UPSB, vecs1, 0)
    read_row(lines, shift, HEADB, last, 0)
    read_matrix(lines, shift, UP2, held, up2)
    read_matrix(lines, shift, DOWN2, held, down2)
    read_matrix(lines, shift, HEAD, held, head)
    tiles = C2 // LANES

    def put(first, stride, count, tile, value):
        k = first % 4
        held[pl.ds((k * tiles + tile) * C1 + first // 4, count, stride=stride // 4), :] = value

    rows, length = shapes_of()[UPS]
    read_rows(lines, offsets()[UPS] - shift, rows, length, put)
    for k in range(4):
        for m in range(tiles):
            at = (k * tiles + m) * C1
            held[at + WIDTH : at + C1, :] = jnp.zeros((C1 - WIDTH, LANES), f32)
            ups_four[k, :, m * LANES : (m + 1) * LANES] = held[at : at + C1, :].astype(bf16)


FRONT = 16


def hold_matrix(held, values, row_tiles, rows):
    tall = rows + 2 * FRONT
    zero = jnp.zeros((FRONT, LANES), f32)
    for m in range(row_tiles):
        at = m * tall
        held[at : at + FRONT, :] = zero
        held[at + FRONT : at + FRONT + rows, :] = values(m)
        held[at + FRONT + rows : at + tall, :] = zero


def write_matrix(lines, shift, piece, held, source):
    rows, length = shapes_of()[piece]
    tall = rows + 2 * FRONT
    hold_matrix(held, lambda m: source[:rows, m * LANES : (m + 1) * LANES], -(-length // LANES), rows)

    def get(first, stride, count, tile):
        return held[pl.ds(tile * tall + FRONT + first, count, stride=stride), :]

    write_rows(lines, offsets()[piece] - shift, rows, length, get)


def write_row(lines, shift, piece, get):
    write_vector(lines, offsets()[piece] - shift, shapes_of()[piece][0], get)


def row_of(source, row):
    return lambda m: source[row : row + 1, m * LANES : (m + 1) * LANES]


def norm_row(got, sums):
    def get(m):
        place = slice(m * LANES, (m + 1) * LANES)
        total = jnp.sum(got[:, :, place], axis=0)
        mean = total[0:1] / total[2:3]
        inverse = lax.rsqrt(total[1:2] / total[2:3] - mean * mean + NORM_EPS)
        return sums[1:2, place] * inverse

    return get


def scatter_out(devices, shard_len, plane_size, planes, place, lines, low, keep, send):
    firsts, tall = shard_places(devices, shard_len)
    half = plane_size // 2
    for k, plane in enumerate(planes):
        for r in range(plane_size):
            first = firsts[plane * plane_size + r] - low
            start, end = max(first, 0), min(first + tall, lines.shape[0])
            seat = seat_of(place, r, plane_size)

            def put(out, index, kind):
                if end <= start:
                    out[index] = jnp.zeros((tall, LANES), kind)
                    return
                if start > first:
                    out[index, : start - first] = jnp.zeros((start - first, LANES), kind)
                out[index, start - first : end - first] = lines[start:end, :].astype(kind)
                if end < first + tall:
                    out[index, end - first :] = jnp.zeros((first + tall - end, LANES), kind)

            @pl.when(seat < half)
            def _():
                put(keep, seat * len(planes) + k, f32)

            @pl.when(seat >= half)
            def _():
                put(send, (seat - half) * len(planes) + k, bf16)


def span(first, last):
    end = offsets()[last] + math.prod(shapes_of()[last])
    return offsets()[first] // 2048 * 16, -(-end // 2048) * 16


def clear_ends(lines, low, first, last):
    start = offsets()[first] // LANES - low + 1
    lines[:start, :] = jnp.zeros((start, LANES), f32)
    end = -(-(offsets()[last] + math.prod(shapes_of()[last])) // LANES) - low
    if end < lines.shape[0]:
        lines[end:, :] = jnp.zeros((lines.shape[0] - end, LANES), f32)


def late_flat_kernel(
    devices, shard_len, plane_size, planes, place, sums2, hidden2, g_up2, g_down2, g_ups, g_head, keep, send, lines, held
):
    low, _ = span(UP2, HEADB)
    shift = low * LANES
    clear_ends(lines, low, UP2, HEADB)
    write_matrix(lines, shift, UP2, held, g_up2)
    write_row(lines, shift, UPB2, row_of(hidden2, 0))
    write_matrix(lines, shift, DOWN2, held, g_down2)
    write_row(lines, shift, DOWNB2, row_of(sums2, 2))
    rows, length = shapes_of()[UPS]
    tiles = C2 // LANES
    tall = WIDTH + 2 * FRONT
    for k in range(4):
        for m in range(tiles):
            at = (k * tiles + m) * tall
            held[at : at + FRONT, :] = jnp.zeros((FRONT, LANES), f32)
            held[at + FRONT : at + FRONT + WIDTH, :] = g_ups[k, :WIDTH, m * LANES : (m + 1) * LANES]
            held[at + FRONT + WIDTH : at + tall, :] = jnp.zeros((FRONT, LANES), f32)

    def get(first, stride, count, tile):
        at = ((first % 4) * tiles + tile) * tall + FRONT + first // 4
        return held[pl.ds(at, count, stride=stride // 4), :]

    write_rows(lines, offsets()[UPS] - shift, rows, length, get)
    write_row(lines, shift, UPSB, row_of(sums2, 3))
    write_matrix(lines, shift, HEAD, held, g_head)
    write_row(lines, shift, HEADB, row_of(sums2, 4))
    scatter_out(devices, shard_len, plane_size, planes, place[0], lines, low, keep, send)


def early_flat_kernel(
    devices, shard_len, plane_size, planes, place, got2, sums1, hidden1, g_up1, g_down1, g_downs, sums_low, g_taps2, sums2,
    keep, send, lines, held,
):
    low, _ = span(UP1, SHIFT2)
    shift = low * LANES
    clear_ends(lines, low, UP1, SHIFT2)
    write_matrix(lines, shift, UP1, held, g_up1)
    write_row(lines, shift, UPB1, row_of(hidden1, 0))
    write_matrix(lines, shift, DOWN1, held, g_down1)
    write_row(lines, shift, DOWNB1, row_of(sums1, 2))
    write_matrix(lines, shift, DOWNS, held, g_downs)
    write_row(lines, shift, DOWNSB, row_of(sums_low, 0))
    across = jnp.concatenate([g_taps2[...], jnp.zeros((LANES - g_taps2.shape[0], C2), f32)], axis=0).T
    held[:C2, :] = across
    write_short(lines, offsets()[TAPS2] - shift, WIDTH2, TAPS, lambda r: held[r : r + 1, :])
    write_row(lines, shift, GAIN2, norm_row(got2, sums2))
    write_row(lines, shift, SHIFT2, row_of(sums2, 0))
    scatter_out(devices, shard_len, plane_size, planes, place[0], lines, low, keep, send)


def group_taps():
    table = []
    for first in (0, 3):
        for p in range(KSIZE):
            table.append([p * KSIZE + first + t for t in range(3)])
    for k in range(3):
        table.append([(3 * k + t) * KSIZE + 6 if 3 * k + t < KSIZE else -1 for t in range(3)])
    return table


def body(fields, targets, ocean_depth, thickness_class, params, moment1, moment2):
    shard_len = params.shape[0]
    devices = lax.axis_size(AXES)
    plane_size = 2 * lax.axis_size("lvl")
    me = lax.axis_index(AXES)
    _, tall = shard_places(devices, shard_len)
    at = (me * (shard_len % 2048)) % 2048
    block = lax.dynamic_update_slice(jnp.zeros((tall * LANES,), bf16), params.astype(bf16), (at,))
    near_planes = planes_of(devices, shard_len, 0, first_end(), plane_size)
    far_planes = [p for p in range(devices // plane_size) if p not in near_planes]
    plane_steps, pick_planes = gather_steps(near_planes, far_planes)
    blocks = block.reshape(1, tall, LANES)
    place_row = jnp.broadcast_to(me % plane_size, (1,)).astype(jnp.int32)

    smem = pl.BlockSpec(memory_space=pltpu.SMEM)
    vmem = pl.BlockSpec(memory_space=pltpu.VMEM)
    parts = lax.axis_size("lvl")
    chans, batch, all_rows, all_cols = fields.shape
    bands = BLOCKS // batch
    rows, cols = all_rows // bands, all_cols // parts
    half_rows, half_cols = rows // 2, cols // 2
    cells, low_cells = rows * cols * 8, half_rows * half_cols * 8
    wide_cols = cols + 2 * REACH
    low_border = (half_rows + 2 * REACH) * (half_cols + 2 * REACH) * 8

    def packed(values, reach):
        width = cols + 2 * reach
        lanes = chans * BLOCKS
        copies = call(
            lambda *refs: pack_kernel(parts, cols, reach, *refs),
            [((parts, rows * width, lanes), bf16)],
            scratch=[
                pltpu.VMEM((-(-all_cols // LANES), chans * batch * all_rows, LANES), f32),
                pltpu.VMEM((16 + -(-all_cols // LANES) * LANES, lanes), f32),
                pltpu.VMEM((parts, rows * width, lanes), f32),
            ],
            micros=3,
            name="pack",
        )(values.reshape(-1, all_cols))[0]
        return copies

    def given(copies):
        return lax.all_to_all(copies, "lvl", 0, 0, tiled=True)

    field_copies = packed(fields, REACH)
    goal_copies = packed(targets, 0)
    for step in plane_steps[:-1]:
        blocks = step(blocks)
    goal_copies, blocks = tie(goal_copies, blocks)
    blocks = plane_steps[-1](blocks)
    send_room = 2 * REACH * -(-wide_cols // 8) * 8
    field_cells, lower, upper = call(
        lambda *refs: fields_kernel(parts, rows, cols, *refs),
        [((rows * wide_cols * 8, LANES), f32), ((send_room, LANES), bf16), ((send_room, LANES), bf16)],
        scratch=[pltpu.VMEM((send_room, LANES), f32)],
        micros=4,
        name="fields",
    )(given(field_copies))
    (field_cells, lower, upper), blocks = tie((field_cells, lower, upper), blocks)
    above, below = lines_out(lower, upper)
    near_blocks, far_blocks = pick_planes(blocks)
    near_steps = within_steps()
    state = near_steps[0](near_blocks)
    (field_cells, above, below), state = tie((field_cells, above, below), state)
    state = near_steps[1](state)
    shifted_rows = (rows + 2 * REACH) * cols * 8
    first_cells, second_cells, third_cells = call(
        lambda *refs: shift_kernel(rows, cols, *refs),
        [((shifted_rows, C1), bf16)] * 3,
        scratch=[
            pltpu.VMEM((2 * REACH * wide_cols * 8, LANES), f32),
            pltpu.VMEM(((rows + 2 * REACH + 2) * wide_cols * 8, LANES), f32),
            pltpu.VMEM(((rows + 2 * REACH + 2) * wide_cols * 8, LANES), f32),
        ],
        micros=6,
        name="shift",
    )(field_cells, above, below)
    (first_cells, second_cells, third_cells), state = tie((first_cells, second_cells, third_cells), state)
    blocks = near_steps[2](state)
    goal = call(
        lambda *refs: targets_kernel(parts, *refs),
        [((cells, LANES), bf16)],
        scratch=[pltpu.VMEM((cells, LANES), f32)],
        micros=4,
        name="targets",
    )(given(goal_copies))[0]
    more_blocks = far_blocks
    for step in within_steps():
        more_blocks = step(more_blocks)

    deep = depth_cells(ocean_depth, batch)
    depth_rows = jnp.broadcast_to(deep.astype(f32)[..., None], deep.shape + (LANES,)).reshape(cells, LANES)
    low = jnp.max(deep.reshape(half_rows, 2, half_cols, 2, 8), axis=(1, 3))
    low_rows = jnp.broadcast_to(low.astype(f32)[..., None], low.shape + (LANES,)).reshape(low_cells, LANES)
    channel = jnp.arange(CI, dtype=jnp.int32)
    level = jnp.where(channel < 4 * LEVELS, channel // 4, 0)
    level_row = jnp.where(channel < CIN, level, LEVELS + 1).astype(f32)
    thickf = thickness_class.astype(f32)
    onehot = (level[:, None] == jnp.arange(LEVELS, dtype=jnp.int32)[None, :]).astype(f32)
    chosen = ((channel % 4 == 0) & (channel < 4 * LEVELS)).astype(f32)
    heat_take = chosen * jnp.sum(onehot * thickf[None, :], axis=1) / jnp.sum(thickf)
    ocean_cells = jnp.sum((level_row[None, None, :] < ocean_depth.astype(f32)[:, :, None]).astype(f32))
    ocean_cells = batch * ocean_cells
    surface_cells = jnp.sum((deep > 0).astype(f32))
    low_surface = jnp.sum((low > 0).astype(f32))
    index8 = jnp.arange(8)[:, None]
    counts1 = jnp.where(index8 == 2, surface_cells, jnp.where(index8 == 3, ocean_cells, 0.0))
    counts1 = jnp.broadcast_to(counts1, (8, C1))
    counts2 = jnp.where(index8 == 2, low_surface, jnp.where(index8 == 3, ocean_cells, 0.0))
    counts2 = jnp.broadcast_to(counts2, (8, C2))

    tables = jnp.pad(jnp.stack([level_row, heat_take]), ((0, 6), (0, 0)))
    source_lane = jnp.arange(C1, dtype=jnp.int32)[None, :, None]
    target_lane = jnp.arange(H1, dtype=jnp.int32)[None, None, :]
    quarter_at = jnp.arange(4, dtype=jnp.int32)[:, None, None]
    perm = ((source_lane * 4 + quarter_at == target_lane) & (source_lane < WIDTH)).astype(bf16)
    table = group_taps()
    third_at = jnp.arange(C1, dtype=jnp.int32) // CIN
    wanted = jnp.array([line + [-1] for line in table], dtype=jnp.int32)[:, third_at]
    pick = (wanted[:, :, None] == jnp.arange(LANES, dtype=jnp.int32)[None, None, :]).astype(bf16)
    held_room = pltpu.VMEM((4 * H2, LANES), f32)
    stem_in, near1, vecs1, up_in1, bias_in1, down_in1, downs_in, downs_four, down_rows = call(
        lambda *refs: first_params_kernel(devices, shard_len, plane_size, near_planes, *refs),
        [
            ((C1, CI), bf16), ((C1, LANES), bf16), ((8, C1), f32), ((H1, C1), bf16),
            ((1, H1), f32), ((C1, H1), bf16), ((C2, H1), bf16), ((4, C2, C1), bf16), ((8, C2), f32),
        ],
        ins=[smem, vmem, vmem],
        scratch=[pltpu.VMEM((first_end(), LANES), f32), held_room],
        micros=8,
        name="first_params",
    )(place_row, blocks, perm)
    taps_in2, vecs2, up_in2, bias_in2, down_in2, ups_four, fine_rows, head_in, last_rows = call(
        lambda *refs: rest_params_kernel(devices, shard_len, plane_size, near_planes, far_planes, *refs),
        [
            ((TAPS, 8, C2), f32), ((8, C2), f32), ((H2, C2), bf16), ((1, H2), f32), ((C2, H2), bf16),
            ((4, C1, C2), bf16), ((8, C1), f32), ((CI, C1), bf16), ((8, CI), f32),
        ],
        ins=[smem, vmem, vmem],
        scratch=[pltpu.VMEM((rest_end() - rest_start(), LANES), f32), held_room],
        micros=13,
        name="rest_params",
    )(place_row, blocks, more_blocks)

    hzero, conv1, stats1 = call(
        lambda *refs: stem_kernel(rows, cols, *refs),
        [((cells, C1), bf16), ((cells, C1), f32), ((devices, 8, C1), f32)],
        scratch=[pltpu.VMEM((GROUPS * C1, C1), bf16), pltpu.VMEM((C1, C1), f32), pltpu.VMEM((8, C1), f32)],
        micros=16,
        name="stem_conv",
    )(first_cells, second_cells, third_cells, near1, stem_in, pick, depth_rows, counts1)
    got1 = swap(stats1)
    chunk, low_chunk = 2 * cols * 8, half_cols * 8
    hone, gated1, slope1, patches, coarse = call(
        lambda *refs: fine_kernel(cols, *refs),
        [
            ((cells, C1), bf16),
            ((cells, H1), bf16),
            ((cells, H1), bf16),
            ((low_cells, H1), bf16),
            ((low_cells, C2), bf16),
        ],
        grid=(half_rows,),
        ins=[
            whole(devices, 8, C1), band(chunk, C1), band(chunk, C1), whole(8, C1), whole(H1, C1), whole(1, H1),
            whole(C1, H1), whole(4, C1, H1), whole(C2, H1), whole(8, C2),
        ],
        out_specs=[
            band(chunk, C1), band(chunk, H1), band(chunk, H1), band(low_chunk, H1), band(low_chunk, C2),
        ],
        scratch=[pltpu.VMEM((chunk, C1), f32)],
        micros=15,
        name="fine_forward",
    )(got1, conv1, hzero, vecs1, up_in1, bias_in1, down_in1, perm, downs_in, down_rows)

    edge = edge_lines(half_cols)
    side = half_rows * REACH * 8

    def halo(*arrays):
        count = len(arrays)
        joined = [columns_out(values, half_rows, half_cols) for values in arrays]
        lower, upper = call(
            lambda *refs: edge_kernel(half_rows, half_cols, count, *refs),
            [((count * edge, C2), bf16)] * 2,
            scratch=[pltpu.VMEM((low_cells + 2 * side, LANES), f32), pltpu.VMEM((edge, LANES), f32)],
            micros=3,
            name="edge",
        )(*[ref for values, sides in zip(arrays, joined) for ref in (values, *sides)])
        above, below = lines_out(lower, upper)
        return [
            [values, *sides, above[k * edge : (k + 1) * edge], below[k * edge : (k + 1) * edge]]
            for k, (values, sides) in enumerate(zip(arrays, joined))
        ]

    def border_tiles(tile):
        return [tile(low_cells), tile(side), tile(side), tile(edge), tile(edge)]

    def edge_tile(rows):
        return pl.BlockSpec((rows, LANES), lambda i: (0, WIDTH2 // LANES))

    (border2,) = halo(coarse)
    conv2, masked2, stats2 = call(
        lambda *refs: coarse_conv_kernel(half_rows, half_cols, *refs),
        [((low_cells, C2), f32), ((low_cells, C2), bf16), ((devices, 8, C2), f32)],
        grid=(C2 // LANES,),
        ins=border_tiles(lane_tile) + [TAP_TILE, whole(low_cells, LANES), lane_tile(8)],
        out_specs=[lane_tile(low_cells), lane_tile(low_cells), stats_tile(devices)],
        scratch=[pltpu.VMEM((low_border, LANES), f32), pltpu.VMEM((edge, LANES), f32)],
        micros=11,
        name="coarse_conv",
    )(*border2, taps_in2, low_rows, counts2)
    got2 = swap(stats2)
    (
        skip, top, dy, ds, du, dtop, dv2, gated2, da2, normal2, dx2, sums2, hidden2, copies2,
    ) = call(
        lambda *refs: middle_kernel(cols, *refs),
        [
            ((cells, C1), bf16), ((low_cells, C2), bf16), ((cells, CI), bf16), ((cells, C1), f32),
            ((4, low_cells, C1), bf16), ((low_cells, C2), f32), ((low_cells, C2), bf16), ((low_cells, H2), bf16),
            ((low_cells, H2), bf16), ((low_cells, C2), bf16), ((low_cells, C2), bf16),
            ((8, C2), f32), ((8, H2), f32), ((devices, 8, C2), f32),
        ],
        grid=(half_rows,),
        ins=[
            whole(devices, 8, C2), band(low_chunk, C2), band(low_chunk, C2), whole(8, C2), whole(H2, C2), whole(1, H2),
            whole(C2, H2), whole(4, C1, C2), whole(8, C1), whole(CI, C1), whole(8, CI), whole(8, CI), band(chunk, C1),
            band(chunk, CI), band(chunk, LANES),
        ],
        out_specs=[
            band(chunk, C1), band(low_chunk, C2), band(chunk, CI), band(chunk, C1),
            pl.BlockSpec((4, low_chunk, C1), lambda i: (0, i, 0)), band(low_chunk, C2), band(low_chunk, C2),
            band(low_chunk, H2), band(low_chunk, H2), band(low_chunk, C2), band(low_chunk, C2),
            whole(8, C2), whole(8, H2), whole(devices, 8, C2),
        ],
        micros=20,
        name="middle",
    )(
        got2, conv2, coarse, vecs2, up_in2, bias_in2, down_in2, ups_four, fine_rows, head_in, last_rows, tables, hone, goal,
        depth_rows,
    )
    back2 = swap(copies2)
    dx_halo, masked_halo = halo(dx2, masked2)
    da2, dx_halo[1] = tie(da2, dx_halo[1])
    g_up2, g_down2, g_ups, g_head = call(
        coarse_weights_kernel,
        [((H2, C2), f32), ((C2, H2), f32), ((4, C1, C2), f32), ((CI, C1), f32)],
        micros=10,
        name="coarse_weights",
    )(da2, normal2, dv2, gated2, du, top, dy, skip)
    late_planes = planes_of(devices, shard_len, *span(UP2, HEADB), plane_size)
    half_seats = plane_size // 2
    late_keep, late_send = call(
        lambda *refs: late_flat_kernel(devices, shard_len, plane_size, late_planes, *refs),
        [((half_seats * len(late_planes), tall, LANES), kind) for kind in (f32, bf16)],
        ins=[smem] + [vmem] * 6,
        scratch=[pltpu.VMEM((span(UP2, HEADB)[1] - span(UP2, HEADB)[0], LANES), f32), held_room],
        micros=9,
        name="late_flat",
    )(place_row, sums2, hidden2, g_up2, g_down2, g_ups, g_head)
    dcells, g_taps2 = call(
        lambda *refs: coarse_conv_back_kernel(half_rows, half_cols, *refs),
        [((low_cells, C2), bf16), ((56, C2), f32)],
        grid=(C2 // LANES,),
        ins=[stats_tile(devices), stats_tile(devices), lane_tile(8)]
        + border_tiles(lane_tile) * 3
        + border_tiles(edge_tile)
        + [TAP_TILE, lane_tile(low_cells)],
        out_specs=[lane_tile(low_cells), lane_tile(56)],
        scratch=[
            pltpu.VMEM((low_border, LANES), f32),
            pltpu.VMEM((low_border, LANES), f32),
            pltpu.VMEM((edge, LANES), f32),
            pltpu.VMEM((low_border, LANES), f32),
        ],
        micros=25,
        name="coarse_conv_back",
    )(got2, back2, vecs2, *border2, *dx_halo, *masked_halo, *masked_halo, taps_in2, dtop)

    state, late_steps = scatter_steps(late_keep, late_send, late_planes)
    dcells, state = tie(dcells, late_steps[0](state))
    for step in late_steps[1:-3]:
        state = step(state)
    dv1, da1, dn1, normal1, sums1, hidden1, sums_low, copies1 = call(
        lambda *refs: fine_back_kernel(cols, *refs),
        [
            ((cells, C1), bf16), ((cells, H1), bf16), ((cells, C1), f32), ((cells, C1), bf16),
            ((8, C1), f32), ((8, H1), f32), ((8, C2), f32), ((devices, 8, C1), f32),
        ],
        grid=(half_rows,),
        ins=[
            whole(devices, 8, C1), band(low_chunk, C2), whole(4, C2, C1), band(chunk, C1), whole(8, C1),
            band(chunk, C1), band(chunk, H1), whole(H1, C1), whole(C1, H1),
        ],
        out_specs=[
            band(chunk, C1), band(chunk, H1), band(chunk, C1), band(chunk, C1), whole(8, C1), whole(8, H1), whole(8, C2),
            whole(devices, 8, C1),
        ],
        micros=13,
        name="fine_backward",
    )(got1, dcells, downs_four, ds, vecs1, conv1, slope1, up_in1, down_in1)
    da1, state = tie(da1, late_steps[-3](state))
    back1 = swap(copies1)
    g_up1, g_down1, g_downs = call(
        fine_weights_kernel,
        [((H1, C1), f32), ((C1, H1), f32), ((C2, H1), f32)],
        micros=11,
        name="fine_weights",
    )(da1, normal1, dv1, gated1, dcells, patches)
    early_planes = planes_of(devices, shard_len, *span(UP1, SHIFT2), plane_size)
    early_keep, early_send = call(
        lambda *refs: early_flat_kernel(devices, shard_len, plane_size, early_planes, *refs),
        [((half_seats * len(early_planes), tall, LANES), kind) for kind in (f32, bf16)],
        ins=[smem] + [vmem] * 9,
        scratch=[pltpu.VMEM((span(UP1, SHIFT2)[1] - span(UP1, SHIFT2)[0], LANES), f32), held_room],
        micros=6,
        name="early_flat",
    )(place_row, got2, sums1, hidden1, g_up1, g_down1, g_downs, sums_low, g_taps2, sums2)
    early_keep, state = tie(early_keep, late_steps[-2](state))
    early_state, early_steps = scatter_steps(early_keep, early_send, early_planes)
    early_state = early_steps[0](early_state)
    dn1, early_state = tie(dn1, early_state)
    late = late_steps[-1](state)
    for step in early_steps[1:]:
        early_state = step(early_state)
    early = early_state
    tail_lines = -(-span(STEM, SHIFT1)[1] // (8 * devices)) * 8
    tail = call(
        lambda *refs: stem_back_kernel(rows, cols, *refs),
        [((devices, tail_lines, LANES), f32)],
        scratch=[
            pltpu.VMEM((C1, cells), bf16), pltpu.VMEM((C1, C1), f32), pltpu.VMEM((C1, LANES), f32), pltpu.VMEM((C1, C1), f32),
            pltpu.VMEM((devices * tail_lines, LANES), f32), pltpu.VMEM((C1, LANES), f32),
        ],
        micros=26,
        name="stem_back",
    )(
        got1, back1, vecs1, dn1, conv1, depth_rows, dv1, first_cells, second_cells, third_cells, near1, stem_in, pick, sums1,
    )[0]

    chunk_sum = jnp.sum(swap(tail), axis=0)
    mine = lax.dynamic_slice_in_dim((late + early).reshape(-1), at, shard_len)
    squares = jnp.sum(mine * mine) + jnp.sum(chunk_sum * chunk_sum)
    loss_part = jnp.sum(sums2[5, :LANES])
    stats = jnp.where(index8 == 0, loss_part, jnp.where(index8 == 1, squares, 0.0))
    last = jnp.concatenate([chunk_sum, jnp.broadcast_to(stats, (8, LANES))], axis=0)
    last = swap(jnp.broadcast_to(last[None], (devices,) + last.shape))
    tail_flat = last[:, :tail_lines].reshape(devices * tail_lines, LANES)
    totals = jnp.sum(last[:, tail_lines:, 0], axis=0)
    loss_total, norm = totals[0], jnp.sqrt(totals[1])
    count = jnp.sum(got1[:, 3, 0])
    tail_flat = jnp.pad(tail_flat, ((0, tall), (0, 0)))
    line = jnp.minimum(me * shard_len // 2048 * 16, devices * tail_lines)
    mine_tail = lax.dynamic_slice_in_dim(tail_flat, line, tall).reshape(-1)
    mine = mine + lax.dynamic_slice_in_dim(mine_tail, at, shard_len)
    clipped = mine * jnp.minimum(1.0, CLIP / norm)
    first = BETA_ONE * moment1 + (1.0 - BETA_ONE) * clipped
    second = BETA_TWO * moment2 + (1.0 - BETA_TWO) * clipped * clipped
    ratio = first / (1.0 - BETA_ONE**STEP) / (jnp.sqrt(second / (1.0 - BETA_TWO**STEP)) + ADAM_EPS)
    updated = params - LRATE * (ratio + DECAY * params)
    return (loss_total, count, norm, updated, first, second)


def solution(mesh):
    in_specs = (
        P("lvl", None, "lat", None),
        P("lvl", None, "lat", None),
        P("lat", "lvl"),
        P(),
        P(("lat", "lvl")),
        P(("lat", "lvl")),
        P(("lat", "lvl")),
    )
    out_specs = (P(), P(), P(), P(("lat", "lvl")), P(("lat", "lvl")), P(("lat", "lvl")))
    return jax.shard_map(body, mesh=mesh, in_specs=in_specs, out_specs=out_specs, check_vma=False)
```

```python
import math

import jax
import jax.numpy as jnp
from jax import lax
from jax.experimental import pallas as pl
from jax.experimental.pallas import tpu as pltpu
from jax.sharding import PartitionSpec as P

CIN = 80
WIDTH = 200
EXPAND = 800
WIDTH2 = 400
EXPAND2 = 1600
KSIZE = 7
TAPS = KSIZE * KSIZE
LEVELS = 19
STEP = 10

CLIP = 0.01
LRATE = 0.05
BETA_ONE = 0.9
BETA_TWO = 0.999
ADAM_EPS = 1e-08
DECAY = 0.1
HEAT_WEIGHT = 40.0
NORM_EPS = 1e-05

AXES = ("lat", "lvl")

CI = 128
C1 = 256
H1 = 896
C2 = 512
H2 = 1664
BLOCKS = 8
LANES = 128
REACH = KSIZE // 2
GROUPS = 17

f32 = jnp.float32
bf16 = jnp.bfloat16
VMEM_LIMIT = 60 * 1024 * 1024


def plane_bits():
    bits = []
    for axis in AXES:
        count = lax.axis_size(axis)
        step = count // 2
        while step >= 1:
            bits.append((axis, count, step))
            step //= 2
    across = [b for b in bits if b[0] == "lat" and b[2] > 1]
    within = [b for b in bits if b not in across]
    return across, within


def exchange(values, axis, count, step):
    return lax.ppermute(values, axis, [(i, i ^ step) for i in range(count)])


def half_rows_of(tall):
    return -(-tall // 32) * 16


def gather_steps(near, far):
    across, (first, second, *others) = plane_bits()

    def plane_step(bit):
        return lambda blocks: jnp.concatenate([blocks, exchange(blocks, *bit)], axis=0)

    def pick(blocks):
        planes = blocks.shape[0]
        plane = lax.axis_index("lat") // 2
        found = [lax.dynamic_index_in_dim(blocks, seat_of(plane, p, planes), 0, False) for p in range(planes)]
        return [jnp.stack([found[p] for p in group]) for group in (near, far)]

    return [plane_step(bit) for bit in across], pick


def within_steps():
    _, (first, second, *others) = plane_bits()

    def halves(blocks):
        cut = half_rows_of(blocks.shape[1])
        left, right = blocks[:, :cut], blocks[:, cut:]
        left = jnp.stack([left, exchange(left, *first)], axis=0)
        right = jnp.stack([right, exchange(right, *second)], axis=0)
        return left, right

    def join(state):
        left, right = state
        left = jnp.stack([left, exchange(left, *second)], axis=0)
        right = jnp.stack([right, exchange(right, *first)], axis=1)
        both = jnp.concatenate([left, right], axis=3)
        return both.reshape((-1,) + both.shape[3:])

    def rest(both):
        for bit in others[:-1]:
            both = jnp.concatenate([both, exchange(both, *bit)], axis=0)
        return both, exchange(both, *others[-1])

    return [halves, join, rest]


def scatter_steps(keep, send, planes):
    _, (first, second, *others) = plane_bits()
    cut = half_rows_of(keep.shape[1])

    def inner(turn, bit):
        def step(state):
            keep, send = state
            if turn > 0:
                half = keep.shape[0] // 2
                keep, send = keep[:half], keep[half:].astype(bf16)
            keep = keep + exchange(send, *bit).astype(f32)
            return keep, None

        return step

    def outer(state):
        keep, _ = state
        parts = keep.reshape((2, 2, len(planes)) + keep.shape[1:])
        left, right = parts[:, :, :, :cut], parts[:, :, :, cut:]
        left = left[0] + exchange(left[1].astype(bf16), *second).astype(f32)
        right = right[:, 0] + exchange(right[:, 1].astype(bf16), *first).astype(f32)
        return left, right

    steps = [inner(turn, bit) for turn, bit in enumerate(reversed(others))]
    return (keep, send), steps + [outer]


def merge_planes(groups):
    total = lax.axis_size("lat") // 2
    merged = []
    for side in range(2):
        rows = []
        for p in range(total):
            held = [state[side][:, planes.index(p)] for state, planes in groups if p in planes]
            rows.append(sum(held[1:], held[0]))
        merged.append(jnp.stack(rows, axis=1))
    return merged


def scatter_last(state):
    _, (first, second, *_) = plane_bits()
    left, right = state
    left = left[0] + exchange(left[1].astype(bf16), *first).astype(f32)
    right = right[0] + exchange(right[1].astype(bf16), *second).astype(f32)
    return jnp.concatenate([left, right], axis=1)


def tie(first, second):
    return lax.optimization_barrier((first, second))


def scatter_planes(rows):
    count = lax.axis_size("lat")
    plane = lax.axis_index("lat") // 2
    mine = lax.dynamic_index_in_dim(rows, plane, 0, False)
    parts = [
        exchange(lax.dynamic_index_in_dim(rows, plane ^ away, 0, False).astype(bf16), "lat", count, 2 * away)
        for away in range(1, count // 2)
    ]
    for part in parts:
        mine = mine + part.astype(f32)
    return mine


def swap(copies):
    return lax.all_to_all(copies, AXES, 0, 0, tiled=True)


def neighbours(axis):
    ends = lax.axis_size(axis) - 1
    return [(i, i + 1) for i in range(ends)], [(i + 1, i) for i in range(ends)]


def columns_out(arrays, rows, cols):
    onward, back = neighbours("lvl")
    sides = []
    for start, pairs in ((cols - REACH, onward), (0, back)):
        own = [values.reshape(rows, cols, 8, -1)[:, start : start + REACH] for values in arrays]
        own = jnp.concatenate([part.reshape(rows * REACH * 8, -1) for part in own], axis=0)
        sides.append(lax.ppermute(own, "lvl", pairs))
    size = rows * REACH * 8
    return [[side[k * size : (k + 1) * size] for side in sides] for k in range(len(arrays))]


def lines_out(lower, upper):
    onward, back = neighbours("lat")
    return lax.ppermute(lower, "lat", onward), lax.ppermute(upper, "lat", back)


def depth_cells(depth, batch):
    rows, cols = depth.shape
    bands = BLOCKS // batch
    split = depth.reshape(bands, rows // bands, cols).transpose(1, 2, 0)
    return jnp.concatenate([split] * batch, axis=2)


def block_shapes(chans, hidden):
    return [
        (chans, TAPS),
        (chans,),
        (chans,),
        (hidden, chans),
        (hidden,),
        (chans, hidden),
        (chans,),
    ]


def shapes_of():
    return (
        [(WIDTH, CIN)]
        + block_shapes(WIDTH, EXPAND)
        + [(WIDTH2, 4 * WIDTH), (WIDTH2,)]
        + block_shapes(WIDTH2, EXPAND2)
        + [(4 * WIDTH, WIDTH2), (WIDTH,), (CIN, WIDTH), (CIN,)]
    )


def fill(values, *shape):
    return jnp.pad(values, [(0, n - m) for n, m in zip(shape, values.shape)])


def nt(left, right):
    return lax.dot_general(left, right, (((1,), (1,)), ((), ())), preferred_element_type=f32)


def nn(left, right):
    return lax.dot_general(left, right, (((1,), (0,)), ((), ())), preferred_element_type=f32)


def tn(left, right):
    return lax.dot_general(left, right, (((0,), (0,)), ((), ())), preferred_element_type=f32)


def rows8(start, amount):
    return pl.ds(pl.multiple_of(start * 8, 8), amount * 8)


def convolve(source, taps, rows, cols, emit, carry, flip=False):
    width = cols + 2 * REACH

    def line(row, carry):
        total = jnp.zeros((cols, 8, LANES), f32)
        for p in range(KSIZE):
            seen = source[rows8((row + p) * width, width), :].reshape(width, 8, LANES)
            for q in range(KSIZE):
                tap = p * KSIZE + q
                total = total + seen[q : q + cols] * taps[TAPS - 1 - tap if flip else tap][None]
        return emit(rows8(row * cols, cols), total, carry)

    return lax.fori_loop(0, rows, line, carry)


def row_sum(values):
    return jnp.sum(values, axis=0, keepdims=True)


def spread_rows(values, tiles):
    return [values[:, m * LANES : (m + 1) * LANES] for m in range(tiles)]


def stats_block(first, second, counts):
    tiles = first.shape[1] // LANES
    rows = spread_rows(first, tiles) + spread_rows(second, tiles)
    if len(rows) < 8:
        rows = rows + [jnp.zeros((8 - len(rows), LANES), f32)]
    block = jnp.concatenate(rows, axis=0)
    return block if counts is None else block + counts


def wide_row(total, start, tiles):
    return jnp.concatenate([total[start + m : start + m + 1] for m in range(tiles)], axis=1)


def count_places(width):
    if width == C1:
        return (4, 0), (5, 0)
    return (WIDTH2 // LANES, WIDTH2 % LANES), (WIDTH2 // LANES, WIDTH2 % LANES + 1)


def norm_rows(got, width):
    tiles = width // LANES
    total = jnp.sum(got[...], axis=0)
    (r, c), (ro, co) = count_places(width)
    cells, ocean = total[r : r + 1, c : c + 1], total[ro : ro + 1, co : co + 1]
    lane = lax.broadcasted_iota(jnp.int32, (1, width), 1)
    sums = jnp.where(lane < (WIDTH if width == C1 else WIDTH2), wide_row(total, 0, tiles), 0.0)
    mean = sums / cells
    inverse = lax.rsqrt(wide_row(total, tiles, tiles) / cells - mean * mean + NORM_EPS)
    return mean, inverse, cells, ocean


def gelu_pair(act):
    square = act * act
    flat = 0.7978845608028654
    cube = 0.044715
    bent = jnp.tanh(act * (flat + (flat * cube) * square))
    half = 0.5 + 0.5 * bent
    slope = half + 0.5 * act * (1.0 - bent * bent) * (flat + (3.0 * flat * cube) * square)
    return act * half, slope


def quarter(values, rows, cols, p, q):
    chans = values.shape[-1]
    split = values.reshape(rows // 2, 2, cols // 2, 2, 8, chans)
    return split[:, p, :, q].reshape(rows * cols * 2, chans)


def from_quarters(parts, rows, cols):
    chans = parts[0].shape[-1]
    cells = [part.reshape(rows // 2, cols // 2, 8, chans) for part in parts]
    lines = [jnp.stack(cells[2 * p : 2 * p + 2], axis=2) for p in range(2)]
    return jnp.stack(lines, axis=1).reshape(rows * cols * 8, chans)


def call(kernel, outs, grid=(), ins=None, out_specs=None, scratch=(), micros=5, name=None):
    params = dict(out_shape=[jax.ShapeDtypeStruct(s, t) for s, t in outs])
    if ins:
        params.update(in_specs=ins)
    if grid:
        params.update(grid=grid, out_specs=out_specs)
    return pl.pallas_call(
        kernel,
        scratch_shapes=list(scratch),
        compiler_params=pltpu.CompilerParams(vmem_limit_bytes=VMEM_LIMIT),
        cost_estimate=pl.CostEstimate(flops=int(micros * 1.1e9), bytes_accessed=100000, transcendentals=0),
        name=name,
        **params,
    )


def whole(*shape):
    return pl.BlockSpec(shape, lambda i: (0,) * len(shape))


def band(rows, cols):
    return pl.BlockSpec((rows, cols), lambda i: (i, 0))


def lane_tile(rows):
    return pl.BlockSpec((rows, LANES), lambda i: (0, i))


def stats_tile(devices):
    return pl.BlockSpec((devices, 8, LANES), lambda i: (0, 0, i))


TAP_TILE = pl.BlockSpec((TAPS, 8, LANES), lambda i: (0, 0, i))


def conv_sums(source, taps, depth, counts, out, stats, rows, cols, block):
    def emit(place, total, carry):
        flat = total.reshape(cols * 8, LANES)
        out[place, :] = flat
        ocean = depth[place, :] > 0.0
        kept = jnp.where(ocean, flat, 0.0)
        kept_cells = kept.reshape(cols, 8, LANES)
        return (carry[0] + jnp.sum(kept_cells, axis=0), carry[1] + jnp.sum(kept_cells * total, axis=0))

    zero = jnp.zeros((8, LANES), f32)
    first, second = convolve(source, taps, rows, cols, emit, (zero, zero))
    tile = pl.program_id(0)
    tiles = pl.num_programs(0)

    @pl.when(tile == 0)
    def _():
        block[...] = counts[...]

    block[pl.ds(tile, 1), :] += row_sum(first)
    block[pl.ds(C2 // LANES + tile, 1), :] += row_sum(second)

    @pl.when(tile == tiles - 1)
    def _():
        stats[...] = jnp.broadcast_to(block[...][None], stats.shape)


def lay_border(rows, cols, source, held, centre, left, right, above, below):
    width = cols + 2 * REACH
    sides = [left[...].astype(f32), right[...].astype(f32)]
    for row in range(rows):
        start = (row + REACH) * width
        source[rows8(start + REACH, cols), :] = centre[rows8(row * cols, cols), :].astype(f32)
        for side, place in zip(sides, (0, cols + REACH)):
            source[rows8(start + place, REACH), :] = side[row * REACH * 8 : (row + 1) * REACH * 8]
    for t in range(REACH):
        for start, target, way in ((rows + t, t, 1), (REACH + t, rows + REACH + t, 7)):
            line = source[rows8(start * width, width), :].reshape(width, 8, LANES)
            source[rows8(target * width, width), :] = pltpu.roll(line, way, 1).reshape(width * 8, LANES)
    amount = REACH * width
    for part, base in ((above, 0), (below, (rows + REACH) * width * 8 + BLOCKS // 2 - 1)):
        held[...] = part[...].astype(f32)
        for b in range(2):
            values = held[pl.ds(b, amount, stride=2), :]
            source[pl.ds(base + b * (BLOCKS // 2), amount, stride=8), :] = values


def pack_kernel(parts, cols, reach, values, out, tiles, flat):
    total = values.shape[1]
    width = cols + 2 * reach
    lines = out.shape[1]
    depth = values.shape[0] // lines
    count = tiles.shape[0]
    for k in range(count):
        size = min(LANES, total - k * LANES)
        tiles[k, :, :size] = values[:, k * LANES : k * LANES + size].astype(f32)
        if size < LANES:
            tiles[k, :, size:] = jnp.zeros((values.shape[0], LANES - size), f32)
    blank = jnp.zeros((lines, LANES), f32)
    for row in range(depth):
        pieces = [tiles[k, pl.ds(row, lines, stride=depth), :] for k in range(count)]
        wide = jnp.concatenate([blank] + pieces + [blank], axis=1)
        for part in range(parts):
            start = LANES + part * cols - reach
            flat[part, :, row * width : (row + 1) * width] = wide[:, start : start + width]
    for part in range(parts):
        out[part] = flat[part].astype(bf16)


def unpack_cells(packed, parts, cells, across):
    lines = packed.shape[1]
    chans = lines // BLOCKS
    amount = packed.shape[2]
    for part in range(parts):
        across[part] = packed[part].astype(f32).T.astype(bf16)
    source = lax.broadcasted_iota(jnp.int32, (lines, LANES), 0)
    target = lax.broadcasted_iota(jnp.int32, (lines, LANES), 1)
    for s in range(BLOCKS):
        total = jnp.zeros((amount, LANES), f32)
        for part in range(parts):
            pick = ((target - part * chans) * BLOCKS + s == source).astype(bf16)
            total = total + nn(across[part], pick)
        cells[pl.ds(s, amount, stride=BLOCKS), :] = total


def targets_kernel(parts, packed, out, cells, across):
    unpack_cells(packed, parts, cells, across)
    out[...] = cells[...].astype(bf16)


def fields_kernel(parts, rows, cols, packed, cells, lower, upper, held, across):
    unpack_cells(packed, parts, cells, across)
    width = cols + 2 * REACH
    room = -(-width // 8) * 8
    held[...] = jnp.zeros(held.shape, f32)
    for out, low, band in ((lower, rows - REACH, BLOCKS // 2 - 1), (upper, 0, 0)):
        for b in range(2):
            for t in range(REACH):
                start = (low + t) * width * 8 + band + b * (BLOCKS // 2)
                at = (b * REACH + t) * room
                held[at : at + width, :] = cells[pl.ds(start, width, stride=8), :]
        out[...] = held[...].astype(bf16)


def lay_ends(rows, cols, cells, above, below, ends):
    width = cols + 2 * REACH
    room = -(-width // 8) * 8
    line = width * 8
    for t in range(REACH):
        for k, row, way in ((t, rows - REACH + t, 1), (REACH + t, t, 7)):
            values = cells[row * line : (row + 1) * line, :].reshape(width, 8, LANES)
            ends[k * line : (k + 1) * line, :] = pltpu.roll(values, way, 1).reshape(line, LANES)
    for part, base, band in ((above, 0, 0), (below, REACH, BLOCKS // 2 - 1)):
        values = part[...].astype(f32)
        for b in range(2):
            for t in range(REACH):
                at = (b * REACH + t) * room
                start = (base + t) * line + band + b * (BLOCKS // 2)
                ends[pl.ds(start, width, stride=8), :] = values[at : at + width]


def lay_shifted(rows, cols, cells, ends, out, col, across):
    line = (cols + 2 * REACH) * 8
    total = rows + 2 * REACH
    amount = cols * 8
    lane = lax.broadcasted_iota(jnp.int32, (amount, LANES), 1)

    def values(row, col):
        if row >= total:
            return jnp.zeros((amount, LANES), f32)
        if row < REACH:
            ref, start = ends, row * line
        elif row < REACH + rows:
            ref, start = cells, (row - REACH) * line
        else:
            ref, start = ends, (row - rows) * line
        return ref[start + col * 8 : start + col * 8 + amount, :]

    for row in range(total):
        near = values(row, col)
        middle = values(row + 1, col) if across else values(row, col + 1)
        last = values(row + 2, col) if across else values(row, col + 2)
        middle = pltpu.roll(middle, CIN, 1)
        last = pltpu.roll(last, 2 * CIN - LANES, 1)
        place = slice(row * amount, (row + 1) * amount)
        out[place, :LANES] = jnp.where(lane < CIN, near, middle).astype(bf16)
        out[place, LANES:] = jnp.where(lane < 2 * CIN - LANES, middle, last).astype(bf16)


def wide_stem(stem):
    return jnp.concatenate([stem.astype(f32), jnp.zeros((C1, C1 - CI), f32)], axis=1)


def triple_stem(stem):
    wide = wide_stem(stem)
    return wide + pltpu.roll(wide, CIN, 1) + pltpu.roll(wide, 2 * CIN, 1)


def stem_kernel(
    rows, cols, cells, above, below, near, stem, pick, depth, counts, hzero, out, stats,
    weights, wide, sums, ends, first, second, third,
):
    amount = cols * 8
    step = pl.program_id(0)
    size = out.shape[0]

    @pl.when(step == 0)
    def _():
        lay_ends(rows, cols, cells, above, below, ends)
        lay_shifted(rows, cols, cells, ends, first, 0, False)
        lay_shifted(rows, cols, cells, ends, second, REACH, False)
        lay_shifted(rows, cols, cells, ends, third, 2 * REACH, True)
        stem3 = triple_stem(stem[...])
        for index in range(GROUPS):
            both = nt(near[...], pick[index]) * stem3
            weights[index * C1 : (index + 1) * C1, :] = both.astype(bf16)
        wide[...] = wide_stem(stem[...]).astype(bf16)
        sums[...] = jnp.zeros(sums.shape, f32)

    def place(shift):
        return pl.ds(pl.multiple_of(step * size + shift * amount, amount), size)

    total = jnp.zeros((size, C1), f32)
    for p in range(KSIZE):
        total = total + nt(first[place(p), :], weights[p * C1 : (p + 1) * C1, :])
        total = total + nt(second[place(p), :], weights[(KSIZE + p) * C1 : (KSIZE + p + 1) * C1, :])
    for k in range(3):
        at = (2 * KSIZE + k) * C1
        total = total + nt(third[place(3 * k), :], weights[at : at + C1, :])
    out[...] = total
    hzero[...] = nt(second[place(REACH), :], wide[...]).astype(bf16)
    ocean = depth[...] > 0.0
    kept = jnp.where(jnp.concatenate([ocean, ocean], axis=1), total, 0.0)
    sums[0:1, :] += row_sum(kept)
    sums[1:2, :] += row_sum(kept * total)

    @pl.when(step == pl.num_programs(0) - 1)
    def _():
        stats[...] = jnp.broadcast_to(stats_block(sums[0:1, :], sums[1:2, :], counts[...])[None], stats.shape)


def edge_kernel(rows, cols, count, *refs):
    inputs, (lower, upper, held, edge) = refs[: 3 * count], refs[3 * count :]
    width = cols + 2 * REACH
    lines = edge_lines(cols)
    amount = rows * cols * 8
    side = rows * REACH * 8
    for k in range(count):
        for tile in range(C2 // LANES):
            lanes = slice(tile * LANES, (tile + 1) * LANES)
            for ref, start, size in zip(inputs[3 * k : 3 * k + 3], (0, amount, amount + side), (amount, side, side)):
                held[start : start + size, :] = ref[:, lanes].astype(f32)
            for out, low, band in ((lower, rows - REACH, BLOCKS // 2 - 1), (upper, 0, 0)):
                edge[lines - 16 :, :] = jnp.zeros((16, LANES), f32)
                for t in range(REACH):
                    for b in range(2):
                        s = band + b * (BLOCKS // 2)
                        at = t * width * 2 + b
                        for start, wide, col in ((amount, REACH, 0), (0, cols, REACH), (amount + side, REACH, REACH + cols)):
                            values = held[pl.ds(start + (low + t) * wide * 8 + s, wide, stride=8), :]
                            edge[pl.ds(at + 2 * col, wide, stride=2), :] = values
                out[k * lines : (k + 1) * lines, lanes] = edge[...].astype(bf16)


def edge_lines(cols):
    return -(-REACH * (cols + 2 * REACH) * 2 // 16) * 16


def coarse_conv_kernel(rows, cols, centre, left, right, above, below, taps, depth, counts, out, stats, source, held, block):
    lay_border(rows, cols, source, held, centre, left, right, above, below)
    conv_sums(source, taps, depth, counts, out, stats, rows, cols, block)


def fine_kernel(cols, got, conv, hzero, vecs, bias_rows, up, up_bias, down, perm, downs, down_rows, hone, gated, slope, patches, coarse, held):
    mean, inverse, _, _ = norm_rows(got, C1)
    scale = inverse * vecs[0:1]
    for part in range(2):
        place = pl.ds(part * cols * 8, cols * 8)
        normal = ((conv[place, :] - mean) * scale + vecs[1:2]).astype(bf16)
        act = nt(normal, up[...]) + up_bias[...]
        value, bend = gelu_pair(act)
        value = value.astype(bf16)
        gated[place, :] = value
        slope[place, :] = bend.astype(bf16)
        branch = nt(value, down[...]) + bias_rows[0:1]
        full = (hzero[place, :].astype(f32) + branch).astype(bf16)
        hone[place, :] = full
        held[place, :] = full.astype(f32)
    cells = held[...]
    mixed = jnp.zeros((cols * 4, H1), f32)
    for p in range(2):
        for q in range(2):
            mixed = mixed + nn(quarter(cells, 2, cols, p, q).astype(bf16), perm[p * 2 + q])
    mixed = mixed.astype(bf16)
    patches[...] = mixed
    coarse[...] = (nt(mixed, downs[...]) + down_rows[0:1]).astype(bf16)


def middle_kernel(
    cols, got, conv, cells, vecs, up, up_bias, down, ups, fine_rows, head, last_rows, tables, hone, targets, depth,
    skip_out, top_out, dy_out, ds_out, du_out, dtop_out, dv_out, gated_out, da_out, normal_out, dx_out,
    sums, hidden_sums, copies,
):
    mean, inverse, _, ocean_count = norm_rows(got, C2)
    scale = inverse * vecs[0:1]
    centred = conv[...] - mean
    normal = (centred * scale + vecs[1:2]).astype(bf16)
    normal_out[...] = normal
    value, bend = gelu_pair(nt(normal, up[...]) + up_bias[...])
    value = value.astype(bf16)
    gated_out[...] = value
    top = (cells[...].astype(f32) + nt(value, down[...]) + vecs[2:3]).astype(bf16)
    top_out[...] = top
    raised = from_quarters([nt(top, ups[k]) + fine_rows[0:1] for k in range(4)], 2, cols)
    skip = (hone[...].astype(f32) + raised).astype(bf16)
    skip_out[...] = skip
    err = nt(skip, head[...]) + last_rows[0:1] - targets[...].astype(f32)
    deep = depth[...]
    ocean = tables[0:1] < deep
    heat_take = tables[1:2]
    err = jnp.where(ocean, err, 0.0)
    heat = jnp.sum(heat_take * err, axis=1, keepdims=True)
    heat = jnp.where(deep > 0.0, heat, 0.0)
    loss = row_sum(err * err) + (HEAT_WEIGHT / LANES) * row_sum(heat * heat)
    dy = jnp.where(ocean, err + HEAT_WEIGHT * heat_take * heat, 0.0) * (2.0 / ocean_count)
    dy = dy.astype(bf16)
    dy_out[...] = dy
    ds = nn(dy, head[...])
    ds_out[...] = ds
    dtop = jnp.zeros(top.shape, f32)
    du_sum = jnp.zeros((1, C1), f32)
    for k in range(4):
        du = quarter(ds, 2, cols, k // 2, k % 2).astype(bf16)
        du_out[k] = du
        du_sum = du_sum + row_sum(du.astype(f32))
        dtop = dtop + nn(du, ups[k])
    dtop_out[...] = dtop
    dv = dtop.astype(bf16)
    dv_out[...] = dv
    da = (nn(dv, down[...]) * bend).astype(bf16)
    da_out[...] = da
    dn = nn(da, up[...])
    dx_out[...] = dn * vecs[0:1]

    @pl.when(pl.program_id(0) == 0)
    def _():
        sums[...] = jnp.zeros(sums.shape, f32)
        hidden_sums[...] = jnp.zeros(hidden_sums.shape, f32)

    sums[0:1, :] += row_sum(dn)
    sums[1:2, :] += row_sum(dn * centred)
    sums[2:3, :] += row_sum(dv.astype(f32))
    sums[3:4, :C1] += du_sum
    sums[4:5, :CI] += row_sum(dy.astype(f32))
    sums[5:6, :LANES] += loss
    hidden_sums[0:1, :] += row_sum(da.astype(f32))

    @pl.when(pl.program_id(0) == pl.num_programs(0) - 1)
    def _():
        copies[...] = jnp.broadcast_to(stats_block(sums[0:1, :], sums[1:2, :], None)[None], copies.shape)


def backward_rows(got, back, gain, width):
    mean, inverse, cells, _ = norm_rows(got, width)
    tiles = width // LANES
    total = jnp.sum(back[...], axis=0)
    total_a = gain * wide_row(total, 0, tiles)
    total_b = gain * wide_row(total, tiles, tiles)
    dvar = -0.5 * inverse * inverse * inverse * total_b
    first = (-inverse * total_a - 2.0 * mean * dvar) / cells
    second = 2.0 * dvar / cells
    return inverse, first, second


def coarse_slope_kernel(got, back, vecs, dx, conv, depth, out):
    inverse, first, second = backward_rows(got, back, vecs[0:1], C2)
    ocean = depth[...] > 0.0
    ocean = jnp.concatenate([ocean] * (C2 // LANES), axis=1)
    value = dx[...] * inverse + jnp.where(ocean, first + conv[...] * second, 0.0)
    out[...] = value.astype(bf16)


def coarse_taps_kernel(rows, cols, centre, left, right, above, below, slope, taps_out, source, held, here):
    lay_border(rows, cols, source, held, centre, left, right, above, below)
    here[...] = slope[...].astype(f32)
    taps_out[TAPS:, :] = jnp.zeros((taps_out.shape[0] - TAPS, LANES), f32)
    width = cols + 2 * REACH
    for p in range(KSIZE):

        def line(row, sums):
            own = here[rows8(row * cols, cols), :].reshape(cols, 8, LANES)
            seen = source[rows8((row + p) * width, width), :].reshape(width, 8, LANES)
            return tuple(sums[q] + jnp.sum(seen[q : q + cols] * own, axis=0) for q in range(KSIZE))

        zero = jnp.zeros((8, LANES), f32)
        sums = lax.fori_loop(0, rows, line, (zero,) * KSIZE)
        for q in range(KSIZE):
            taps_out[p * KSIZE + q : p * KSIZE + q + 1, :] = row_sum(sums[q])


def coarse_conv_back_kernel(rows, cols, centre, left, right, above, below, taps, dtop, dcells, slope, held):
    lay_border(rows, cols, slope, held, centre, left, right, above, below)

    def emit(place, total, carry):
        dcells[place, :] = (dtop[place, :] + total.reshape(cols * 8, LANES)).astype(bf16)
        return carry

    convolve(slope, taps, rows, cols, emit, 0, flip=True)


def fine_back_kernel(
    cols, got, dcells, downs, ds, vecs, conv, slope, up, down, dv_out, da_out, dn_out, normal_out, sums, hidden_sums, coarse_sums, copies
):
    mean, inverse, _, _ = norm_rows(got, C1)
    dlow = dcells[...]
    dh = ds[...] + from_quarters([nn(dlow, downs[k]) for k in range(4)], 2, cols)
    dv = dh.astype(bf16)
    dv_out[...] = dv

    @pl.when(pl.program_id(0) == 0)
    def _():
        sums[...] = jnp.zeros(sums.shape, f32)
        hidden_sums[...] = jnp.zeros(hidden_sums.shape, f32)
        coarse_sums[...] = jnp.zeros(coarse_sums.shape, f32)

    coarse_sums[0:1, :] += row_sum(dlow.astype(f32))
    sums[2:3, :] += row_sum(dv.astype(f32))
    for part in range(2):
        place = pl.ds(part * cols * 8, cols * 8)
        centred = conv[place, :] - mean
        normal_out[place, :] = (centred * (inverse * vecs[0:1]) + vecs[1:2]).astype(bf16)
        da = (nn(dv_out[place, :], down[...]) * slope[place, :].astype(f32)).astype(bf16)
        da_out[place, :] = da
        hidden_sums[0:1, :] += row_sum(da.astype(f32))
        dn = nn(da, up[...])
        dn_out[place, :] = dn.astype(bf16)
        sums[0:1, :] += row_sum(dn)
        sums[1:2, :] += row_sum(dn * centred)

    @pl.when(pl.program_id(0) == pl.num_programs(0) - 1)
    def _():
        copies[...] = jnp.broadcast_to(stats_block(sums[0:1, :], sums[1:2, :], None)[None], copies.shape)


def turn_kernel(rows, cols, cells, above, below, out, ends):
    line = (cols + 2 * REACH) * 8
    amount = cols * 8
    lay_ends(rows, cols, cells, above, below, ends)
    for row in range(rows + 2 * REACH):
        if row < REACH:
            values = ends[row * line : (row + 1) * line, :]
        elif row < REACH + rows:
            values = cells[(row - REACH) * line : (row - REACH + 1) * line, :]
        else:
            values = ends[(row - rows) * line : (row - rows + 1) * line, :]
        across = values.T[:CIN]
        for q in range(KSIZE):
            piece = across[:, q * 8 : q * 8 + amount].astype(bf16)
            out[q * CIN : (q + 1) * CIN, row * amount : (row + 1) * amount] = piece


def fetch(sources, rooms, sems):
    return [pltpu.make_async_copy(a, b, sems.at[k]) for k, (a, b) in enumerate(zip(sources, rooms))]


def start(copies):
    for copy in copies:
        copy.start()


def wait(copies):
    for copy in copies:
        copy.wait()


def stem_back_kernel(rows, cols, got, back, vecs, near, stem, sums, conv, dn, depth, dv, shifted, tail, *scratch):
    rooms, (slope, acc, tap_acc, stem_acc, lines, held, sems) = scratch[:5], scratch[5:]
    copies = fetch((conv, dn, depth, dv, shifted), rooms, sems)
    start(copies)
    conv, dn, depth, dv, shifted = rooms
    amount = cols * 8
    inverse, first, second = backward_rows(got, back, vecs[0:1], C1)
    scale = inverse * vecs[0:1]
    taps = near[...].astype(f32).T
    stem_turned = stem[...].astype(f32).T
    wait(copies[:3])

    def slopes(row, carry):
        place = pl.ds(pl.multiple_of(row * amount, amount), amount)
        ocean = depth[place, :] > 0.0
        ocean = jnp.concatenate([ocean, ocean], axis=1)
        value = dn[place, :].astype(f32) * scale + jnp.where(ocean, first + conv[place, :] * second, 0.0)
        slope[place, :] = value.astype(bf16)
        return carry

    lax.fori_loop(0, rows, slopes, 0)
    wait(copies[3:])
    total = rows * amount
    straight = shifted[REACH * CIN : (REACH + 1) * CIN, REACH * amount : REACH * amount + total]
    stem_acc[...] = nn(straight, dv[...])
    tap_acc[...] = jnp.zeros(tap_acc.shape, f32)
    for p in range(KSIZE):
        acc[...] = nn(shifted[:, p * amount : p * amount + total], slope[...])
        sum_here = stem_acc[...]
        for q in range(KSIZE):
            tap = p * KSIZE + q
            part = acc[q * CIN : (q + 1) * CIN, :]
            sum_here = sum_here + part * taps[tap : tap + 1]
            tap_acc[tap : tap + 1, :] = row_sum(part * stem_turned[:CIN])
        stem_acc[...] = sum_here
    acc[:CIN, :] = stem_acc[...]
    acc[CIN : 2 * LANES, :] = jnp.zeros((2 * LANES - CIN, C1), f32)
    lines[...] = jnp.zeros(lines.shape, f32)
    turned = acc[:LANES, :].T
    acc[:C1, :LANES] = turned
    write_matrix(lines, 0, STEM, held, acc)
    held[:C1, :] = tap_acc[...].T
    write_short(lines, offsets()[TAPS1], WIDTH, TAPS, lambda r: held[r : r + 1, :])
    write_row(lines, 0, GAIN1, norm_row(got, sums, C1))
    write_row(lines, 0, SHIFT1, row_of(sums, 0))
    used = lines.shape[0] // tail.shape[0]
    for k in range(tail.shape[0]):
        tail[k, :used] = lines[k * used : (k + 1) * used, :]
        tail[k, used:] = jnp.zeros((tail.shape[1] - used, LANES), f32)


def period(length):
    return LANES // math.gcd(length, LANES)


def offsets():
    starts = []
    start = 0
    for shape in shapes_of():
        starts.append(start)
        start += math.prod(shape)
    return starts


def shard_places(devices, shard_len):
    firsts = [e * shard_len // 2048 * 16 for e in range(devices)]
    needed = [(e * shard_len % 2048 + shard_len + 2047) // 2048 * 16 for e in range(devices)]
    return firsts, max(needed)


def lane_ids(rows):
    return lax.broadcasted_iota(jnp.int32, (rows, LANES), 1)


def turn_lanes(values, amount):
    amount = amount % LANES
    return values if amount == 0 else pltpu.roll(values, amount, 1)


def read_rows(lines, base, rows, length, put):
    cycle = period(length)
    count = rows // cycle
    step = cycle * length // LANES
    lane = lane_ids(count)
    tiles = -(-length // LANES)
    for s in range(cycle):
        start = base + s * length
        line, phase = start // LANES, start % LANES
        held = [
            lines[pl.ds(line + k, count, stride=step), :] for k in range(-(-(phase + length) // LANES))
        ]
        for m in range(tiles):
            value = held[m]
            if phase and m + 1 < len(held):
                value = jnp.where(lane >= phase, value, held[m + 1])
            value = turn_lanes(value, -phase)
            if length - m * LANES < LANES:
                value = jnp.where(lane < length - m * LANES, value, 0.0)
            put(s, cycle, count, m, value)


def read_vector(lines, base, length, put):
    line, phase = base // LANES, base % LANES
    lane = lane_ids(1)
    for m in range(-(-length // LANES)):
        value = lines[line + m : line + m + 1, :]
        if phase and phase + length > (m + 1) * LANES:
            value = jnp.where(lane >= phase, value, lines[line + m + 1 : line + m + 2, :])
        value = turn_lanes(value, -phase)
        if length - m * LANES < LANES:
            value = jnp.where(lane < length - m * LANES, value, 0.0)
        put(m, value)


def write_rows(lines, base, rows, length, get):
    cycle = period(length)
    count = rows // cycle
    step = cycle * length // LANES
    line, phase = base // LANES, base % LANES
    for k in range(step):
        shared = k == 0 and phase > 0
        amount = count + 1 if shared else count
        lane = lane_ids(amount)
        total = None
        at = 0
        while at < LANES:
            place = k * LANES - phase + at
            row, col = place // length, place % length
            run = min(length - col, LANES - at)
            tile = col // LANES
            value = get(row, cycle, amount, tile)
            if col % LANES + run > LANES:
                value = jnp.where(lane >= col % LANES, value, get(row, cycle, amount, tile + 1))
            value = turn_lanes(value, at - col)
            total = value if total is None else jnp.where(lane >= at, value, total)
            at += run
        put_lines(lines, line + k, amount, step, total, shared)


def put_lines(lines, line, amount, step, values, shared):
    if not shared:
        lines[pl.ds(line, amount, stride=step), :] = values
        return
    before = lines[line : line + 1, :]
    lines[pl.ds(line, amount, stride=step), :] = values
    lines[line : line + 1, :] = lines[line : line + 1, :] + before


def write_vector(lines, base, length, get):
    line, phase = base // LANES, base % LANES
    lane = lane_ids(1)
    tiles = -(-length // LANES)
    zero = jnp.zeros((1, LANES), f32)
    for k in range(-(-(phase + length) // LANES)):
        value = get(k) if k < tiles else zero
        if phase:
            earlier = get(k - 1) if k > 0 else zero
            value = turn_lanes(jnp.where(lane >= LANES - phase, earlier, value), phase)
        if k == 0 and phase:
            value = value + lines[line : line + 1, :]
        lines[line + k : line + k + 1, :] = value


def write_short(lines, base, rows, length, get):
    line, phase = base // LANES, base % LANES
    lane = lane_ids(1)
    for k in range(-(-(phase + rows * length) // LANES)):
        low = k * LANES - phase
        total = jnp.zeros((1, LANES), f32)
        for row in range(max(low // length, 0), min(-(-(low + LANES) // length), rows)):
            at = row * length - low
            value = turn_lanes(get(row), at)
            if at < 0:
                value = jnp.where(lane < at + length, value, 0.0)
            elif at + length > LANES:
                value = jnp.where(lane >= at, value, 0.0)
            total = total + value
        if k == 0 and phase:
            total = total + lines[line : line + 1, :]
        lines[line + k : line + k + 1, :] = total


def read_short(lines, base, rows, length, put):
    lane = lane_ids(1)
    for row in range(rows):
        start = base + row * length
        line, phase = start // LANES, start % LANES
        value = lines[line : line + 1, :]
        if phase + length > LANES:
            value = jnp.where(lane >= phase, value, lines[line + 1 : line + 2, :])
        put(row, jnp.where(lane < length, turn_lanes(value, -phase), 0.0))


STEM, TAPS1, GAIN1, SHIFT1, UP1, UPB1, DOWN1, DOWNB1, DOWNS, DOWNSB = range(10)
TAPS2, GAIN2, SHIFT2, UP2, UPB2, DOWN2, DOWNB2, UPS, UPSB, HEAD, HEADB = range(10, 21)


def planes_of(devices, shard_len, low, high, plane_size):
    firsts, tall = shard_places(devices, shard_len)
    found = {e // plane_size for e in range(devices) if firsts[e] < high and firsts[e] + tall > low}
    return sorted(found)


def collect(devices, shard_len, plane_size, place, parts, lines, low, high):
    firsts, tall = shard_places(devices, shard_len)
    started = False
    half = plane_size // 2
    for e in range(devices):
        end = firsts[e + 1] + 16 if e + 1 < devices else firsts[e] + tall
        if end <= low or firsts[e] >= high:
            continue
        planes, blocks = next((p, b) for p, b in parts if e // plane_size in p)
        plane = planes.index(e // plane_size)
        seat = seat_of(place, e % plane_size, plane_size)
        first = firsts[e] - low
        skip = max(0, -first)
        take = min(tall, high - firsts[e])

        def put(ref, index, skip, shared):
            if shared:
                lines[pl.ds(first, 16), :] += ref[index, :16, :].astype(f32)
                skip = 16
            if take > skip:
                lines[pl.ds(first + skip, take - skip), :] = ref[index, skip:take, :].astype(f32)

        for side, ref in enumerate(blocks):

            @pl.when((seat >= half) == (side == 1))
            def _():
                put(ref, (seat - half * side) * len(planes) + plane, skip, started)

        started = True


def seat_of(me, other, devices):
    away = me ^ other
    seat = 0
    bits = devices.bit_length() - 1
    for b in range(bits):
        seat = seat + ((away >> b) & 1) * (1 << (bits - 1 - b))
    return seat


def matrix_out(held, tall, out, tiles, rows):
    for m in range(tiles):
        if tall > rows:
            held[m * tall + rows : (m + 1) * tall, :] = jnp.zeros((tall - rows, LANES), f32)
        out[:, m * LANES : (m + 1) * LANES] = held[m * tall : (m + 1) * tall, :].astype(bf16)


def read_matrix(lines, shift, piece, held, out):
    rows, length = shapes_of()[piece]
    tall = out.shape[0]

    def put(first, stride, count, tile, value):
        held[pl.ds(tile * tall + first, count, stride=stride), :] = value

    read_rows(lines, offsets()[piece] - shift, rows, length, put)
    matrix_out(held, tall, out, -(-length // LANES), rows)


def read_row(lines, shift, piece, out, row):
    def put(tile, value):
        out[row : row + 1, tile * LANES : (tile + 1) * LANES] = value

    read_vector(lines, offsets()[piece] - shift, shapes_of()[piece][0], put)


def read_taps(lines, shift, piece, held, out, tall):
    def put(row, value):
        held[pl.ds(row, 1), :] = value

    rows = shapes_of()[piece][0]
    read_short(lines, offsets()[piece] - shift, rows, TAPS, put)
    held[rows:tall, :] = jnp.zeros((tall - rows, LANES), f32)
    if out is None:
        return
    across = held[:tall, :].T
    for t in range(TAPS):
        out[t] = jnp.broadcast_to(across[t : t + 1, :], (8, tall))


def first_end():
    return -(-offsets()[TAPS2] // 2048) * 16


def rest_start():
    return offsets()[TAPS2] // 2048 * 16


def rest_end():
    return -(-(offsets()[HEADB] + CIN) // 2048) * 16


def stem_params_kernel(parts, stem, near, vecs, lines, held):
    lines[...] = parts[...].astype(f32)
    vecs[...] = jnp.zeros(vecs.shape, f32)
    read_taps(lines, 0, TAPS1, held, None, C1)
    near[...] = held[:C1, :].astype(bf16)
    read_matrix(lines, 0, STEM, held, stem)
    read_row(lines, 0, GAIN1, vecs, 0)
    read_row(lines, 0, SHIFT1, vecs, 1)


def fine_params_kernel(
    devices, shard_len, plane_size, planes, place, own, other, perm, up, bias, down, downs, downs_four, down_rows, vecs, lines, held
):
    low, high = span(UP1, DOWNSB)
    shift = low * LANES
    collect(devices, shard_len, plane_size, place[0], [(planes, (own, other))], lines, low, high)
    for out in (down_rows, bias, vecs):
        out[...] = jnp.zeros(out.shape, f32)
    read_row(lines, shift, DOWNB1, vecs, 0)
    read_row(lines, shift, UPB1, bias, 0)
    read_row(lines, shift, DOWNSB, down_rows, 0)
    read_matrix(lines, shift, UP1, held, up)
    read_matrix(lines, shift, DOWN1, held, down)
    read_matrix(lines, shift, DOWNS, held, downs)
    for k in range(4):
        downs_four[k] = nt(downs[...], perm[k]).astype(bf16)


def rest_params_kernel(
    devices, shard_len, plane_size, planes, others, place, own, other, far_own, far_other, taps2, vecs2, up2, bias2, down2, ups_four, vecs1, head, last, lines, held
):
    shift = rest_start() * LANES
    parts = [(planes, (own, other)), (others, (far_own, far_other))]
    collect(devices, shard_len, plane_size, place[0], parts, lines, rest_start(), rest_end())
    for out in (vecs1, vecs2, bias2, last):
        out[...] = jnp.zeros(out.shape, f32)
    read_taps(lines, shift, TAPS2, held, taps2, C2)
    read_row(lines, shift, GAIN2, vecs2, 0)
    read_row(lines, shift, SHIFT2, vecs2, 1)
    read_row(lines, shift, DOWNB2, vecs2, 2)
    read_row(lines, shift, UPB2, bias2, 0)
    read_row(lines, shift, UPSB, vecs1, 0)
    read_row(lines, shift, HEADB, last, 0)
    read_matrix(lines, shift, UP2, held, up2)
    read_matrix(lines, shift, DOWN2, held, down2)
    read_matrix(lines, shift, HEAD, held, head)
    tiles = C2 // LANES

    def put(first, stride, count, tile, value):
        k = first % 4
        held[pl.ds((k * tiles + tile) * C1 + first // 4, count, stride=stride // 4), :] = value

    rows, length = shapes_of()[UPS]
    read_rows(lines, offsets()[UPS] - shift, rows, length, put)
    for k in range(4):
        for m in range(tiles):
            at = (k * tiles + m) * C1
            held[at + WIDTH : at + C1, :] = jnp.zeros((C1 - WIDTH, LANES), f32)
            ups_four[k, :, m * LANES : (m + 1) * LANES] = held[at : at + C1, :].astype(bf16)


FRONT = 16


def hold_matrix(held, values, row_tiles, rows):
    tall = rows + 2 * FRONT
    zero = jnp.zeros((FRONT, LANES), f32)
    for m in range(row_tiles):
        at = m * tall
        held[at : at + FRONT, :] = zero
        held[at + FRONT : at + FRONT + rows, :] = values(m)
        held[at + FRONT + rows : at + tall, :] = zero


def write_matrix(lines, shift, piece, held, source):
    rows, length = shapes_of()[piece]
    tall = rows + 2 * FRONT
    hold_matrix(held, lambda m: source[:rows, m * LANES : (m + 1) * LANES], -(-length // LANES), rows)

    def get(first, stride, count, tile):
        return held[pl.ds(tile * tall + FRONT + first, count, stride=stride), :]

    write_rows(lines, offsets()[piece] - shift, rows, length, get)


def write_row(lines, shift, piece, get):
    write_vector(lines, offsets()[piece] - shift, shapes_of()[piece][0], get)


def row_of(source, row):
    return lambda m: source[row : row + 1, m * LANES : (m + 1) * LANES]


def norm_row(got, sums, width):
    _, inverse, _, _ = norm_rows(got, width)
    value = sums[1:2, :] * inverse
    return lambda m: value[:, m * LANES : (m + 1) * LANES]


def scatter_out(devices, shard_len, plane_size, planes, place, lines, low, keep, send):
    firsts, tall = shard_places(devices, shard_len)
    half = plane_size // 2
    for k, plane in enumerate(planes):
        for r in range(plane_size):
            first = firsts[plane * plane_size + r] - low
            start, end = max(first, 0), min(first + tall, lines.shape[0])
            seat = seat_of(place, r, plane_size)

            def put(out, index, kind):
                if end <= start:
                    out[index] = jnp.zeros((tall, LANES), kind)
                    return
                if start > first:
                    out[index, : start - first] = jnp.zeros((start - first, LANES), kind)
                out[index, start - first : end - first] = lines[start:end, :].astype(kind)
                if end < first + tall:
                    out[index, end - first :] = jnp.zeros((first + tall - end, LANES), kind)

            @pl.when(seat < half)
            def _():
                put(keep, seat * len(planes) + k, f32)

            @pl.when(seat >= half)
            def _():
                put(send, (seat - half) * len(planes) + k, bf16)


def span(first, last):
    end = offsets()[last] + math.prod(shapes_of()[last])
    return offsets()[first] // 2048 * 16, -(-end // 2048) * 16


def clear_ends(lines, low, first, last):
    start = offsets()[first] // LANES - low + 1
    lines[:start, :] = jnp.zeros((start, LANES), f32)
    end = -(-(offsets()[last] + math.prod(shapes_of()[last])) // LANES) - low
    if end < lines.shape[0]:
        lines[end:, :] = jnp.zeros((lines.shape[0] - end, LANES), f32)


def late_flat_kernel(
    devices, shard_len, plane_size, planes, place, sums2, hidden2, da, normal, dv, gated, du, top, dy, skip, keep, send, *scratch
):
    rooms, (lines, held, g_up2, g_down2, g_ups, g_head, sems) = scratch[:8], scratch[8:]
    copies = fetch((da, normal, dv, gated, du, top, dy, skip), rooms, sems)
    da, normal, dv, gated, du, top, dy, skip = rooms
    start(copies[6:])
    start(copies[4:6])
    wait(copies[6:])
    start(copies[:2])
    g_head[...] = tn(dy[...], skip[...])
    wait(copies[4:6])
    start(copies[2:4])
    for k in range(4):
        g_ups[k] = tn(du[k], top[...])
    wait(copies[:2])
    g_up2[...] = tn(da[...], normal[...])
    wait(copies[2:4])
    g_down2[...] = tn(dv[...], gated[...])
    low, _ = span(UP2, HEADB)
    shift = low * LANES
    clear_ends(lines, low, UP2, HEADB)
    write_matrix(lines, shift, UP2, held, g_up2)
    write_row(lines, shift, UPB2, row_of(hidden2, 0))
    write_matrix(lines, shift, DOWN2, held, g_down2)
    write_row(lines, shift, DOWNB2, row_of(sums2, 2))
    rows, length = shapes_of()[UPS]
    tiles = C2 // LANES
    tall = WIDTH + 2 * FRONT
    for k in range(4):
        for m in range(tiles):
            at = (k * tiles + m) * tall
            held[at : at + FRONT, :] = jnp.zeros((FRONT, LANES), f32)
            held[at + FRONT : at + FRONT + WIDTH, :] = g_ups[k, :WIDTH, m * LANES : (m + 1) * LANES]
            held[at + FRONT + WIDTH : at + tall, :] = jnp.zeros((FRONT, LANES), f32)

    def get(first, stride, count, tile):
        at = ((first % 4) * tiles + tile) * tall + FRONT + first // 4
        return held[pl.ds(at, count, stride=stride // 4), :]

    write_rows(lines, offsets()[UPS] - shift, rows, length, get)
    write_row(lines, shift, UPSB, row_of(sums2, 3))
    write_matrix(lines, shift, HEAD, held, g_head)
    write_row(lines, shift, HEADB, row_of(sums2, 4))
    scatter_out(devices, shard_len, plane_size, planes, place[0], lines, low, keep, send)


def early_flat_kernel(
    devices, shard_len, plane_size, planes, place, got2, sums1, hidden1, sums_low, g_taps2, sums2,
    da, normal, dv, gated, dcells, patches, keep, send, *scratch,
):
    rooms, (lines, held, g_up1, g_down1, g_downs, sems) = scratch[:6], scratch[6:]
    copies = fetch((da, normal, dv, gated, dcells, patches), rooms, sems)
    da, normal, dv, gated, dcells, patches = rooms
    start(copies[4:])
    start(copies[2:4])
    wait(copies[4:])
    start(copies[:2])
    g_downs[...] = tn(dcells[...], patches[...])
    wait(copies[2:4])
    g_down1[...] = tn(dv[...], gated[...])
    wait(copies[:2])
    g_up1[...] = tn(da[...], normal[...])
    low, _ = span(UP1, SHIFT2)
    shift = low * LANES
    clear_ends(lines, low, UP1, SHIFT2)
    write_matrix(lines, shift, UP1, held, g_up1)
    write_row(lines, shift, UPB1, row_of(hidden1, 0))
    write_matrix(lines, shift, DOWN1, held, g_down1)
    write_row(lines, shift, DOWNB1, row_of(sums1, 2))
    write_matrix(lines, shift, DOWNS, held, g_downs)
    write_row(lines, shift, DOWNSB, row_of(sums_low, 0))
    across = jnp.concatenate([g_taps2[...], jnp.zeros((LANES - g_taps2.shape[0], C2), f32)], axis=0).T
    held[:C2, :] = across
    write_short(lines, offsets()[TAPS2] - shift, WIDTH2, TAPS, lambda r: held[r : r + 1, :])
    write_row(lines, shift, GAIN2, norm_row(got2, sums2, C2))
    write_row(lines, shift, SHIFT2, row_of(sums2, 0))
    scatter_out(devices, shard_len, plane_size, planes, place[0], lines, low, keep, send)


def group_taps():
    table = []
    for first in (0, 3):
        for p in range(KSIZE):
            table.append([p * KSIZE + first + t for t in range(3)])
    for k in range(3):
        table.append([(3 * k + t) * KSIZE + 6 if 3 * k + t < KSIZE else -1 for t in range(3)])
    return table


def body(fields, targets, ocean_depth, thickness_class, params, moment1, moment2):
    shard_len = params.shape[0]
    devices = lax.axis_size(AXES)
    plane_size = 2 * lax.axis_size("lvl")
    me = lax.axis_index(AXES)
    _, tall = shard_places(devices, shard_len)
    at = (me * (shard_len % 2048)) % 2048
    block = lax.dynamic_update_slice(jnp.zeros((tall * LANES,), bf16), params.astype(bf16), (at,))
    block = block.reshape(tall, LANES)
    near_planes = planes_of(devices, shard_len, 0, first_end(), plane_size)
    far_planes = [p for p in range(devices // plane_size) if p not in near_planes]
    plane_steps, pick_planes = gather_steps(near_planes, far_planes)
    blocks = block.reshape(1, tall, LANES)
    place_row = jnp.broadcast_to(me % plane_size, (1,)).astype(jnp.int32)

    smem = pl.BlockSpec(memory_space=pltpu.SMEM)
    vmem = pl.BlockSpec(memory_space=pltpu.VMEM)
    parts = lax.axis_size("lvl")
    chans, batch, all_rows, all_cols = fields.shape
    bands = BLOCKS // batch
    rows, cols = all_rows // bands, all_cols // parts
    half_rows, half_cols = rows // 2, cols // 2
    cells, low_cells = rows * cols * 8, half_rows * half_cols * 8
    wide_cols = cols + 2 * REACH
    low_border = (half_rows + 2 * REACH) * (half_cols + 2 * REACH) * 8

    def packed(values, reach):
        width = cols + 2 * reach
        lanes = chans * BLOCKS
        copies = call(
            lambda *refs: pack_kernel(parts, cols, reach, *refs),
            [((parts, lanes, rows * width), bf16)],
            scratch=[
                pltpu.VMEM((-(-all_cols // LANES), chans * batch * all_rows, LANES), f32),
                pltpu.VMEM((parts, lanes, rows * width), f32),
            ],
            micros=3,
            name="pack",
        )(values.reshape(-1, all_cols))[0]
        return copies

    def given(copies):
        return lax.all_to_all(copies, "lvl", 0, 0, tiled=True)

    field_given = given(packed(fields, REACH))
    goal_copies = packed(targets, 0)
    chunk_lines = -(-span(STEM, SHIFT1)[1] // (8 * devices)) * 8
    head_lines = chunk_lines * devices
    window = jnp.pad(block, ((head_lines, head_lines), (0, 0)))
    first_line = me * shard_len // 2048 * 16
    window = lax.dynamic_slice_in_dim(window, head_lines - jnp.minimum(first_line, head_lines), head_lines)
    field_given, window = tie(field_given, window)
    chunk = jnp.sum(swap(window.reshape(devices, chunk_lines, LANES)).astype(f32), axis=0).astype(bf16)
    stem_lines = swap(jnp.broadcast_to(chunk[None], (devices,) + chunk.shape)).reshape(head_lines, LANES)
    for step in plane_steps[:-1]:
        blocks = step(blocks)
    goal_copies, blocks = tie(goal_copies, blocks)
    goal_copies, stem_lines = tie(goal_copies, stem_lines)
    goal_given = given(goal_copies)
    blocks = plane_steps[-1](blocks)
    send_room = 2 * REACH * -(-wide_cols // 8) * 8
    field_cells, lower, upper = call(
        lambda *refs: fields_kernel(parts, rows, cols, *refs),
        [((rows * wide_cols * 8, LANES), f32), ((send_room, LANES), bf16), ((send_room, LANES), bf16)],
        scratch=[pltpu.VMEM((send_room, LANES), f32), pltpu.VMEM((parts, rows * wide_cols, chans * BLOCKS), bf16)],
        micros=4,
        name="fields",
    )(field_given)
    (field_cells, lower, upper), blocks = tie((field_cells, lower, upper), blocks)
    above, below = lines_out(lower, upper)
    near_blocks, far_blocks = pick_planes(blocks)
    near_steps, far_steps = within_steps(), within_steps()
    near_state = near_steps[0](near_blocks)
    (field_cells, above, below), near_state = tie((field_cells, above, below), near_state)
    far_state = far_steps[0](far_blocks)
    near_state = near_steps[1](near_state)

    deep = depth_cells(ocean_depth, batch)
    depth_rows = jnp.broadcast_to(deep.astype(f32)[..., None], deep.shape + (LANES,)).reshape(cells, LANES)
    low = jnp.max(deep.reshape(half_rows, 2, half_cols, 2, 8), axis=(1, 3))
    low_rows = jnp.broadcast_to(low.astype(f32)[..., None], low.shape + (LANES,)).reshape(low_cells, LANES)
    channel = jnp.arange(CI, dtype=jnp.int32)
    level = jnp.where(channel < 4 * LEVELS, channel // 4, 0)
    level_row = jnp.where(channel < CIN, level, LEVELS + 1).astype(f32)
    thickf = thickness_class.astype(f32)
    onehot = (level[:, None] == jnp.arange(LEVELS, dtype=jnp.int32)[None, :]).astype(f32)
    chosen = ((channel % 4 == 0) & (channel < 4 * LEVELS)).astype(f32)
    heat_take = chosen * jnp.sum(onehot * thickf[None, :], axis=1) / jnp.sum(thickf)
    ocean_cells = jnp.sum((level_row[None, None, :] < ocean_depth.astype(f32)[:, :, None]).astype(f32))
    ocean_cells = batch * ocean_cells
    surface_cells = jnp.sum((deep > 0).astype(f32))
    low_surface = jnp.sum((low > 0).astype(f32))
    index8 = jnp.arange(8)[:, None]
    lane8 = jnp.arange(LANES)[None, :]

    def counts_of(width, cells_count):
        (r, c), (ro, co) = count_places(width)
        at_cells = (index8 == r) & (lane8 == c)
        at_ocean = (index8 == ro) & (lane8 == co)
        return jnp.where(at_cells, cells_count, jnp.where(at_ocean, ocean_cells, 0.0))

    counts1 = counts_of(C1, surface_cells)
    counts2 = counts_of(C2, low_surface)

    tables = jnp.pad(jnp.stack([level_row, heat_take]), ((0, 6), (0, 0)))
    source_lane = jnp.arange(C1, dtype=jnp.int32)[None, :, None]
    target_lane = jnp.arange(H1, dtype=jnp.int32)[None, None, :]
    quarter_at = jnp.arange(4, dtype=jnp.int32)[:, None, None]
    perm = ((source_lane * 4 + quarter_at == target_lane) & (source_lane < WIDTH)).astype(bf16)
    table = group_taps()
    third_at = jnp.arange(C1, dtype=jnp.int32) // CIN
    wanted = jnp.array([line + [-1] for line in table], dtype=jnp.int32)[:, third_at]
    pick = (wanted[:, :, None] == jnp.arange(LANES, dtype=jnp.int32)[None, None, :]).astype(bf16)
    held_room = pltpu.VMEM((4 * H2, LANES), f32)
    stem_in, near1, vecs1 = call(
        stem_params_kernel,
        [((C1, CI), bf16), ((C1, LANES), bf16), ((8, C1), f32)],
        scratch=[pltpu.VMEM(stem_lines.shape, f32), pltpu.VMEM((2 * C1, LANES), f32)],
        micros=3,
        name="stem_params",
    )(stem_lines)

    ends_room = pltpu.VMEM((2 * REACH * wide_cols * 8, LANES), f32)
    shifted_room = pltpu.VMEM(((rows + 2 * REACH) * cols * 8, C1), bf16)
    hzero, conv1, stats1 = call(
        lambda *refs: stem_kernel(rows, cols, *refs),
        [((cells, C1), bf16), ((cells, C1), f32), ((devices, 8, LANES), f32)],
        grid=(half_rows,),
        ins=[
            whole(rows * wide_cols * 8, LANES), whole(send_room, LANES), whole(send_room, LANES), whole(C1, LANES), whole(C1, CI),
            whole(GROUPS, C1, LANES), band(2 * cols * 8, LANES), whole(8, LANES),
        ],
        out_specs=[band(2 * cols * 8, C1), band(2 * cols * 8, C1), whole(devices, 8, LANES)],
        scratch=[
            pltpu.VMEM((GROUPS * C1, C1), bf16), pltpu.VMEM((C1, C1), bf16), pltpu.VMEM((8, C1), f32),
            ends_room, shifted_room, shifted_room, shifted_room,
        ],
        micros=17,
        name="stem_conv",
    )(field_cells, above, below, near1, stem_in, pick, depth_rows, counts1)
    stats1, (near_state, far_state, goal_given) = tie(stats1, (near_state, far_state, goal_given))
    got1 = swap(stats1)
    blocks = near_steps[2](near_state)
    far_state = far_steps[1](far_state)
    up_in1, bias_in1, down_in1, downs_in, downs_four, down_rows, bias_rows = call(
        lambda *refs: fine_params_kernel(devices, shard_len, plane_size, near_planes, *refs),
        [
            ((H1, C1), bf16), ((1, H1), f32), ((C1, H1), bf16), ((C2, H1), bf16), ((4, C2, C1), bf16), ((8, C2), f32),
            ((8, C1), f32),
        ],
        ins=[smem, vmem, vmem, vmem],
        scratch=[pltpu.VMEM((span(UP1, DOWNSB)[1] - span(UP1, DOWNSB)[0], LANES), f32), held_room],
        micros=8,
        name="fine_params",
    )(place_row, *blocks, perm)
    chunk, low_chunk = 2 * cols * 8, half_cols * 8
    hone, gated1, slope1, patches, coarse = call(
        lambda *refs: fine_kernel(cols, *refs),
        [
            ((cells, C1), bf16),
            ((cells, H1), bf16),
            ((cells, H1), bf16),
            ((low_cells, H1), bf16),
            ((low_cells, C2), bf16),
        ],
        grid=(half_rows,),
        ins=[
            whole(devices, 8, LANES), band(chunk, C1), band(chunk, C1), whole(8, C1), whole(8, C1), whole(H1, C1), whole(1, H1),
            whole(C1, H1), whole(4, C1, H1), whole(C2, H1), whole(8, C2),
        ],
        out_specs=[
            band(chunk, C1), band(chunk, H1), band(chunk, H1), band(low_chunk, H1), band(low_chunk, C2),
        ],
        scratch=[pltpu.VMEM((chunk, C1), f32)],
        micros=15,
        name="fine_forward",
    )(got1, conv1, hzero, vecs1, bias_rows, up_in1, bias_in1, down_in1, perm, downs_in, down_rows)

    edge = edge_lines(half_cols)
    side = half_rows * REACH * 8

    def edges(values, left, right):
        return call(
            lambda *refs: edge_kernel(half_rows, half_cols, 1, *refs),
            [((edge, C2), bf16)] * 2,
            scratch=[pltpu.VMEM((low_cells + 2 * side, LANES), f32), pltpu.VMEM((edge, LANES), f32)],
            micros=3,
            name="edge",
        )(values, left, right)

    def border_tiles(tile):
        return [tile(low_cells), tile(side), tile(side), tile(edge), tile(edge)]

    coarse, far_state = tie(coarse, far_state)
    more_blocks = far_steps[2](far_state)
    sides = columns_out((coarse,), half_rows, half_cols)[0]
    goal_given, coarse = tie(goal_given, coarse)
    goal = call(
        lambda *refs: targets_kernel(parts, *refs),
        [((cells, LANES), bf16)],
        scratch=[pltpu.VMEM((cells, LANES), f32), pltpu.VMEM((parts, rows * cols, chans * BLOCKS), bf16)],
        micros=4,
        name="targets",
    )(goal_given)[0]
    sides, goal = tie(sides, goal)
    border2 = (coarse, *sides, *lines_out(*edges(coarse, *sides)))
    taps_in2, vecs2, up_in2, bias_in2, down_in2, ups_four, fine_rows, head_in, last_rows = call(
        lambda *refs: rest_params_kernel(devices, shard_len, plane_size, near_planes, far_planes, *refs),
        [
            ((TAPS, 8, C2), f32), ((8, C2), f32), ((H2, C2), bf16), ((1, H2), f32), ((C2, H2), bf16),
            ((4, C1, C2), bf16), ((8, C1), f32), ((CI, C1), bf16), ((8, CI), f32),
        ],
        ins=[smem] + [vmem] * 4,
        scratch=[pltpu.VMEM((rest_end() - rest_start(), LANES), f32), held_room],
        micros=13,
        name="rest_params",
    )(place_row, *blocks, *more_blocks)
    conv2, stats2 = call(
        lambda *refs: coarse_conv_kernel(half_rows, half_cols, *refs),
        [((low_cells, C2), f32), ((devices, 8, LANES), f32)],
        grid=(C2 // LANES,),
        ins=border_tiles(lane_tile) + [TAP_TILE, whole(low_cells, LANES), whole(8, LANES)],
        out_specs=[lane_tile(low_cells), whole(devices, 8, LANES)],
        scratch=[pltpu.VMEM((low_border, LANES), f32), pltpu.VMEM((edge, LANES), f32), pltpu.VMEM((8, LANES), f32)],
        micros=11,
        name="coarse_conv",
    )(*border2, taps_in2, low_rows, counts2)
    got2 = swap(stats2)
    field_cells, stats2 = tie(field_cells, stats2)
    turned = call(
        lambda *refs: turn_kernel(rows, cols, *refs),
        [((KSIZE * CIN, (rows + 2 * REACH) * cols * 8), bf16)],
        scratch=[ends_room],
        micros=8,
        name="turn",
    )(field_cells, above, below)[0]
    conv2, turned = tie(conv2, turned)
    (
        skip, top, dy, ds, du, dtop, dv2, gated2, da2, normal2, dx2, sums2, hidden2, copies2,
    ) = call(
        lambda *refs: middle_kernel(cols, *refs),
        [
            ((cells, C1), bf16), ((low_cells, C2), bf16), ((cells, CI), bf16), ((cells, C1), f32),
            ((4, low_cells, C1), bf16), ((low_cells, C2), f32), ((low_cells, C2), bf16), ((low_cells, H2), bf16),
            ((low_cells, H2), bf16), ((low_cells, C2), bf16), ((low_cells, C2), f32),
            ((8, C2), f32), ((8, H2), f32), ((devices, 8, LANES), f32),
        ],
        grid=(half_rows,),
        ins=[
            whole(devices, 8, LANES), band(low_chunk, C2), band(low_chunk, C2), whole(8, C2), whole(H2, C2), whole(1, H2),
            whole(C2, H2), whole(4, C1, C2), whole(8, C1), whole(CI, C1), whole(8, CI), whole(8, CI), band(chunk, C1),
            band(chunk, CI), band(chunk, LANES),
        ],
        out_specs=[
            band(chunk, C1), band(low_chunk, C2), band(chunk, CI), band(chunk, C1),
            pl.BlockSpec((4, low_chunk, C1), lambda i: (0, i, 0)), band(low_chunk, C2), band(low_chunk, C2),
            band(low_chunk, H2), band(low_chunk, H2), band(low_chunk, C2), band(low_chunk, C2),
            whole(8, C2), whole(8, H2), whole(devices, 8, LANES),
        ],
        micros=20,
        name="middle",
    )(
        got2, conv2, coarse, vecs2, up_in2, bias_in2, down_in2, ups_four, fine_rows, head_in, last_rows, tables, hone, goal,
        depth_rows,
    )
    back2 = swap(copies2)
    late_planes = planes_of(devices, shard_len, *span(UP2, HEADB), plane_size)
    half_seats = plane_size // 2

    def sums_out(planes):
        return [((half_seats * len(planes), tall, LANES), kind) for kind in (f32, bf16)]

    late_args = (da2, normal2, dv2, gated2, du, top, dy, skip)
    hbm = pl.BlockSpec(memory_space=pltpu.HBM)
    late_keep, late_send = call(
        lambda *refs: late_flat_kernel(devices, shard_len, plane_size, late_planes, *refs),
        sums_out(late_planes),
        ins=[smem, vmem, vmem] + [hbm] * 8,
        scratch=[
            *[pltpu.VMEM(value.shape, bf16) for value in late_args],
            pltpu.VMEM((span(UP2, HEADB)[1] - span(UP2, HEADB)[0], LANES), f32), held_room,
            pltpu.VMEM((H2, C2), f32), pltpu.VMEM((C2, H2), f32), pltpu.VMEM((4, C1, C2), f32), pltpu.VMEM((CI, C1), f32),
            pltpu.SemaphoreType.DMA((8,)),
        ],
        micros=10,
        name="late_flat",
    )(place_row, sums2, hidden2, *late_args)
    back2, late_keep = tie(back2, late_keep)
    slope2 = call(
        coarse_slope_kernel,
        [((low_cells, C2), bf16)],
        micros=2,
        name="coarse_slope",
    )(got2, back2, vecs2, dx2, conv2, low_rows)[0]

    def taps_back(values, start, count):
        def tile(rows):
            return pl.BlockSpec((rows, LANES), lambda i: (0, i + start))

        return call(
            lambda *refs: coarse_taps_kernel(half_rows, half_cols, *refs),
            [((56, count * LANES), f32)],
            grid=(count,),
            ins=border_tiles(tile) + [tile(low_cells)],
            out_specs=[lane_tile(56)],
            scratch=[
                pltpu.VMEM((low_border, LANES), f32), pltpu.VMEM((edge, LANES), f32), pltpu.VMEM((low_cells, LANES), f32),
            ],
            micros=5,
            name="coarse_taps",
        )(*border2, values)[0]

    split = C2 // LANES // 2
    sides = columns_out((slope2,), half_rows, half_cols)[0]
    g_first = taps_back(slope2, 0, split)
    sides, g_first = tie(sides, g_first)
    lower, upper = edges(slope2, *sides)
    ends = lines_out(lower, upper)
    slope2, lower = tie(slope2, lower)
    g_second = taps_back(slope2, split, C2 // LANES - split)
    ends, g_second = tie(ends, g_second)
    g_taps2 = jnp.concatenate([g_first, g_second], axis=1)
    dcells = call(
        lambda *refs: coarse_conv_back_kernel(half_rows, half_cols, *refs),
        [((low_cells, C2), bf16)],
        grid=(C2 // LANES,),
        ins=border_tiles(lane_tile) + [TAP_TILE, lane_tile(low_cells)],
        out_specs=[lane_tile(low_cells)],
        scratch=[pltpu.VMEM((low_border, LANES), f32), pltpu.VMEM((edge, LANES), f32)],
        micros=9,
        name="coarse_conv_back",
    )(slope2, *sides, *ends, taps_in2, dtop)[0]

    state, late_steps = scatter_steps(late_keep, late_send, late_planes)
    for step in late_steps[:-1]:
        state = step(state)
    dcells, state = tie(dcells, state)
    dv1, da1, dn1, normal1, sums1, hidden1, sums_low, copies1 = call(
        lambda *refs: fine_back_kernel(cols, *refs),
        [
            ((cells, C1), bf16), ((cells, H1), bf16), ((cells, C1), bf16), ((cells, C1), bf16),
            ((8, C1), f32), ((8, H1), f32), ((8, C2), f32), ((devices, 8, LANES), f32),
        ],
        grid=(half_rows,),
        ins=[
            whole(devices, 8, LANES), band(low_chunk, C2), whole(4, C2, C1), band(chunk, C1), whole(8, C1),
            band(chunk, C1), band(chunk, H1), whole(H1, C1), whole(C1, H1),
        ],
        out_specs=[
            band(chunk, C1), band(chunk, H1), band(chunk, C1), band(chunk, C1), whole(8, C1), whole(8, H1), whole(8, C2),
            whole(devices, 8, LANES),
        ],
        micros=13,
        name="fine_backward",
    )(got1, dcells, downs_four, ds, vecs1, conv1, slope1, up_in1, down_in1)
    da1, state = tie(da1, late_steps[-1](state))
    back1 = swap(copies1)
    early_planes = planes_of(devices, shard_len, *span(UP1, SHIFT2), plane_size)
    early_args = (da1, normal1, dv1, gated1, dcells, patches)
    early_keep, early_send = call(
        lambda *refs: early_flat_kernel(devices, shard_len, plane_size, early_planes, *refs),
        sums_out(early_planes),
        ins=[smem] + [vmem] * 6 + [hbm] * 6,
        scratch=[
            *[pltpu.VMEM(value.shape, bf16) for value in early_args],
            pltpu.VMEM((span(UP1, SHIFT2)[1] - span(UP1, SHIFT2)[0], LANES), f32), held_room,
            pltpu.VMEM((H1, C1), f32), pltpu.VMEM((C1, H1), f32), pltpu.VMEM((C2, H1), f32),
            pltpu.SemaphoreType.DMA((6,)),
        ],
        micros=8,
        name="early_flat",
    )(place_row, got2, sums1, hidden1, sums_low, g_taps2, sums2, *early_args)
    early_send, back1 = tie(early_send, back1)
    early_state, early_steps = scatter_steps(early_keep, early_send, early_planes)
    tail_used = -(-span(STEM, SHIFT1)[1] // devices)
    tail_lines = -(-(tail_used + 1) // 8) * 8
    for step in early_steps[:-1]:
        early_state = step(early_state)
    conv1, early_state = tie(conv1, early_state)
    back_args = (conv1, dn1, depth_rows, dv1, turned)
    tail = call(
        lambda *refs: stem_back_kernel(rows, cols, *refs),
        [((devices, tail_lines, LANES), f32)],
        ins=[vmem] * 6 + [hbm] * 5,
        scratch=[
            *[pltpu.VMEM(value.shape, value.dtype) for value in back_args],
            pltpu.VMEM((cells, C1), bf16), pltpu.VMEM((KSIZE * CIN, C1), f32), pltpu.VMEM((LANES, C1), f32),
            pltpu.VMEM((CIN, C1), f32), pltpu.VMEM((devices * tail_used, LANES), f32), pltpu.VMEM((C1, LANES), f32),
            pltpu.SemaphoreType.DMA((5,)),
        ],
        micros=14,
        name="stem_back",
    )(got1, back1, vecs1, near1, stem_in, sums1, *back_args)[0]
    tail, early_state = tie(tail, early_steps[-1](early_state))

    chunk_sum = jnp.sum(swap(tail), axis=0)
    summed = scatter_planes(scatter_last(merge_planes([(state, late_planes), (early_state, early_planes)])))
    mine = lax.dynamic_slice_in_dim(summed.reshape(-1), at, shard_len)
    squares = jnp.sum(mine * mine) + jnp.sum(chunk_sum * chunk_sum)
    loss_part = jnp.sum(sums2[5, :LANES])
    lane = lax.broadcasted_iota(jnp.int32, chunk_sum.shape, 1)
    line = lax.broadcasted_iota(jnp.int32, chunk_sum.shape, 0)
    totals = jnp.where(lane == 0, loss_part, jnp.where(lane == 1, squares, 0.0))
    last = jnp.where(line == tail_used, totals, chunk_sum)
    last = swap(jnp.broadcast_to(last[None], (devices,) + last.shape))
    tail_flat = last[:, :tail_used].reshape(devices * tail_used, LANES)
    totals = jnp.sum(last[:, tail_used, :2], axis=0)
    loss_total, norm = totals[0], jnp.sqrt(totals[1])
    row, lane = count_places(C1)[1]
    count = jnp.sum(got1[:, row, lane])
    tail_flat = jnp.pad(tail_flat, ((0, tall), (0, 0)))
    line = jnp.minimum(me * shard_len // 2048 * 16, devices * tail_used)
    mine_tail = lax.dynamic_slice_in_dim(tail_flat, line, tall).reshape(-1)
    mine = mine + lax.dynamic_slice_in_dim(mine_tail, at, shard_len)
    clipped = mine * jnp.minimum(1.0, CLIP / norm)
    first = BETA_ONE * moment1 + (1.0 - BETA_ONE) * clipped
    second = BETA_TWO * moment2 + (1.0 - BETA_TWO) * clipped * clipped
    ratio = first / (1.0 - BETA_ONE**STEP) / (jnp.sqrt(second / (1.0 - BETA_TWO**STEP)) + ADAM_EPS)
    updated = params - LRATE * (ratio + DECAY * params)
    return (loss_total, count, norm, updated, first, second)


def solution(mesh):
    in_specs = (
        P("lvl", None, "lat", None),
        P("lvl", None, "lat", None),
        P("lat", "lvl"),
        P(),
        P(("lat", "lvl")),
        P(("lat", "lvl")),
        P(("lat", "lvl")),
    )
    out_specs = (P(), P(), P(), P(("lat", "lvl")), P(("lat", "lvl")), P(("lat", "lvl")))
    return jax.shard_map(body, mesh=mesh, in_specs=in_specs, out_specs=out_specs, check_vma=False)
```

```python
import math

import jax
import jax.numpy as jnp
import numpy as np
from jax import lax
from jax.experimental import pallas as pl
from jax.experimental.pallas import tpu as pltpu
from jax.sharding import PartitionSpec as P

CIN = 80
WIDTH = 200
EXPAND = 800
WIDTH2 = 400
EXPAND2 = 1600
KSIZE = 7
TAPS = KSIZE * KSIZE
LEVELS = 19
STEP = 10

CLIP = 0.01
LRATE = 0.05
BETA_ONE = 0.9
BETA_TWO = 0.999
ADAM_EPS = 1e-08
DECAY = 0.1
HEAT_WEIGHT = 40.0
NORM_EPS = 1e-05

AXES = ("lat", "lvl")

CI = 128
C1 = 256
H1 = 896
C2 = 512
H2 = 1664
BLOCKS = 8
LANES = 128
REACH = KSIZE // 2
GROUPS = 17

f32 = jnp.float32
bf16 = jnp.bfloat16
VMEM_LIMIT = 60 * 1024 * 1024


def plane_bits():
    bits = []
    for axis in AXES:
        count = lax.axis_size(axis)
        step = count // 2
        while step >= 1:
            bits.append((axis, count, step))
            step //= 2
    across = [b for b in bits if b[0] == "lat" and b[2] > 1]
    within = [b for b in bits if b not in across]
    return across, within


def exchange(values, axis, count, step):
    return lax.ppermute(values, axis, [(i, i ^ step) for i in range(count)])


def half_rows_of(tall):
    return -(-tall // 32) * 16


def scatter_steps(keep, send, planes):
    _, (first, second, *others) = plane_bits()
    cut = half_rows_of(keep.shape[1])

    def inner(turn, bit):
        def step(state):
            keep, send = state
            if turn > 0:
                half = keep.shape[0] // 2
                keep, send = keep[:half], keep[half:].astype(bf16)
            keep = keep + exchange(send, *bit).astype(f32)
            return keep, None

        return step

    def outer(state):
        keep, _ = state
        parts = keep.reshape((2, 2, len(planes)) + keep.shape[1:])
        left, right = parts[:, :, :, :cut], parts[:, :, :, cut:]
        left = left[0] + exchange(left[1].astype(bf16), *second).astype(f32)
        right = right[:, 0] + exchange(right[:, 1].astype(bf16), *first).astype(f32)
        return left, right

    steps = [inner(turn, bit) for turn, bit in enumerate(reversed(others))]
    return (keep, send), steps + [outer]


def merge_planes(groups):
    total = lax.axis_size("lat") // 2
    merged = []
    for side in range(2):
        rows = []
        for p in range(total):
            held = [state[side][:, planes.index(p)] for state, planes in groups if p in planes]
            rows.append(sum(held[1:], held[0]))
        merged.append(jnp.stack(rows, axis=1))
    return merged


def scatter_last(state):
    _, (first, second, *_) = plane_bits()
    left, right = state
    left = left[0] + exchange(left[1].astype(bf16), *first).astype(f32)
    right = right[0] + exchange(right[1].astype(bf16), *second).astype(f32)
    return jnp.concatenate([left, right], axis=1)


def tie(first, second):
    return lax.optimization_barrier((first, second))


def scatter_planes(rows):
    count = lax.axis_size("lat")
    plane = lax.axis_index("lat") // 2
    mine = lax.dynamic_index_in_dim(rows, plane, 0, False)
    parts = [
        exchange(lax.dynamic_index_in_dim(rows, plane ^ away, 0, False).astype(bf16), "lat", count, 2 * away)
        for away in range(1, count // 2)
    ]
    for part in parts:
        mine = mine + part.astype(f32)
    return mine


def swap(copies):
    return lax.all_to_all(copies, AXES, 0, 0, tiled=True)


def neighbours(axis):
    ends = lax.axis_size(axis) - 1
    return [(i, i + 1) for i in range(ends)], [(i + 1, i) for i in range(ends)]


def columns_out(arrays, rows, cols):
    onward, back = neighbours("lvl")
    sides = []
    for start, pairs in ((cols - REACH, onward), (0, back)):
        own = [values.reshape(rows, cols, 8, -1)[:, start : start + REACH] for values in arrays]
        own = jnp.concatenate([part.reshape(rows * REACH * 8, -1) for part in own], axis=0)
        sides.append(lax.ppermute(own, "lvl", pairs))
    size = rows * REACH * 8
    return [[side[k * size : (k + 1) * size] for side in sides] for k in range(len(arrays))]


def lines_out(lower, upper):
    onward, back = neighbours("lat")
    return lax.ppermute(lower, "lat", onward), lax.ppermute(upper, "lat", back)


def depth_cells(depth, batch):
    rows, cols = depth.shape
    bands = BLOCKS // batch
    split = depth.reshape(bands, rows // bands, cols).transpose(1, 2, 0)
    return jnp.concatenate([split] * batch, axis=2)


def block_shapes(chans, hidden):
    return [
        (chans, TAPS),
        (chans,),
        (chans,),
        (hidden, chans),
        (hidden,),
        (chans, hidden),
        (chans,),
    ]


def shapes_of():
    return (
        [(WIDTH, CIN)]
        + block_shapes(WIDTH, EXPAND)
        + [(WIDTH2, 4 * WIDTH), (WIDTH2,)]
        + block_shapes(WIDTH2, EXPAND2)
        + [(4 * WIDTH, WIDTH2), (WIDTH,), (CIN, WIDTH), (CIN,)]
    )


def fill(values, *shape):
    return jnp.pad(values, [(0, n - m) for n, m in zip(shape, values.shape)])


def nt(left, right):
    return lax.dot_general(left, right, (((1,), (1,)), ((), ())), preferred_element_type=f32)


def nn(left, right):
    return lax.dot_general(left, right, (((1,), (0,)), ((), ())), preferred_element_type=f32)


def tn(left, right):
    return lax.dot_general(left, right, (((0,), (0,)), ((), ())), preferred_element_type=f32)


def rows8(start, amount):
    return pl.ds(pl.multiple_of(start * 8, 8), amount * 8)


def convolve(source, taps, rows, cols, emit, carry, flip=False):
    width = cols + 2 * REACH

    def line(row, carry):
        total = jnp.zeros((cols, 8, LANES), f32)
        for p in range(KSIZE):
            seen = source[rows8((row + p) * width, width), :].reshape(width, 8, LANES)
            for q in range(KSIZE):
                tap = p * KSIZE + q
                total = total + seen[q : q + cols] * taps[TAPS - 1 - tap if flip else tap][None]
        return emit(rows8(row * cols, cols), total, carry)

    return lax.fori_loop(0, rows, line, carry)


def row_sum(values):
    return jnp.sum(values, axis=0, keepdims=True)


def spread_rows(values, tiles):
    return [values[:, m * LANES : (m + 1) * LANES] for m in range(tiles)]


def stats_block(first, second, counts):
    tiles = first.shape[1] // LANES
    rows = spread_rows(first, tiles) + spread_rows(second, tiles)
    if len(rows) < 8:
        rows = rows + [jnp.zeros((8 - len(rows), LANES), f32)]
    block = jnp.concatenate(rows, axis=0)
    return block if counts is None else block + counts


def wide_row(total, start, tiles):
    return jnp.concatenate([total[start + m : start + m + 1] for m in range(tiles)], axis=1)


def count_places(width):
    if width == C1:
        return (4, 0), (5, 0)
    return (WIDTH2 // LANES, WIDTH2 % LANES), (WIDTH2 // LANES, WIDTH2 % LANES + 1)


def norm_rows(got, width):
    tiles = width // LANES
    total = jnp.sum(got[...], axis=0)
    (r, c), (ro, co) = count_places(width)
    cells, ocean = total[r : r + 1, c : c + 1], total[ro : ro + 1, co : co + 1]
    lane = lax.broadcasted_iota(jnp.int32, (1, width), 1)
    sums = jnp.where(lane < (WIDTH if width == C1 else WIDTH2), wide_row(total, 0, tiles), 0.0)
    mean = sums / cells
    inverse = lax.rsqrt(wide_row(total, tiles, tiles) / cells - mean * mean + NORM_EPS)
    return mean, inverse, cells, ocean


def gelu_pair(act):
    square = act * act
    flat = 0.7978845608028654
    cube = flat * 0.044715
    half = 0.5 + 0.5 * jnp.tanh(act * (flat + cube * square))
    value = act * half
    return value, half + value * (1.0 - half) * (2.0 * flat + (6.0 * cube) * square)


def quarter(values, rows, cols, p, q):
    chans = values.shape[-1]
    split = values.reshape(rows // 2, 2, cols // 2, 2, 8, chans)
    return split[:, p, :, q].reshape(rows * cols * 2, chans)


def from_quarters(parts, rows, cols):
    chans = parts[0].shape[-1]
    cells = [part.reshape(rows // 2, cols // 2, 8, chans) for part in parts]
    lines = [jnp.stack(cells[2 * p : 2 * p + 2], axis=2) for p in range(2)]
    return jnp.stack(lines, axis=1).reshape(rows * cols * 8, chans)


def call(kernel, outs, grid=(), ins=None, out_specs=None, scratch=(), micros=5, name=None):
    params = dict(out_shape=[jax.ShapeDtypeStruct(s, t) for s, t in outs])
    if ins:
        params.update(in_specs=ins)
    if grid:
        params.update(grid=grid, out_specs=out_specs)
    return pl.pallas_call(
        kernel,
        scratch_shapes=list(scratch),
        compiler_params=pltpu.CompilerParams(vmem_limit_bytes=VMEM_LIMIT),
        cost_estimate=pl.CostEstimate(flops=int(micros * 1.1e9), bytes_accessed=100000, transcendentals=0),
        name=name,
        **params,
    )


def whole(*shape):
    return pl.BlockSpec(shape, lambda i: (0,) * len(shape))


def band(rows, cols):
    return pl.BlockSpec((rows, cols), lambda i: (i, 0))


def lane_tile(rows):
    return pl.BlockSpec((rows, LANES), lambda i: (0, i))


def stats_tile(devices):
    return pl.BlockSpec((devices, 8, LANES), lambda i: (0, 0, i))


TAP_TILE = pl.BlockSpec((TAPS, 8, LANES), lambda i: (0, 0, i))


def conv_sums(source, taps, depth, counts, out, stats, rows, cols, block):
    def emit(place, total, carry):
        flat = total.reshape(cols * 8, LANES)
        out[place, :] = flat
        ocean = depth[place, :] > 0.0
        kept = jnp.where(ocean, flat, 0.0)
        kept_cells = kept.reshape(cols, 8, LANES)
        return (carry[0] + jnp.sum(kept_cells, axis=0), carry[1] + jnp.sum(kept_cells * total, axis=0))

    zero = jnp.zeros((8, LANES), f32)
    first, second = convolve(source, taps, rows, cols, emit, (zero, zero))
    tile = pl.program_id(0)
    tiles = pl.num_programs(0)

    @pl.when(tile == 0)
    def _():
        block[...] = counts[...]

    block[pl.ds(tile, 1), :] += row_sum(first)
    block[pl.ds(C2 // LANES + tile, 1), :] += row_sum(second)

    @pl.when(tile == tiles - 1)
    def _():
        stats[...] = jnp.broadcast_to(block[...][None], stats.shape)


def lay_border(rows, cols, source, held, centre, left, right, above, below):
    width = cols + 2 * REACH
    sides = [left[...].astype(f32), right[...].astype(f32)]
    for row in range(rows):
        start = (row + REACH) * width
        source[rows8(start + REACH, cols), :] = centre[rows8(row * cols, cols), :].astype(f32)
        for side, place in zip(sides, (0, cols + REACH)):
            source[rows8(start + place, REACH), :] = side[row * REACH * 8 : (row + 1) * REACH * 8]
    for t in range(REACH):
        for start, target, way in ((rows + t, t, 1), (REACH + t, rows + REACH + t, 7)):
            line = source[rows8(start * width, width), :].reshape(width, 8, LANES)
            source[rows8(target * width, width), :] = pltpu.roll(line, way, 1).reshape(width * 8, LANES)
    amount = REACH * width
    for part, base in ((above, 0), (below, (rows + REACH) * width * 8 + BLOCKS // 2 - 1)):
        held[...] = part[...].astype(f32)
        for b in range(2):
            values = held[pl.ds(b, amount, stride=2), :]
            source[pl.ds(base + b * (BLOCKS // 2), amount, stride=8), :] = values


def pack_kernel(parts, cols, reach, values, out, tiles, flat):
    total = values.shape[1]
    width = cols + 2 * reach
    lines = out.shape[1]
    depth = values.shape[0] // lines
    count = tiles.shape[0]
    for k in range(count):
        size = min(LANES, total - k * LANES)
        tiles[k, :, :size] = values[:, k * LANES : k * LANES + size].astype(f32)
        if size < LANES:
            tiles[k, :, size:] = jnp.zeros((values.shape[0], LANES - size), f32)
    blank = jnp.zeros((lines, LANES), f32)
    for row in range(depth):
        pieces = [tiles[k, pl.ds(row, lines, stride=depth), :] for k in range(count)]
        wide = jnp.concatenate([blank] + pieces + [blank], axis=1)
        for part in range(parts):
            start = LANES + part * cols - reach
            flat[part, :, row * width : (row + 1) * width] = wide[:, start : start + width]
    for part in range(parts):
        out[part] = flat[part].astype(bf16)


def unpack_cells(packed, parts, first, amount, cells, across):
    lines = packed.shape[1]
    chans = lines // BLOCKS
    for part in range(parts):
        across[part] = packed[part, :, first : first + amount].astype(f32).T.astype(bf16)
    source = lax.broadcasted_iota(jnp.int32, (lines, LANES), 0)
    target = lax.broadcasted_iota(jnp.int32, (lines, LANES), 1)
    for s in range(BLOCKS):
        total = jnp.zeros((amount, LANES), f32)
        for part in range(parts):
            pick = ((target - part * chans) * BLOCKS + s == source).astype(bf16)
            total = total + nn(across[part], pick)
        cells[pl.ds(s, amount, stride=BLOCKS), :] = total


def targets_kernel(parts, first, packed, out, cells, across):
    unpack_cells(packed, parts, first, across.shape[1], cells, across)
    out[...] = cells[...].astype(bf16)


def fields_kernel(parts, rows, cols, packed, cells, lower, upper, held, across):
    unpack_cells(packed, parts, 0, across.shape[1], cells, across)
    width = cols + 2 * REACH
    room = -(-width // 8) * 8
    held[...] = jnp.zeros(held.shape, f32)
    for out, low, band in ((lower, rows - REACH, BLOCKS // 2 - 1), (upper, 0, 0)):
        for b in range(2):
            for t in range(REACH):
                start = (low + t) * width * 8 + band + b * (BLOCKS // 2)
                at = (b * REACH + t) * room
                held[at : at + width, :] = cells[pl.ds(start, width, stride=8), :]
        out[...] = held[...].astype(bf16)


def lay_ends(rows, cols, cells, above, below, ends):
    width = cols + 2 * REACH
    room = -(-width // 8) * 8
    line = width * 8
    for t in range(REACH):
        for k, row, way in ((t, rows - REACH + t, 1), (REACH + t, t, 7)):
            values = cells[row * line : (row + 1) * line, :].reshape(width, 8, LANES)
            ends[k * line : (k + 1) * line, :] = pltpu.roll(values, way, 1).reshape(line, LANES)
    for part, base, band in ((above, 0, 0), (below, REACH, BLOCKS // 2 - 1)):
        values = part[...].astype(f32)
        for b in range(2):
            for t in range(REACH):
                at = (b * REACH + t) * room
                start = (base + t) * line + band + b * (BLOCKS // 2)
                ends[pl.ds(start, width, stride=8), :] = values[at : at + width]


def lay_shifted(rows, cols, cells, ends, out, col, across):
    line = (cols + 2 * REACH) * 8
    total = rows + 2 * REACH
    amount = cols * 8
    lane = lax.broadcasted_iota(jnp.int32, (amount, LANES), 1)

    def values(row, col):
        if row >= total:
            return jnp.zeros((amount, LANES), f32)
        if row < REACH:
            ref, start = ends, row * line
        elif row < REACH + rows:
            ref, start = cells, (row - REACH) * line
        else:
            ref, start = ends, (row - rows) * line
        return ref[start + col * 8 : start + col * 8 + amount, :]

    for row in range(total):
        near = values(row, col)
        middle = values(row + 1, col) if across else values(row, col + 1)
        last = values(row + 2, col) if across else values(row, col + 2)
        middle = pltpu.roll(middle, CIN, 1)
        last = pltpu.roll(last, 2 * CIN - LANES, 1)
        place = slice(row * amount, (row + 1) * amount)
        out[place, :LANES] = jnp.where(lane < CIN, near, middle).astype(bf16)
        out[place, LANES:] = jnp.where(lane < 2 * CIN - LANES, middle, last).astype(bf16)


def wide_stem(stem):
    return jnp.concatenate([stem.astype(f32), jnp.zeros((C1, C1 - CI), f32)], axis=1)


def triple_stem(stem):
    wide = wide_stem(stem)
    return wide + pltpu.roll(wide, CIN, 1) + pltpu.roll(wide, 2 * CIN, 1)


def stem_kernel(
    rows, cols, cells, above, below, near, stem, pick, depth, counts, hzero, out, stats,
    weights, wide, sums, ends, first, second, third,
):
    amount = cols * 8
    step = pl.program_id(0)
    size = out.shape[0]

    @pl.when(step == 0)
    def _():
        lay_ends(rows, cols, cells, above, below, ends)
        lay_shifted(rows, cols, cells, ends, first, 0, False)
        lay_shifted(rows, cols, cells, ends, second, REACH, False)
        lay_shifted(rows, cols, cells, ends, third, 2 * REACH, True)
        stem3 = triple_stem(stem[...])
        for index in range(GROUPS):
            both = nt(near[...], pick[index]) * stem3
            weights[index * C1 : (index + 1) * C1, :] = both.astype(bf16)
        wide[...] = wide_stem(stem[...]).astype(bf16)
        sums[...] = jnp.zeros(sums.shape, f32)

    def place(shift):
        return pl.ds(pl.multiple_of(step * size + shift * amount, amount), size)

    total = jnp.zeros((size, C1), f32)
    for p in range(KSIZE):
        total = total + nt(first[place(p), :], weights[p * C1 : (p + 1) * C1, :])
        total = total + nt(second[place(p), :], weights[(KSIZE + p) * C1 : (KSIZE + p + 1) * C1, :])
    for k in range(3):
        at = (2 * KSIZE + k) * C1
        total = total + nt(third[place(3 * k), :], weights[at : at + C1, :])
    out[...] = total
    hzero[...] = nt(second[place(REACH), :], wide[...]).astype(bf16)
    ocean = depth[...] > 0.0
    kept = jnp.where(jnp.concatenate([ocean, ocean], axis=1), total, 0.0)
    sums[0:1, :] += row_sum(kept)
    sums[1:2, :] += row_sum(kept * total)

    @pl.when(step == pl.num_programs(0) - 1)
    def _():
        stats[...] = jnp.broadcast_to(stats_block(sums[0:1, :], sums[1:2, :], counts[...])[None], stats.shape)


def edge_kernel(rows, cols, count, *refs):
    inputs, (lower, upper, held, edge) = refs[: 3 * count], refs[3 * count :]
    width = cols + 2 * REACH
    lines = edge_lines(cols)
    amount = rows * cols * 8
    side = rows * REACH * 8
    for k in range(count):
        for tile in range(C2 // LANES):
            lanes = slice(tile * LANES, (tile + 1) * LANES)
            for ref, start, size in zip(inputs[3 * k : 3 * k + 3], (0, amount, amount + side), (amount, side, side)):
                held[start : start + size, :] = ref[:, lanes].astype(f32)
            for out, low, band in ((lower, rows - REACH, BLOCKS // 2 - 1), (upper, 0, 0)):
                edge[lines - 16 :, :] = jnp.zeros((16, LANES), f32)
                for t in range(REACH):
                    for b in range(2):
                        s = band + b * (BLOCKS // 2)
                        at = t * width * 2 + b
                        for start, wide, col in ((amount, REACH, 0), (0, cols, REACH), (amount + side, REACH, REACH + cols)):
                            values = held[pl.ds(start + (low + t) * wide * 8 + s, wide, stride=8), :]
                            edge[pl.ds(at + 2 * col, wide, stride=2), :] = values
                out[k * lines : (k + 1) * lines, lanes] = edge[...].astype(bf16)


def edge_lines(cols):
    return -(-REACH * (cols + 2 * REACH) * 2 // 16) * 16


def coarse_conv_kernel(rows, cols, centre, left, right, above, below, taps, depth, counts, out, stats, source, held, block):
    lay_border(rows, cols, source, held, centre, left, right, above, below)
    conv_sums(source, taps, depth, counts, out, stats, rows, cols, block)


def fine_kernel(cols, got, conv, hzero, vecs, bias_rows, up, up_bias, down, perm, downs, down_rows, hone, gated, slope, patches, coarse, held):
    mean, inverse, _, _ = norm_rows(got, C1)
    scale = inverse * vecs[0:1]
    for part in range(2):
        place = pl.ds(part * cols * 8, cols * 8)
        normal = ((conv[place, :] - mean) * scale + vecs[1:2]).astype(bf16)
        act = nt(normal, up[...]) + up_bias[...]
        value, bend = gelu_pair(act)
        value = value.astype(bf16)
        gated[place, :] = value
        slope[place, :] = bend.astype(bf16)
        branch = nt(value, down[...]) + bias_rows[0:1]
        full = (hzero[place, :].astype(f32) + branch).astype(bf16)
        hone[place, :] = full
        held[place, :] = full.astype(f32)
    cells = held[...]
    mixed = jnp.zeros((cols * 4, H1), f32)
    for p in range(2):
        for q in range(2):
            mixed = mixed + nn(quarter(cells, 2, cols, p, q).astype(bf16), perm[p * 2 + q])
    mixed = mixed.astype(bf16)
    patches[...] = mixed
    coarse[...] = (nt(mixed, downs[...]) + down_rows[0:1]).astype(bf16)


def middle_kernel(
    cols, got, conv, cells, vecs, up, up_bias, down, ups, fine_rows, head, last_rows, tables, hone, targets, depth,
    skip_out, top_out, dy_out, ds_out, du_out, dtop_out, dv_out, gated_out, da_out, normal_out, dx_out,
    sums, hidden_sums, copies,
):
    mean, inverse, _, ocean_count = norm_rows(got, C2)
    scale = inverse * vecs[0:1]
    centred = conv[...] - mean
    normal = (centred * scale + vecs[1:2]).astype(bf16)
    normal_out[...] = normal
    value, bend = gelu_pair(nt(normal, up[...]) + up_bias[...])
    value = value.astype(bf16)
    gated_out[...] = value
    top = (cells[...].astype(f32) + nt(value, down[...]) + vecs[2:3]).astype(bf16)
    top_out[...] = top
    raised = from_quarters([nt(top, ups[k]) + fine_rows[0:1] for k in range(4)], 2, cols)
    skip = (hone[...].astype(f32) + raised).astype(bf16)
    skip_out[...] = skip
    err = nt(skip, head[...]) + last_rows[0:1] - targets[...].astype(f32)
    deep = depth[...]
    ocean = tables[0:1] < deep
    heat_take = tables[1:2]
    err = jnp.where(ocean, err, 0.0)
    heat = jnp.sum(heat_take * err, axis=1, keepdims=True)
    heat = jnp.where(deep > 0.0, heat, 0.0)
    loss = row_sum(err * err) + (HEAT_WEIGHT / LANES) * row_sum(heat * heat)
    dy = jnp.where(ocean, err + HEAT_WEIGHT * heat_take * heat, 0.0) * (2.0 / ocean_count)
    dy = dy.astype(bf16)
    dy_out[...] = dy
    ds = nn(dy, head[...])
    ds_out[...] = ds
    dtop = jnp.zeros(top.shape, f32)
    du_sum = jnp.zeros((1, C1), f32)
    for k in range(4):
        du = quarter(ds, 2, cols, k // 2, k % 2).astype(bf16)
        du_out[k] = du
        du_sum = du_sum + row_sum(du.astype(f32))
        dtop = dtop + nn(du, ups[k])
    dtop_out[...] = dtop
    dv = dtop.astype(bf16)
    dv_out[...] = dv
    da = (nn(dv, down[...]) * bend).astype(bf16)
    da_out[...] = da
    dn = nn(da, up[...])
    dx_out[...] = dn * vecs[0:1]

    @pl.when(pl.program_id(0) == 0)
    def _():
        sums[...] = jnp.zeros(sums.shape, f32)
        hidden_sums[...] = jnp.zeros(hidden_sums.shape, f32)

    sums[0:1, :] += row_sum(dn)
    sums[1:2, :] += row_sum(dn * centred)
    sums[2:3, :] += row_sum(dv.astype(f32))
    sums[3:4, :C1] += du_sum
    sums[4:5, :CI] += row_sum(dy.astype(f32))
    sums[5:6, :LANES] += loss
    hidden_sums[0:1, :] += row_sum(da.astype(f32))

    @pl.when(pl.program_id(0) == pl.num_programs(0) - 1)
    def _():
        copies[...] = jnp.broadcast_to(stats_block(sums[0:1, :], sums[1:2, :], None)[None], copies.shape)


def backward_rows(got, back, gain, width):
    mean, inverse, cells, _ = norm_rows(got, width)
    tiles = width // LANES
    total = jnp.sum(back[...], axis=0)
    total_a = gain * wide_row(total, 0, tiles)
    total_b = gain * wide_row(total, tiles, tiles)
    dvar = -0.5 * inverse * inverse * inverse * total_b
    first = (-inverse * total_a - 2.0 * mean * dvar) / cells
    second = 2.0 * dvar / cells
    return inverse, first, second


def coarse_slope_kernel(got, back, vecs, dx, conv, depth, out):
    inverse, first, second = backward_rows(got, back, vecs[0:1], C2)
    ocean = depth[...] > 0.0
    ocean = jnp.concatenate([ocean] * (C2 // LANES), axis=1)
    value = dx[...] * inverse + jnp.where(ocean, first + conv[...] * second, 0.0)
    out[...] = value.astype(bf16)


def coarse_taps_kernel(rows, cols, centre, left, right, above, below, slope, taps_out, source, held, here):
    lay_border(rows, cols, source, held, centre, left, right, above, below)
    here[...] = slope[...].astype(f32)
    taps_out[TAPS:, :] = jnp.zeros((taps_out.shape[0] - TAPS, LANES), f32)
    width = cols + 2 * REACH
    for p in range(KSIZE):

        def line(row, sums):
            own = here[rows8(row * cols, cols), :].reshape(cols, 8, LANES)
            seen = source[rows8((row + p) * width, width), :].reshape(width, 8, LANES)
            return tuple(sums[q] + jnp.sum(seen[q : q + cols] * own, axis=0) for q in range(KSIZE))

        zero = jnp.zeros((8, LANES), f32)
        sums = lax.fori_loop(0, rows, line, (zero,) * KSIZE)
        for q in range(KSIZE):
            taps_out[p * KSIZE + q : p * KSIZE + q + 1, :] = row_sum(sums[q])


def coarse_conv_back_kernel(rows, cols, centre, left, right, above, below, taps, dtop, dcells, slope, held):
    lay_border(rows, cols, slope, held, centre, left, right, above, below)

    def emit(place, total, carry):
        dcells[place, :] = (dtop[place, :] + total.reshape(cols * 8, LANES)).astype(bf16)
        return carry

    convolve(slope, taps, rows, cols, emit, 0, flip=True)


def fine_back_kernel(
    cols, got, dcells, downs, ds, vecs, conv, slope, up, down, dv_out, da_out, dn_out, normal_out, sums, hidden_sums, coarse_sums, copies
):
    mean, inverse, _, _ = norm_rows(got, C1)
    dlow = dcells[...]
    dh = ds[...] + from_quarters([nn(dlow, downs[k]) for k in range(4)], 2, cols)
    dv = dh.astype(bf16)
    dv_out[...] = dv

    @pl.when(pl.program_id(0) == 0)
    def _():
        sums[...] = jnp.zeros(sums.shape, f32)
        hidden_sums[...] = jnp.zeros(hidden_sums.shape, f32)
        coarse_sums[...] = jnp.zeros(coarse_sums.shape, f32)

    coarse_sums[0:1, :] += row_sum(dlow.astype(f32))
    sums[2:3, :] += row_sum(dv.astype(f32))
    for part in range(2):
        place = pl.ds(part * cols * 8, cols * 8)
        centred = conv[place, :] - mean
        normal_out[place, :] = (centred * (inverse * vecs[0:1]) + vecs[1:2]).astype(bf16)
        da = (nn(dv_out[place, :], down[...]) * slope[place, :].astype(f32)).astype(bf16)
        da_out[place, :] = da
        hidden_sums[0:1, :] += row_sum(da.astype(f32))
        dn = nn(da, up[...])
        dn_out[place, :] = dn.astype(bf16)
        sums[0:1, :] += row_sum(dn)
        sums[1:2, :] += row_sum(dn * centred)

    @pl.when(pl.program_id(0) == pl.num_programs(0) - 1)
    def _():
        copies[...] = jnp.broadcast_to(stats_block(sums[0:1, :], sums[1:2, :], None)[None], copies.shape)


def turn_kernel(rows, cols, cells, above, below, out, ends):
    line = (cols + 2 * REACH) * 8
    amount = cols * 8
    lay_ends(rows, cols, cells, above, below, ends)
    for row in range(rows + 2 * REACH):
        if row < REACH:
            values = ends[row * line : (row + 1) * line, :]
        elif row < REACH + rows:
            values = cells[(row - REACH) * line : (row - REACH + 1) * line, :]
        else:
            values = ends[(row - rows) * line : (row - rows + 1) * line, :]
        across = values.T[:CIN]
        for q in range(KSIZE):
            piece = across[:, q * 8 : q * 8 + amount].astype(bf16)
            out[q * CIN : (q + 1) * CIN, row * amount : (row + 1) * amount] = piece


def fetch(sources, rooms, sems):
    return [pltpu.make_async_copy(a, b, sems.at[k]) for k, (a, b) in enumerate(zip(sources, rooms))]


def start(copies):
    for copy in copies:
        copy.start()


def wait(copies):
    for copy in copies:
        copy.wait()


def stem_back_kernel(rows, cols, got, back, vecs, near, stem, sums, conv, dn, depth, dv, shifted, tail, *scratch):
    rooms, (slope, acc, tap_acc, stem_acc, lines, held, sems) = scratch[:5], scratch[5:]
    copies = fetch((conv, dn, depth, dv, shifted), rooms, sems)
    start(copies)
    conv, dn, depth, dv, shifted = rooms
    amount = cols * 8
    inverse, first, second = backward_rows(got, back, vecs[0:1], C1)
    scale = inverse * vecs[0:1]
    taps = near[...].astype(f32).T
    stem_turned = stem[...].astype(f32).T
    wait(copies[:3])

    def slopes(row, carry):
        place = pl.ds(pl.multiple_of(row * amount, amount), amount)
        ocean = depth[place, :] > 0.0
        ocean = jnp.concatenate([ocean, ocean], axis=1)
        value = dn[place, :].astype(f32) * scale + jnp.where(ocean, first + conv[place, :] * second, 0.0)
        slope[place, :] = value.astype(bf16)
        return carry

    lax.fori_loop(0, rows, slopes, 0)
    wait(copies[3:])
    total = rows * amount
    straight = shifted[REACH * CIN : (REACH + 1) * CIN, REACH * amount : REACH * amount + total]
    stem_acc[...] = nn(straight, dv[...])
    tap_acc[...] = jnp.zeros(tap_acc.shape, f32)
    for p in range(KSIZE):
        acc[...] = nn(shifted[:, p * amount : p * amount + total], slope[...])
        sum_here = stem_acc[...]
        for q in range(KSIZE):
            tap = p * KSIZE + q
            part = acc[q * CIN : (q + 1) * CIN, :]
            sum_here = sum_here + part * taps[tap : tap + 1]
            tap_acc[tap : tap + 1, :] = row_sum(part * stem_turned[:CIN])
        stem_acc[...] = sum_here
    acc[:CIN, :] = stem_acc[...]
    acc[CIN : 2 * LANES, :] = jnp.zeros((2 * LANES - CIN, C1), f32)
    lines[...] = jnp.zeros(lines.shape, f32)
    turned = acc[:LANES, :].T
    acc[:C1, :LANES] = turned
    write_matrix(lines, 0, STEM, held, acc)
    held[:C1, :] = tap_acc[...].T
    write_short(lines, offsets()[TAPS1], WIDTH, TAPS, lambda r: held[r : r + 1, :])
    write_row(lines, 0, GAIN1, norm_row(got, sums, C1))
    write_row(lines, 0, SHIFT1, row_of(sums, 0))
    used = lines.shape[0] // tail.shape[0]
    for k in range(tail.shape[0]):
        tail[k, :used] = lines[k * used : (k + 1) * used, :]
        tail[k, used:] = jnp.zeros((tail.shape[1] - used, LANES), f32)


def period(length):
    return LANES // math.gcd(length, LANES)


def offsets():
    starts = []
    start = 0
    for shape in shapes_of():
        starts.append(start)
        start += math.prod(shape)
    return starts


def shard_places(devices, shard_len):
    firsts = [e * shard_len // 2048 * 16 for e in range(devices)]
    needed = [(e * shard_len % 2048 + shard_len + 2047) // 2048 * 16 for e in range(devices)]
    return firsts, max(needed)


def lane_ids(rows):
    return lax.broadcasted_iota(jnp.int32, (rows, LANES), 1)


def turn_lanes(values, amount):
    amount = amount % LANES
    return values if amount == 0 else pltpu.roll(values, amount, 1)


def read_rows(lines, base, rows, length, put):
    cycle = period(length)
    count = rows // cycle
    step = cycle * length // LANES
    lane = lane_ids(count)
    tiles = -(-length // LANES)
    for s in range(cycle):
        start = base + s * length
        line, phase = start // LANES, start % LANES
        held = [
            lines[pl.ds(line + k, count, stride=step), :] for k in range(-(-(phase + length) // LANES))
        ]
        for m in range(tiles):
            value = held[m]
            if phase and m + 1 < len(held):
                value = jnp.where(lane >= phase, value, held[m + 1])
            value = turn_lanes(value, -phase)
            if length - m * LANES < LANES:
                value = jnp.where(lane < length - m * LANES, value, 0.0)
            put(s, cycle, count, m, value)


def read_vector(lines, base, length, put):
    line, phase = base // LANES, base % LANES
    lane = lane_ids(1)
    for m in range(-(-length // LANES)):
        value = lines[line + m : line + m + 1, :]
        if phase and phase + length > (m + 1) * LANES:
            value = jnp.where(lane >= phase, value, lines[line + m + 1 : line + m + 2, :])
        value = turn_lanes(value, -phase)
        if length - m * LANES < LANES:
            value = jnp.where(lane < length - m * LANES, value, 0.0)
        put(m, value)


def write_rows(lines, base, rows, length, get):
    cycle = period(length)
    count = rows // cycle
    step = cycle * length // LANES
    line, phase = base // LANES, base % LANES
    for k in range(step):
        shared = k == 0 and phase > 0
        amount = count + 1 if shared else count
        lane = lane_ids(amount)
        total = None
        at = 0
        while at < LANES:
            place = k * LANES - phase + at
            row, col = place // length, place % length
            run = min(length - col, LANES - at)
            tile = col // LANES
            value = get(row, cycle, amount, tile)
            if col % LANES + run > LANES:
                value = jnp.where(lane >= col % LANES, value, get(row, cycle, amount, tile + 1))
            value = turn_lanes(value, at - col)
            total = value if total is None else jnp.where(lane >= at, value, total)
            at += run
        put_lines(lines, line + k, amount, step, total, shared)


def put_lines(lines, line, amount, step, values, shared):
    if not shared:
        lines[pl.ds(line, amount, stride=step), :] = values
        return
    before = lines[line : line + 1, :]
    lines[pl.ds(line, amount, stride=step), :] = values
    lines[line : line + 1, :] = lines[line : line + 1, :] + before


def write_vector(lines, base, length, get):
    line, phase = base // LANES, base % LANES
    lane = lane_ids(1)
    tiles = -(-length // LANES)
    zero = jnp.zeros((1, LANES), f32)
    for k in range(-(-(phase + length) // LANES)):
        value = get(k) if k < tiles else zero
        if phase:
            earlier = get(k - 1) if k > 0 else zero
            value = turn_lanes(jnp.where(lane >= LANES - phase, earlier, value), phase)
        if k == 0 and phase:
            value = value + lines[line : line + 1, :]
        lines[line + k : line + k + 1, :] = value


def write_short(lines, base, rows, length, get):
    line, phase = base // LANES, base % LANES
    lane = lane_ids(1)
    for k in range(-(-(phase + rows * length) // LANES)):
        low = k * LANES - phase
        total = jnp.zeros((1, LANES), f32)
        for row in range(max(low // length, 0), min(-(-(low + LANES) // length), rows)):
            at = row * length - low
            value = turn_lanes(get(row), at)
            if at < 0:
                value = jnp.where(lane < at + length, value, 0.0)
            elif at + length > LANES:
                value = jnp.where(lane >= at, value, 0.0)
            total = total + value
        if k == 0 and phase:
            total = total + lines[line : line + 1, :]
        lines[line + k : line + k + 1, :] = total


def read_short(lines, base, rows, length, put):
    lane = lane_ids(1)
    for row in range(rows):
        start = base + row * length
        line, phase = start // LANES, start % LANES
        value = lines[line : line + 1, :]
        if phase + length > LANES:
            value = jnp.where(lane >= phase, value, lines[line + 1 : line + 2, :])
        put(row, jnp.where(lane < length, turn_lanes(value, -phase), 0.0))


STEM, TAPS1, GAIN1, SHIFT1, UP1, UPB1, DOWN1, DOWNB1, DOWNS, DOWNSB = range(10)
TAPS2, GAIN2, SHIFT2, UP2, UPB2, DOWN2, DOWNB2, UPS, UPSB, HEAD, HEADB = range(10, 21)


def planes_of(devices, shard_len, low, high, plane_size):
    firsts, tall = shard_places(devices, shard_len)
    found = {e // plane_size for e in range(devices) if firsts[e] < high and firsts[e] + tall > low}
    return sorted(found)


def collect(devices, shard_len, blocks, lines, low, high):
    firsts, tall = shard_places(devices, shard_len)
    started = False
    for e in range(devices):
        end = firsts[e + 1] + 16 if e + 1 < devices else firsts[e] + tall
        if end <= low or firsts[e] >= high:
            continue
        first = firsts[e] - low
        skip = max(0, -first)
        take = min(tall, high - firsts[e])
        if started:
            lines[pl.ds(first, 16), :] += blocks[e, :16, :].astype(f32)
            skip = 16
        started = True
        if take > skip:
            lines[pl.ds(first + skip, take - skip), :] = blocks[e, skip:take, :].astype(f32)


def seat_of(me, other, devices):
    away = me ^ other
    seat = 0
    bits = devices.bit_length() - 1
    for b in range(bits):
        seat = seat + ((away >> b) & 1) * (1 << (bits - 1 - b))
    return seat


def matrix_out(held, tall, out, tiles, rows):
    for m in range(tiles):
        if tall > rows:
            held[m * tall + rows : (m + 1) * tall, :] = jnp.zeros((tall - rows, LANES), f32)
        out[:, m * LANES : (m + 1) * LANES] = held[m * tall : (m + 1) * tall, :].astype(bf16)


def read_matrix(lines, shift, piece, held, out):
    rows, length = shapes_of()[piece]
    tall = out.shape[0]

    def put(first, stride, count, tile, value):
        held[pl.ds(tile * tall + first, count, stride=stride), :] = value

    read_rows(lines, offsets()[piece] - shift, rows, length, put)
    matrix_out(held, tall, out, -(-length // LANES), rows)


def read_row(lines, shift, piece, out, row):
    def put(tile, value):
        out[row : row + 1, tile * LANES : (tile + 1) * LANES] = value

    read_vector(lines, offsets()[piece] - shift, shapes_of()[piece][0], put)


def read_taps(lines, shift, piece, held, out, tall):
    def put(row, value):
        held[pl.ds(row, 1), :] = value

    rows = shapes_of()[piece][0]
    read_short(lines, offsets()[piece] - shift, rows, TAPS, put)
    held[rows:tall, :] = jnp.zeros((tall - rows, LANES), f32)
    if out is None:
        return
    across = held[:tall, :].T
    for t in range(TAPS):
        out[t] = jnp.broadcast_to(across[t : t + 1, :], (8, tall))


def first_end():
    return -(-offsets()[TAPS2] // 2048) * 16


def rest_start():
    return offsets()[TAPS2] // 2048 * 16


def rest_end():
    return -(-(offsets()[HEADB] + CIN) // 2048) * 16


def stem_params_kernel(parts, stem, near, vecs, lines, held):
    lines[...] = parts[...].astype(f32)
    vecs[...] = jnp.zeros(vecs.shape, f32)
    read_taps(lines, 0, TAPS1, held, None, C1)
    near[...] = held[:C1, :].astype(bf16)
    read_matrix(lines, 0, STEM, held, stem)
    read_row(lines, 0, GAIN1, vecs, 0)
    read_row(lines, 0, SHIFT1, vecs, 1)


def fine_params_kernel(
    devices, shard_len, blocks, perm, up, bias, down, downs, downs_four, down_rows, vecs, lines, held
):
    low, high = span(UP1, DOWNSB)
    shift = low * LANES
    collect(devices, shard_len, blocks, lines, low, high)
    for out in (down_rows, bias, vecs):
        out[...] = jnp.zeros(out.shape, f32)
    read_row(lines, shift, DOWNB1, vecs, 0)
    read_row(lines, shift, UPB1, bias, 0)
    read_row(lines, shift, DOWNSB, down_rows, 0)
    read_matrix(lines, shift, UP1, held, up)
    read_matrix(lines, shift, DOWN1, held, down)
    read_matrix(lines, shift, DOWNS, held, downs)
    for k in range(4):
        downs_four[k] = nt(downs[...], perm[k]).astype(bf16)


def rest_params_kernel(
    devices, shard_len, blocks, taps2, vecs2, up2, bias2, down2, ups_four, vecs1, head, last, lines, held
):
    shift = rest_start() * LANES
    collect(devices, shard_len, blocks, lines, rest_start(), rest_end())
    for out in (vecs1, vecs2, bias2, last):
        out[...] = jnp.zeros(out.shape, f32)
    read_taps(lines, shift, TAPS2, held, taps2, C2)
    read_row(lines, shift, GAIN2, vecs2, 0)
    read_row(lines, shift, SHIFT2, vecs2, 1)
    read_row(lines, shift, DOWNB2, vecs2, 2)
    read_row(lines, shift, UPB2, bias2, 0)
    read_row(lines, shift, UPSB, vecs1, 0)
    read_row(lines, shift, HEADB, last, 0)
    read_matrix(lines, shift, UP2, held, up2)
    read_matrix(lines, shift, DOWN2, held, down2)
    read_matrix(lines, shift, HEAD, held, head)
    tiles = C2 // LANES

    def put(first, stride, count, tile, value):
        k = first % 4
        held[pl.ds((k * tiles + tile) * C1 + first // 4, count, stride=stride // 4), :] = value

    rows, length = shapes_of()[UPS]
    read_rows(lines, offsets()[UPS] - shift, rows, length, put)
    for k in range(4):
        for m in range(tiles):
            at = (k * tiles + m) * C1
            held[at + WIDTH : at + C1, :] = jnp.zeros((C1 - WIDTH, LANES), f32)
            ups_four[k, :, m * LANES : (m + 1) * LANES] = held[at : at + C1, :].astype(bf16)


FRONT = 16


def hold_matrix(held, values, row_tiles, rows):
    tall = rows + 2 * FRONT
    zero = jnp.zeros((FRONT, LANES), f32)
    for m in range(row_tiles):
        at = m * tall
        held[at : at + FRONT, :] = zero
        held[at + FRONT : at + FRONT + rows, :] = values(m)
        held[at + FRONT + rows : at + tall, :] = zero


def write_matrix(lines, shift, piece, held, source):
    rows, length = shapes_of()[piece]
    tall = rows + 2 * FRONT
    hold_matrix(held, lambda m: source[:rows, m * LANES : (m + 1) * LANES], -(-length // LANES), rows)

    def get(first, stride, count, tile):
        return held[pl.ds(tile * tall + FRONT + first, count, stride=stride), :]

    write_rows(lines, offsets()[piece] - shift, rows, length, get)


def write_row(lines, shift, piece, get):
    write_vector(lines, offsets()[piece] - shift, shapes_of()[piece][0], get)


def row_of(source, row):
    return lambda m: source[row : row + 1, m * LANES : (m + 1) * LANES]


def norm_row(got, sums, width):
    _, inverse, _, _ = norm_rows(got, width)
    value = sums[1:2, :] * inverse
    return lambda m: value[:, m * LANES : (m + 1) * LANES]


def scatter_out(devices, shard_len, plane_size, planes, place, lines, low, keep, send):
    firsts, tall = shard_places(devices, shard_len)
    half = plane_size // 2
    for k, plane in enumerate(planes):
        for r in range(plane_size):
            first = firsts[plane * plane_size + r] - low
            start, end = max(first, 0), min(first + tall, lines.shape[0])
            seat = seat_of(place, r, plane_size)

            def put(out, index, kind):
                if end <= start:
                    out[index] = jnp.zeros((tall, LANES), kind)
                    return
                if start > first:
                    out[index, : start - first] = jnp.zeros((start - first, LANES), kind)
                out[index, start - first : end - first] = lines[start:end, :].astype(kind)
                if end < first + tall:
                    out[index, end - first :] = jnp.zeros((first + tall - end, LANES), kind)

            @pl.when(seat < half)
            def _():
                put(keep, seat * len(planes) + k, f32)

            @pl.when(seat >= half)
            def _():
                put(send, (seat - half) * len(planes) + k, bf16)


def span(first, last):
    end = offsets()[last] + math.prod(shapes_of()[last])
    return offsets()[first] // 2048 * 16, -(-end // 2048) * 16


def clear_ends(lines, low, first, last):
    start = offsets()[first] // LANES - low + 1
    lines[:start, :] = jnp.zeros((start, LANES), f32)
    end = -(-(offsets()[last] + math.prod(shapes_of()[last])) // LANES) - low
    if end < lines.shape[0]:
        lines[end:, :] = jnp.zeros((lines.shape[0] - end, LANES), f32)


def late_flat_kernel(
    devices, shard_len, plane_size, planes, place, sums2, hidden2, da, normal, dv, gated, du, top, dy, skip, keep, send, *scratch
):
    rooms, (lines, held, g_up2, g_down2, g_ups, g_head, sems) = scratch[:8], scratch[8:]
    copies = fetch((da, normal, dv, gated, du, top, dy, skip), rooms, sems)
    da, normal, dv, gated, du, top, dy, skip = rooms
    start(copies[6:])
    start(copies[4:6])
    wait(copies[6:])
    start(copies[:2])
    g_head[...] = tn(dy[...], skip[...])
    wait(copies[4:6])
    start(copies[2:4])
    for k in range(4):
        g_ups[k] = tn(du[k], top[...])
    wait(copies[:2])
    g_up2[...] = tn(da[...], normal[...])
    wait(copies[2:4])
    g_down2[...] = tn(dv[...], gated[...])
    low, _ = span(UP2, HEADB)
    shift = low * LANES
    clear_ends(lines, low, UP2, HEADB)
    write_matrix(lines, shift, UP2, held, g_up2)
    write_row(lines, shift, UPB2, row_of(hidden2, 0))
    write_matrix(lines, shift, DOWN2, held, g_down2)
    write_row(lines, shift, DOWNB2, row_of(sums2, 2))
    rows, length = shapes_of()[UPS]
    tiles = C2 // LANES
    tall = WIDTH + 2 * FRONT
    for k in range(4):
        for m in range(tiles):
            at = (k * tiles + m) * tall
            held[at : at + FRONT, :] = jnp.zeros((FRONT, LANES), f32)
            held[at + FRONT : at + FRONT + WIDTH, :] = g_ups[k, :WIDTH, m * LANES : (m + 1) * LANES]
            held[at + FRONT + WIDTH : at + tall, :] = jnp.zeros((FRONT, LANES), f32)

    def get(first, stride, count, tile):
        at = ((first % 4) * tiles + tile) * tall + FRONT + first // 4
        return held[pl.ds(at, count, stride=stride // 4), :]

    write_rows(lines, offsets()[UPS] - shift, rows, length, get)
    write_row(lines, shift, UPSB, row_of(sums2, 3))
    write_matrix(lines, shift, HEAD, held, g_head)
    write_row(lines, shift, HEADB, row_of(sums2, 4))
    scatter_out(devices, shard_len, plane_size, planes, place[0], lines, low, keep, send)


def early_flat_kernel(
    devices, shard_len, plane_size, planes, place, got2, sums1, hidden1, sums_low, g_taps2, more_taps2, sums2,
    da, normal, dv, gated, dcells, patches, keep, send, *scratch,
):
    rooms, (lines, held, g_up1, g_down1, g_downs, sems) = scratch[:6], scratch[6:]
    copies = fetch((da, normal, dv, gated, dcells, patches), rooms, sems)
    da, normal, dv, gated, dcells, patches = rooms
    start(copies[4:])
    start(copies[2:4])
    wait(copies[4:])
    start(copies[:2])
    g_downs[...] = tn(dcells[...], patches[...])
    wait(copies[2:4])
    g_down1[...] = tn(dv[...], gated[...])
    wait(copies[:2])
    g_up1[...] = tn(da[...], normal[...])
    low, _ = span(UP1, SHIFT2)
    shift = low * LANES
    clear_ends(lines, low, UP1, SHIFT2)
    write_matrix(lines, shift, UP1, held, g_up1)
    write_row(lines, shift, UPB1, row_of(hidden1, 0))
    write_matrix(lines, shift, DOWN1, held, g_down1)
    write_row(lines, shift, DOWNB1, row_of(sums1, 2))
    write_matrix(lines, shift, DOWNS, held, g_downs)
    write_row(lines, shift, DOWNSB, row_of(sums_low, 0))
    across = jnp.concatenate([g_taps2[...], more_taps2[...]], axis=1)
    across = jnp.concatenate([across, jnp.zeros((LANES - across.shape[0], C2), f32)], axis=0).T
    held[:C2, :] = across
    write_short(lines, offsets()[TAPS2] - shift, WIDTH2, TAPS, lambda r: held[r : r + 1, :])
    write_row(lines, shift, GAIN2, norm_row(got2, sums2, C2))
    write_row(lines, shift, SHIFT2, row_of(sums2, 0))
    scatter_out(devices, shard_len, plane_size, planes, place[0], lines, low, keep, send)


def group_taps():
    table = []
    for first in (0, 3):
        for p in range(KSIZE):
            table.append([p * KSIZE + first + t for t in range(3)])
    for k in range(3):
        table.append([(3 * k + t) * KSIZE + 6 if 3 * k + t < KSIZE else -1 for t in range(3)])
    return table


def quarter_lanes():
    at = np.arange(C1)[None, :, None] * 4 + np.arange(4)[:, None, None]
    hot = (at == np.arange(H1)[None, None, :]) & (np.arange(C1) < WIDTH)[None, :, None]
    return hot.astype(jnp.bfloat16)


def tap_lanes():
    table = np.array([line + [-1] for line in group_taps()])
    wanted = table[:, np.arange(C1) // CIN]
    return (wanted[:, :, None] == np.arange(LANES)).astype(jnp.bfloat16)


def body(fields, targets, ocean_depth, thickness_class, params, moment1, moment2):
    shard_len = params.shape[0]
    devices = lax.axis_size(AXES)
    plane_size = 2 * lax.axis_size("lvl")
    me = lax.axis_index(AXES)
    _, tall = shard_places(devices, shard_len)
    at = (me * (shard_len % 2048)) % 2048
    place_row = jnp.broadcast_to(me % plane_size, (1,)).astype(jnp.int32)

    smem = pl.BlockSpec(memory_space=pltpu.SMEM)
    vmem = pl.BlockSpec(memory_space=pltpu.VMEM)
    parts = lax.axis_size("lvl")
    chans, batch, all_rows, all_cols = fields.shape
    bands = BLOCKS // batch
    rows, cols = all_rows // bands, all_cols // parts
    half_rows, half_cols = rows // 2, cols // 2
    cells, low_cells = rows * cols * 8, half_rows * half_cols * 8
    wide_cols = cols + 2 * REACH
    low_border = (half_rows + 2 * REACH) * (half_cols + 2 * REACH) * 8

    def packed(values, reach):
        lanes = rows * (cols + 2 * reach)
        return call(
            lambda *refs: pack_kernel(parts, cols, reach, *refs),
            [((parts, chans * BLOCKS, lanes), bf16)],
            scratch=[
                pltpu.VMEM((-(-all_cols // LANES), chans * batch * all_rows, LANES), f32),
                pltpu.VMEM((parts, chans * BLOCKS, lanes), f32),
            ],
            micros=3,
            name="pack",
        )(values.reshape(-1, all_cols))[0]

    copies, placed = tie(packed(fields, REACH), params)
    field_given = lax.all_to_all(copies, "lvl", 0, 0, tiled=True)
    goal_copies = packed(targets, 0)
    block = lax.dynamic_update_slice(jnp.zeros((tall * LANES,), bf16), placed.astype(bf16), (at,))
    block = block.reshape(tall, LANES)
    gathered = lax.all_gather(block, AXES, axis=0)
    near_shards = 1
    while near_shards < -(-first_end() * LANES // shard_len):
        near_shards *= 2
    chunk_lines = -(-span(STEM, SHIFT1)[1] // (8 * devices)) * 8
    head_lines = chunk_lines * devices
    window = jnp.pad(block, ((head_lines, head_lines), (0, 0)))
    first_line = me * shard_len // 2048 * 16
    window = lax.dynamic_slice_in_dim(window, head_lines - jnp.minimum(first_line, head_lines), head_lines)
    field_given, (window, goal_copies) = tie(field_given, (window, goal_copies))
    chunk = jnp.sum(swap(window.reshape(devices, chunk_lines, LANES)).astype(f32), axis=0).astype(bf16)
    send_room = 2 * REACH * -(-wide_cols // 8) * 8
    field_cells, lower, upper = call(
        lambda *refs: fields_kernel(parts, rows, cols, *refs),
        [((rows * wide_cols * 8, LANES), f32), ((send_room, LANES), bf16), ((send_room, LANES), bf16)],
        scratch=[pltpu.VMEM((send_room, LANES), f32), pltpu.VMEM((parts, rows * wide_cols, chans * BLOCKS), bf16)],
        micros=4,
        name="fields",
    )(field_given)
    chunk, (field_cells, lower, upper) = tie(chunk, (field_cells, lower, upper))
    above, below = lines_out(lower, upper)
    stem_lines = swap(jnp.broadcast_to(chunk[None], (devices,) + chunk.shape)).reshape(head_lines, LANES)
    stem_lines, (above, below, goal_copies) = tie(stem_lines, (above, below, goal_copies))
    goal_given = lax.all_to_all(goal_copies, "lvl", 0, 0, tiled=True)

    deep = depth_cells(ocean_depth, batch)
    depth_rows = jnp.broadcast_to(deep.astype(f32)[..., None], deep.shape + (LANES,)).reshape(cells, LANES)
    low = jnp.max(deep.reshape(half_rows, 2, half_cols, 2, 8), axis=(1, 3))
    low_rows = jnp.broadcast_to(low.astype(f32)[..., None], low.shape + (LANES,)).reshape(low_cells, LANES)
    channel = jnp.arange(CI, dtype=jnp.int32)
    level = jnp.where(channel < 4 * LEVELS, channel // 4, 0)
    level_row = jnp.where(channel < CIN, level, LEVELS + 1).astype(f32)
    thickf = thickness_class.astype(f32)
    onehot = (level[:, None] == jnp.arange(LEVELS, dtype=jnp.int32)[None, :]).astype(f32)
    chosen = ((channel % 4 == 0) & (channel < 4 * LEVELS)).astype(f32)
    heat_take = chosen * jnp.sum(onehot * thickf[None, :], axis=1) / jnp.sum(thickf)
    ocean_cells = jnp.sum((level_row[None, None, :] < ocean_depth.astype(f32)[:, :, None]).astype(f32))
    ocean_cells = batch * ocean_cells
    surface_cells = jnp.sum((deep > 0).astype(f32))
    low_surface = jnp.sum((low > 0).astype(f32))
    index8 = jnp.arange(8)[:, None]
    lane8 = jnp.arange(LANES)[None, :]

    def counts_of(width, cells_count):
        (r, c), (ro, co) = count_places(width)
        at_cells = (index8 == r) & (lane8 == c)
        at_ocean = (index8 == ro) & (lane8 == co)
        return jnp.where(at_cells, cells_count, jnp.where(at_ocean, ocean_cells, 0.0))

    counts1 = counts_of(C1, surface_cells)
    counts2 = counts_of(C2, low_surface)

    tables = jnp.pad(jnp.stack([level_row, heat_take]), ((0, 6), (0, 0)))
    perm, pick = jnp.asarray(quarter_lanes()), jnp.asarray(tap_lanes())
    held_room = pltpu.VMEM((4 * H2, LANES), f32)
    stem_in, near1, vecs1 = call(
        stem_params_kernel,
        [((C1, CI), bf16), ((C1, LANES), bf16), ((8, C1), f32)],
        scratch=[pltpu.VMEM(stem_lines.shape, f32), pltpu.VMEM((2 * C1, LANES), f32)],
        micros=3,
        name="stem_params",
    )(stem_lines)

    smalls = (perm, low_rows, counts1, counts2, tables, place_row, depth_rows, pick)
    field_cells, smalls = tie(field_cells, smalls)
    perm, low_rows, counts1, counts2, tables, place_row, depth_rows, pick = smalls

    ends_room = pltpu.VMEM((2 * REACH * wide_cols * 8, LANES), f32)
    shifted_room = pltpu.VMEM(((rows + 2 * REACH) * cols * 8, C1), bf16)
    hzero, conv1, stats1 = call(
        lambda *refs: stem_kernel(rows, cols, *refs),
        [((cells, C1), bf16), ((cells, C1), f32), ((devices, 8, LANES), f32)],
        grid=(half_rows,),
        ins=[
            whole(rows * wide_cols * 8, LANES), whole(send_room, LANES), whole(send_room, LANES), whole(C1, LANES), whole(C1, CI),
            whole(GROUPS, C1, LANES), band(2 * cols * 8, LANES), whole(8, LANES),
        ],
        out_specs=[band(2 * cols * 8, C1), band(2 * cols * 8, C1), whole(devices, 8, LANES)],
        scratch=[
            pltpu.VMEM((GROUPS * C1, C1), bf16), pltpu.VMEM((C1, C1), bf16), pltpu.VMEM((8, C1), f32),
            ends_room, shifted_room, shifted_room, shifted_room,
        ],
        micros=17,
        name="stem_conv",
    )(field_cells, above, below, near1, stem_in, pick, depth_rows, counts1)
    got1 = swap(stats1)
    hzero, goal_given = tie(hzero, goal_given)
    up_in1, bias_in1, down_in1, downs_in, downs_four, down_rows, bias_rows = call(
        lambda *refs: fine_params_kernel(devices, shard_len, *refs),
        [
            ((H1, C1), bf16), ((1, H1), f32), ((C1, H1), bf16), ((C2, H1), bf16), ((4, C2, C1), bf16), ((8, C2), f32),
            ((8, C1), f32),
        ],
        grid=(1,),
        ins=[whole(near_shards, tall, LANES), whole(4, C1, H1)],
        out_specs=[
            whole(H1, C1), whole(1, H1), whole(C1, H1), whole(C2, H1), whole(4, C2, C1), whole(8, C2), whole(8, C1),
        ],
        scratch=[pltpu.VMEM((span(UP1, DOWNSB)[1] - span(UP1, DOWNSB)[0], LANES), f32), held_room],
        micros=8,
        name="fine_params",
    )(gathered, perm)
    chunk, low_chunk = 2 * cols * 8, half_cols * 8
    hone, gated1, slope1, patches, coarse = call(
        lambda *refs: fine_kernel(cols, *refs),
        [
            ((cells, C1), bf16),
            ((cells, H1), bf16),
            ((cells, H1), bf16),
            ((low_cells, H1), bf16),
            ((low_cells, C2), bf16),
        ],
        grid=(half_rows,),
        ins=[
            whole(devices, 8, LANES), band(chunk, C1), band(chunk, C1), whole(8, C1), whole(8, C1), whole(H1, C1), whole(1, H1),
            whole(C1, H1), whole(4, C1, H1), whole(C2, H1), whole(8, C2),
        ],
        out_specs=[
            band(chunk, C1), band(chunk, H1), band(chunk, H1), band(low_chunk, H1), band(low_chunk, C2),
        ],
        scratch=[pltpu.VMEM((chunk, C1), f32)],
        micros=15,
        name="fine_forward",
    )(got1, conv1, hzero, vecs1, bias_rows, up_in1, bias_in1, down_in1, perm, downs_in, down_rows)

    edge = edge_lines(half_cols)
    side = half_rows * REACH * 8

    def edges(values, left, right):
        return call(
            lambda *refs: edge_kernel(half_rows, half_cols, 1, *refs),
            [((edge, C2), bf16)] * 2,
            scratch=[pltpu.VMEM((low_cells + 2 * side, LANES), f32), pltpu.VMEM((edge, LANES), f32)],
            micros=3,
            name="edge",
        )(values, left, right)

    def border_tiles(tile):
        return [tile(low_cells), tile(side), tile(side), tile(edge), tile(edge)]

    sides = columns_out((coarse,), half_rows, half_cols)[0]
    goal_given, coarse = tie(goal_given, coarse)
    goal = call(
        lambda *refs: targets_kernel(parts, 0, *refs),
        [((cells, LANES), bf16)],
        scratch=[pltpu.VMEM((cells, LANES), f32), pltpu.VMEM((parts, rows * cols, chans * BLOCKS), bf16)],
        micros=4,
        name="targets",
    )(goal_given)[0]
    sides, goal = tie(sides, goal)
    border2 = (coarse, *sides, *lines_out(*edges(coarse, *sides)))
    taps_in2, vecs2, up_in2, bias_in2, down_in2, ups_four, fine_rows, head_in, last_rows = call(
        lambda *refs: rest_params_kernel(devices, shard_len, *refs),
        [
            ((TAPS, 8, C2), f32), ((8, C2), f32), ((H2, C2), bf16), ((1, H2), f32), ((C2, H2), bf16),
            ((4, C1, C2), bf16), ((8, C1), f32), ((CI, C1), bf16), ((8, CI), f32),
        ],
        ins=[vmem],
        scratch=[pltpu.VMEM((rest_end() - rest_start(), LANES), f32), held_room],
        micros=13,
        name="rest_params",
    )(gathered)
    conv2, stats2 = call(
        lambda *refs: coarse_conv_kernel(half_rows, half_cols, *refs),
        [((low_cells, C2), f32), ((devices, 8, LANES), f32)],
        grid=(C2 // LANES,),
        ins=border_tiles(lane_tile) + [TAP_TILE, whole(low_cells, LANES), whole(8, LANES)],
        out_specs=[lane_tile(low_cells), whole(devices, 8, LANES)],
        scratch=[pltpu.VMEM((low_border, LANES), f32), pltpu.VMEM((edge, LANES), f32), pltpu.VMEM((8, LANES), f32)],
        micros=11,
        name="coarse_conv",
    )(*border2, taps_in2, low_rows, counts2)
    got2 = swap(stats2)
    field_cells, stats2 = tie(field_cells, stats2)
    turned = call(
        lambda *refs: turn_kernel(rows, cols, *refs),
        [((KSIZE * CIN, (rows + 2 * REACH) * cols * 8), bf16)],
        scratch=[ends_room],
        micros=8,
        name="turn",
    )(field_cells, above, below)[0]
    conv2, turned = tie(conv2, turned)
    (
        skip, top, dy, ds, du, dtop, dv2, gated2, da2, normal2, dx2, sums2, hidden2, copies2,
    ) = call(
        lambda *refs: middle_kernel(cols, *refs),
        [
            ((cells, C1), bf16), ((low_cells, C2), bf16), ((cells, CI), bf16), ((cells, C1), f32),
            ((4, low_cells, C1), bf16), ((low_cells, C2), f32), ((low_cells, C2), bf16), ((low_cells, H2), bf16),
            ((low_cells, H2), bf16), ((low_cells, C2), bf16), ((low_cells, C2), f32),
            ((8, C2), f32), ((8, H2), f32), ((devices, 8, LANES), f32),
        ],
        grid=(half_rows,),
        ins=[
            whole(devices, 8, LANES), band(low_chunk, C2), band(low_chunk, C2), whole(8, C2), whole(H2, C2), whole(1, H2),
            whole(C2, H2), whole(4, C1, C2), whole(8, C1), whole(CI, C1), whole(8, CI), whole(8, CI), band(chunk, C1),
            band(chunk, CI), band(chunk, LANES),
        ],
        out_specs=[
            band(chunk, C1), band(low_chunk, C2), band(chunk, CI), band(chunk, C1),
            pl.BlockSpec((4, low_chunk, C1), lambda i: (0, i, 0)), band(low_chunk, C2), band(low_chunk, C2),
            band(low_chunk, H2), band(low_chunk, H2), band(low_chunk, C2), band(low_chunk, C2),
            whole(8, C2), whole(8, H2), whole(devices, 8, LANES),
        ],
        micros=20,
        name="middle",
    )(
        got2, conv2, coarse, vecs2, up_in2, bias_in2, down_in2, ups_four, fine_rows, head_in, last_rows, tables, hone, goal,
        depth_rows,
    )
    back2 = swap(copies2)
    late_planes = planes_of(devices, shard_len, *span(UP2, HEADB), plane_size)
    half_seats = plane_size // 2

    def sums_out(planes):
        return [((half_seats * len(planes), tall, LANES), kind) for kind in (f32, bf16)]

    late_args = (da2, normal2, dv2, gated2, du, top, dy, skip)
    hbm = pl.BlockSpec(memory_space=pltpu.HBM)
    late_keep, late_send = call(
        lambda *refs: late_flat_kernel(devices, shard_len, plane_size, late_planes, *refs),
        sums_out(late_planes),
        ins=[smem, vmem, vmem] + [hbm] * 8,
        scratch=[
            *[pltpu.VMEM(value.shape, bf16) for value in late_args],
            pltpu.VMEM((span(UP2, HEADB)[1] - span(UP2, HEADB)[0], LANES), f32), held_room,
            pltpu.VMEM((H2, C2), f32), pltpu.VMEM((C2, H2), f32), pltpu.VMEM((4, C1, C2), f32), pltpu.VMEM((CI, C1), f32),
            pltpu.SemaphoreType.DMA((8,)),
        ],
        micros=10,
        name="late_flat",
    )(place_row, sums2, hidden2, *late_args)
    back2, late_keep = tie(back2, late_keep)
    slope2 = call(
        coarse_slope_kernel,
        [((low_cells, C2), bf16)],
        micros=2,
        name="coarse_slope",
    )(got2, back2, vecs2, dx2, conv2, low_rows)[0]

    def taps_back(values, start, count):
        def tile(rows):
            return pl.BlockSpec((rows, LANES), lambda i: (0, i + start))

        return call(
            lambda *refs: coarse_taps_kernel(half_rows, half_cols, *refs),
            [((56, count * LANES), f32)],
            grid=(count,),
            ins=border_tiles(tile) + [tile(low_cells)],
            out_specs=[lane_tile(56)],
            scratch=[
                pltpu.VMEM((low_border, LANES), f32), pltpu.VMEM((edge, LANES), f32), pltpu.VMEM((low_cells, LANES), f32),
            ],
            micros=5,
            name="coarse_taps",
        )(*border2, values)[0]

    split = C2 // LANES // 2
    sides = columns_out((slope2,), half_rows, half_cols)[0]
    g_first = taps_back(slope2, 0, split)
    sides, g_first = tie(sides, g_first)
    lower, upper = edges(slope2, *sides)
    ends = lines_out(lower, upper)
    slope2, lower = tie(slope2, lower)
    g_second = taps_back(slope2, split, C2 // LANES - split)
    ends, g_second = tie(ends, g_second)
    dcells = call(
        lambda *refs: coarse_conv_back_kernel(half_rows, half_cols, *refs),
        [((low_cells, C2), bf16)],
        grid=(C2 // LANES,),
        ins=border_tiles(lane_tile) + [TAP_TILE, lane_tile(low_cells)],
        out_specs=[lane_tile(low_cells)],
        scratch=[pltpu.VMEM((low_border, LANES), f32), pltpu.VMEM((edge, LANES), f32)],
        micros=9,
        name="coarse_conv_back",
    )(slope2, *sides, *ends, taps_in2, dtop)[0]

    state, late_steps = scatter_steps(late_keep, late_send, late_planes)
    for step in late_steps[:-1]:
        state = step(state)
    dcells, state = tie(dcells, state)
    dv1, da1, dn1, normal1, sums1, hidden1, sums_low, copies1 = call(
        lambda *refs: fine_back_kernel(cols, *refs),
        [
            ((cells, C1), bf16), ((cells, H1), bf16), ((cells, C1), bf16), ((cells, C1), bf16),
            ((8, C1), f32), ((8, H1), f32), ((8, C2), f32), ((devices, 8, LANES), f32),
        ],
        grid=(half_rows,),
        ins=[
            whole(devices, 8, LANES), band(low_chunk, C2), whole(4, C2, C1), band(chunk, C1), whole(8, C1),
            band(chunk, C1), band(chunk, H1), whole(H1, C1), whole(C1, H1),
        ],
        out_specs=[
            band(chunk, C1), band(chunk, H1), band(chunk, C1), band(chunk, C1), whole(8, C1), whole(8, H1), whole(8, C2),
            whole(devices, 8, LANES),
        ],
        micros=13,
        name="fine_backward",
    )(got1, dcells, downs_four, ds, vecs1, conv1, slope1, up_in1, down_in1)
    da1, state = tie(da1, late_steps[-1](state))
    back1 = swap(copies1)
    early_planes = planes_of(devices, shard_len, *span(UP1, SHIFT2), plane_size)
    early_args = (da1, normal1, dv1, gated1, dcells, patches)
    early_keep, early_send = call(
        lambda *refs: early_flat_kernel(devices, shard_len, plane_size, early_planes, *refs),
        sums_out(early_planes),
        ins=[smem] + [vmem] * 7 + [hbm] * 6,
        scratch=[
            *[pltpu.VMEM(value.shape, bf16) for value in early_args],
            pltpu.VMEM((span(UP1, SHIFT2)[1] - span(UP1, SHIFT2)[0], LANES), f32), held_room,
            pltpu.VMEM((H1, C1), f32), pltpu.VMEM((C1, H1), f32), pltpu.VMEM((C2, H1), f32),
            pltpu.SemaphoreType.DMA((6,)),
        ],
        micros=8,
        name="early_flat",
    )(place_row, got2, sums1, hidden1, sums_low, g_first, g_second, sums2, *early_args)
    early_send, back1 = tie(early_send, back1)
    early_state, early_steps = scatter_steps(early_keep, early_send, early_planes)
    tail_used = -(-span(STEM, SHIFT1)[1] // devices)
    tail_lines = -(-(tail_used + 1) // 8) * 8
    for step in early_steps[:-1]:
        early_state = step(early_state)
    conv1, early_state = tie(conv1, early_state)
    back_args = (conv1, dn1, depth_rows, dv1, turned)
    tail = call(
        lambda *refs: stem_back_kernel(rows, cols, *refs),
        [((devices, tail_lines, LANES), f32)],
        ins=[vmem] * 6 + [hbm] * 5,
        scratch=[
            *[pltpu.VMEM(value.shape, value.dtype) for value in back_args],
            pltpu.VMEM((cells, C1), bf16), pltpu.VMEM((KSIZE * CIN, C1), f32), pltpu.VMEM((LANES, C1), f32),
            pltpu.VMEM((CIN, C1), f32), pltpu.VMEM((devices * tail_used, LANES), f32), pltpu.VMEM((C1, LANES), f32),
            pltpu.SemaphoreType.DMA((5,)),
        ],
        micros=14,
        name="stem_back",
    )(got1, back1, vecs1, near1, stem_in, sums1, *back_args)[0]
    tail, early_state = tie(tail, early_steps[-1](early_state))

    chunk_sum = jnp.sum(swap(tail), axis=0)
    summed = scatter_planes(scatter_last(merge_planes([(state, late_planes), (early_state, early_planes)])))
    mine = lax.dynamic_slice_in_dim(summed.reshape(-1), at, shard_len)
    squares = jnp.sum(mine * mine) + jnp.sum(chunk_sum * chunk_sum)
    loss_part = jnp.sum(sums2[5, :LANES])
    lane = lax.broadcasted_iota(jnp.int32, chunk_sum.shape, 1)
    line = lax.broadcasted_iota(jnp.int32, chunk_sum.shape, 0)
    totals = jnp.where(lane == 0, loss_part, jnp.where(lane == 1, squares, 0.0))
    last = jnp.where(line == tail_used, totals, chunk_sum)
    last = swap(jnp.broadcast_to(last[None], (devices,) + last.shape))
    tail_flat = last[:, :tail_used].reshape(devices * tail_used, LANES)
    totals = jnp.sum(last[:, tail_used, :2], axis=0)
    loss_total, norm = totals[0], jnp.sqrt(totals[1])
    row, lane = count_places(C1)[1]
    count = jnp.sum(got1[:, row, lane])
    tail_flat = jnp.pad(tail_flat, ((0, tall), (0, 0)))
    line = jnp.minimum(me * shard_len // 2048 * 16, devices * tail_used)
    mine_tail = lax.dynamic_slice_in_dim(tail_flat, line, tall).reshape(-1)
    mine = mine + lax.dynamic_slice_in_dim(mine_tail, at, shard_len)
    clipped = mine * jnp.minimum(1.0, CLIP / norm)
    first = BETA_ONE * moment1 + (1.0 - BETA_ONE) * clipped
    second = BETA_TWO * moment2 + (1.0 - BETA_TWO) * clipped * clipped
    ratio = first / (1.0 - BETA_ONE**STEP) / (jnp.sqrt(second / (1.0 - BETA_TWO**STEP)) + ADAM_EPS)
    updated = params - LRATE * (ratio + DECAY * params)
    return (loss_total, count, norm, updated, first, second)


def solution(mesh):
    in_specs = (
        P("lvl", None, "lat", None),
        P("lvl", None, "lat", None),
        P("lat", "lvl"),
        P(),
        P(("lat", "lvl")),
        P(("lat", "lvl")),
        P(("lat", "lvl")),
    )
    out_specs = (P(), P(), P(), P(("lat", "lvl")), P(("lat", "lvl")), P(("lat", "lvl")))
    return jax.shard_map(body, mesh=mesh, in_specs=in_specs, out_specs=out_specs, check_vma=False)
```

```python
import math

import jax
import jax.numpy as jnp
import numpy as np
from jax import lax
from jax.experimental import pallas as pl
from jax.experimental.pallas import tpu as pltpu
from jax.sharding import PartitionSpec as P

CIN = 80
WIDTH = 200
EXPAND = 800
WIDTH2 = 400
EXPAND2 = 1600
KSIZE = 7
TAPS = KSIZE * KSIZE
LEVELS = 19
STEP = 10

CLIP = 0.01
LRATE = 0.05
BETA_ONE = 0.9
BETA_TWO = 0.999
ADAM_EPS = 1e-08
DECAY = 0.1
HEAT_WEIGHT = 40.0
NORM_EPS = 1e-05

AXES = ("lat", "lvl")

CI = 128
C1 = 256
H1 = 896
C2 = 512
H2 = 1664
BLOCKS = 8
LANES = 128
REACH = KSIZE // 2
GROUPS = 17

f32 = jnp.float32
bf16 = jnp.bfloat16
VMEM_LIMIT = 60 * 1024 * 1024


def plane_bits():
    bits = []
    for axis in AXES:
        count = lax.axis_size(axis)
        step = count // 2
        while step >= 1:
            bits.append((axis, count, step))
            step //= 2
    across = [b for b in bits if b[0] == "lat" and b[2] > 1]
    within = [b for b in bits if b not in across]
    return across, within


def exchange(values, axis, count, step):
    return lax.ppermute(values, axis, [(i, i ^ step) for i in range(count)])


def half_rows_of(tall):
    return -(-tall // 32) * 16


def scatter_steps(keep, send, planes):
    _, (first, second, *others) = plane_bits()
    cut = half_rows_of(keep.shape[1])

    def inner(turn, bit):
        def step(state):
            keep, send = state
            if turn > 0:
                half = keep.shape[0] // 2
                keep, send = keep[:half], keep[half:].astype(bf16)
            keep = keep + exchange(send, *bit).astype(f32)
            return keep, None

        return step

    def outer(state):
        keep, _ = state
        parts = keep.reshape((2, 2, len(planes)) + keep.shape[1:])
        left, right = parts[:, :, :, :cut], parts[:, :, :, cut:]
        left = left[0] + exchange(left[1].astype(bf16), *second).astype(f32)
        right = right[:, 0] + exchange(right[:, 1].astype(bf16), *first).astype(f32)
        return left, right

    steps = [inner(turn, bit) for turn, bit in enumerate(reversed(others))]
    return (keep, send), steps + [outer]


def merge_planes(groups):
    total = lax.axis_size("lat") // 2
    merged = []
    for side in range(2):
        rows = []
        for p in range(total):
            held = [state[side][:, planes.index(p)] for state, planes in groups if p in planes]
            rows.append(sum(held[1:], held[0]))
        merged.append(jnp.stack(rows, axis=1))
    return merged


def scatter_last(state):
    _, (first, second, *_) = plane_bits()
    left, right = state
    left = left[0] + exchange(left[1].astype(bf16), *first).astype(f32)
    right = right[0] + exchange(right[1].astype(bf16), *second).astype(f32)
    return jnp.concatenate([left, right], axis=1)


def tie(first, second):
    return lax.optimization_barrier((first, second))


def scatter_planes(rows):
    count = lax.axis_size("lat")
    plane = lax.axis_index("lat") // 2
    mine = lax.dynamic_index_in_dim(rows, plane, 0, False)
    parts = [
        exchange(lax.dynamic_index_in_dim(rows, plane ^ away, 0, False).astype(bf16), "lat", count, 2 * away)
        for away in range(1, count // 2)
    ]
    for part in parts:
        mine = mine + part.astype(f32)
    return mine


def swap(copies):
    return lax.all_to_all(copies, AXES, 0, 0, tiled=True)


def neighbours(axis):
    ends = lax.axis_size(axis) - 1
    return [(i, i + 1) for i in range(ends)], [(i + 1, i) for i in range(ends)]


def columns_out(arrays, rows, cols):
    onward, back = neighbours("lvl")
    sides = []
    for start, pairs in ((cols - REACH, onward), (0, back)):
        own = [values.reshape(rows, cols, 8, -1)[:, start : start + REACH] for values in arrays]
        own = jnp.concatenate([part.reshape(rows * REACH * 8, -1) for part in own], axis=0)
        sides.append(lax.ppermute(own, "lvl", pairs))
    size = rows * REACH * 8
    return [[side[k * size : (k + 1) * size] for side in sides] for k in range(len(arrays))]


def lines_out(lower, upper):
    onward, back = neighbours("lat")
    return lax.ppermute(lower, "lat", onward), lax.ppermute(upper, "lat", back)


def depth_cells(depth, batch):
    rows, cols = depth.shape
    bands = BLOCKS // batch
    split = depth.reshape(bands, rows // bands, cols).transpose(1, 2, 0)
    return jnp.concatenate([split] * batch, axis=2)


def block_shapes(chans, hidden):
    return [
        (chans, TAPS),
        (chans,),
        (chans,),
        (hidden, chans),
        (hidden,),
        (chans, hidden),
        (chans,),
    ]


def shapes_of():
    return (
        [(WIDTH, CIN)]
        + block_shapes(WIDTH, EXPAND)
        + [(WIDTH2, 4 * WIDTH), (WIDTH2,)]
        + block_shapes(WIDTH2, EXPAND2)
        + [(4 * WIDTH, WIDTH2), (WIDTH,), (CIN, WIDTH), (CIN,)]
    )


def fill(values, *shape):
    return jnp.pad(values, [(0, n - m) for n, m in zip(shape, values.shape)])


def nt(left, right):
    return lax.dot_general(left, right, (((1,), (1,)), ((), ())), preferred_element_type=f32)


def nn(left, right):
    return lax.dot_general(left, right, (((1,), (0,)), ((), ())), preferred_element_type=f32)


def tn(left, right):
    return lax.dot_general(left, right, (((0,), (0,)), ((), ())), preferred_element_type=f32)


def rows8(start, amount):
    return pl.ds(pl.multiple_of(start * 8, 8), amount * 8)


def convolve(source, taps, rows, cols, emit, carry, flip=False):
    width = cols + 2 * REACH
    wide = 4

    def strip(turn, carry):
        col = turn * wide
        totals = [jnp.zeros((wide, 8, LANES), f32) for _ in range(rows)]
        for line in range(rows + 2 * REACH):
            seen = source[rows8(line * width + col, wide + 2 * REACH), :].reshape(wide + 2 * REACH, 8, LANES)
            for q in range(KSIZE):
                for row in range(max(0, line - 2 * REACH), min(rows, line + 1)):
                    tap = (line - row) * KSIZE + q
                    totals[row] = totals[row] + seen[q : q + wide] * taps[TAPS - 1 - tap if flip else tap][None]
        for row in range(rows):
            carry = emit(rows8(row * cols + col, wide), totals[row], carry)
        return carry

    return lax.fori_loop(0, cols // wide, strip, carry)


def row_sum(values):
    return jnp.sum(values, axis=0, keepdims=True)


def spread_rows(values, tiles):
    return [values[:, m * LANES : (m + 1) * LANES] for m in range(tiles)]


def stats_block(first, second, counts):
    tiles = first.shape[1] // LANES
    rows = spread_rows(first, tiles) + spread_rows(second, tiles)
    if len(rows) < 8:
        rows = rows + [jnp.zeros((8 - len(rows), LANES), f32)]
    block = jnp.concatenate(rows, axis=0)
    return block if counts is None else block + counts


def wide_row(total, start, tiles):
    return jnp.concatenate([total[start + m : start + m + 1] for m in range(tiles)], axis=1)


def count_places(width):
    if width == C1:
        return (4, 0), (5, 0)
    return (WIDTH2 // LANES, WIDTH2 % LANES), (WIDTH2 // LANES, WIDTH2 % LANES + 1)


def norm_rows(got, width):
    tiles = width // LANES
    total = jnp.sum(got[...], axis=0)
    (r, c), (ro, co) = count_places(width)
    cells, ocean = total[r : r + 1, c : c + 1], total[ro : ro + 1, co : co + 1]
    lane = lax.broadcasted_iota(jnp.int32, (1, width), 1)
    sums = jnp.where(lane < (WIDTH if width == C1 else WIDTH2), wide_row(total, 0, tiles), 0.0)
    mean = sums / cells
    inverse = lax.rsqrt(wide_row(total, tiles, tiles) / cells - mean * mean + NORM_EPS)
    return mean, inverse, cells, ocean


def gelu_pair(act):
    square = act * act
    flat = 0.7978845608028654
    cube = flat * 0.044715
    half = 0.5 + 0.5 * jnp.tanh(act * (flat + cube * square))
    value = act * half
    return value, half + value * (1.0 - half) * (2.0 * flat + (6.0 * cube) * square)


def quarter(values, rows, cols, p, q):
    chans = values.shape[-1]
    split = values.reshape(rows // 2, 2, cols // 2, 2, 8, chans)
    return split[:, p, :, q].reshape(rows * cols * 2, chans)


def from_quarters(parts, rows, cols):
    chans = parts[0].shape[-1]
    cells = [part.reshape(rows // 2, cols // 2, 8, chans) for part in parts]
    lines = [jnp.stack(cells[2 * p : 2 * p + 2], axis=2) for p in range(2)]
    return jnp.stack(lines, axis=1).reshape(rows * cols * 8, chans)


def call(kernel, outs, grid=(), ins=None, out_specs=None, scratch=(), micros=5, name=None):
    params = dict(out_shape=[jax.ShapeDtypeStruct(s, t) for s, t in outs])
    if ins:
        params.update(in_specs=ins)
    if grid:
        params.update(grid=grid, out_specs=out_specs)
    return pl.pallas_call(
        kernel,
        scratch_shapes=list(scratch),
        compiler_params=pltpu.CompilerParams(vmem_limit_bytes=VMEM_LIMIT),
        cost_estimate=pl.CostEstimate(flops=int(micros * 1.1e9), bytes_accessed=100000, transcendentals=0),
        name=name,
        **params,
    )


def whole(*shape):
    return pl.BlockSpec(shape, lambda i: (0,) * len(shape))


def band(rows, cols):
    return pl.BlockSpec((rows, cols), lambda i: (i, 0))


def lane_tile(rows):
    return pl.BlockSpec((rows, LANES), lambda i: (0, i))


def stats_tile(devices):
    return pl.BlockSpec((devices, 8, LANES), lambda i: (0, 0, i))


TAP_TILE = pl.BlockSpec((TAPS, 8, LANES), lambda i: (0, 0, i))


def conv_sums(source, taps, depth, counts, out, stats, rows, cols, block):
    def emit(place, total, carry):
        flat = total.reshape(-1, LANES)
        out[place, :] = flat
        ocean = depth[place, :] > 0.0
        kept = jnp.where(ocean, flat, 0.0)
        kept_cells = kept.reshape(-1, 8, LANES)
        return (carry[0] + jnp.sum(kept_cells, axis=0), carry[1] + jnp.sum(kept_cells * total, axis=0))

    zero = jnp.zeros((8, LANES), f32)
    first, second = convolve(source, taps, rows, cols, emit, (zero, zero))
    tile = pl.program_id(0)
    tiles = pl.num_programs(0)

    @pl.when(tile == 0)
    def _():
        block[...] = counts[...]

    block[pl.ds(tile, 1), :] += row_sum(first)
    block[pl.ds(C2 // LANES + tile, 1), :] += row_sum(second)

    @pl.when(tile == tiles - 1)
    def _():
        stats[...] = jnp.broadcast_to(block[...][None], stats.shape)


def lay_border(rows, cols, source, held, centre, left, right, above, below):
    width = cols + 2 * REACH
    sides = [left[...].astype(f32), right[...].astype(f32)]
    for row in range(rows):
        start = (row + REACH) * width
        source[rows8(start + REACH, cols), :] = centre[rows8(row * cols, cols), :].astype(f32)
        for side, place in zip(sides, (0, cols + REACH)):
            source[rows8(start + place, REACH), :] = side[row * REACH * 8 : (row + 1) * REACH * 8]
    for t in range(REACH):
        for start, target, way in ((rows + t, t, 1), (REACH + t, rows + REACH + t, 7)):
            line = source[rows8(start * width, width), :].reshape(width, 8, LANES)
            source[rows8(target * width, width), :] = pltpu.roll(line, way, 1).reshape(width * 8, LANES)
    amount = REACH * width
    for part, base in ((above, 0), (below, (rows + REACH) * width * 8 + BLOCKS // 2 - 1)):
        held[...] = part[...].astype(f32)
        for b in range(2):
            values = held[pl.ds(b, amount, stride=2), :]
            source[pl.ds(base + b * (BLOCKS // 2), amount, stride=8), :] = values


def pack_kernel(parts, cols, reach, values, out, tiles, flat):
    total = values.shape[1]
    width = cols + 2 * reach
    lines = out.shape[1]
    depth = values.shape[0] // lines
    count = tiles.shape[0]
    for k in range(count):
        size = min(LANES, total - k * LANES)
        tiles[k, :, :size] = values[:, k * LANES : k * LANES + size].astype(f32)
        if size < LANES:
            tiles[k, :, size:] = jnp.zeros((values.shape[0], LANES - size), f32)
    blank = jnp.zeros((lines, LANES), f32)
    for row in range(depth):
        pieces = [tiles[k, pl.ds(row, lines, stride=depth), :] for k in range(count)]
        wide = jnp.concatenate([blank] + pieces + [blank], axis=1)
        for part in range(parts):
            start = LANES + part * cols - reach
            flat[part, :, row * width : (row + 1) * width] = wide[:, start : start + width]
    for part in range(parts):
        out[part] = flat[part].astype(bf16)


def unpack_cells(packed, parts, first, amount, cells, across):
    lines = packed.shape[1]
    chans = lines // BLOCKS
    for part in range(parts):
        across[part] = packed[part, :, first : first + amount].astype(f32).T.astype(bf16)
    source = lax.broadcasted_iota(jnp.int32, (lines, LANES), 0)
    target = lax.broadcasted_iota(jnp.int32, (lines, LANES), 1)
    for s in range(BLOCKS):
        total = jnp.zeros((amount, LANES), f32)
        for part in range(parts):
            pick = ((target - part * chans) * BLOCKS + s == source).astype(bf16)
            total = total + nn(across[part], pick)
        cells[pl.ds(s, amount, stride=BLOCKS), :] = total


def targets_kernel(parts, first, packed, out, cells, across):
    unpack_cells(packed, parts, first, across.shape[1], cells, across)
    out[...] = cells[...].astype(bf16)


def fields_kernel(parts, rows, cols, packed, cells, lower, upper, held, across):
    unpack_cells(packed, parts, 0, across.shape[1], cells, across)
    width = cols + 2 * REACH
    room = -(-width // 8) * 8
    held[...] = jnp.zeros(held.shape, f32)
    for out, low, band in ((lower, rows - REACH, BLOCKS // 2 - 1), (upper, 0, 0)):
        for b in range(2):
            for t in range(REACH):
                start = (low + t) * width * 8 + band + b * (BLOCKS // 2)
                at = (b * REACH + t) * room
                held[at : at + width, :] = cells[pl.ds(start, width, stride=8), :]
        out[...] = held[...].astype(bf16)


def lay_ends(rows, cols, cells, above, below, ends):
    width = cols + 2 * REACH
    room = -(-width // 8) * 8
    line = width * 8
    for t in range(REACH):
        for k, row, way in ((t, rows - REACH + t, 1), (REACH + t, t, 7)):
            values = cells[row * line : (row + 1) * line, :].reshape(width, 8, LANES)
            ends[k * line : (k + 1) * line, :] = pltpu.roll(values, way, 1).reshape(line, LANES)
    for part, base, band in ((above, 0, 0), (below, REACH, BLOCKS // 2 - 1)):
        values = part[...].astype(f32)
        for b in range(2):
            for t in range(REACH):
                at = (b * REACH + t) * room
                start = (base + t) * line + band + b * (BLOCKS // 2)
                ends[pl.ds(start, width, stride=8), :] = values[at : at + width]


def lay_shifted(rows, cols, cells, ends, out, col, across):
    line = (cols + 2 * REACH) * 8
    total = rows + 2 * REACH
    amount = cols * 8
    lane = lax.broadcasted_iota(jnp.int32, (amount, LANES), 1)

    def values(row, col):
        if row >= total:
            return jnp.zeros((amount, LANES), f32)
        if row < REACH:
            ref, start = ends, row * line
        elif row < REACH + rows:
            ref, start = cells, (row - REACH) * line
        else:
            ref, start = ends, (row - rows) * line
        return ref[start + col * 8 : start + col * 8 + amount, :]

    for row in range(total):
        near = values(row, col)
        middle = values(row + 1, col) if across else values(row, col + 1)
        last = values(row + 2, col) if across else values(row, col + 2)
        middle = pltpu.roll(middle, CIN, 1)
        last = pltpu.roll(last, 2 * CIN - LANES, 1)
        place = slice(row * amount, (row + 1) * amount)
        out[place, :LANES] = jnp.where(lane < CIN, near, middle).astype(bf16)
        out[place, LANES:] = jnp.where(lane < 2 * CIN - LANES, middle, last).astype(bf16)


def wide_stem(stem):
    return jnp.concatenate([stem.astype(f32), jnp.zeros((C1, C1 - CI), f32)], axis=1)


def triple_stem(stem):
    wide = wide_stem(stem)
    return wide + pltpu.roll(wide, CIN, 1) + pltpu.roll(wide, 2 * CIN, 1)


def stem_kernel(
    rows, cols, cells, above, below, near, stem, pick, depth, counts, hzero, out, stats,
    weights, wide, sums, ends, first, second, third,
):
    amount = cols * 8
    step = pl.program_id(0)
    size = out.shape[0]

    @pl.when(step == 0)
    def _():
        lay_ends(rows, cols, cells, above, below, ends)
        lay_shifted(rows, cols, cells, ends, first, 0, False)
        lay_shifted(rows, cols, cells, ends, second, REACH, False)
        lay_shifted(rows, cols, cells, ends, third, 2 * REACH, True)
        stem3 = triple_stem(stem[...])
        for index in range(GROUPS):
            both = nt(near[...], pick[index]) * stem3
            weights[index * C1 : (index + 1) * C1, :] = both.astype(bf16)
        wide[...] = wide_stem(stem[...]).astype(bf16)
        sums[...] = jnp.zeros(sums.shape, f32)

    def place(shift):
        return pl.ds(pl.multiple_of(step * size + shift * amount, amount), size)

    total = jnp.zeros((size, C1), f32)
    for p in range(KSIZE):
        total = total + nt(first[place(p), :], weights[p * C1 : (p + 1) * C1, :])
        total = total + nt(second[place(p), :], weights[(KSIZE + p) * C1 : (KSIZE + p + 1) * C1, :])
    for k in range(3):
        at = (2 * KSIZE + k) * C1
        total = total + nt(third[place(3 * k), :], weights[at : at + C1, :])
    out[...] = total
    hzero[...] = nt(second[place(REACH), :], wide[...]).astype(bf16)
    ocean = depth[...] > 0.0
    kept = jnp.where(jnp.concatenate([ocean, ocean], axis=1), total, 0.0)
    sums[0:1, :] += row_sum(kept)
    sums[1:2, :] += row_sum(kept * total)

    @pl.when(step == pl.num_programs(0) - 1)
    def _():
        stats[...] = jnp.broadcast_to(stats_block(sums[0:1, :], sums[1:2, :], counts[...])[None], stats.shape)


def edge_kernel(rows, cols, count, *refs):
    inputs, (lower, upper, held, edge) = refs[: 3 * count], refs[3 * count :]
    width = cols + 2 * REACH
    lines = edge_lines(cols)
    amount = rows * cols * 8
    side = rows * REACH * 8
    for k in range(count):
        for tile in range(C2 // LANES):
            lanes = slice(tile * LANES, (tile + 1) * LANES)
            for ref, start, size in zip(inputs[3 * k : 3 * k + 3], (0, amount, amount + side), (amount, side, side)):
                held[start : start + size, :] = ref[:, lanes].astype(f32)
            for out, low, band in ((lower, rows - REACH, BLOCKS // 2 - 1), (upper, 0, 0)):
                edge[lines - 16 :, :] = jnp.zeros((16, LANES), f32)
                for t in range(REACH):
                    for b in range(2):
                        s = band + b * (BLOCKS // 2)
                        at = t * width * 2 + b
                        for start, wide, col in ((amount, REACH, 0), (0, cols, REACH), (amount + side, REACH, REACH + cols)):
                            values = held[pl.ds(start + (low + t) * wide * 8 + s, wide, stride=8), :]
                            edge[pl.ds(at + 2 * col, wide, stride=2), :] = values
                out[k * lines : (k + 1) * lines, lanes] = edge[...].astype(bf16)


def edge_lines(cols):
    return -(-REACH * (cols + 2 * REACH) * 2 // 16) * 16


def coarse_conv_kernel(rows, cols, centre, left, right, above, below, taps, depth, counts, out, stats, source, held, block):
    lay_border(rows, cols, source, held, centre, left, right, above, below)
    conv_sums(source, taps, depth, counts, out, stats, rows, cols, block)


def fine_kernel(cols, got, conv, hzero, vecs, bias_rows, up, up_bias, down, perm, downs, down_rows, hone, gated, slope, patches, coarse, held):
    mean, inverse, _, _ = norm_rows(got, C1)
    scale = inverse * vecs[0:1]
    for part in range(2):
        place = pl.ds(part * cols * 8, cols * 8)
        normal = ((conv[place, :] - mean) * scale + vecs[1:2]).astype(bf16)
        act = nt(normal, up[...]) + up_bias[...]
        value, bend = gelu_pair(act)
        value = value.astype(bf16)
        gated[place, :] = value
        slope[place, :] = bend.astype(bf16)
        branch = nt(value, down[...]) + bias_rows[0:1]
        full = (hzero[place, :].astype(f32) + branch).astype(bf16)
        hone[place, :] = full
        held[place, :] = full.astype(f32)
    cells = held[...]
    mixed = jnp.zeros((cols * 4, H1), f32)
    for p in range(2):
        for q in range(2):
            mixed = mixed + nn(quarter(cells, 2, cols, p, q).astype(bf16), perm[p * 2 + q])
    mixed = mixed.astype(bf16)
    patches[...] = mixed
    coarse[...] = (nt(mixed, downs[...]) + down_rows[0:1]).astype(bf16)


def middle_kernel(
    cols, got, conv, cells, vecs, up, up_bias, down, ups, fine_rows, head, last_rows, tables, hone, targets, depth,
    skip_out, top_out, dy_out, ds_out, du_out, dtop_out, dv_out, gated_out, da_out, normal_out, dx_out,
    sums, hidden_sums, copies,
):
    mean, inverse, _, ocean_count = norm_rows(got, C2)
    scale = inverse * vecs[0:1]
    centred = conv[...] - mean
    normal = (centred * scale + vecs[1:2]).astype(bf16)
    normal_out[...] = normal
    value, bend = gelu_pair(nt(normal, up[...]) + up_bias[...])
    value = value.astype(bf16)
    gated_out[...] = value
    top = (cells[...].astype(f32) + nt(value, down[...]) + vecs[2:3]).astype(bf16)
    top_out[...] = top
    raised = from_quarters([nt(top, ups[k]) + fine_rows[0:1] for k in range(4)], 2, cols)
    skip = (hone[...].astype(f32) + raised).astype(bf16)
    skip_out[...] = skip
    err = nt(skip, head[...]) + last_rows[0:1] - targets[...].astype(f32)
    deep = depth[...]
    ocean = tables[0:1] < deep
    heat_take = tables[1:2]
    err = jnp.where(ocean, err, 0.0)
    heat = jnp.sum(heat_take * err, axis=1, keepdims=True)
    heat = jnp.where(deep > 0.0, heat, 0.0)
    loss = row_sum(err * err) + (HEAT_WEIGHT / LANES) * row_sum(heat * heat)
    dy = jnp.where(ocean, err + HEAT_WEIGHT * heat_take * heat, 0.0) * (2.0 / ocean_count)
    dy = dy.astype(bf16)
    dy_out[...] = dy
    ds = nn(dy, head[...])
    ds_out[...] = ds
    dtop = jnp.zeros(top.shape, f32)
    du_sum = jnp.zeros((1, C1), f32)
    for k in range(4):
        du = quarter(ds, 2, cols, k // 2, k % 2).astype(bf16)
        du_out[k] = du
        du_sum = du_sum + row_sum(du.astype(f32))
        dtop = dtop + nn(du, ups[k])
    dtop_out[...] = dtop
    dv = dtop.astype(bf16)
    dv_out[...] = dv
    da = (nn(dv, down[...]) * bend).astype(bf16)
    da_out[...] = da
    dn = nn(da, up[...])
    dx_out[...] = dn * vecs[0:1]

    @pl.when(pl.program_id(0) == 0)
    def _():
        sums[...] = jnp.zeros(sums.shape, f32)
        hidden_sums[...] = jnp.zeros(hidden_sums.shape, f32)

    sums[0:1, :] += row_sum(dn)
    sums[1:2, :] += row_sum(dn * centred)
    sums[2:3, :] += row_sum(dv.astype(f32))
    sums[3:4, :C1] += du_sum
    sums[4:5, :CI] += row_sum(dy.astype(f32))
    sums[5:6, :LANES] += loss
    hidden_sums[0:1, :] += row_sum(da.astype(f32))

    @pl.when(pl.program_id(0) == pl.num_programs(0) - 1)
    def _():
        copies[...] = jnp.broadcast_to(stats_block(sums[0:1, :], sums[1:2, :], None)[None], copies.shape)


def backward_rows(got, back, gain, width):
    mean, inverse, cells, _ = norm_rows(got, width)
    tiles = width // LANES
    total = jnp.sum(back[...], axis=0)
    total_a = gain * wide_row(total, 0, tiles)
    total_b = gain * wide_row(total, tiles, tiles)
    dvar = -0.5 * inverse * inverse * inverse * total_b
    first = (-inverse * total_a - 2.0 * mean * dvar) / cells
    second = 2.0 * dvar / cells
    return inverse, first, second


def coarse_slope_kernel(rows, cols, got, back, vecs, dx, conv, depth, out, last, first_out):
    inverse, first, second = backward_rows(got, back, vecs[0:1], C2)
    ocean = depth[...] > 0.0
    ocean = jnp.concatenate([ocean] * (C2 // LANES), axis=1)
    value = dx[...] * inverse + jnp.where(ocean, first + conv[...] * second, 0.0)
    out[...] = value.astype(bf16)
    for ref, start in ((last, cols - REACH), (first_out, 0)):
        places = [(row * cols + start) * 8 for row in range(rows)]
        ref[...] = jnp.concatenate([value[at : at + REACH * 8] for at in places], axis=0).astype(bf16)


def coarse_taps_kernel(rows, cols, centre, left, right, above, below, slope, taps_out, source, held, here):
    lay_border(rows, cols, source, held, centre, left, right, above, below)
    here[...] = slope[...].astype(f32)
    taps_out[TAPS:, :] = jnp.zeros((taps_out.shape[0] - TAPS, LANES), f32)
    width = cols + 2 * REACH
    for p in range(KSIZE):

        def line(row, sums):
            own = here[rows8(row * cols, cols), :].reshape(cols, 8, LANES)
            seen = source[rows8((row + p) * width, width), :].reshape(width, 8, LANES)
            return tuple(sums[q] + jnp.sum(seen[q : q + cols] * own, axis=0) for q in range(KSIZE))

        zero = jnp.zeros((8, LANES), f32)
        sums = lax.fori_loop(0, rows, line, (zero,) * KSIZE)
        for q in range(KSIZE):
            taps_out[p * KSIZE + q : p * KSIZE + q + 1, :] = row_sum(sums[q])


def coarse_conv_back_kernel(rows, cols, centre, left, right, above, below, taps, dtop, dcells, slope, held):
    lay_border(rows, cols, slope, held, centre, left, right, above, below)

    def emit(place, total, carry):
        dcells[place, :] = (dtop[place, :] + total.reshape(-1, LANES)).astype(bf16)
        return carry

    convolve(slope, taps, rows, cols, emit, 0, flip=True)


def fine_back_kernel(
    cols, got, dcells, downs, ds, vecs, conv, slope, up, down, dv_out, da_out, dn_out, normal_out, sums, hidden_sums, coarse_sums, copies
):
    mean, inverse, _, _ = norm_rows(got, C1)
    dlow = dcells[...]
    dh = ds[...] + from_quarters([nn(dlow, downs[k]) for k in range(4)], 2, cols)
    dv = dh.astype(bf16)
    dv_out[...] = dv

    @pl.when(pl.program_id(0) == 0)
    def _():
        sums[...] = jnp.zeros(sums.shape, f32)
        hidden_sums[...] = jnp.zeros(hidden_sums.shape, f32)
        coarse_sums[...] = jnp.zeros(coarse_sums.shape, f32)

    coarse_sums[0:1, :] += row_sum(dlow.astype(f32))
    sums[2:3, :] += row_sum(dv.astype(f32))
    for part in range(2):
        place = pl.ds(part * cols * 8, cols * 8)
        centred = conv[place, :] - mean
        normal_out[place, :] = (centred * (inverse * vecs[0:1]) + vecs[1:2]).astype(bf16)
        da = (nn(dv_out[place, :], down[...]) * slope[place, :].astype(f32)).astype(bf16)
        da_out[place, :] = da
        hidden_sums[0:1, :] += row_sum(da.astype(f32))
        dn = nn(da, up[...])
        dn_out[place, :] = dn.astype(bf16)
        sums[0:1, :] += row_sum(dn)
        sums[1:2, :] += row_sum(dn * centred)

    @pl.when(pl.program_id(0) == pl.num_programs(0) - 1)
    def _():
        copies[...] = jnp.broadcast_to(stats_block(sums[0:1, :], sums[1:2, :], None)[None], copies.shape)


def turn_kernel(rows, cols, cells, above, below, out, ends):
    line = (cols + 2 * REACH) * 8
    amount = cols * 8
    lay_ends(rows, cols, cells, above, below, ends)
    for row in range(rows + 2 * REACH):
        if row < REACH:
            values = ends[row * line : (row + 1) * line, :]
        elif row < REACH + rows:
            values = cells[(row - REACH) * line : (row - REACH + 1) * line, :]
        else:
            values = ends[(row - rows) * line : (row - rows + 1) * line, :]
        across = values.T[:CIN]
        for q in range(KSIZE):
            piece = across[:, q * 8 : q * 8 + amount].astype(bf16)
            out[q * CIN : (q + 1) * CIN, row * amount : (row + 1) * amount] = piece


def fetch(sources, rooms, sems):
    return [pltpu.make_async_copy(a, b, sems.at[k]) for k, (a, b) in enumerate(zip(sources, rooms))]


def start(copies):
    for copy in copies:
        copy.start()


def wait(copies):
    for copy in copies:
        copy.wait()


def stem_back_kernel(rows, cols, got, back, vecs, near, stem, sums, conv, dn, depth, dv, shifted, tail, *scratch):
    rooms, (slope, acc, tap_acc, stem_acc, lines, held, sems) = scratch[:5], scratch[5:]
    copies = fetch((conv, dn, depth, dv, shifted), rooms, sems)
    start(copies)
    conv, dn, depth, dv, shifted = rooms
    amount = cols * 8
    inverse, first, second = backward_rows(got, back, vecs[0:1], C1)
    scale = inverse * vecs[0:1]
    taps = near[...].astype(f32).T
    stem_turned = stem[...].astype(f32).T
    wait(copies[:3])

    def slopes(row, carry):
        place = pl.ds(pl.multiple_of(row * amount, amount), amount)
        ocean = depth[place, :] > 0.0
        ocean = jnp.concatenate([ocean, ocean], axis=1)
        value = dn[place, :].astype(f32) * scale + jnp.where(ocean, first + conv[place, :] * second, 0.0)
        slope[place, :] = value.astype(bf16)
        return carry

    lax.fori_loop(0, rows, slopes, 0)
    wait(copies[3:])
    total = rows * amount
    straight = shifted[REACH * CIN : (REACH + 1) * CIN, REACH * amount : REACH * amount + total]
    stem_acc[...] = nn(straight, dv[...])
    tap_acc[...] = jnp.zeros(tap_acc.shape, f32)
    for p in range(KSIZE):
        acc[...] = nn(shifted[:, p * amount : p * amount + total], slope[...])
        sum_here = stem_acc[...]
        for q in range(KSIZE):
            tap = p * KSIZE + q
            part = acc[q * CIN : (q + 1) * CIN, :]
            sum_here = sum_here + part * taps[tap : tap + 1]
            tap_acc[tap : tap + 1, :] = row_sum(part * stem_turned[:CIN])
        stem_acc[...] = sum_here
    acc[:CIN, :] = stem_acc[...]
    acc[CIN : 2 * LANES, :] = jnp.zeros((2 * LANES - CIN, C1), f32)
    lines[...] = jnp.zeros(lines.shape, f32)
    turned = acc[:LANES, :].T
    acc[:C1, :LANES] = turned
    write_matrix(lines, 0, STEM, held, acc)
    held[:C1, :] = tap_acc[...].T
    write_short(lines, offsets()[TAPS1], WIDTH, TAPS, lambda r: held[r : r + 1, :])
    write_row(lines, 0, GAIN1, norm_row(got, sums, C1))
    write_row(lines, 0, SHIFT1, row_of(sums, 0))
    used = lines.shape[0] // tail.shape[0]
    for k in range(tail.shape[0]):
        tail[k, :used] = lines[k * used : (k + 1) * used, :]
        tail[k, used:] = jnp.zeros((tail.shape[1] - used, LANES), f32)


def period(length):
    return LANES // math.gcd(length, LANES)


def offsets():
    starts = []
    start = 0
    for shape in shapes_of():
        starts.append(start)
        start += math.prod(shape)
    return starts


def shard_places(devices, shard_len):
    firsts = [e * shard_len // 2048 * 16 for e in range(devices)]
    needed = [(e * shard_len % 2048 + shard_len + 2047) // 2048 * 16 for e in range(devices)]
    return firsts, max(needed)


def lane_ids(rows):
    return lax.broadcasted_iota(jnp.int32, (rows, LANES), 1)


def turn_lanes(values, amount):
    amount = amount % LANES
    return values if amount == 0 else pltpu.roll(values, amount, 1)


def read_rows(lines, base, rows, length, put):
    cycle = period(length)
    count = rows // cycle
    step = cycle * length // LANES
    lane = lane_ids(count)
    tiles = -(-length // LANES)
    for s in range(cycle):
        start = base + s * length
        line, phase = start // LANES, start % LANES
        held = [
            lines[pl.ds(line + k, count, stride=step), :] for k in range(-(-(phase + length) // LANES))
        ]
        for m in range(tiles):
            value = held[m]
            if phase and m + 1 < len(held):
                value = jnp.where(lane >= phase, value, held[m + 1])
            value = turn_lanes(value, -phase)
            if length - m * LANES < LANES:
                value = jnp.where(lane < length - m * LANES, value, 0.0)
            put(s, cycle, count, m, value)


def read_vector(lines, base, length, put):
    line, phase = base // LANES, base % LANES
    lane = lane_ids(1)
    for m in range(-(-length // LANES)):
        value = lines[line + m : line + m + 1, :]
        if phase and phase + length > (m + 1) * LANES:
            value = jnp.where(lane >= phase, value, lines[line + m + 1 : line + m + 2, :])
        value = turn_lanes(value, -phase)
        if length - m * LANES < LANES:
            value = jnp.where(lane < length - m * LANES, value, 0.0)
        put(m, value)


def write_rows(lines, base, rows, length, get):
    cycle = period(length)
    count = rows // cycle
    step = cycle * length // LANES
    line, phase = base // LANES, base % LANES
    for k in range(step):
        shared = k == 0 and phase > 0
        amount = count + 1 if shared else count
        lane = lane_ids(amount)
        total = None
        at = 0
        while at < LANES:
            place = k * LANES - phase + at
            row, col = place // length, place % length
            run = min(length - col, LANES - at)
            tile = col // LANES
            value = get(row, cycle, amount, tile)
            if col % LANES + run > LANES:
                value = jnp.where(lane >= col % LANES, value, get(row, cycle, amount, tile + 1))
            value = turn_lanes(value, at - col)
            total = value if total is None else jnp.where(lane >= at, value, total)
            at += run
        put_lines(lines, line + k, amount, step, total, shared)


def put_lines(lines, line, amount, step, values, shared):
    if not shared:
        lines[pl.ds(line, amount, stride=step), :] = values
        return
    before = lines[line : line + 1, :]
    lines[pl.ds(line, amount, stride=step), :] = values
    lines[line : line + 1, :] = lines[line : line + 1, :] + before


def write_vector(lines, base, length, get):
    line, phase = base // LANES, base % LANES
    lane = lane_ids(1)
    tiles = -(-length // LANES)
    zero = jnp.zeros((1, LANES), f32)
    for k in range(-(-(phase + length) // LANES)):
        value = get(k) if k < tiles else zero
        if phase:
            earlier = get(k - 1) if k > 0 else zero
            value = turn_lanes(jnp.where(lane >= LANES - phase, earlier, value), phase)
        if k == 0 and phase:
            value = value + lines[line : line + 1, :]
        lines[line + k : line + k + 1, :] = value


def write_short(lines, base, rows, length, get):
    line, phase = base // LANES, base % LANES
    lane = lane_ids(1)
    for k in range(-(-(phase + rows * length) // LANES)):
        low = k * LANES - phase
        total = jnp.zeros((1, LANES), f32)
        for row in range(max(low // length, 0), min(-(-(low + LANES) // length), rows)):
            at = row * length - low
            value = turn_lanes(get(row), at)
            if at < 0:
                value = jnp.where(lane < at + length, value, 0.0)
            elif at + length > LANES:
                value = jnp.where(lane >= at, value, 0.0)
            total = total + value
        if k == 0 and phase:
            total = total + lines[line : line + 1, :]
        lines[line + k : line + k + 1, :] = total


def read_short(lines, base, rows, length, put):
    lane = lane_ids(1)
    for row in range(rows):
        start = base + row * length
        line, phase = start // LANES, start % LANES
        value = lines[line : line + 1, :]
        if phase + length > LANES:
            value = jnp.where(lane >= phase, value, lines[line + 1 : line + 2, :])
        put(row, jnp.where(lane < length, turn_lanes(value, -phase), 0.0))


STEM, TAPS1, GAIN1, SHIFT1, UP1, UPB1, DOWN1, DOWNB1, DOWNS, DOWNSB = range(10)
TAPS2, GAIN2, SHIFT2, UP2, UPB2, DOWN2, DOWNB2, UPS, UPSB, HEAD, HEADB = range(10, 21)


def planes_of(devices, shard_len, low, high, plane_size):
    firsts, tall = shard_places(devices, shard_len)
    found = {e // plane_size for e in range(devices) if firsts[e] < high and firsts[e] + tall > low}
    return sorted(found)


def collect(devices, shard_len, blocks, lines, low, high):
    firsts, tall = shard_places(devices, shard_len)
    started = False
    for e in range(devices):
        end = firsts[e + 1] + 16 if e + 1 < devices else firsts[e] + tall
        if end <= low or firsts[e] >= high:
            continue
        first = firsts[e] - low
        skip = max(0, -first)
        take = min(tall, high - firsts[e])
        if started:
            lines[pl.ds(first, 16), :] += blocks[e, :16, :].astype(f32)
            skip = 16
        started = True
        if take > skip:
            lines[pl.ds(first + skip, take - skip), :] = blocks[e, skip:take, :].astype(f32)


def seat_of(me, other, devices):
    away = me ^ other
    seat = 0
    bits = devices.bit_length() - 1
    for b in range(bits):
        seat = seat + ((away >> b) & 1) * (1 << (bits - 1 - b))
    return seat


def matrix_out(held, tall, out, tiles, rows):
    for m in range(tiles):
        if tall > rows:
            held[m * tall + rows : (m + 1) * tall, :] = jnp.zeros((tall - rows, LANES), f32)
        out[:, m * LANES : (m + 1) * LANES] = held[m * tall : (m + 1) * tall, :].astype(bf16)


def read_matrix(lines, shift, piece, held, out):
    rows, length = shapes_of()[piece]
    tall = out.shape[0]

    def put(first, stride, count, tile, value):
        held[pl.ds(tile * tall + first, count, stride=stride), :] = value

    read_rows(lines, offsets()[piece] - shift, rows, length, put)
    matrix_out(held, tall, out, -(-length // LANES), rows)


def read_row(lines, shift, piece, out, row):
    def put(tile, value):
        out[row : row + 1, tile * LANES : (tile + 1) * LANES] = value

    read_vector(lines, offsets()[piece] - shift, shapes_of()[piece][0], put)


def read_taps(lines, shift, piece, held, out, tall):
    def put(row, value):
        held[pl.ds(row, 1), :] = value

    rows = shapes_of()[piece][0]
    read_short(lines, offsets()[piece] - shift, rows, TAPS, put)
    held[rows:tall, :] = jnp.zeros((tall - rows, LANES), f32)
    if out is None:
        return
    across = held[:tall, :].T
    for t in range(TAPS):
        out[t] = jnp.broadcast_to(across[t : t + 1, :], (8, tall))


def first_end():
    return -(-offsets()[TAPS2] // 2048) * 16


def rest_start():
    return offsets()[TAPS2] // 2048 * 16


def rest_end():
    return -(-(offsets()[HEADB] + CIN) // 2048) * 16


def stem_params_kernel(parts, stem, near, vecs, lines, held):
    lines[...] = parts[...].astype(f32)
    vecs[...] = jnp.zeros(vecs.shape, f32)
    read_taps(lines, 0, TAPS1, held, None, C1)
    near[...] = held[:C1, :].astype(bf16)
    read_matrix(lines, 0, STEM, held, stem)
    read_row(lines, 0, GAIN1, vecs, 0)
    read_row(lines, 0, SHIFT1, vecs, 1)


def fine_params_kernel(
    devices, shard_len, blocks, perm, up, bias, down, downs, downs_four, down_rows, vecs, lines, held
):
    low, high = span(UP1, DOWNSB)
    shift = low * LANES
    collect(devices, shard_len, blocks, lines, low, high)
    for out in (down_rows, bias, vecs):
        out[...] = jnp.zeros(out.shape, f32)
    read_row(lines, shift, DOWNB1, vecs, 0)
    read_row(lines, shift, UPB1, bias, 0)
    read_row(lines, shift, DOWNSB, down_rows, 0)
    read_matrix(lines, shift, UP1, held, up)
    read_matrix(lines, shift, DOWN1, held, down)
    read_matrix(lines, shift, DOWNS, held, downs)
    for k in range(4):
        downs_four[k] = nt(downs[...], perm[k]).astype(bf16)


def rest_params_kernel(
    devices, shard_len, blocks, taps2, vecs2, up2, bias2, down2, ups_four, vecs1, head, last, lines, held
):
    shift = rest_start() * LANES
    collect(devices, shard_len, blocks, lines, rest_start(), rest_end())
    for out in (vecs1, vecs2, bias2, last):
        out[...] = jnp.zeros(out.shape, f32)
    read_taps(lines, shift, TAPS2, held, taps2, C2)
    read_row(lines, shift, GAIN2, vecs2, 0)
    read_row(lines, shift, SHIFT2, vecs2, 1)
    read_row(lines, shift, DOWNB2, vecs2, 2)
    read_row(lines, shift, UPB2, bias2, 0)
    read_row(lines, shift, UPSB, vecs1, 0)
    read_row(lines, shift, HEADB, last, 0)
    read_matrix(lines, shift, UP2, held, up2)
    read_matrix(lines, shift, DOWN2, held, down2)
    read_matrix(lines, shift, HEAD, held, head)
    tiles = C2 // LANES

    def put(first, stride, count, tile, value):
        k = first % 4
        held[pl.ds((k * tiles + tile) * C1 + first // 4, count, stride=stride // 4), :] = value

    rows, length = shapes_of()[UPS]
    read_rows(lines, offsets()[UPS] - shift, rows, length, put)
    for k in range(4):
        for m in range(tiles):
            at = (k * tiles + m) * C1
            held[at + WIDTH : at + C1, :] = jnp.zeros((C1 - WIDTH, LANES), f32)
            ups_four[k, :, m * LANES : (m + 1) * LANES] = held[at : at + C1, :].astype(bf16)


FRONT = 16


def hold_matrix(held, values, row_tiles, rows):
    tall = rows + 2 * FRONT
    zero = jnp.zeros((FRONT, LANES), f32)
    for m in range(row_tiles):
        at = m * tall
        held[at : at + FRONT, :] = zero
        held[at + FRONT : at + FRONT + rows, :] = values(m)
        held[at + FRONT + rows : at + tall, :] = zero


def write_matrix(lines, shift, piece, held, source):
    rows, length = shapes_of()[piece]
    tall = rows + 2 * FRONT
    hold_matrix(held, lambda m: source[:rows, m * LANES : (m + 1) * LANES], -(-length // LANES), rows)

    def get(first, stride, count, tile):
        return held[pl.ds(tile * tall + FRONT + first, count, stride=stride), :]

    write_rows(lines, offsets()[piece] - shift, rows, length, get)


def write_row(lines, shift, piece, get):
    write_vector(lines, offsets()[piece] - shift, shapes_of()[piece][0], get)


def row_of(source, row):
    return lambda m: source[row : row + 1, m * LANES : (m + 1) * LANES]


def norm_row(got, sums, width):
    _, inverse, _, _ = norm_rows(got, width)
    value = sums[1:2, :] * inverse
    return lambda m: value[:, m * LANES : (m + 1) * LANES]


def scatter_out(devices, shard_len, plane_size, planes, place, lines, low, keep, send):
    firsts, tall = shard_places(devices, shard_len)
    half = plane_size // 2
    for k, plane in enumerate(planes):
        for r in range(plane_size):
            first = firsts[plane * plane_size + r] - low
            start, end = max(first, 0), min(first + tall, lines.shape[0])
            seat = seat_of(place, r, plane_size)

            def put(out, index, kind):
                if end <= start:
                    out[index] = jnp.zeros((tall, LANES), kind)
                    return
                if start > first:
                    out[index, : start - first] = jnp.zeros((start - first, LANES), kind)
                out[index, start - first : end - first] = lines[start:end, :].astype(kind)
                if end < first + tall:
                    out[index, end - first :] = jnp.zeros((first + tall - end, LANES), kind)

            @pl.when(seat < half)
            def _():
                put(keep, seat * len(planes) + k, f32)

            @pl.when(seat >= half)
            def _():
                put(send, (seat - half) * len(planes) + k, bf16)


def span(first, last):
    end = offsets()[last] + math.prod(shapes_of()[last])
    return offsets()[first] // 2048 * 16, -(-end // 2048) * 16


def clear_ends(lines, low, first, last):
    start = offsets()[first] // LANES - low + 1
    lines[:start, :] = jnp.zeros((start, LANES), f32)
    end = -(-(offsets()[last] + math.prod(shapes_of()[last])) // LANES) - low
    if end < lines.shape[0]:
        lines[end:, :] = jnp.zeros((lines.shape[0] - end, LANES), f32)


def late_flat_kernel(
    devices, shard_len, plane_size, planes, place, sums2, hidden2, da, normal, dv, gated, du, top, dy, skip, keep, send, *scratch
):
    rooms, (lines, held, g_up2, g_down2, g_ups, g_head, sems) = scratch[:8], scratch[8:]
    copies = fetch((da, normal, dv, gated, du, top, dy, skip), rooms, sems)
    da, normal, dv, gated, du, top, dy, skip = rooms
    start(copies[6:])
    start(copies[4:6])
    wait(copies[6:])
    start(copies[:2])
    g_head[...] = tn(dy[...], skip[...])
    wait(copies[4:6])
    start(copies[2:4])
    for k in range(4):
        g_ups[k] = tn(du[k], top[...])
    wait(copies[:2])
    g_up2[...] = tn(da[...], normal[...])
    wait(copies[2:4])
    g_down2[...] = tn(dv[...], gated[...])
    low, _ = span(UP2, HEADB)
    shift = low * LANES
    clear_ends(lines, low, UP2, HEADB)
    write_matrix(lines, shift, UP2, held, g_up2)
    write_row(lines, shift, UPB2, row_of(hidden2, 0))
    write_matrix(lines, shift, DOWN2, held, g_down2)
    write_row(lines, shift, DOWNB2, row_of(sums2, 2))
    rows, length = shapes_of()[UPS]
    tiles = C2 // LANES
    tall = WIDTH + 2 * FRONT
    for k in range(4):
        for m in range(tiles):
            at = (k * tiles + m) * tall
            held[at : at + FRONT, :] = jnp.zeros((FRONT, LANES), f32)
            held[at + FRONT : at + FRONT + WIDTH, :] = g_ups[k, :WIDTH, m * LANES : (m + 1) * LANES]
            held[at + FRONT + WIDTH : at + tall, :] = jnp.zeros((FRONT, LANES), f32)

    def get(first, stride, count, tile):
        at = ((first % 4) * tiles + tile) * tall + FRONT + first // 4
        return held[pl.ds(at, count, stride=stride // 4), :]

    write_rows(lines, offsets()[UPS] - shift, rows, length, get)
    write_row(lines, shift, UPSB, row_of(sums2, 3))
    write_matrix(lines, shift, HEAD, held, g_head)
    write_row(lines, shift, HEADB, row_of(sums2, 4))
    scatter_out(devices, shard_len, plane_size, planes, place[0], lines, low, keep, send)


def early_flat_kernel(
    devices, shard_len, plane_size, planes, place, got2, sums1, hidden1, sums_low, g_taps2, more_taps2, sums2,
    da, normal, dv, gated, dcells, patches, keep, send, *scratch,
):
    rooms, (lines, held, g_up1, g_down1, g_downs, sems) = scratch[:6], scratch[6:]
    copies = fetch((da, normal, dv, gated, dcells, patches), rooms, sems)
    da, normal, dv, gated, dcells, patches = rooms
    start(copies[4:])
    start(copies[2:4])
    wait(copies[4:])
    start(copies[:2])
    g_downs[...] = tn(dcells[...], patches[...])
    wait(copies[2:4])
    g_down1[...] = tn(dv[...], gated[...])
    wait(copies[:2])
    g_up1[...] = tn(da[...], normal[...])
    low, _ = span(UP1, SHIFT2)
    shift = low * LANES
    clear_ends(lines, low, UP1, SHIFT2)
    write_matrix(lines, shift, UP1, held, g_up1)
    write_row(lines, shift, UPB1, row_of(hidden1, 0))
    write_matrix(lines, shift, DOWN1, held, g_down1)
    write_row(lines, shift, DOWNB1, row_of(sums1, 2))
    write_matrix(lines, shift, DOWNS, held, g_downs)
    write_row(lines, shift, DOWNSB, row_of(sums_low, 0))
    across = jnp.concatenate([g_taps2[...], more_taps2[...]], axis=1)
    across = jnp.concatenate([across, jnp.zeros((LANES - across.shape[0], C2), f32)], axis=0).T
    held[:C2, :] = across
    write_short(lines, offsets()[TAPS2] - shift, WIDTH2, TAPS, lambda r: held[r : r + 1, :])
    write_row(lines, shift, GAIN2, norm_row(got2, sums2, C2))
    write_row(lines, shift, SHIFT2, row_of(sums2, 0))
    scatter_out(devices, shard_len, plane_size, planes, place[0], lines, low, keep, send)


def group_taps():
    table = []
    for first in (0, 3):
        for p in range(KSIZE):
            table.append([p * KSIZE + first + t for t in range(3)])
    for k in range(3):
        table.append([(3 * k + t) * KSIZE + 6 if 3 * k + t < KSIZE else -1 for t in range(3)])
    return table


def quarter_lanes():
    at = np.arange(C1)[None, :, None] * 4 + np.arange(4)[:, None, None]
    hot = (at == np.arange(H1)[None, None, :]) & (np.arange(C1) < WIDTH)[None, :, None]
    return hot.astype(jnp.bfloat16)


def tap_lanes():
    table = np.array([line + [-1] for line in group_taps()])
    wanted = table[:, np.arange(C1) // CIN]
    return (wanted[:, :, None] == np.arange(LANES)).astype(jnp.bfloat16)


def body(fields, targets, ocean_depth, thickness_class, params, moment1, moment2):
    shard_len = params.shape[0]
    devices = lax.axis_size(AXES)
    plane_size = 2 * lax.axis_size("lvl")
    me = lax.axis_index(AXES)
    _, tall = shard_places(devices, shard_len)
    at = (me * (shard_len % 2048)) % 2048
    place_row = jnp.broadcast_to(me % plane_size, (1,)).astype(jnp.int32)

    smem = pl.BlockSpec(memory_space=pltpu.SMEM)
    vmem = pl.BlockSpec(memory_space=pltpu.VMEM)
    parts = lax.axis_size("lvl")
    chans, batch, all_rows, all_cols = fields.shape
    bands = BLOCKS // batch
    rows, cols = all_rows // bands, all_cols // parts
    half_rows, half_cols = rows // 2, cols // 2
    cells, low_cells = rows * cols * 8, half_rows * half_cols * 8
    wide_cols = cols + 2 * REACH
    low_border = (half_rows + 2 * REACH) * (half_cols + 2 * REACH) * 8

    def packed(values, reach):
        lanes = rows * (cols + 2 * reach)
        return call(
            lambda *refs: pack_kernel(parts, cols, reach, *refs),
            [((parts, chans * BLOCKS, lanes), bf16)],
            scratch=[
                pltpu.VMEM((-(-all_cols // LANES), chans * batch * all_rows, LANES), f32),
                pltpu.VMEM((parts, chans * BLOCKS, lanes), f32),
            ],
            micros=3,
            name="pack",
        )(values.reshape(-1, all_cols))[0]

    copies, placed = tie(packed(fields, REACH), params)
    field_given = lax.all_to_all(copies, "lvl", 0, 0, tiled=True)
    goal_copies = packed(targets, 0)
    block = lax.dynamic_update_slice(jnp.zeros((tall * LANES,), bf16), placed.astype(bf16), (at,))
    block = block.reshape(tall, LANES)
    gathered = lax.all_gather(block, AXES, axis=0)
    near_shards = 1
    while near_shards < -(-first_end() * LANES // shard_len):
        near_shards *= 2
    chunk_lines = -(-span(STEM, SHIFT1)[1] // (8 * devices)) * 8
    head_lines = chunk_lines * devices
    window = jnp.pad(block, ((head_lines, head_lines), (0, 0)))
    first_line = me * shard_len // 2048 * 16
    window = lax.dynamic_slice_in_dim(window, head_lines - jnp.minimum(first_line, head_lines), head_lines)
    field_given, (window, goal_copies) = tie(field_given, (window, goal_copies))
    chunk = jnp.sum(swap(window.reshape(devices, chunk_lines, LANES)).astype(f32), axis=0).astype(bf16)
    send_room = 2 * REACH * -(-wide_cols // 8) * 8
    field_cells, lower, upper = call(
        lambda *refs: fields_kernel(parts, rows, cols, *refs),
        [((rows * wide_cols * 8, LANES), f32), ((send_room, LANES), bf16), ((send_room, LANES), bf16)],
        scratch=[pltpu.VMEM((send_room, LANES), f32), pltpu.VMEM((parts, rows * wide_cols, chans * BLOCKS), bf16)],
        micros=4,
        name="fields",
    )(field_given)
    chunk, (field_cells, lower, upper) = tie(chunk, (field_cells, lower, upper))
    above, below = lines_out(lower, upper)
    stem_lines = swap(jnp.broadcast_to(chunk[None], (devices,) + chunk.shape)).reshape(head_lines, LANES)
    stem_lines, (above, below, goal_copies) = tie(stem_lines, (above, below, goal_copies))
    goal_given = lax.all_to_all(goal_copies, "lvl", 0, 0, tiled=True)

    deep = depth_cells(ocean_depth, batch)
    depth_rows = jnp.broadcast_to(deep.astype(f32)[..., None], deep.shape + (LANES,)).reshape(cells, LANES)
    low = jnp.max(deep.reshape(half_rows, 2, half_cols, 2, 8), axis=(1, 3))
    low_rows = jnp.broadcast_to(low.astype(f32)[..., None], low.shape + (LANES,)).reshape(low_cells, LANES)
    channel = jnp.arange(CI, dtype=jnp.int32)
    level = jnp.where(channel < 4 * LEVELS, channel // 4, 0)
    level_row = jnp.where(channel < CIN, level, LEVELS + 1).astype(f32)
    thickf = thickness_class.astype(f32)
    onehot = (level[:, None] == jnp.arange(LEVELS, dtype=jnp.int32)[None, :]).astype(f32)
    chosen = ((channel % 4 == 0) & (channel < 4 * LEVELS)).astype(f32)
    heat_take = chosen * jnp.sum(onehot * thickf[None, :], axis=1) / jnp.sum(thickf)
    ocean_cells = jnp.sum((level_row[None, None, :] < ocean_depth.astype(f32)[:, :, None]).astype(f32))
    ocean_cells = batch * ocean_cells
    surface_cells = jnp.sum((deep > 0).astype(f32))
    low_surface = jnp.sum((low > 0).astype(f32))
    index8 = jnp.arange(8)[:, None]
    lane8 = jnp.arange(LANES)[None, :]

    def counts_of(width, cells_count):
        (r, c), (ro, co) = count_places(width)
        at_cells = (index8 == r) & (lane8 == c)
        at_ocean = (index8 == ro) & (lane8 == co)
        return jnp.where(at_cells, cells_count, jnp.where(at_ocean, ocean_cells, 0.0))

    counts1 = counts_of(C1, surface_cells)
    counts2 = counts_of(C2, low_surface)

    tables = jnp.pad(jnp.stack([level_row, heat_take]), ((0, 6), (0, 0)))
    perm, pick = jnp.asarray(quarter_lanes()), jnp.asarray(tap_lanes())
    held_room = pltpu.VMEM((4 * H2, LANES), f32)
    stem_in, near1, vecs1 = call(
        stem_params_kernel,
        [((C1, CI), bf16), ((C1, LANES), bf16), ((8, C1), f32)],
        scratch=[pltpu.VMEM(stem_lines.shape, f32), pltpu.VMEM((2 * C1, LANES), f32)],
        micros=3,
        name="stem_params",
    )(stem_lines)

    smalls = (perm, low_rows, counts1, counts2, tables, place_row, depth_rows, pick)
    field_cells, smalls = tie(field_cells, smalls)
    perm, low_rows, counts1, counts2, tables, place_row, depth_rows, pick = smalls

    ends_room = pltpu.VMEM((2 * REACH * wide_cols * 8, LANES), f32)
    shifted_room = pltpu.VMEM(((rows + 2 * REACH) * cols * 8, C1), bf16)
    hzero, conv1, stats1 = call(
        lambda *refs: stem_kernel(rows, cols, *refs),
        [((cells, C1), bf16), ((cells, C1), f32), ((devices, 8, LANES), f32)],
        grid=(half_rows,),
        ins=[
            whole(rows * wide_cols * 8, LANES), whole(send_room, LANES), whole(send_room, LANES), whole(C1, LANES), whole(C1, CI),
            whole(GROUPS, C1, LANES), band(2 * cols * 8, LANES), whole(8, LANES),
        ],
        out_specs=[band(2 * cols * 8, C1), band(2 * cols * 8, C1), whole(devices, 8, LANES)],
        scratch=[
            pltpu.VMEM((GROUPS * C1, C1), bf16), pltpu.VMEM((C1, C1), bf16), pltpu.VMEM((8, C1), f32),
            ends_room, shifted_room, shifted_room, shifted_room,
        ],
        micros=17,
        name="stem_conv",
    )(field_cells, above, below, near1, stem_in, pick, depth_rows, counts1)
    got1 = swap(stats1)
    hzero, goal_given = tie(hzero, goal_given)
    up_in1, bias_in1, down_in1, downs_in, downs_four, down_rows, bias_rows = call(
        lambda *refs: fine_params_kernel(devices, shard_len, *refs),
        [
            ((H1, C1), bf16), ((1, H1), f32), ((C1, H1), bf16), ((C2, H1), bf16), ((4, C2, C1), bf16), ((8, C2), f32),
            ((8, C1), f32),
        ],
        grid=(1,),
        ins=[whole(near_shards, tall, LANES), whole(4, C1, H1)],
        out_specs=[
            whole(H1, C1), whole(1, H1), whole(C1, H1), whole(C2, H1), whole(4, C2, C1), whole(8, C2), whole(8, C1),
        ],
        scratch=[pltpu.VMEM((span(UP1, DOWNSB)[1] - span(UP1, DOWNSB)[0], LANES), f32), held_room],
        micros=8,
        name="fine_params",
    )(gathered, perm)
    chunk, low_chunk = 2 * cols * 8, half_cols * 8
    hone, gated1, slope1, patches, coarse = call(
        lambda *refs: fine_kernel(cols, *refs),
        [
            ((cells, C1), bf16),
            ((cells, H1), bf16),
            ((cells, H1), bf16),
            ((low_cells, H1), bf16),
            ((low_cells, C2), bf16),
        ],
        grid=(half_rows,),
        ins=[
            whole(devices, 8, LANES), band(chunk, C1), band(chunk, C1), whole(8, C1), whole(8, C1), whole(H1, C1), whole(1, H1),
            whole(C1, H1), whole(4, C1, H1), whole(C2, H1), whole(8, C2),
        ],
        out_specs=[
            band(chunk, C1), band(chunk, H1), band(chunk, H1), band(low_chunk, H1), band(low_chunk, C2),
        ],
        scratch=[pltpu.VMEM((chunk, C1), f32)],
        micros=15,
        name="fine_forward",
    )(got1, conv1, hzero, vecs1, bias_rows, up_in1, bias_in1, down_in1, perm, downs_in, down_rows)

    edge = edge_lines(half_cols)
    side = half_rows * REACH * 8

    def edges(values, left, right):
        return call(
            lambda *refs: edge_kernel(half_rows, half_cols, 1, *refs),
            [((edge, C2), bf16)] * 2,
            scratch=[pltpu.VMEM((low_cells + 2 * side, LANES), f32), pltpu.VMEM((edge, LANES), f32)],
            micros=3,
            name="edge",
        )(values, left, right)

    def border_tiles(tile):
        return [tile(low_cells), tile(side), tile(side), tile(edge), tile(edge)]

    sides = columns_out((coarse,), half_rows, half_cols)[0]
    goal_given, coarse = tie(goal_given, coarse)
    goal = call(
        lambda *refs: targets_kernel(parts, 0, *refs),
        [((cells, LANES), bf16)],
        scratch=[pltpu.VMEM((cells, LANES), f32), pltpu.VMEM((parts, rows * cols, chans * BLOCKS), bf16)],
        micros=4,
        name="targets",
    )(goal_given)[0]
    sides, goal = tie(sides, goal)
    border2 = (coarse, *sides, *lines_out(*edges(coarse, *sides)))
    taps_in2, vecs2, up_in2, bias_in2, down_in2, ups_four, fine_rows, head_in, last_rows = call(
        lambda *refs: rest_params_kernel(devices, shard_len, *refs),
        [
            ((TAPS, 8, C2), f32), ((8, C2), f32), ((H2, C2), bf16), ((1, H2), f32), ((C2, H2), bf16),
            ((4, C1, C2), bf16), ((8, C1), f32), ((CI, C1), bf16), ((8, CI), f32),
        ],
        ins=[vmem],
        scratch=[pltpu.VMEM((rest_end() - rest_start(), LANES), f32), held_room],
        micros=13,
        name="rest_params",
    )(gathered)
    conv2, stats2 = call(
        lambda *refs: coarse_conv_kernel(half_rows, half_cols, *refs),
        [((low_cells, C2), f32), ((devices, 8, LANES), f32)],
        grid=(C2 // LANES,),
        ins=border_tiles(lane_tile) + [TAP_TILE, whole(low_cells, LANES), whole(8, LANES)],
        out_specs=[lane_tile(low_cells), whole(devices, 8, LANES)],
        scratch=[pltpu.VMEM((low_border, LANES), f32), pltpu.VMEM((edge, LANES), f32), pltpu.VMEM((8, LANES), f32)],
        micros=11,
        name="coarse_conv",
    )(*border2, taps_in2, low_rows, counts2)
    got2 = swap(stats2)
    field_cells, stats2 = tie(field_cells, stats2)
    turned = call(
        lambda *refs: turn_kernel(rows, cols, *refs),
        [((KSIZE * CIN, (rows + 2 * REACH) * cols * 8), bf16)],
        scratch=[ends_room],
        micros=8,
        name="turn",
    )(field_cells, above, below)[0]
    conv2, turned = tie(conv2, turned)
    (
        skip, top, dy, ds, du, dtop, dv2, gated2, da2, normal2, dx2, sums2, hidden2, copies2,
    ) = call(
        lambda *refs: middle_kernel(cols, *refs),
        [
            ((cells, C1), bf16), ((low_cells, C2), bf16), ((cells, CI), bf16), ((cells, C1), f32),
            ((4, low_cells, C1), bf16), ((low_cells, C2), f32), ((low_cells, C2), bf16), ((low_cells, H2), bf16),
            ((low_cells, H2), bf16), ((low_cells, C2), bf16), ((low_cells, C2), f32),
            ((8, C2), f32), ((8, H2), f32), ((devices, 8, LANES), f32),
        ],
        grid=(half_rows,),
        ins=[
            whole(devices, 8, LANES), band(low_chunk, C2), band(low_chunk, C2), whole(8, C2), whole(H2, C2), whole(1, H2),
            whole(C2, H2), whole(4, C1, C2), whole(8, C1), whole(CI, C1), whole(8, CI), whole(8, CI), band(chunk, C1),
            band(chunk, CI), band(chunk, LANES),
        ],
        out_specs=[
            band(chunk, C1), band(low_chunk, C2), band(chunk, CI), band(chunk, C1),
            pl.BlockSpec((4, low_chunk, C1), lambda i: (0, i, 0)), band(low_chunk, C2), band(low_chunk, C2),
            band(low_chunk, H2), band(low_chunk, H2), band(low_chunk, C2), band(low_chunk, C2),
            whole(8, C2), whole(8, H2), whole(devices, 8, LANES),
        ],
        micros=20,
        name="middle",
    )(
        got2, conv2, coarse, vecs2, up_in2, bias_in2, down_in2, ups_four, fine_rows, head_in, last_rows, tables, hone, goal,
        depth_rows,
    )
    back2 = swap(copies2)
    late_planes = planes_of(devices, shard_len, *span(UP2, HEADB), plane_size)
    half_seats = plane_size // 2

    def sums_out(planes):
        return [((half_seats * len(planes), tall, LANES), kind) for kind in (f32, bf16)]

    late_args = (da2, normal2, dv2, gated2, du, top, dy, skip)
    hbm = pl.BlockSpec(memory_space=pltpu.HBM)
    late_keep, late_send = call(
        lambda *refs: late_flat_kernel(devices, shard_len, plane_size, late_planes, *refs),
        sums_out(late_planes),
        ins=[smem, vmem, vmem] + [hbm] * 8,
        scratch=[
            *[pltpu.VMEM(value.shape, bf16) for value in late_args],
            pltpu.VMEM((span(UP2, HEADB)[1] - span(UP2, HEADB)[0], LANES), f32), held_room,
            pltpu.VMEM((H2, C2), f32), pltpu.VMEM((C2, H2), f32), pltpu.VMEM((4, C1, C2), f32), pltpu.VMEM((CI, C1), f32),
            pltpu.SemaphoreType.DMA((8,)),
        ],
        micros=10,
        name="late_flat",
    )(place_row, sums2, hidden2, *late_args)
    back2, late_keep = tie(back2, late_keep)
    slope2, last_cols, first_cols = call(
        lambda *refs: coarse_slope_kernel(half_rows, half_cols, *refs),
        [((low_cells, C2), bf16), ((side, C2), bf16), ((side, C2), bf16)],
        micros=2,
        name="coarse_slope",
    )(got2, back2, vecs2, dx2, conv2, low_rows)

    def taps_back(values, start, count):
        def tile(rows):
            return pl.BlockSpec((rows, LANES), lambda i: (0, i + start))

        return call(
            lambda *refs: coarse_taps_kernel(half_rows, half_cols, *refs),
            [((56, count * LANES), f32)],
            grid=(count,),
            ins=border_tiles(tile) + [tile(low_cells)],
            out_specs=[lane_tile(56)],
            scratch=[
                pltpu.VMEM((low_border, LANES), f32), pltpu.VMEM((edge, LANES), f32), pltpu.VMEM((low_cells, LANES), f32),
            ],
            micros=5,
            name="coarse_taps",
        )(*border2, values)[0]

    split = C2 // LANES // 2
    onward, backward = neighbours("lvl")
    sides = [lax.ppermute(last_cols, "lvl", onward), lax.ppermute(first_cols, "lvl", backward)]
    g_first = taps_back(slope2, 0, split)
    sides, g_first = tie(sides, g_first)
    lower, upper = edges(slope2, *sides)
    ends = lines_out(lower, upper)
    slope2, lower = tie(slope2, lower)
    g_second = taps_back(slope2, split, C2 // LANES - split)
    ends, g_second = tie(ends, g_second)
    dcells = call(
        lambda *refs: coarse_conv_back_kernel(half_rows, half_cols, *refs),
        [((low_cells, C2), bf16)],
        grid=(C2 // LANES,),
        ins=border_tiles(lane_tile) + [TAP_TILE, lane_tile(low_cells)],
        out_specs=[lane_tile(low_cells)],
        scratch=[pltpu.VMEM((low_border, LANES), f32), pltpu.VMEM((edge, LANES), f32)],
        micros=9,
        name="coarse_conv_back",
    )(slope2, *sides, *ends, taps_in2, dtop)[0]

    state, late_steps = scatter_steps(late_keep, late_send, late_planes)
    for step in late_steps[:-1]:
        state = step(state)
    dcells, state = tie(dcells, state)
    dv1, da1, dn1, normal1, sums1, hidden1, sums_low, copies1 = call(
        lambda *refs: fine_back_kernel(cols, *refs),
        [
            ((cells, C1), bf16), ((cells, H1), bf16), ((cells, C1), bf16), ((cells, C1), bf16),
            ((8, C1), f32), ((8, H1), f32), ((8, C2), f32), ((devices, 8, LANES), f32),
        ],
        grid=(half_rows,),
        ins=[
            whole(devices, 8, LANES), band(low_chunk, C2), whole(4, C2, C1), band(chunk, C1), whole(8, C1),
            band(chunk, C1), band(chunk, H1), whole(H1, C1), whole(C1, H1),
        ],
        out_specs=[
            band(chunk, C1), band(chunk, H1), band(chunk, C1), band(chunk, C1), whole(8, C1), whole(8, H1), whole(8, C2),
            whole(devices, 8, LANES),
        ],
        micros=13,
        name="fine_backward",
    )(got1, dcells, downs_four, ds, vecs1, conv1, slope1, up_in1, down_in1)
    da1, state = tie(da1, late_steps[-1](state))
    back1 = swap(copies1)
    early_planes = planes_of(devices, shard_len, *span(UP1, SHIFT2), plane_size)
    early_args = (da1, normal1, dv1, gated1, dcells, patches)
    early_keep, early_send = call(
        lambda *refs: early_flat_kernel(devices, shard_len, plane_size, early_planes, *refs),
        sums_out(early_planes),
        ins=[smem] + [vmem] * 7 + [hbm] * 6,
        scratch=[
            *[pltpu.VMEM(value.shape, bf16) for value in early_args],
            pltpu.VMEM((span(UP1, SHIFT2)[1] - span(UP1, SHIFT2)[0], LANES), f32), held_room,
            pltpu.VMEM((H1, C1), f32), pltpu.VMEM((C1, H1), f32), pltpu.VMEM((C2, H1), f32),
            pltpu.SemaphoreType.DMA((6,)),
        ],
        micros=8,
        name="early_flat",
    )(place_row, got2, sums1, hidden1, sums_low, g_first, g_second, sums2, *early_args)
    early_send, back1 = tie(early_send, back1)
    early_state, early_steps = scatter_steps(early_keep, early_send, early_planes)
    tail_used = -(-span(STEM, SHIFT1)[1] // devices)
    tail_lines = -(-(tail_used + 1) // 8) * 8
    for step in early_steps[:-1]:
        early_state = step(early_state)
    conv1, early_state = tie(conv1, early_state)
    back_args = (conv1, dn1, depth_rows, dv1, turned)
    tail = call(
        lambda *refs: stem_back_kernel(rows, cols, *refs),
        [((devices, tail_lines, LANES), f32)],
        ins=[vmem] * 6 + [hbm] * 5,
        scratch=[
            *[pltpu.VMEM(value.shape, value.dtype) for value in back_args],
            pltpu.VMEM((cells, C1), bf16), pltpu.VMEM((KSIZE * CIN, C1), f32), pltpu.VMEM((LANES, C1), f32),
            pltpu.VMEM((CIN, C1), f32), pltpu.VMEM((devices * tail_used, LANES), f32), pltpu.VMEM((C1, LANES), f32),
            pltpu.SemaphoreType.DMA((5,)),
        ],
        micros=14,
        name="stem_back",
    )(got1, back1, vecs1, near1, stem_in, sums1, *back_args)[0]
    tail, early_state = tie(tail, early_steps[-1](early_state))

    chunk_sum = jnp.sum(swap(tail), axis=0)
    summed = scatter_planes(scatter_last(merge_planes([(state, late_planes), (early_state, early_planes)])))
    mine = lax.dynamic_slice_in_dim(summed.reshape(-1), at, shard_len)
    squares = jnp.sum(mine * mine) + jnp.sum(chunk_sum * chunk_sum)
    loss_part = jnp.sum(sums2[5, :LANES])
    lane = lax.broadcasted_iota(jnp.int32, chunk_sum.shape, 1)
    line = lax.broadcasted_iota(jnp.int32, chunk_sum.shape, 0)
    totals = jnp.where(lane == 0, loss_part, jnp.where(lane == 1, squares, 0.0))
    last = jnp.where(line == tail_used, totals, chunk_sum)
    last = swap(jnp.broadcast_to(last[None], (devices,) + last.shape))
    tail_flat = last[:, :tail_used].reshape(devices * tail_used, LANES)
    totals = jnp.sum(last[:, tail_used, :2], axis=0)
    loss_total, norm = totals[0], jnp.sqrt(totals[1])
    row, lane = count_places(C1)[1]
    count = jnp.sum(got1[:, row, lane])
    tail_flat = jnp.pad(tail_flat, ((0, tall), (0, 0)))
    line = jnp.minimum(me * shard_len // 2048 * 16, devices * tail_used)
    mine_tail = lax.dynamic_slice_in_dim(tail_flat, line, tall).reshape(-1)
    mine = mine + lax.dynamic_slice_in_dim(mine_tail, at, shard_len)
    clipped = mine * jnp.minimum(1.0, CLIP / norm)
    first = BETA_ONE * moment1 + (1.0 - BETA_ONE) * clipped
    second = BETA_TWO * moment2 + (1.0 - BETA_TWO) * clipped * clipped
    ratio = first / (1.0 - BETA_ONE**STEP) / (jnp.sqrt(second / (1.0 - BETA_TWO**STEP)) + ADAM_EPS)
    updated = params - LRATE * (ratio + DECAY * params)
    return (loss_total, count, norm, updated, first, second)


def solution(mesh):
    in_specs = (
        P("lvl", None, "lat", None),
        P("lvl", None, "lat", None),
        P("lat", "lvl"),
        P(),
        P(("lat", "lvl")),
        P(("lat", "lvl")),
        P(("lat", "lvl")),
    )
    out_specs = (P(), P(), P(), P(("lat", "lvl")), P(("lat", "lvl")), P(("lat", "lvl")))
    return jax.shard_map(body, mesh=mesh, in_specs=in_specs, out_specs=out_specs, check_vma=False)
```

```python
import math

import jax
import jax.numpy as jnp
import numpy as np
from jax import lax
from jax.experimental import pallas as pl
from jax.experimental.pallas import tpu as pltpu
from jax.sharding import PartitionSpec as P

CIN = 80
WIDTH = 200
EXPAND = 800
WIDTH2 = 400
EXPAND2 = 1600
KSIZE = 7
TAPS = KSIZE * KSIZE
LEVELS = 19
STEP = 10

CLIP = 0.01
LRATE = 0.05
BETA_ONE = 0.9
BETA_TWO = 0.999
ADAM_EPS = 1e-08
DECAY = 0.1
HEAT_WEIGHT = 40.0
NORM_EPS = 1e-05

AXES = ("lat", "lvl")

CI = 128
C1 = 256
H1 = 896
C2 = 512
H2 = 1664
BLOCKS = 8
LANES = 128
REACH = KSIZE // 2
GROUPS = 17

f32 = jnp.float32
bf16 = jnp.bfloat16
VMEM_LIMIT = 60 * 1024 * 1024


def plane_bits():
    bits = []
    for axis in AXES:
        count = lax.axis_size(axis)
        step = count // 2
        while step >= 1:
            bits.append((axis, count, step))
            step //= 2
    across = [b for b in bits if b[0] == "lat" and b[2] > 1]
    within = [b for b in bits if b not in across]
    return across, within


def exchange(values, axis, count, step):
    return lax.ppermute(values, axis, [(i, i ^ step) for i in range(count)])


def half_rows_of(tall):
    return -(-tall // 32) * 16


def scatter_steps(keep, send, planes):
    _, (first, second, *others) = plane_bits()
    cut = half_rows_of(keep.shape[1])

    def inner(turn, bit):
        def step(state):
            keep, send = state
            if turn > 0:
                half = keep.shape[0] // 2
                keep, send = keep[:half], keep[half:].astype(bf16)
            keep = keep.astype(f32) + exchange(send, *bit).astype(f32)
            return keep, None

        return step

    def outer(state):
        keep, _ = state
        parts = keep.reshape((2, 2, len(planes)) + keep.shape[1:])
        left, right = parts[:, :, :, :cut], parts[:, :, :, cut:]
        left = left[0] + exchange(left[1].astype(bf16), *second).astype(f32)
        right = right[:, 0] + exchange(right[:, 1].astype(bf16), *first).astype(f32)
        return left, right

    steps = [inner(turn, bit) for turn, bit in enumerate(reversed(others))]
    return (keep, send), steps + [outer]


def merge_planes(groups):
    total = lax.axis_size("lat") // 2
    merged = []
    for side in range(2):
        rows = []
        for p in range(total):
            held = [state[side][:, planes.index(p)] for state, planes in groups if p in planes]
            rows.append(sum(held[1:], held[0]))
        merged.append(jnp.stack(rows, axis=1))
    return merged


def scatter_last(state):
    _, (first, second, *_) = plane_bits()
    left, right = state
    left = left[0] + exchange(left[1].astype(bf16), *first).astype(f32)
    right = right[0] + exchange(right[1].astype(bf16), *second).astype(f32)
    return jnp.concatenate([left, right], axis=1)


def tie(first, second):
    return lax.optimization_barrier((first, second))


def scatter_planes(rows):
    count = lax.axis_size("lat")
    plane = lax.axis_index("lat") // 2
    mine = lax.dynamic_index_in_dim(rows, plane, 0, False)
    parts = [
        exchange(lax.dynamic_index_in_dim(rows, plane ^ away, 0, False).astype(bf16), "lat", count, 2 * away)
        for away in range(1, count // 2)
    ]
    for part in parts:
        mine = mine + part.astype(f32)
    return mine


def swap(copies):
    return lax.all_to_all(copies, AXES, 0, 0, tiled=True)


def neighbours(axis):
    ends = lax.axis_size(axis) - 1
    return [(i, i + 1) for i in range(ends)], [(i + 1, i) for i in range(ends)]


def columns_out(arrays, rows, cols):
    onward, back = neighbours("lvl")
    sides = []
    for start, pairs in ((cols - REACH, onward), (0, back)):
        own = [values.reshape(rows, cols, 8, -1)[:, start : start + REACH] for values in arrays]
        own = jnp.concatenate([part.reshape(rows * REACH * 8, -1) for part in own], axis=0)
        sides.append(lax.ppermute(own, "lvl", pairs))
    size = rows * REACH * 8
    return [[side[k * size : (k + 1) * size] for side in sides] for k in range(len(arrays))]


def lines_out(lower, upper):
    onward, back = neighbours("lat")
    return lax.ppermute(lower, "lat", onward), lax.ppermute(upper, "lat", back)


def depth_cells(depth, batch):
    rows, cols = depth.shape
    bands = BLOCKS // batch
    split = depth.reshape(bands, rows // bands, cols).transpose(1, 2, 0)
    return jnp.concatenate([split] * batch, axis=2)


def block_shapes(chans, hidden):
    return [
        (chans, TAPS),
        (chans,),
        (chans,),
        (hidden, chans),
        (hidden,),
        (chans, hidden),
        (chans,),
    ]


def shapes_of():
    return (
        [(WIDTH, CIN)]
        + block_shapes(WIDTH, EXPAND)
        + [(WIDTH2, 4 * WIDTH), (WIDTH2,)]
        + block_shapes(WIDTH2, EXPAND2)
        + [(4 * WIDTH, WIDTH2), (WIDTH,), (CIN, WIDTH), (CIN,)]
    )


def fill(values, *shape):
    return jnp.pad(values, [(0, n - m) for n, m in zip(shape, values.shape)])


def nt(left, right):
    return lax.dot_general(left, right, (((1,), (1,)), ((), ())), preferred_element_type=f32)


def nn(left, right):
    return lax.dot_general(left, right, (((1,), (0,)), ((), ())), preferred_element_type=f32)


def tn(left, right):
    return lax.dot_general(left, right, (((0,), (0,)), ((), ())), preferred_element_type=f32)


def rows8(start, amount):
    return pl.ds(pl.multiple_of(start * 8, 8), amount * 8)


def convolve(source, taps, rows, cols, emit, carry, flip=False):
    width = cols + 2 * REACH
    wide = 4

    def strip(turn, carry):
        col = turn * wide
        totals = [jnp.zeros((wide, 8, LANES), f32) for _ in range(rows)]
        for line in range(rows + 2 * REACH):
            seen = source[rows8(line * width + col, wide + 2 * REACH), :].reshape(wide + 2 * REACH, 8, LANES)
            for q in range(KSIZE):
                for row in range(max(0, line - 2 * REACH), min(rows, line + 1)):
                    tap = (line - row) * KSIZE + q
                    totals[row] = totals[row] + seen[q : q + wide] * taps[TAPS - 1 - tap if flip else tap][None]
        for row in range(rows):
            carry = emit(rows8(row * cols + col, wide), totals[row], carry)
        return carry

    return lax.fori_loop(0, cols // wide, strip, carry)


def row_sum(values):
    return jnp.sum(values, axis=0, keepdims=True)


def spread_rows(values, tiles):
    return [values[:, m * LANES : (m + 1) * LANES] for m in range(tiles)]


def stats_block(first, second, counts):
    tiles = first.shape[1] // LANES
    rows = spread_rows(first, tiles) + spread_rows(second, tiles)
    if len(rows) < 8:
        rows = rows + [jnp.zeros((8 - len(rows), LANES), f32)]
    block = jnp.concatenate(rows, axis=0)
    return block if counts is None else block + counts


def wide_row(total, start, tiles):
    return jnp.concatenate([total[start + m : start + m + 1] for m in range(tiles)], axis=1)


def count_places(width):
    if width == C1:
        return (4, 0), (5, 0)
    return (WIDTH2 // LANES, WIDTH2 % LANES), (WIDTH2 // LANES, WIDTH2 % LANES + 1)


def norm_rows(got, width):
    tiles = width // LANES
    total = jnp.sum(got[...], axis=0)
    (r, c), (ro, co) = count_places(width)
    cells, ocean = total[r : r + 1, c : c + 1], total[ro : ro + 1, co : co + 1]
    lane = lax.broadcasted_iota(jnp.int32, (1, width), 1)
    sums = jnp.where(lane < (WIDTH if width == C1 else WIDTH2), wide_row(total, 0, tiles), 0.0)
    mean = sums / cells
    inverse = lax.rsqrt(wide_row(total, tiles, tiles) / cells - mean * mean + NORM_EPS)
    return mean, inverse, cells, ocean


def gelu_pair(act):
    square = act * act
    flat = 0.7978845608028654
    cube = flat * 0.044715
    half = 0.5 + 0.5 * jnp.tanh(act * (flat + cube * square))
    value = act * half
    return value, half + value * (1.0 - half) * (2.0 * flat + (6.0 * cube) * square)


def quarter(values, rows, cols, p, q):
    chans = values.shape[-1]
    split = values.reshape(rows // 2, 2, cols // 2, 2, 8, chans)
    return split[:, p, :, q].reshape(rows * cols * 2, chans)


def from_quarters(parts, rows, cols):
    chans = parts[0].shape[-1]
    cells = [part.reshape(rows // 2, cols // 2, 8, chans) for part in parts]
    lines = [jnp.stack(cells[2 * p : 2 * p + 2], axis=2) for p in range(2)]
    return jnp.stack(lines, axis=1).reshape(rows * cols * 8, chans)


def call(kernel, outs, grid=(), ins=None, out_specs=None, scratch=(), micros=5, name=None):
    params = dict(out_shape=[jax.ShapeDtypeStruct(s, t) for s, t in outs])
    if ins:
        params.update(in_specs=ins)
    if grid:
        params.update(grid=grid, out_specs=out_specs)
    return pl.pallas_call(
        kernel,
        scratch_shapes=list(scratch),
        compiler_params=pltpu.CompilerParams(vmem_limit_bytes=VMEM_LIMIT),
        cost_estimate=pl.CostEstimate(flops=int(micros * 1.1e9), bytes_accessed=100000, transcendentals=0),
        name=name,
        **params,
    )


def whole(*shape):
    return pl.BlockSpec(shape, lambda i: (0,) * len(shape))


def band(rows, cols):
    return pl.BlockSpec((rows, cols), lambda i: (i, 0))


def lane_tile(rows):
    return pl.BlockSpec((rows, LANES), lambda i: (0, i))


def stats_tile(devices):
    return pl.BlockSpec((devices, 8, LANES), lambda i: (0, 0, i))


TAP_TILE = pl.BlockSpec((TAPS, 8, LANES), lambda i: (0, 0, i))


def conv_sums(source, taps, depth, counts, out, stats, rows, cols, block):
    def emit(place, total, carry):
        flat = total.reshape(-1, LANES)
        out[place, :] = flat
        ocean = depth[place, :] > 0.0
        kept = jnp.where(ocean, flat, 0.0)
        kept_cells = kept.reshape(-1, 8, LANES)
        return (carry[0] + jnp.sum(kept_cells, axis=0), carry[1] + jnp.sum(kept_cells * total, axis=0))

    zero = jnp.zeros((8, LANES), f32)
    first, second = convolve(source, taps, rows, cols, emit, (zero, zero))
    tile = pl.program_id(0)
    tiles = pl.num_programs(0)

    @pl.when(tile == 0)
    def _():
        block[...] = counts[...]

    block[pl.ds(tile, 1), :] += row_sum(first)
    block[pl.ds(C2 // LANES + tile, 1), :] += row_sum(second)

    @pl.when(tile == tiles - 1)
    def _():
        stats[...] = jnp.broadcast_to(block[...][None], stats.shape)


def lay_border(rows, cols, source, held, centre, left, right, above, below):
    width = cols + 2 * REACH
    sides = [left[...].astype(f32), right[...].astype(f32)]
    for row in range(rows):
        start = (row + REACH) * width
        source[rows8(start + REACH, cols), :] = centre[rows8(row * cols, cols), :].astype(f32)
        for side, place in zip(sides, (0, cols + REACH)):
            source[rows8(start + place, REACH), :] = side[row * REACH * 8 : (row + 1) * REACH * 8]
    for t in range(REACH):
        for start, target, way in ((rows + t, t, 1), (REACH + t, rows + REACH + t, 7)):
            line = source[rows8(start * width, width), :].reshape(width, 8, LANES)
            source[rows8(target * width, width), :] = pltpu.roll(line, way, 1).reshape(width * 8, LANES)
    amount = REACH * width
    for part, base in ((above, 0), (below, (rows + REACH) * width * 8 + BLOCKS // 2 - 1)):
        held[...] = part[...].astype(f32)
        for b in range(2):
            values = held[pl.ds(b, amount, stride=2), :]
            source[pl.ds(base + b * (BLOCKS // 2), amount, stride=8), :] = values


def pack_kernel(parts, cols, reach, values, out, tiles, flat):
    total = values.shape[1]
    width = cols + 2 * reach
    lines = out.shape[1]
    depth = values.shape[0] // lines
    count = tiles.shape[0]
    for k in range(count):
        size = min(LANES, total - k * LANES)
        tiles[k, :, :size] = values[:, k * LANES : k * LANES + size].astype(f32)
        if size < LANES:
            tiles[k, :, size:] = jnp.zeros((values.shape[0], LANES - size), f32)
    blank = jnp.zeros((lines, LANES), f32)
    for row in range(depth):
        pieces = [tiles[k, pl.ds(row, lines, stride=depth), :] for k in range(count)]
        wide = jnp.concatenate([blank] + pieces + [blank], axis=1)
        for part in range(parts):
            start = LANES + part * cols - reach
            flat[part, :, row * width : (row + 1) * width] = wide[:, start : start + width]
    for part in range(parts):
        out[part] = flat[part].astype(bf16)


def unpack_cells(packed, parts, first, amount, cells, across):
    lines = packed.shape[1]
    chans = lines // BLOCKS
    for part in range(parts):
        across[part] = packed[part, :, first : first + amount].astype(f32).T.astype(bf16)
    source = lax.broadcasted_iota(jnp.int32, (lines, LANES), 0)
    target = lax.broadcasted_iota(jnp.int32, (lines, LANES), 1)
    for s in range(BLOCKS):
        total = jnp.zeros((amount, LANES), f32)
        for part in range(parts):
            pick = ((target - part * chans) * BLOCKS + s == source).astype(bf16)
            total = total + nn(across[part], pick)
        cells[pl.ds(s, amount, stride=BLOCKS), :] = total


def targets_kernel(parts, first, packed, out, cells, across):
    unpack_cells(packed, parts, first, across.shape[1], cells, across)
    out[...] = cells[...].astype(bf16)


def fields_kernel(parts, rows, cols, packed, cells, lower, upper, held, across):
    unpack_cells(packed, parts, 0, across.shape[1], cells, across)
    width = cols + 2 * REACH
    room = -(-width // 8) * 8
    held[...] = jnp.zeros(held.shape, f32)
    for out, low, band in ((lower, rows - REACH, BLOCKS // 2 - 1), (upper, 0, 0)):
        for b in range(2):
            for t in range(REACH):
                start = (low + t) * width * 8 + band + b * (BLOCKS // 2)
                at = (b * REACH + t) * room
                held[at : at + width, :] = cells[pl.ds(start, width, stride=8), :]
        out[...] = held[...].astype(bf16)


def lay_ends(rows, cols, cells, above, below, ends):
    width = cols + 2 * REACH
    room = -(-width // 8) * 8
    line = width * 8
    for t in range(REACH):
        for k, row, way in ((t, rows - REACH + t, 1), (REACH + t, t, 7)):
            values = cells[row * line : (row + 1) * line, :].reshape(width, 8, LANES)
            ends[k * line : (k + 1) * line, :] = pltpu.roll(values, way, 1).reshape(line, LANES)
    for part, base, band in ((above, 0, 0), (below, REACH, BLOCKS // 2 - 1)):
        values = part[...].astype(f32)
        for b in range(2):
            for t in range(REACH):
                at = (b * REACH + t) * room
                start = (base + t) * line + band + b * (BLOCKS // 2)
                ends[pl.ds(start, width, stride=8), :] = values[at : at + width]


def lay_shifted(rows, cols, cells, ends, out, col, across):
    line = (cols + 2 * REACH) * 8
    total = rows + 2 * REACH
    amount = cols * 8
    lane = lax.broadcasted_iota(jnp.int32, (amount, LANES), 1)

    def values(row, col):
        if row >= total:
            return jnp.zeros((amount, LANES), f32)
        if row < REACH:
            ref, start = ends, row * line
        elif row < REACH + rows:
            ref, start = cells, (row - REACH) * line
        else:
            ref, start = ends, (row - rows) * line
        return ref[start + col * 8 : start + col * 8 + amount, :]

    for row in range(total):
        near = values(row, col)
        middle = values(row + 1, col) if across else values(row, col + 1)
        last = values(row + 2, col) if across else values(row, col + 2)
        middle = pltpu.roll(middle, CIN, 1)
        last = pltpu.roll(last, 2 * CIN - LANES, 1)
        place = slice(row * amount, (row + 1) * amount)
        out[place, :LANES] = jnp.where(lane < CIN, near, middle).astype(bf16)
        out[place, LANES:] = jnp.where(lane < 2 * CIN - LANES, middle, last).astype(bf16)


def wide_stem(stem):
    return jnp.concatenate([stem.astype(f32), jnp.zeros((C1, C1 - CI), f32)], axis=1)


def triple_stem(stem):
    wide = wide_stem(stem)
    return wide + pltpu.roll(wide, CIN, 1) + pltpu.roll(wide, 2 * CIN, 1)


def stem_kernel(
    rows, cols, cells, above, below, near, stem, pick, depth, counts, hzero, out, stats,
    weights, wide, sums, ends, first, second, third,
):
    amount = cols * 8
    step = pl.program_id(0)
    size = out.shape[0]

    @pl.when(step == 0)
    def _():
        lay_ends(rows, cols, cells, above, below, ends)
        lay_shifted(rows, cols, cells, ends, first, 0, False)
        lay_shifted(rows, cols, cells, ends, second, REACH, False)
        lay_shifted(rows, cols, cells, ends, third, 2 * REACH, True)
        stem3 = triple_stem(stem[...])
        for index in range(GROUPS):
            both = nt(near[...], pick[index]) * stem3
            weights[index * C1 : (index + 1) * C1, :] = both.astype(bf16)
        wide[...] = wide_stem(stem[...]).astype(bf16)
        sums[...] = jnp.zeros(sums.shape, f32)

    def place(shift):
        return pl.ds(pl.multiple_of(step * size + shift * amount, amount), size)

    total = jnp.zeros((size, C1), f32)
    for p in range(KSIZE):
        total = total + nt(first[place(p), :], weights[p * C1 : (p + 1) * C1, :])
        total = total + nt(second[place(p), :], weights[(KSIZE + p) * C1 : (KSIZE + p + 1) * C1, :])
    for k in range(3):
        at = (2 * KSIZE + k) * C1
        total = total + nt(third[place(3 * k), :], weights[at : at + C1, :])
    out[...] = total
    hzero[...] = nt(second[place(REACH), :], wide[...]).astype(bf16)
    ocean = depth[...] > 0.0
    kept = jnp.where(jnp.concatenate([ocean, ocean], axis=1), total, 0.0)
    sums[0:1, :] += row_sum(kept)
    sums[1:2, :] += row_sum(kept * total)

    @pl.when(step == pl.num_programs(0) - 1)
    def _():
        stats[...] = jnp.broadcast_to(stats_block(sums[0:1, :], sums[1:2, :], counts[...])[None], stats.shape)


def edge_kernel(rows, cols, count, *refs):
    inputs, (lower, upper, held, edge) = refs[: 3 * count], refs[3 * count :]
    width = cols + 2 * REACH
    lines = edge_lines(cols)
    amount = rows * cols * 8
    side = rows * REACH * 8
    for k in range(count):
        for tile in range(C2 // LANES):
            lanes = slice(tile * LANES, (tile + 1) * LANES)
            for ref, start, size in zip(inputs[3 * k : 3 * k + 3], (0, amount, amount + side), (amount, side, side)):
                held[start : start + size, :] = ref[:, lanes].astype(f32)
            for out, low, band in ((lower, rows - REACH, BLOCKS // 2 - 1), (upper, 0, 0)):
                edge[lines - 16 :, :] = jnp.zeros((16, LANES), f32)
                for t in range(REACH):
                    for b in range(2):
                        s = band + b * (BLOCKS // 2)
                        at = t * width * 2 + b
                        for start, wide, col in ((amount, REACH, 0), (0, cols, REACH), (amount + side, REACH, REACH + cols)):
                            values = held[pl.ds(start + (low + t) * wide * 8 + s, wide, stride=8), :]
                            edge[pl.ds(at + 2 * col, wide, stride=2), :] = values
                out[k * lines : (k + 1) * lines, lanes] = edge[...].astype(bf16)


def edge_lines(cols):
    return -(-REACH * (cols + 2 * REACH) * 2 // 16) * 16


def coarse_conv_kernel(rows, cols, centre, left, right, above, below, taps, depth, counts, out, stats, source, held, block):
    lay_border(rows, cols, source, held, centre, left, right, above, below)
    conv_sums(source, taps, depth, counts, out, stats, rows, cols, block)


def fine_kernel(cols, got, conv, hzero, vecs, bias_rows, up, up_bias, down, perm, downs, down_rows, hone, gated, slope, patches, coarse, held):
    mean, inverse, _, _ = norm_rows(got, C1)
    scale = inverse * vecs[0:1]
    for part in range(2):
        place = pl.ds(part * cols * 8, cols * 8)
        normal = ((conv[place, :] - mean) * scale + vecs[1:2]).astype(bf16)
        act = nt(normal, up[...]) + up_bias[...]
        value, bend = gelu_pair(act)
        value = value.astype(bf16)
        gated[place, :] = value
        slope[place, :] = bend.astype(bf16)
        branch = nt(value, down[...]) + bias_rows[0:1]
        full = (hzero[place, :].astype(f32) + branch).astype(bf16)
        hone[place, :] = full
        held[place, :] = full.astype(f32)
    cells = held[...]
    mixed = jnp.zeros((cols * 4, H1), f32)
    for p in range(2):
        for q in range(2):
            mixed = mixed + nn(quarter(cells, 2, cols, p, q).astype(bf16), perm[p * 2 + q])
    mixed = mixed.astype(bf16)
    patches[...] = mixed
    coarse[...] = (nt(mixed, downs[...]) + down_rows[0:1]).astype(bf16)


def middle_kernel(
    cols, got, conv, cells, vecs, up, up_bias, down, ups, fine_rows, head, last_rows, tables, hone, targets, depth,
    skip_out, top_out, dy_out, ds_out, du_out, dtop_out, dv_out, gated_out, da_out, normal_out, dx_out,
    sums, hidden_sums, copies,
):
    mean, inverse, _, ocean_count = norm_rows(got, C2)
    scale = inverse * vecs[0:1]
    centred = conv[...] - mean
    normal = (centred * scale + vecs[1:2]).astype(bf16)
    normal_out[...] = normal
    value, bend = gelu_pair(nt(normal, up[...]) + up_bias[...])
    value = value.astype(bf16)
    gated_out[...] = value
    top = (cells[...].astype(f32) + nt(value, down[...]) + vecs[2:3]).astype(bf16)
    top_out[...] = top
    raised = from_quarters([nt(top, ups[k]) + fine_rows[0:1] for k in range(4)], 2, cols)
    skip = (hone[...].astype(f32) + raised).astype(bf16)
    skip_out[...] = skip
    err = nt(skip, head[...]) + last_rows[0:1] - targets[...].astype(f32)
    deep = depth[...]
    ocean = tables[0:1] < deep
    heat_take = tables[1:2]
    err = jnp.where(ocean, err, 0.0)
    heat = jnp.sum(heat_take * err, axis=1, keepdims=True)
    heat = jnp.where(deep > 0.0, heat, 0.0)
    loss = row_sum(err * err) + (HEAT_WEIGHT / LANES) * row_sum(heat * heat)
    dy = jnp.where(ocean, err + HEAT_WEIGHT * heat_take * heat, 0.0) * (2.0 / ocean_count)
    dy = dy.astype(bf16)
    dy_out[...] = dy
    ds = nn(dy, head[...])
    ds_out[...] = ds
    dtop = jnp.zeros(top.shape, f32)
    du_sum = jnp.zeros((1, C1), f32)
    for k in range(4):
        du = quarter(ds, 2, cols, k // 2, k % 2).astype(bf16)
        du_out[k] = du
        du_sum = du_sum + row_sum(du.astype(f32))
        dtop = dtop + nn(du, ups[k])
    dtop_out[...] = dtop
    dv = dtop.astype(bf16)
    dv_out[...] = dv
    da = (nn(dv, down[...]) * bend).astype(bf16)
    da_out[...] = da
    dn = nn(da, up[...])
    dx_out[...] = dn * vecs[0:1]

    @pl.when(pl.program_id(0) == 0)
    def _():
        sums[...] = jnp.zeros(sums.shape, f32)
        hidden_sums[...] = jnp.zeros(hidden_sums.shape, f32)

    sums[0:1, :] += row_sum(dn)
    sums[1:2, :] += row_sum(dn * centred)
    sums[2:3, :] += row_sum(dv.astype(f32))
    sums[3:4, :C1] += du_sum
    sums[4:5, :CI] += row_sum(dy.astype(f32))
    sums[5:6, :LANES] += loss
    hidden_sums[0:1, :] += row_sum(da.astype(f32))

    @pl.when(pl.program_id(0) == pl.num_programs(0) - 1)
    def _():
        copies[...] = jnp.broadcast_to(stats_block(sums[0:1, :], sums[1:2, :], None)[None], copies.shape)


def backward_rows(got, back, gain, width):
    mean, inverse, cells, _ = norm_rows(got, width)
    tiles = width // LANES
    total = jnp.sum(back[...], axis=0)
    total_a = gain * wide_row(total, 0, tiles)
    total_b = gain * wide_row(total, tiles, tiles)
    dvar = -0.5 * inverse * inverse * inverse * total_b
    first = (-inverse * total_a - 2.0 * mean * dvar) / cells
    second = 2.0 * dvar / cells
    return inverse, first, second


def coarse_slope_kernel(rows, cols, got, back, vecs, dx, conv, depth, out, last, first_out):
    inverse, first, second = backward_rows(got, back, vecs[0:1], C2)
    ocean = depth[...] > 0.0
    ocean = jnp.concatenate([ocean] * (C2 // LANES), axis=1)
    value = dx[...] * inverse + jnp.where(ocean, first + conv[...] * second, 0.0)
    out[...] = value.astype(bf16)
    for ref, start in ((last, cols - REACH), (first_out, 0)):
        places = [(row * cols + start) * 8 for row in range(rows)]
        ref[...] = jnp.concatenate([value[at : at + REACH * 8] for at in places], axis=0).astype(bf16)


def coarse_taps_kernel(rows, cols, centre, left, right, above, below, slope, taps_out, source, held, here):
    lay_border(rows, cols, source, held, centre, left, right, above, below)
    here[...] = slope[...].astype(f32)
    taps_out[TAPS:, :] = jnp.zeros((taps_out.shape[0] - TAPS, LANES), f32)
    width = cols + 2 * REACH
    for p in range(KSIZE):

        def line(row, sums):
            own = here[rows8(row * cols, cols), :].reshape(cols, 8, LANES)
            seen = source[rows8((row + p) * width, width), :].reshape(width, 8, LANES)
            return tuple(sums[q] + jnp.sum(seen[q : q + cols] * own, axis=0) for q in range(KSIZE))

        zero = jnp.zeros((8, LANES), f32)
        sums = lax.fori_loop(0, rows, line, (zero,) * KSIZE)
        for q in range(KSIZE):
            taps_out[p * KSIZE + q : p * KSIZE + q + 1, :] = row_sum(sums[q])


def coarse_conv_back_kernel(rows, cols, centre, left, right, above, below, taps, dtop, dcells, slope, held):
    lay_border(rows, cols, slope, held, centre, left, right, above, below)

    def emit(place, total, carry):
        dcells[place, :] = (dtop[place, :] + total.reshape(-1, LANES)).astype(bf16)
        return carry

    convolve(slope, taps, rows, cols, emit, 0, flip=True)


def fine_back_kernel(
    cols, got, dcells, downs, ds, vecs, conv, slope, up, down, dv_out, da_out, dn_out, normal_out, sums, hidden_sums, coarse_sums, copies
):
    mean, inverse, _, _ = norm_rows(got, C1)
    dlow = dcells[...]
    dh = ds[...] + from_quarters([nn(dlow, downs[k]) for k in range(4)], 2, cols)
    dv = dh.astype(bf16)
    dv_out[...] = dv

    @pl.when(pl.program_id(0) == 0)
    def _():
        sums[...] = jnp.zeros(sums.shape, f32)
        hidden_sums[...] = jnp.zeros(hidden_sums.shape, f32)
        coarse_sums[...] = jnp.zeros(coarse_sums.shape, f32)

    coarse_sums[0:1, :] += row_sum(dlow.astype(f32))
    sums[2:3, :] += row_sum(dv.astype(f32))
    for part in range(2):
        place = pl.ds(part * cols * 8, cols * 8)
        centred = conv[place, :] - mean
        normal_out[place, :] = (centred * (inverse * vecs[0:1]) + vecs[1:2]).astype(bf16)
        da = (nn(dv_out[place, :], down[...]) * slope[place, :].astype(f32)).astype(bf16)
        da_out[place, :] = da
        hidden_sums[0:1, :] += row_sum(da.astype(f32))
        dn = nn(da, up[...])
        dn_out[place, :] = dn.astype(bf16)
        sums[0:1, :] += row_sum(dn)
        sums[1:2, :] += row_sum(dn * centred)

    @pl.when(pl.program_id(0) == pl.num_programs(0) - 1)
    def _():
        copies[...] = jnp.broadcast_to(stats_block(sums[0:1, :], sums[1:2, :], None)[None], copies.shape)


def turn_kernel(rows, cols, cells, above, below, out, ends):
    line = (cols + 2 * REACH) * 8
    amount = cols * 8
    lay_ends(rows, cols, cells, above, below, ends)
    for row in range(rows + 2 * REACH):
        if row < REACH:
            values = ends[row * line : (row + 1) * line, :]
        elif row < REACH + rows:
            values = cells[(row - REACH) * line : (row - REACH + 1) * line, :]
        else:
            values = ends[(row - rows) * line : (row - rows + 1) * line, :]
        across = values.T[:CIN]
        for q in range(KSIZE):
            piece = across[:, q * 8 : q * 8 + amount].astype(bf16)
            out[q * CIN : (q + 1) * CIN, row * amount : (row + 1) * amount] = piece


def fetch(sources, rooms, sems):
    return [pltpu.make_async_copy(a, b, sems.at[k]) for k, (a, b) in enumerate(zip(sources, rooms))]


def start(copies):
    for copy in copies:
        copy.start()


def wait(copies):
    for copy in copies:
        copy.wait()


def stem_back_kernel(rows, cols, got, back, vecs, near, stem, sums, conv, dn, depth, dv, shifted, tail, *scratch):
    rooms, (slope, acc, tap_acc, stem_acc, lines, held, sems) = scratch[:5], scratch[5:]
    copies = fetch((conv, dn, depth, dv, shifted), rooms, sems)
    start(copies)
    conv, dn, depth, dv, shifted = rooms
    amount = cols * 8
    inverse, first, second = backward_rows(got, back, vecs[0:1], C1)
    scale = inverse * vecs[0:1]
    taps = near[...].astype(f32).T
    stem_turned = stem[...].astype(f32).T
    wait(copies[:3])

    def slopes(row, carry):
        place = pl.ds(pl.multiple_of(row * amount, amount), amount)
        ocean = depth[place, :] > 0.0
        ocean = jnp.concatenate([ocean, ocean], axis=1)
        value = dn[place, :].astype(f32) * scale + jnp.where(ocean, first + conv[place, :] * second, 0.0)
        slope[place, :] = value.astype(bf16)
        return carry

    lax.fori_loop(0, rows, slopes, 0)
    wait(copies[3:])
    total = rows * amount
    straight = shifted[REACH * CIN : (REACH + 1) * CIN, REACH * amount : REACH * amount + total]
    stem_acc[...] = nn(straight, dv[...])
    tap_acc[...] = jnp.zeros(tap_acc.shape, f32)
    for p in range(KSIZE):
        acc[...] = nn(shifted[:, p * amount : p * amount + total], slope[...])
        sum_here = stem_acc[...]
        for q in range(KSIZE):
            tap = p * KSIZE + q
            part = acc[q * CIN : (q + 1) * CIN, :]
            sum_here = sum_here + part * taps[tap : tap + 1]
            tap_acc[tap : tap + 1, :] = row_sum(part * stem_turned[:CIN])
        stem_acc[...] = sum_here
    acc[:CIN, :] = stem_acc[...]
    acc[CIN : 2 * LANES, :] = jnp.zeros((2 * LANES - CIN, C1), f32)
    lines[...] = jnp.zeros(lines.shape, f32)
    turned = acc[:LANES, :].T
    acc[:C1, :LANES] = turned
    write_matrix(lines, 0, STEM, held, acc)
    held[:C1, :] = tap_acc[...].T
    write_short(lines, offsets()[TAPS1], WIDTH, TAPS, lambda r: held[r : r + 1, :])
    write_row(lines, 0, GAIN1, norm_row(got, sums, C1))
    write_row(lines, 0, SHIFT1, row_of(sums, 0))
    used = lines.shape[0] // tail.shape[0]
    for k in range(tail.shape[0]):
        tail[k, :used] = lines[k * used : (k + 1) * used, :]
        tail[k, used:] = jnp.zeros((tail.shape[1] - used, LANES), f32)


def period(length):
    return LANES // math.gcd(length, LANES)


def offsets():
    starts = []
    start = 0
    for shape in shapes_of():
        starts.append(start)
        start += math.prod(shape)
    return starts


def shard_places(devices, shard_len):
    firsts = [e * shard_len // 2048 * 16 for e in range(devices)]
    needed = [(e * shard_len % 2048 + shard_len + 2047) // 2048 * 16 for e in range(devices)]
    return firsts, max(needed)


def lane_ids(rows):
    return lax.broadcasted_iota(jnp.int32, (rows, LANES), 1)


def turn_lanes(values, amount):
    amount = amount % LANES
    return values if amount == 0 else pltpu.roll(values, amount, 1)


def read_rows(lines, base, rows, length, put):
    cycle = period(length)
    count = rows // cycle
    step = cycle * length // LANES
    lane = lane_ids(count)
    tiles = -(-length // LANES)
    for s in range(cycle):
        start = base + s * length
        line, phase = start // LANES, start % LANES
        held = [
            lines[pl.ds(line + k, count, stride=step), :] for k in range(-(-(phase + length) // LANES))
        ]
        for m in range(tiles):
            value = held[m]
            if phase and m + 1 < len(held):
                value = jnp.where(lane >= phase, value, held[m + 1])
            value = turn_lanes(value, -phase)
            if length - m * LANES < LANES:
                value = jnp.where(lane < length - m * LANES, value, 0.0)
            put(s, cycle, count, m, value)


def read_vector(lines, base, length, put):
    line, phase = base // LANES, base % LANES
    lane = lane_ids(1)
    for m in range(-(-length // LANES)):
        value = lines[line + m : line + m + 1, :]
        if phase and phase + length > (m + 1) * LANES:
            value = jnp.where(lane >= phase, value, lines[line + m + 1 : line + m + 2, :])
        value = turn_lanes(value, -phase)
        if length - m * LANES < LANES:
            value = jnp.where(lane < length - m * LANES, value, 0.0)
        put(m, value)


def write_rows(lines, base, rows, length, get):
    cycle = period(length)
    count = rows // cycle
    step = cycle * length // LANES
    line, phase = base // LANES, base % LANES
    for k in range(step):
        shared = k == 0 and phase > 0
        amount = count + 1 if shared else count
        lane = lane_ids(amount)
        total = None
        at = 0
        while at < LANES:
            place = k * LANES - phase + at
            row, col = place // length, place % length
            run = min(length - col, LANES - at)
            tile = col // LANES
            value = get(row, cycle, amount, tile)
            if col % LANES + run > LANES:
                value = jnp.where(lane >= col % LANES, value, get(row, cycle, amount, tile + 1))
            value = turn_lanes(value, at - col)
            total = value if total is None else jnp.where(lane >= at, value, total)
            at += run
        put_lines(lines, line + k, amount, step, total, shared)


def put_lines(lines, line, amount, step, values, shared):
    if not shared:
        lines[pl.ds(line, amount, stride=step), :] = values
        return
    before = lines[line : line + 1, :]
    lines[pl.ds(line, amount, stride=step), :] = values
    lines[line : line + 1, :] = lines[line : line + 1, :] + before


def write_vector(lines, base, length, get):
    line, phase = base // LANES, base % LANES
    lane = lane_ids(1)
    tiles = -(-length // LANES)
    zero = jnp.zeros((1, LANES), f32)
    for k in range(-(-(phase + length) // LANES)):
        value = get(k) if k < tiles else zero
        if phase:
            earlier = get(k - 1) if k > 0 else zero
            value = turn_lanes(jnp.where(lane >= LANES - phase, earlier, value), phase)
        if k == 0 and phase:
            value = value + lines[line : line + 1, :]
        lines[line + k : line + k + 1, :] = value


def write_short(lines, base, rows, length, get):
    line, phase = base // LANES, base % LANES
    lane = lane_ids(1)
    for k in range(-(-(phase + rows * length) // LANES)):
        low = k * LANES - phase
        total = jnp.zeros((1, LANES), f32)
        for row in range(max(low // length, 0), min(-(-(low + LANES) // length), rows)):
            at = row * length - low
            value = turn_lanes(get(row), at)
            if at < 0:
                value = jnp.where(lane < at + length, value, 0.0)
            elif at + length > LANES:
                value = jnp.where(lane >= at, value, 0.0)
            total = total + value
        if k == 0 and phase:
            total = total + lines[line : line + 1, :]
        lines[line + k : line + k + 1, :] = total


def read_short(lines, base, rows, length, put):
    lane = lane_ids(1)
    for row in range(rows):
        start = base + row * length
        line, phase = start // LANES, start % LANES
        value = lines[line : line + 1, :]
        if phase + length > LANES:
            value = jnp.where(lane >= phase, value, lines[line + 1 : line + 2, :])
        put(row, jnp.where(lane < length, turn_lanes(value, -phase), 0.0))


STEM, TAPS1, GAIN1, SHIFT1, UP1, UPB1, DOWN1, DOWNB1, DOWNS, DOWNSB = range(10)
TAPS2, GAIN2, SHIFT2, UP2, UPB2, DOWN2, DOWNB2, UPS, UPSB, HEAD, HEADB = range(10, 21)


def planes_of(devices, shard_len, low, high, plane_size):
    firsts, tall = shard_places(devices, shard_len)
    found = {e // plane_size for e in range(devices) if firsts[e] < high and firsts[e] + tall > low}
    return sorted(found)


def collect(devices, shard_len, blocks, lines, low, high):
    firsts, tall = shard_places(devices, shard_len)
    started = False
    for e in range(devices):
        end = firsts[e + 1] + 16 if e + 1 < devices else firsts[e] + tall
        if end <= low or firsts[e] >= high:
            continue
        first = firsts[e] - low
        skip = max(0, -first)
        take = min(tall, high - firsts[e])
        if started:
            lines[pl.ds(first, 16), :] += blocks[e, :16, :].astype(f32)
            skip = 16
        started = True
        if take > skip:
            lines[pl.ds(first + skip, take - skip), :] = blocks[e, skip:take, :].astype(f32)


def seat_of(me, other, devices):
    away = me ^ other
    seat = 0
    bits = devices.bit_length() - 1
    for b in range(bits):
        seat = seat + ((away >> b) & 1) * (1 << (bits - 1 - b))
    return seat


def matrix_out(held, tall, out, tiles, rows):
    for m in range(tiles):
        if tall > rows:
            held[m * tall + rows : (m + 1) * tall, :] = jnp.zeros((tall - rows, LANES), f32)
        out[:, m * LANES : (m + 1) * LANES] = held[m * tall : (m + 1) * tall, :].astype(bf16)


def read_matrix(lines, shift, piece, held, out):
    rows, length = shapes_of()[piece]
    tall = out.shape[0]

    def put(first, stride, count, tile, value):
        held[pl.ds(tile * tall + first, count, stride=stride), :] = value

    read_rows(lines, offsets()[piece] - shift, rows, length, put)
    matrix_out(held, tall, out, -(-length // LANES), rows)


def read_row(lines, shift, piece, out, row):
    def put(tile, value):
        out[row : row + 1, tile * LANES : (tile + 1) * LANES] = value

    read_vector(lines, offsets()[piece] - shift, shapes_of()[piece][0], put)


def read_taps(lines, shift, piece, held, out, tall):
    def put(row, value):
        held[pl.ds(row, 1), :] = value

    rows = shapes_of()[piece][0]
    read_short(lines, offsets()[piece] - shift, rows, TAPS, put)
    held[rows:tall, :] = jnp.zeros((tall - rows, LANES), f32)
    if out is None:
        return
    across = held[:tall, :].T
    for t in range(TAPS):
        out[t] = jnp.broadcast_to(across[t : t + 1, :], (8, tall))


def first_end():
    return -(-offsets()[TAPS2] // 2048) * 16


def rest_start():
    return offsets()[TAPS2] // 2048 * 16


def rest_end():
    return -(-(offsets()[HEADB] + CIN) // 2048) * 16


def stem_params_kernel(parts, stem, near, vecs, lines, held):
    lines[...] = parts[...].astype(f32)
    vecs[...] = jnp.zeros(vecs.shape, f32)
    read_taps(lines, 0, TAPS1, held, None, C1)
    near[...] = held[:C1, :].astype(bf16)
    read_matrix(lines, 0, STEM, held, stem)
    read_row(lines, 0, GAIN1, vecs, 0)
    read_row(lines, 0, SHIFT1, vecs, 1)


def fine_params_kernel(
    devices, shard_len, blocks, perm, up, bias, down, downs, downs_four, down_rows, vecs, lines, held
):
    low, high = span(UP1, DOWNSB)
    shift = low * LANES
    collect(devices, shard_len, blocks, lines, low, high)
    for out in (down_rows, bias, vecs):
        out[...] = jnp.zeros(out.shape, f32)
    read_row(lines, shift, DOWNB1, vecs, 0)
    read_row(lines, shift, UPB1, bias, 0)
    read_row(lines, shift, DOWNSB, down_rows, 0)
    read_matrix(lines, shift, UP1, held, up)
    read_matrix(lines, shift, DOWN1, held, down)
    read_matrix(lines, shift, DOWNS, held, downs)
    for k in range(4):
        downs_four[k] = nt(downs[...], perm[k]).astype(bf16)


def rest_params_kernel(
    devices, shard_len, blocks, taps2, vecs2, up2, bias2, down2, ups_four, vecs1, head, last, lines, held
):
    shift = rest_start() * LANES
    collect(devices, shard_len, blocks, lines, rest_start(), rest_end())
    for out in (vecs1, vecs2, bias2, last):
        out[...] = jnp.zeros(out.shape, f32)
    read_taps(lines, shift, TAPS2, held, taps2, C2)
    read_row(lines, shift, GAIN2, vecs2, 0)
    read_row(lines, shift, SHIFT2, vecs2, 1)
    read_row(lines, shift, DOWNB2, vecs2, 2)
    read_row(lines, shift, UPB2, bias2, 0)
    read_row(lines, shift, UPSB, vecs1, 0)
    read_row(lines, shift, HEADB, last, 0)
    read_matrix(lines, shift, UP2, held, up2)
    read_matrix(lines, shift, DOWN2, held, down2)
    read_matrix(lines, shift, HEAD, held, head)
    tiles = C2 // LANES

    def put(first, stride, count, tile, value):
        k = first % 4
        held[pl.ds((k * tiles + tile) * C1 + first // 4, count, stride=stride // 4), :] = value

    rows, length = shapes_of()[UPS]
    read_rows(lines, offsets()[UPS] - shift, rows, length, put)
    for k in range(4):
        for m in range(tiles):
            at = (k * tiles + m) * C1
            held[at + WIDTH : at + C1, :] = jnp.zeros((C1 - WIDTH, LANES), f32)
            ups_four[k, :, m * LANES : (m + 1) * LANES] = held[at : at + C1, :].astype(bf16)


FRONT = 16


def hold_matrix(held, values, row_tiles, rows):
    tall = rows + 2 * FRONT
    zero = jnp.zeros((FRONT, LANES), f32)
    for m in range(row_tiles):
        at = m * tall
        held[at : at + FRONT, :] = zero
        held[at + FRONT : at + FRONT + rows, :] = values(m)
        held[at + FRONT + rows : at + tall, :] = zero


def write_matrix(lines, shift, piece, held, source):
    rows, length = shapes_of()[piece]
    tall = rows + 2 * FRONT
    hold_matrix(held, lambda m: source[:rows, m * LANES : (m + 1) * LANES], -(-length // LANES), rows)

    def get(first, stride, count, tile):
        return held[pl.ds(tile * tall + FRONT + first, count, stride=stride), :]

    write_rows(lines, offsets()[piece] - shift, rows, length, get)


def write_row(lines, shift, piece, get):
    write_vector(lines, offsets()[piece] - shift, shapes_of()[piece][0], get)


def row_of(source, row):
    return lambda m: source[row : row + 1, m * LANES : (m + 1) * LANES]


def norm_row(got, sums, width):
    _, inverse, _, _ = norm_rows(got, width)
    value = sums[1:2, :] * inverse
    return lambda m: value[:, m * LANES : (m + 1) * LANES]


def scatter_out(devices, shard_len, plane_size, planes, place, lines, low, keep, send):
    firsts, tall = shard_places(devices, shard_len)
    half = plane_size // 2
    for k, plane in enumerate(planes):
        for r in range(plane_size):
            first = firsts[plane * plane_size + r] - low
            start, end = max(first, 0), min(first + tall, lines.shape[0])
            seat = seat_of(place, r, plane_size)

            def put(out, index, kind):
                if end <= start:
                    out[index] = jnp.zeros((tall, LANES), kind)
                    return
                if start > first:
                    out[index, : start - first] = jnp.zeros((start - first, LANES), kind)
                out[index, start - first : end - first] = lines[start:end, :].astype(kind)
                if end < first + tall:
                    out[index, end - first :] = jnp.zeros((first + tall - end, LANES), kind)

            @pl.when(seat < half)
            def _():
                put(keep, seat * len(planes) + k, bf16)

            @pl.when(seat >= half)
            def _():
                put(send, (seat - half) * len(planes) + k, bf16)


def span(first, last):
    end = offsets()[last] + math.prod(shapes_of()[last])
    return offsets()[first] // 2048 * 16, -(-end // 2048) * 16


def clear_ends(lines, low, first, last):
    start = offsets()[first] // LANES - low + 1
    lines[:start, :] = jnp.zeros((start, LANES), f32)
    end = -(-(offsets()[last] + math.prod(shapes_of()[last])) // LANES) - low
    if end < lines.shape[0]:
        lines[end:, :] = jnp.zeros((lines.shape[0] - end, LANES), f32)


def late_flat_kernel(
    devices, shard_len, plane_size, planes, place, sums2, hidden2, da, normal, dv, gated, du, top, dy, skip, keep, send, *scratch
):
    rooms, (lines, held, g_up2, g_down2, g_ups, g_head, sems) = scratch[:8], scratch[8:]
    copies = fetch((da, normal, dv, gated, du, top, dy, skip), rooms, sems)
    da, normal, dv, gated, du, top, dy, skip = rooms
    start(copies[6:])
    start(copies[4:6])
    wait(copies[6:])
    start(copies[:2])
    g_head[...] = tn(dy[...], skip[...])
    wait(copies[4:6])
    start(copies[2:4])
    for k in range(4):
        g_ups[k] = tn(du[k], top[...])
    wait(copies[:2])
    g_up2[...] = tn(da[...], normal[...])
    wait(copies[2:4])
    g_down2[...] = tn(dv[...], gated[...])
    low, _ = span(UP2, HEADB)
    shift = low * LANES
    clear_ends(lines, low, UP2, HEADB)
    write_matrix(lines, shift, UP2, held, g_up2)
    write_row(lines, shift, UPB2, row_of(hidden2, 0))
    write_matrix(lines, shift, DOWN2, held, g_down2)
    write_row(lines, shift, DOWNB2, row_of(sums2, 2))
    rows, length = shapes_of()[UPS]
    tiles = C2 // LANES
    tall = WIDTH + 2 * FRONT
    for k in range(4):
        for m in range(tiles):
            at = (k * tiles + m) * tall
            held[at : at + FRONT, :] = jnp.zeros((FRONT, LANES), f32)
            held[at + FRONT : at + FRONT + WIDTH, :] = g_ups[k, :WIDTH, m * LANES : (m + 1) * LANES]
            held[at + FRONT + WIDTH : at + tall, :] = jnp.zeros((FRONT, LANES), f32)

    def get(first, stride, count, tile):
        at = ((first % 4) * tiles + tile) * tall + FRONT + first // 4
        return held[pl.ds(at, count, stride=stride // 4), :]

    write_rows(lines, offsets()[UPS] - shift, rows, length, get)
    write_row(lines, shift, UPSB, row_of(sums2, 3))
    write_matrix(lines, shift, HEAD, held, g_head)
    write_row(lines, shift, HEADB, row_of(sums2, 4))
    scatter_out(devices, shard_len, plane_size, planes, place[0], lines, low, keep, send)


def early_flat_kernel(
    devices, shard_len, plane_size, planes, place, got2, sums1, hidden1, sums_low, g_taps2, more_taps2, sums2,
    da, normal, dv, gated, dcells, patches, keep, send, *scratch,
):
    rooms, (lines, held, g_up1, g_down1, g_downs, sems) = scratch[:6], scratch[6:]
    copies = fetch((da, normal, dv, gated, dcells, patches), rooms, sems)
    da, normal, dv, gated, dcells, patches = rooms
    start(copies[4:])
    start(copies[2:4])
    wait(copies[4:])
    start(copies[:2])
    g_downs[...] = tn(dcells[...], patches[...])
    wait(copies[2:4])
    g_down1[...] = tn(dv[...], gated[...])
    wait(copies[:2])
    g_up1[...] = tn(da[...], normal[...])
    low, _ = span(UP1, SHIFT2)
    shift = low * LANES
    clear_ends(lines, low, UP1, SHIFT2)
    write_matrix(lines, shift, UP1, held, g_up1)
    write_row(lines, shift, UPB1, row_of(hidden1, 0))
    write_matrix(lines, shift, DOWN1, held, g_down1)
    write_row(lines, shift, DOWNB1, row_of(sums1, 2))
    write_matrix(lines, shift, DOWNS, held, g_downs)
    write_row(lines, shift, DOWNSB, row_of(sums_low, 0))
    across = jnp.concatenate([g_taps2[...], more_taps2[...]], axis=1)
    across = jnp.concatenate([across, jnp.zeros((LANES - across.shape[0], C2), f32)], axis=0).T
    held[:C2, :] = across
    write_short(lines, offsets()[TAPS2] - shift, WIDTH2, TAPS, lambda r: held[r : r + 1, :])
    write_row(lines, shift, GAIN2, norm_row(got2, sums2, C2))
    write_row(lines, shift, SHIFT2, row_of(sums2, 0))
    scatter_out(devices, shard_len, plane_size, planes, place[0], lines, low, keep, send)


def group_taps():
    table = []
    for first in (0, 3):
        for p in range(KSIZE):
            table.append([p * KSIZE + first + t for t in range(3)])
    for k in range(3):
        table.append([(3 * k + t) * KSIZE + 6 if 3 * k + t < KSIZE else -1 for t in range(3)])
    return table


def quarter_lanes():
    at = np.arange(C1)[None, :, None] * 4 + np.arange(4)[:, None, None]
    hot = (at == np.arange(H1)[None, None, :]) & (np.arange(C1) < WIDTH)[None, :, None]
    return hot.astype(jnp.bfloat16)


def tap_lanes():
    table = np.array([line + [-1] for line in group_taps()])
    wanted = table[:, np.arange(C1) // CIN]
    return (wanted[:, :, None] == np.arange(LANES)).astype(jnp.bfloat16)


def body(fields, targets, ocean_depth, thickness_class, params, moment1, moment2):
    shard_len = params.shape[0]
    devices = lax.axis_size(AXES)
    plane_size = 2 * lax.axis_size("lvl")
    me = lax.axis_index(AXES)
    _, tall = shard_places(devices, shard_len)
    at = (me * (shard_len % 2048)) % 2048
    place_row = jnp.broadcast_to(me % plane_size, (1,)).astype(jnp.int32)

    smem = pl.BlockSpec(memory_space=pltpu.SMEM)
    vmem = pl.BlockSpec(memory_space=pltpu.VMEM)
    parts = lax.axis_size("lvl")
    chans, batch, all_rows, all_cols = fields.shape
    bands = BLOCKS // batch
    rows, cols = all_rows // bands, all_cols // parts
    half_rows, half_cols = rows // 2, cols // 2
    cells, low_cells = rows * cols * 8, half_rows * half_cols * 8
    wide_cols = cols + 2 * REACH
    low_border = (half_rows + 2 * REACH) * (half_cols + 2 * REACH) * 8

    def packed(values, reach):
        lanes = rows * (cols + 2 * reach)
        return call(
            lambda *refs: pack_kernel(parts, cols, reach, *refs),
            [((parts, chans * BLOCKS, lanes), bf16)],
            scratch=[
                pltpu.VMEM((-(-all_cols // LANES), chans * batch * all_rows, LANES), f32),
                pltpu.VMEM((parts, chans * BLOCKS, lanes), f32),
            ],
            micros=3,
            name="pack",
        )(values.reshape(-1, all_cols))[0]

    copies, placed = tie(packed(fields, REACH), params)
    field_given = lax.all_to_all(copies, "lvl", 0, 0, tiled=True)
    goal_copies = packed(targets, 0)
    block = lax.dynamic_update_slice(jnp.zeros((tall * LANES,), bf16), placed.astype(bf16), (at,))
    block = block.reshape(tall, LANES)
    gathered = lax.all_gather(block, AXES, axis=0)
    near_shards = 1
    while near_shards < -(-first_end() * LANES // shard_len):
        near_shards *= 2
    chunk_lines = -(-span(STEM, SHIFT1)[1] // (8 * devices)) * 8
    head_lines = chunk_lines * devices
    window = jnp.pad(block, ((head_lines, head_lines), (0, 0)))
    first_line = me * shard_len // 2048 * 16
    window = lax.dynamic_slice_in_dim(window, head_lines - jnp.minimum(first_line, head_lines), head_lines)
    field_given, (window, goal_copies) = tie(field_given, (window, goal_copies))
    chunk = jnp.sum(swap(window.reshape(devices, chunk_lines, LANES)).astype(f32), axis=0).astype(bf16)
    send_room = 2 * REACH * -(-wide_cols // 8) * 8
    field_cells, lower, upper = call(
        lambda *refs: fields_kernel(parts, rows, cols, *refs),
        [((rows * wide_cols * 8, LANES), f32), ((send_room, LANES), bf16), ((send_room, LANES), bf16)],
        scratch=[pltpu.VMEM((send_room, LANES), f32), pltpu.VMEM((parts, rows * wide_cols, chans * BLOCKS), bf16)],
        micros=4,
        name="fields",
    )(field_given)
    chunk, (field_cells, lower, upper) = tie(chunk, (field_cells, lower, upper))
    above, below = lines_out(lower, upper)
    stem_lines = swap(jnp.broadcast_to(chunk[None], (devices,) + chunk.shape)).reshape(head_lines, LANES)
    stem_lines, (above, below, goal_copies) = tie(stem_lines, (above, below, goal_copies))
    goal_given = lax.all_to_all(goal_copies, "lvl", 0, 0, tiled=True)

    deep = depth_cells(ocean_depth, batch)
    depth_rows = jnp.broadcast_to(deep.astype(f32)[..., None], deep.shape + (LANES,)).reshape(cells, LANES)
    low = jnp.max(deep.reshape(half_rows, 2, half_cols, 2, 8), axis=(1, 3))
    low_rows = jnp.broadcast_to(low.astype(f32)[..., None], low.shape + (LANES,)).reshape(low_cells, LANES)
    channel = jnp.arange(CI, dtype=jnp.int32)
    level = jnp.where(channel < 4 * LEVELS, channel // 4, 0)
    level_row = jnp.where(channel < CIN, level, LEVELS + 1).astype(f32)
    thickf = thickness_class.astype(f32)
    onehot = (level[:, None] == jnp.arange(LEVELS, dtype=jnp.int32)[None, :]).astype(f32)
    chosen = ((channel % 4 == 0) & (channel < 4 * LEVELS)).astype(f32)
    heat_take = chosen * jnp.sum(onehot * thickf[None, :], axis=1) / jnp.sum(thickf)
    ocean_cells = jnp.sum((level_row[None, None, :] < ocean_depth.astype(f32)[:, :, None]).astype(f32))
    ocean_cells = batch * ocean_cells
    surface_cells = jnp.sum((deep > 0).astype(f32))
    low_surface = jnp.sum((low > 0).astype(f32))
    index8 = jnp.arange(8)[:, None]
    lane8 = jnp.arange(LANES)[None, :]

    def counts_of(width, cells_count):
        (r, c), (ro, co) = count_places(width)
        at_cells = (index8 == r) & (lane8 == c)
        at_ocean = (index8 == ro) & (lane8 == co)
        return jnp.where(at_cells, cells_count, jnp.where(at_ocean, ocean_cells, 0.0))

    counts1 = counts_of(C1, surface_cells)
    counts2 = counts_of(C2, low_surface)

    tables = jnp.pad(jnp.stack([level_row, heat_take]), ((0, 6), (0, 0)))
    perm, pick = jnp.asarray(quarter_lanes()), jnp.asarray(tap_lanes())
    held_room = pltpu.VMEM((4 * H2, LANES), f32)
    stem_in, near1, vecs1 = call(
        stem_params_kernel,
        [((C1, CI), bf16), ((C1, LANES), bf16), ((8, C1), f32)],
        scratch=[pltpu.VMEM(stem_lines.shape, f32), pltpu.VMEM((2 * C1, LANES), f32)],
        micros=3,
        name="stem_params",
    )(stem_lines)

    smalls = (perm, low_rows, counts1, counts2, tables, place_row, depth_rows, pick)
    field_cells, smalls = tie(field_cells, smalls)
    perm, low_rows, counts1, counts2, tables, place_row, depth_rows, pick = smalls

    ends_room = pltpu.VMEM((2 * REACH * wide_cols * 8, LANES), f32)
    shifted_room = pltpu.VMEM(((rows + 2 * REACH) * cols * 8, C1), bf16)
    hzero, conv1, stats1 = call(
        lambda *refs: stem_kernel(rows, cols, *refs),
        [((cells, C1), bf16), ((cells, C1), f32), ((devices, 8, LANES), f32)],
        grid=(half_rows,),
        ins=[
            whole(rows * wide_cols * 8, LANES), whole(send_room, LANES), whole(send_room, LANES), whole(C1, LANES), whole(C1, CI),
            whole(GROUPS, C1, LANES), band(2 * cols * 8, LANES), whole(8, LANES),
        ],
        out_specs=[band(2 * cols * 8, C1), band(2 * cols * 8, C1), whole(devices, 8, LANES)],
        scratch=[
            pltpu.VMEM((GROUPS * C1, C1), bf16), pltpu.VMEM((C1, C1), bf16), pltpu.VMEM((8, C1), f32),
            ends_room, shifted_room, shifted_room, shifted_room,
        ],
        micros=17,
        name="stem_conv",
    )(field_cells, above, below, near1, stem_in, pick, depth_rows, counts1)
    got1 = swap(stats1)
    hzero, goal_given = tie(hzero, goal_given)
    up_in1, bias_in1, down_in1, downs_in, downs_four, down_rows, bias_rows = call(
        lambda *refs: fine_params_kernel(devices, shard_len, *refs),
        [
            ((H1, C1), bf16), ((1, H1), f32), ((C1, H1), bf16), ((C2, H1), bf16), ((4, C2, C1), bf16), ((8, C2), f32),
            ((8, C1), f32),
        ],
        grid=(1,),
        ins=[whole(near_shards, tall, LANES), whole(4, C1, H1)],
        out_specs=[
            whole(H1, C1), whole(1, H1), whole(C1, H1), whole(C2, H1), whole(4, C2, C1), whole(8, C2), whole(8, C1),
        ],
        scratch=[pltpu.VMEM((span(UP1, DOWNSB)[1] - span(UP1, DOWNSB)[0], LANES), f32), held_room],
        micros=8,
        name="fine_params",
    )(gathered, perm)
    chunk, low_chunk = 2 * cols * 8, half_cols * 8
    hone, gated1, slope1, patches, coarse = call(
        lambda *refs: fine_kernel(cols, *refs),
        [
            ((cells, C1), bf16),
            ((cells, H1), bf16),
            ((cells, H1), bf16),
            ((low_cells, H1), bf16),
            ((low_cells, C2), bf16),
        ],
        grid=(half_rows,),
        ins=[
            whole(devices, 8, LANES), band(chunk, C1), band(chunk, C1), whole(8, C1), whole(8, C1), whole(H1, C1), whole(1, H1),
            whole(C1, H1), whole(4, C1, H1), whole(C2, H1), whole(8, C2),
        ],
        out_specs=[
            band(chunk, C1), band(chunk, H1), band(chunk, H1), band(low_chunk, H1), band(low_chunk, C2),
        ],
        scratch=[pltpu.VMEM((chunk, C1), f32)],
        micros=15,
        name="fine_forward",
    )(got1, conv1, hzero, vecs1, bias_rows, up_in1, bias_in1, down_in1, perm, downs_in, down_rows)

    edge = edge_lines(half_cols)
    side = half_rows * REACH * 8

    def edges(values, left, right):
        return call(
            lambda *refs: edge_kernel(half_rows, half_cols, 1, *refs),
            [((edge, C2), bf16)] * 2,
            scratch=[pltpu.VMEM((low_cells + 2 * side, LANES), f32), pltpu.VMEM((edge, LANES), f32)],
            micros=3,
            name="edge",
        )(values, left, right)

    def border_tiles(tile):
        return [tile(low_cells), tile(side), tile(side), tile(edge), tile(edge)]

    sides = columns_out((coarse,), half_rows, half_cols)[0]
    goal_given, coarse = tie(goal_given, coarse)
    goal = call(
        lambda *refs: targets_kernel(parts, 0, *refs),
        [((cells, LANES), bf16)],
        scratch=[pltpu.VMEM((cells, LANES), f32), pltpu.VMEM((parts, rows * cols, chans * BLOCKS), bf16)],
        micros=4,
        name="targets",
    )(goal_given)[0]
    sides, goal = tie(sides, goal)
    border2 = (coarse, *sides, *lines_out(*edges(coarse, *sides)))
    taps_in2, vecs2, up_in2, bias_in2, down_in2, ups_four, fine_rows, head_in, last_rows = call(
        lambda *refs: rest_params_kernel(devices, shard_len, *refs),
        [
            ((TAPS, 8, C2), f32), ((8, C2), f32), ((H2, C2), bf16), ((1, H2), f32), ((C2, H2), bf16),
            ((4, C1, C2), bf16), ((8, C1), f32), ((CI, C1), bf16), ((8, CI), f32),
        ],
        ins=[vmem],
        scratch=[pltpu.VMEM((rest_end() - rest_start(), LANES), f32), held_room],
        micros=13,
        name="rest_params",
    )(gathered)
    conv2, stats2 = call(
        lambda *refs: coarse_conv_kernel(half_rows, half_cols, *refs),
        [((low_cells, C2), f32), ((devices, 8, LANES), f32)],
        grid=(C2 // LANES,),
        ins=border_tiles(lane_tile) + [TAP_TILE, whole(low_cells, LANES), whole(8, LANES)],
        out_specs=[lane_tile(low_cells), whole(devices, 8, LANES)],
        scratch=[pltpu.VMEM((low_border, LANES), f32), pltpu.VMEM((edge, LANES), f32), pltpu.VMEM((8, LANES), f32)],
        micros=11,
        name="coarse_conv",
    )(*border2, taps_in2, low_rows, counts2)
    got2 = swap(stats2)
    field_cells, stats2 = tie(field_cells, stats2)
    turned = call(
        lambda *refs: turn_kernel(rows, cols, *refs),
        [((KSIZE * CIN, (rows + 2 * REACH) * cols * 8), bf16)],
        scratch=[ends_room],
        micros=8,
        name="turn",
    )(field_cells, above, below)[0]
    conv2, turned = tie(conv2, turned)
    (
        skip, top, dy, ds, du, dtop, dv2, gated2, da2, normal2, dx2, sums2, hidden2, copies2,
    ) = call(
        lambda *refs: middle_kernel(cols, *refs),
        [
            ((cells, C1), bf16), ((low_cells, C2), bf16), ((cells, CI), bf16), ((cells, C1), f32),
            ((4, low_cells, C1), bf16), ((low_cells, C2), f32), ((low_cells, C2), bf16), ((low_cells, H2), bf16),
            ((low_cells, H2), bf16), ((low_cells, C2), bf16), ((low_cells, C2), f32),
            ((8, C2), f32), ((8, H2), f32), ((devices, 8, LANES), f32),
        ],
        grid=(half_rows,),
        ins=[
            whole(devices, 8, LANES), band(low_chunk, C2), band(low_chunk, C2), whole(8, C2), whole(H2, C2), whole(1, H2),
            whole(C2, H2), whole(4, C1, C2), whole(8, C1), whole(CI, C1), whole(8, CI), whole(8, CI), band(chunk, C1),
            band(chunk, CI), band(chunk, LANES),
        ],
        out_specs=[
            band(chunk, C1), band(low_chunk, C2), band(chunk, CI), band(chunk, C1),
            pl.BlockSpec((4, low_chunk, C1), lambda i: (0, i, 0)), band(low_chunk, C2), band(low_chunk, C2),
            band(low_chunk, H2), band(low_chunk, H2), band(low_chunk, C2), band(low_chunk, C2),
            whole(8, C2), whole(8, H2), whole(devices, 8, LANES),
        ],
        micros=20,
        name="middle",
    )(
        got2, conv2, coarse, vecs2, up_in2, bias_in2, down_in2, ups_four, fine_rows, head_in, last_rows, tables, hone, goal,
        depth_rows,
    )
    back2 = swap(copies2)
    late_planes = planes_of(devices, shard_len, *span(UP2, HEADB), plane_size)
    half_seats = plane_size // 2

    def sums_out(planes):
        return [((half_seats * len(planes), tall, LANES), kind) for kind in (bf16, bf16)]

    late_args = (da2, normal2, dv2, gated2, du, top, dy, skip)
    hbm = pl.BlockSpec(memory_space=pltpu.HBM)
    late_keep, late_send = call(
        lambda *refs: late_flat_kernel(devices, shard_len, plane_size, late_planes, *refs),
        sums_out(late_planes),
        ins=[smem, vmem, vmem] + [hbm] * 8,
        scratch=[
            *[pltpu.VMEM(value.shape, bf16) for value in late_args],
            pltpu.VMEM((span(UP2, HEADB)[1] - span(UP2, HEADB)[0], LANES), f32), held_room,
            pltpu.VMEM((H2, C2), f32), pltpu.VMEM((C2, H2), f32), pltpu.VMEM((4, C1, C2), f32), pltpu.VMEM((CI, C1), f32),
            pltpu.SemaphoreType.DMA((8,)),
        ],
        micros=10,
        name="late_flat",
    )(place_row, sums2, hidden2, *late_args)
    back2, late_keep = tie(back2, late_keep)
    slope2, last_cols, first_cols = call(
        lambda *refs: coarse_slope_kernel(half_rows, half_cols, *refs),
        [((low_cells, C2), bf16), ((side, C2), bf16), ((side, C2), bf16)],
        micros=2,
        name="coarse_slope",
    )(got2, back2, vecs2, dx2, conv2, low_rows)

    def taps_back(values, start, count):
        def tile(rows):
            return pl.BlockSpec((rows, LANES), lambda i: (0, i + start))

        return call(
            lambda *refs: coarse_taps_kernel(half_rows, half_cols, *refs),
            [((56, count * LANES), f32)],
            grid=(count,),
            ins=border_tiles(tile) + [tile(low_cells)],
            out_specs=[lane_tile(56)],
            scratch=[
                pltpu.VMEM((low_border, LANES), f32), pltpu.VMEM((edge, LANES), f32), pltpu.VMEM((low_cells, LANES), f32),
            ],
            micros=5,
            name="coarse_taps",
        )(*border2, values)[0]

    split = C2 // LANES // 2
    onward, backward = neighbours("lvl")
    sides = [lax.ppermute(last_cols, "lvl", onward), lax.ppermute(first_cols, "lvl", backward)]
    g_first = taps_back(slope2, 0, split)
    sides, g_first = tie(sides, g_first)
    lower, upper = edges(slope2, *sides)
    ends = lines_out(lower, upper)
    slope2, lower = tie(slope2, lower)
    g_second = taps_back(slope2, split, C2 // LANES - split)
    ends, g_second = tie(ends, g_second)
    dcells = call(
        lambda *refs: coarse_conv_back_kernel(half_rows, half_cols, *refs),
        [((low_cells, C2), bf16)],
        grid=(C2 // LANES,),
        ins=border_tiles(lane_tile) + [TAP_TILE, lane_tile(low_cells)],
        out_specs=[lane_tile(low_cells)],
        scratch=[pltpu.VMEM((low_border, LANES), f32), pltpu.VMEM((edge, LANES), f32)],
        micros=9,
        name="coarse_conv_back",
    )(slope2, *sides, *ends, taps_in2, dtop)[0]

    state, late_steps = scatter_steps(late_keep, late_send, late_planes)
    for step in late_steps[:-1]:
        state = step(state)
    dcells, state = tie(dcells, state)
    dv1, da1, dn1, normal1, sums1, hidden1, sums_low, copies1 = call(
        lambda *refs: fine_back_kernel(cols, *refs),
        [
            ((cells, C1), bf16), ((cells, H1), bf16), ((cells, C1), bf16), ((cells, C1), bf16),
            ((8, C1), f32), ((8, H1), f32), ((8, C2), f32), ((devices, 8, LANES), f32),
        ],
        grid=(half_rows,),
        ins=[
            whole(devices, 8, LANES), band(low_chunk, C2), whole(4, C2, C1), band(chunk, C1), whole(8, C1),
            band(chunk, C1), band(chunk, H1), whole(H1, C1), whole(C1, H1),
        ],
        out_specs=[
            band(chunk, C1), band(chunk, H1), band(chunk, C1), band(chunk, C1), whole(8, C1), whole(8, H1), whole(8, C2),
            whole(devices, 8, LANES),
        ],
        micros=13,
        name="fine_backward",
    )(got1, dcells, downs_four, ds, vecs1, conv1, slope1, up_in1, down_in1)
    da1, state = tie(da1, late_steps[-1](state))
    back1 = swap(copies1)
    early_planes = planes_of(devices, shard_len, *span(UP1, SHIFT2), plane_size)
    early_args = (da1, normal1, dv1, gated1, dcells, patches)
    early_keep, early_send = call(
        lambda *refs: early_flat_kernel(devices, shard_len, plane_size, early_planes, *refs),
        sums_out(early_planes),
        ins=[smem] + [vmem] * 7 + [hbm] * 6,
        scratch=[
            *[pltpu.VMEM(value.shape, bf16) for value in early_args],
            pltpu.VMEM((span(UP1, SHIFT2)[1] - span(UP1, SHIFT2)[0], LANES), f32), held_room,
            pltpu.VMEM((H1, C1), f32), pltpu.VMEM((C1, H1), f32), pltpu.VMEM((C2, H1), f32),
            pltpu.SemaphoreType.DMA((6,)),
        ],
        micros=8,
        name="early_flat",
    )(place_row, got2, sums1, hidden1, sums_low, g_first, g_second, sums2, *early_args)
    early_send, back1 = tie(early_send, back1)
    early_state, early_steps = scatter_steps(early_keep, early_send, early_planes)
    tail_used = -(-span(STEM, SHIFT1)[1] // devices)
    tail_lines = -(-(tail_used + 1) // 8) * 8
    for step in early_steps[:-1]:
        early_state = step(early_state)
    conv1, early_state = tie(conv1, early_state)
    back_args = (conv1, dn1, depth_rows, dv1, turned)
    tail = call(
        lambda *refs: stem_back_kernel(rows, cols, *refs),
        [((devices, tail_lines, LANES), f32)],
        ins=[vmem] * 6 + [hbm] * 5,
        scratch=[
            *[pltpu.VMEM(value.shape, value.dtype) for value in back_args],
            pltpu.VMEM((cells, C1), bf16), pltpu.VMEM((KSIZE * CIN, C1), f32), pltpu.VMEM((LANES, C1), f32),
            pltpu.VMEM((CIN, C1), f32), pltpu.VMEM((devices * tail_used, LANES), f32), pltpu.VMEM((C1, LANES), f32),
            pltpu.SemaphoreType.DMA((5,)),
        ],
        micros=14,
        name="stem_back",
    )(got1, back1, vecs1, near1, stem_in, sums1, *back_args)[0]
    tail, early_state = tie(tail, early_steps[-1](early_state))

    chunk_sum = jnp.sum(swap(tail), axis=0)
    summed = scatter_planes(scatter_last(merge_planes([(state, late_planes), (early_state, early_planes)])))
    mine = lax.dynamic_slice_in_dim(summed.reshape(-1), at, shard_len)
    squares = jnp.sum(mine * mine) + jnp.sum(chunk_sum * chunk_sum)
    loss_part = jnp.sum(sums2[5, :LANES])
    lane = lax.broadcasted_iota(jnp.int32, chunk_sum.shape, 1)
    line = lax.broadcasted_iota(jnp.int32, chunk_sum.shape, 0)
    totals = jnp.where(lane == 0, loss_part, jnp.where(lane == 1, squares, 0.0))
    last = jnp.where(line == tail_used, totals, chunk_sum)
    last = swap(jnp.broadcast_to(last[None], (devices,) + last.shape))
    tail_flat = last[:, :tail_used].reshape(devices * tail_used, LANES)
    totals = jnp.sum(last[:, tail_used, :2], axis=0)
    loss_total, norm = totals[0], jnp.sqrt(totals[1])
    row, lane = count_places(C1)[1]
    count = jnp.sum(got1[:, row, lane])
    tail_flat = jnp.pad(tail_flat, ((0, tall), (0, 0)))
    line = jnp.minimum(me * shard_len // 2048 * 16, devices * tail_used)
    mine_tail = lax.dynamic_slice_in_dim(tail_flat, line, tall).reshape(-1)
    mine = mine + lax.dynamic_slice_in_dim(mine_tail, at, shard_len)
    clipped = mine * jnp.minimum(1.0, CLIP / norm)
    first = BETA_ONE * moment1 + (1.0 - BETA_ONE) * clipped
    second = BETA_TWO * moment2 + (1.0 - BETA_TWO) * clipped * clipped
    ratio = first / (1.0 - BETA_ONE**STEP) / (jnp.sqrt(second / (1.0 - BETA_TWO**STEP)) + ADAM_EPS)
    updated = params - LRATE * (ratio + DECAY * params)
    return (loss_total, count, norm, updated, first, second)


def solution(mesh):
    in_specs = (
        P("lvl", None, "lat", None),
        P("lvl", None, "lat", None),
        P("lat", "lvl"),
        P(),
        P(("lat", "lvl")),
        P(("lat", "lvl")),
        P(("lat", "lvl")),
    )
    out_specs = (P(), P(), P(), P(("lat", "lvl")), P(("lat", "lvl")), P(("lat", "lvl")))
    return jax.shard_map(body, mesh=mesh, in_specs=in_specs, out_specs=out_specs, check_vma=False)
```
